128 devices in a mesh: tile: 32 (over y, z, core), grp: 4 (over x).
Axes of the slice: x: 4, y: 4, z: 4, core: 2. Of those that a mesh axis runs over, the one named last changes fastest.
Arguments:
- flood_state: float32 [4, 128, 3, 256, 256], P('grp', 'tile'), may hold values from -1.6 to 3.5, as said below
- terrain: float32 [4, 128, 2, 256, 256], P('grp', 'tile'), may hold values from 0 to 1.5, as said below
- destination: int32 [4, 128], P('grp'), may hold values from 0 to 127, as said below
- wet_mask: int32 [4, 128], P('grp', 'tile'), may hold values from 0 to 1, as said below
- neighbours: int32 [4, 128, 4], P('grp', 'tile'), may hold values from -1 to 7, as said below
- inflow_cells: int32 [4, 128, 16], P('grp', 'tile'), may hold values from 0 to 65535
- inflow_rates: float32 [4, 128, 16], P('grp', 'tile'), may hold values from 1 to 50
Outputs:
- new_state: float32 [4, 128, 3, 256, 256], P('grp', 'tile')
The draws below stay inside these ranges and needn't reach their ends.
Inputs may be any that keep to these rules, and one draw needn't show every extreme that they name: `flood_state`: field 0 is the water depth, 1.5 to 3.5; fields 1 and 2 the unit discharges. `terrain`: field 0 is the bed elevation, 0 to 1.5; field 1 the Manning coefficient, 0.03 to 0.3. `destination`: in each band a permutation of the positions; the 4 blocks of device t (positions t * 4 to t * 4 + 3) go to the devices (t + k) modulo 32 of the same band for k = 0 to 3, one block to each. `wet_mask`: a dry block has only -1 entries and no entry names it. `neighbours`: entries follow the encoding of the steps, from -1 to 7, and are mutual: if a block names another on one side, that one names it on the opposite side.
All inputs are finite; a program needn't handle non-finite values.
Results may differ from the reference program's by a relative error of at most 0.00002.
Values sent between devices are 32-bit elements; how exact they have to be, the bound alone decides.
No kernel may reach another device: no remote copies, remote signals or barrier semaphores. Data moves between devices by JAX's collectives and lax.ppermute only.
A program may use at most 64 MiB of HBM per device.

```python
import math
import jax
import jax.numpy as jnp
from jax import lax

BLOCK_SIDE = 256
PATCH_ROWS = 1
PATCH_COLS = 4
TIME_STEPS = 2
RIVERS = 16
BLOCKS_DEV = 4
ROW_SLOTS = 128
N_TILE = 32
N_GRP = 4


def layout(key):
    wet_key = jax.random.fold_in(key, 101)
    place_key = jax.random.fold_in(key, 102)
    wet_grid = (jax.random.randint(wet_key, (N_GRP * PATCH_ROWS, N_TILE * PATCH_COLS), 0, 4) > 0).astype(jnp.int32)
    place_keys = jax.random.split(place_key, N_GRP * N_TILE)

    def shuffle(perm_key):
        return jax.random.permutation(perm_key, BLOCKS_DEV).astype(jnp.int32)
    place = jax.vmap(shuffle)(place_keys).reshape(N_GRP, N_TILE, BLOCKS_DEV)
    position = jnp.argsort(place, axis=-1).astype(jnp.int32)
    grp_ids = jnp.arange(N_GRP, dtype=jnp.int32)[:, None, None]
    tile_ids = jnp.arange(N_TILE, dtype=jnp.int32)[None, :, None]
    grid_row = grp_ids * PATCH_ROWS + position // PATCH_COLS
    grid_col = tile_ids * PATCH_COLS + position % PATCH_COLS
    own_wet = wet_grid[grid_row, grid_col]

    def side(row_step, col_step):
        near_row = grid_row + row_step
        near_col = grid_col + col_step
        inside = (near_row >= 0) & (near_row < N_GRP * PATCH_ROWS) & (near_col >= 0) & (near_col < N_TILE * PATCH_COLS)
        near_row = jnp.clip(near_row, 0, N_GRP * PATCH_ROWS - 1)
        near_col = jnp.clip(near_col, 0, N_TILE * PATCH_COLS - 1)
        near_grp = near_row // PATCH_ROWS
        near_tile = near_col // PATCH_COLS
        near_slot = place[near_grp, near_tile, near_row % PATCH_ROWS * PATCH_COLS + near_col % PATCH_COLS]
        same_dev = (near_grp == grp_ids) & (near_tile == tile_ids)
        entry = jnp.where(same_dev, near_slot, BLOCKS_DEV + near_slot)
        alive = inside & (own_wet == 1) & (wet_grid[near_row, near_col] == 1)
        return jnp.where(alive, entry, -1).astype(jnp.int32)
    sides = jnp.stack([side(0, -1), side(0, 1), side(-1, 0), side(1, 0)], axis=-1)
    return (own_wet.reshape(N_GRP, N_TILE * BLOCKS_DEV), sides.reshape(N_GRP, N_TILE * BLOCKS_DEV, 4))


def draw_wet_mask(key, part):
    shared = layout(key)
    return shared[0]


def draw_neighbours(key, part):
    shared = layout(key)
    return shared[1]


def draw_destination(key, part):
    key = jax.random.fold_in(key, 5)

    def shuffle(perm_key):
        return jax.random.permutation(perm_key, BLOCKS_DEV).astype(jnp.int32)

    def one_band(band_key):
        offset_key, slot_key = jax.random.split(band_key)
        offsets = jax.vmap(shuffle)(jax.random.split(offset_key, N_TILE))
        orders = jax.vmap(shuffle)(jax.random.split(slot_key, N_TILE))
        tiles = jnp.arange(N_TILE, dtype=jnp.int32)[:, None]
        target = (tiles + offsets) % N_TILE
        landing = orders[target, offsets]
        return (target * BLOCKS_DEV + landing).reshape(-1).astype(jnp.int32)
    return jax.vmap(one_band)(jax.random.split(key, N_GRP))


def draw_flood_state(key, part):
    key = jax.random.fold_in(key, 11)
    depth_key, flow_key = jax.random.split(key)
    depth_shape = (N_GRP, ROW_SLOTS, 1, BLOCK_SIDE, BLOCK_SIDE)
    flow_shape = (N_GRP, ROW_SLOTS, 2, BLOCK_SIDE, BLOCK_SIDE)
    depths = 1.5 + 2.0 * jax.random.uniform(depth_key, depth_shape, jnp.float32)
    fluxes = jnp.clip(0.4 * jax.random.normal(flow_key, flow_shape, jnp.float32), -1.6, 1.6)
    return jnp.concatenate([depths, fluxes], axis=2)


def draw_terrain(key, part):
    key = jax.random.fold_in(key, 12)
    bed_key, rough_key = jax.random.split(key)
    shape = (N_GRP, ROW_SLOTS, 1, BLOCK_SIDE, BLOCK_SIDE)
    low_log = jnp.log(0.03)
    bed_level = 1.5 * jax.random.uniform(bed_key, shape, jnp.float32)
    manning = jnp.exp(low_log + jnp.log(10.0) * jax.random.uniform(rough_key, shape, jnp.float32))
    manning = jnp.clip(manning, 0.03, 0.3)
    return jnp.concatenate([bed_level, manning], axis=2)


def place_ends(values, stream_key, smallest, high):
    longest = values.shape.index(max(values.shape))
    spots = []
    for shift in (0, 1):
        where = [jax.random.randint(jax.random.fold_in(stream_key, axis), (), 0, length) for axis, length in enumerate(values.shape)]
        where[longest] = (where[longest] + shift) % values.shape[longest]
        spots.append(tuple(where))
    return values.at[spots[0]].set(smallest).at[spots[1]].set(high)


def shard_levels(rng, dims, cuts, least, top_value):
    def one(dim, parts):
        draws = jax.random.uniform(jax.random.fold_in(jax.random.fold_in(rng, 6), dim), (parts,), jnp.float32, least / len(cuts), top_value / len(cuts))
        return jnp.repeat(jnp.exp(draws), dims[dim] // parts).reshape((-1,) + (1,) * (len(dims) - dim - 1))

    loudness = one(*cuts[0])
    for cut in cuts[1:]:
        loudness = loudness * one(*cut)
    return loudness


def setup_inputs(seed: int = 0) -> dict:
    key_of = jax.random.split(jax.random.key(seed), 8)
    flood_state = draw_flood_state(jax.random.fold_in(key_of[7], 71), 0)
    terrain = draw_terrain(jax.random.fold_in(key_of[7], 71), 0)
    destination = draw_destination(jax.random.fold_in(key_of[7], 71), 0)
    wet_mask = draw_wet_mask(jax.random.fold_in(key_of[7], 71), 0)
    neighbours = draw_neighbours(jax.random.fold_in(key_of[7], 71), 0)
    inflow_cells = place_ends(jax.random.randint(key_of[5], (N_GRP, ROW_SLOTS, RIVERS), 0, BLOCK_SIDE * BLOCK_SIDE), jax.random.fold_in(key_of[5], 1), 0, (BLOCK_SIDE * BLOCK_SIDE) - 1).astype(jnp.int32)
    inflow_rates = jnp.clip(jnp.exp(math.log(50.0) - 3.912023 * jax.random.uniform(key_of[6], (N_GRP, ROW_SLOTS, RIVERS), jnp.float32) ** shard_levels(key_of[6], (N_GRP, ROW_SLOTS, RIVERS), ((0, 4), (1, 32)), -0.2, 0.2)), 1.0, 50.0)
    return dict(flood_state=flood_state, terrain=terrain, destination=destination, wet_mask=wet_mask, neighbours=neighbours, inflow_cells=inflow_cells, inflow_rates=inflow_rates)


GRAVITY = 9.81
SPACING = 10.0
TIMESTEP = 0.2
CENTRE_WEIGHT = 0.7
DEPTH_FLOOR = 0.1


def face_flux(depths, fluxes, bed_level, manning, along, extent):
    def window(values, first):
        return lax.slice_in_dim(values, first, first + extent + 1, axis=along)

    left_h = window(depths, 1)
    right_h = window(depths, 2)
    left_z = window(bed_level, 1)
    right_z = window(bed_level, 2)
    rough_n = window(manning, 1)
    flow_mid = window(fluxes, 1)
    flow_left = window(fluxes, 0)
    flow_right = window(fluxes, 2)
    left_eta = left_h + left_z
    right_eta = right_h + right_z
    flow_depth = jnp.maximum(left_eta, right_eta) - jnp.maximum(left_z, right_z)
    floored = jnp.maximum(flow_depth, DEPTH_FLOOR)
    blended = CENTRE_WEIGHT * flow_mid + 0.5 * (1.0 - CENTRE_WEIGHT) * (flow_left + flow_right)
    slope_term = GRAVITY * flow_depth * TIMESTEP * (right_eta - left_eta) / SPACING
    friction = 1.0 + GRAVITY * TIMESTEP * rough_n * rough_n * jnp.abs(flow_mid) * jnp.exp(-7.0 / 3.0 * jnp.log(floored))
    return (blended - slope_term) / friction


def edge_weights(values, low_flag, high_flag, along, extent):
    weights = jnp.concatenate([low_flag[None], jnp.ones((extent - 1,), values.dtype), high_flag[None]])
    if along == 1:
        return values * weights[None, :]
    return values * weights[:, None]


def block_step(current, ground, west_rim, east_rim, south_rim, north_rim, has_side, cell_ids, rate_vals, wetness):
    extent = current.shape[-1]
    fields = jnp.concatenate([current, ground], axis=0)
    across = jnp.concatenate([west_rim, fields, east_rim], axis=2)
    upward = jnp.concatenate([south_rim, fields, north_rim], axis=1)
    flux_x = face_flux(across[0], across[1], across[3], across[4], 1, extent)
    flux_x = edge_weights(flux_x, has_side[0], has_side[1], 1, extent)
    flux_y = face_flux(upward[0], upward[2], upward[3], upward[4], 0, extent)
    flux_y = edge_weights(flux_y, has_side[2], has_side[3], 0, extent)
    source = jnp.zeros((extent * extent,), current.dtype).at[cell_ids].add(rate_vals).reshape(extent, extent)
    new_depth = current[0] + TIMESTEP / SPACING * (flux_x[:, :-1] - flux_x[:, 1:] + flux_y[:-1] - flux_y[1:]) + TIMESTEP / (SPACING * SPACING) * source
    return jnp.stack([new_depth, flux_x[:, 1:], flux_y[1:]]) * wetness


def neighbour_rims(strips, entries, band_ids, slot_ids, band_step, device_step, has_one):
    groups, slots = entries.shape
    same_dev = entries < BLOCKS_DEV
    device = slot_ids // BLOCKS_DEV
    source_slot = jnp.where(same_dev, device * BLOCKS_DEV + entries, (device + device_step) * BLOCKS_DEV + entries - BLOCKS_DEV)
    source_band = jnp.where(same_dev, band_ids, band_ids + band_step)
    source_slot = jnp.clip(source_slot, 0, slots - 1).astype(jnp.int32)
    source_band = jnp.clip(source_band, 0, groups - 1).astype(jnp.int32)
    return strips[source_band, source_slot] * has_one[:, :, None, None, None]


def reference(flood_state, terrain, destination, wet_mask, neighbours, inflow_cells, inflow_rates):
    groups, slots = destination.shape
    extent = flood_state.shape[-1]
    band_col = jnp.arange(groups, dtype=jnp.int32)[:, None]
    current = jnp.zeros_like(flood_state).at[band_col, destination].set(flood_state)
    band_ids = jnp.broadcast_to(band_col, (groups, slots))
    slot_ids = jnp.broadcast_to(jnp.arange(slots, dtype=jnp.int32)[None, :], (groups, slots))
    has_side = (neighbours >= 0).astype(flood_state.dtype)
    wetness = wet_mask.astype(flood_state.dtype)
    devices = groups * slots // BLOCKS_DEV
    for turn_no in range(TIME_STEPS):
        first_cols = jnp.concatenate([current[..., :, :2], terrain[..., :, :2]], axis=2)
        last_cols = jnp.concatenate([current[..., :, -2:], terrain[..., :, -2:]], axis=2)
        first_rows = jnp.concatenate([current[..., :2, :], terrain[..., :2, :]], axis=2)
        last_rows = jnp.concatenate([current[..., -2:, :], terrain[..., -2:, :]], axis=2)
        west_rim = neighbour_rims(last_cols, neighbours[..., 0], band_ids, slot_ids, 0, -1, has_side[..., 0])
        east_rim = neighbour_rims(first_cols, neighbours[..., 1], band_ids, slot_ids, 0, 1, has_side[..., 1])
        south_rim = neighbour_rims(last_rows, neighbours[..., 2], band_ids, slot_ids, -1, 0, has_side[..., 2])
        north_rim = neighbour_rims(first_rows, neighbours[..., 3], band_ids, slot_ids, 1, 0, has_side[..., 3])

        def per_device(pieces):
            return jax.vmap(block_step)(*pieces)

        pieces = (current, terrain, west_rim, east_rim, south_rim, north_rim, has_side, inflow_cells, inflow_rates, wetness)
        pieces = tuple(piece.reshape((devices, BLOCKS_DEV) + piece.shape[2:]) for piece in pieces)
        result = lax.map(per_device, pieces)
        current = result.reshape(groups, slots, 3, extent, extent)
    return current
```

```python
import functools

import jax
import jax.numpy as jnp
from jax import lax
from jax.experimental import pallas as pl
from jax.experimental.pallas import tpu as pltpu
from jax.sharding import PartitionSpec as P

F32 = jnp.float32
GRAVITY = 9.81
SPACING = 10.0
TIMESTEP = 0.2
CENTRE_WEIGHT = 0.7
DEPTH_FLOOR = 0.1
SIDE = 256
HALF = 128
BLOCKS = 4
RIVERS = 16
PAD = 8
ROWS = 16

ANY = pl.BlockSpec(memory_space=pl.ANY)
VMEM = pl.BlockSpec(memory_space=pltpu.VMEM)
SMEM = pl.BlockSpec(memory_space=pltpu.SMEM)
SHIFTS = (3, 2, 1)


def shape(*dims):
    return jax.ShapeDtypeStruct(dims, F32)


def cost(flops, bytes_accessed):
    return pl.CostEstimate(flops=flops, bytes_accessed=bytes_accessed, transcendentals=0)


def face(eta_l, eta_r, z_l, z_r, rough, flow_left, flow_mid, flow_right):
    depth = jnp.maximum(eta_l, eta_r) - jnp.maximum(z_l, z_r)
    floored = jnp.maximum(depth, DEPTH_FLOOR)
    blended = CENTRE_WEIGHT * flow_mid + 0.5 * (1.0 - CENTRE_WEIGHT) * (flow_left + flow_right)
    slope = (GRAVITY * TIMESTEP / SPACING) * depth * (eta_r - eta_l)
    friction = 1.0 + (GRAVITY * TIMESTEP) * rough * rough * jnp.abs(flow_mid) * jnp.exp(
        (-7.0 / 3.0) * jnp.log(floored)
    )
    return (blended - slope) / friction


def tile_offset(dest_ref, tile, slot):
    tiles = lax.axis_size("tile")
    return lax.rem(lax.div(dest_ref[0, tile * BLOCKS + slot], BLOCKS) - tile + tiles, tiles)


def leaving_slot(dest_ref, shift):
    me = lax.axis_index("tile")
    slot = jnp.int32(0)
    for j in range(1, BLOCKS):
        slot = jnp.where(tile_offset(dest_ref, me, j) == shift, j, slot)
    return slot


def landing_slot(dest_ref, shift):
    tiles = lax.axis_size("tile")
    sender = lax.rem(lax.axis_index("tile") - shift + tiles, tiles)
    slot = jnp.int32(0)
    for j in range(BLOCKS):
        place = lax.rem(dest_ref[0, sender * BLOCKS + j], BLOCKS)
        slot = jnp.where(tile_offset(dest_ref, sender, j) == shift, place, slot)
    return slot


def lanes(rows, columns):
    return lax.broadcasted_iota(jnp.int32, (rows, columns), 1)


def prepare_kernel(dest, state, out1, out2, out3, strip0, strip1, strip2, strip3, held, in_sem, out_sem):
    outs = (None, out1, out2, out3)
    strips = (strip0, strip1, strip2, strip3)
    order = SHIFTS + (0,)
    slots = {k: leaving_slot(dest, k) for k in order}
    loads = {k: pltpu.make_async_copy(state.at[0, slots[k]], held.at[k], in_sem.at[k]) for k in order}
    sends = {k: pltpu.make_async_copy(held.at[k], outs[k], out_sem.at[k]) for k in SHIFTS}
    for k in order:
        loads[k].start()
    lane = lanes(SIDE, HALF)
    for k in order:
        loads[k].wait()
        if k:
            sends[k].start()
        west = [held[k, f, :, :HALF] for f in range(3)]
        east = [held[k, f, :, HALF:] for f in range(3)]
        packed = jnp.where(lane < 3, west[0], pltpu.roll(west[1], 3, 1))
        packed = jnp.where(lane < 6, packed, pltpu.roll(west[2], 6, 1))
        packed = jnp.where(lane < 8, packed, pltpu.roll(east[0], 10, 1))
        packed = jnp.where(lane < 10, packed, pltpu.roll(east[1], 13, 1))
        packed = jnp.where(lane < 13, packed, pltpu.roll(east[2], 14, 1))
        turned = packed.T
        strips[k][0] = turned[0:8]
        strips[k][2] = turned[8:16]
        strips[k][1, 0:3] = held[k, 0, 0:3]
        strips[k][1, 3:6] = held[k, 2, 0:3]
        strips[k][1, 6:8] = held[k, 1, 0:2]
        strips[k][3, 0:2] = held[k, 0, SIDE - 2 : SIDE]
        strips[k][3, 2:5] = held[k, 2, SIDE - 3 : SIDE]
        strips[k][3, 5:6] = held[k, 1, SIDE - 1 : SIDE]
        strips[k][3, 6:8] = jnp.zeros((2, SIDE), F32)
    for k in SHIFTS:
        sends[k].wait()


def prepare(dest, state):
    return pl.pallas_call(
        prepare_kernel,
        out_shape=[shape(3, SIDE, SIDE)] * 3 + [shape(4, 8, SIDE)] * 4,
        in_specs=[SMEM, ANY],
        out_specs=[ANY] * 3 + [VMEM] * 4,
        scratch_shapes=[
            pltpu.VMEM((BLOCKS, 3, SIDE, SIDE), F32),
            pltpu.SemaphoreType.DMA((BLOCKS,)),
            pltpu.SemaphoreType.DMA((BLOCKS,)),
        ],
        compiler_params=pltpu.CompilerParams(vmem_limit_bytes=16 << 20),
        cost_estimate=cost(0, 6 << 20),
    )(dest, state)


def ground_kernel(terrain, low, high):
    lane = lanes(SIDE, HALF)
    for b in range(BLOCKS):
        west = [terrain[0, b, f, :, :HALF] for f in range(2)]
        east = [terrain[0, b, f, :, HALF:] for f in range(2)]
        packed = jnp.where(lane < 3, west[0], pltpu.roll(west[1], 3, 1))
        packed = jnp.where(lane < 5, packed, pltpu.roll(east[0], 7, 1))
        packed = jnp.where(lane < 7, packed, pltpu.roll(east[1], 9, 1))
        turned = packed.T
        for q in range(5):
            low[q, b : b + 1] = turned[q : q + 1]
        for q in range(4):
            high[q, b : b + 1] = turned[5 + q : 6 + q]
        for q in range(3):
            low[q, 4 + b : 5 + b] = terrain[0, b, 0, q : q + 1]
        for q in range(2):
            low[3 + q, 4 + b : 5 + b] = terrain[0, b, 1, q : q + 1]
            high[q, 4 + b : 5 + b] = terrain[0, b, 0, SIDE - 2 + q : SIDE - 1 + q]
            high[2 + q, 4 + b : 5 + b] = terrain[0, b, 1, SIDE - 2 + q : SIDE - 1 + q]


def ground_strips(terrain):
    return pl.pallas_call(
        ground_kernel,
        out_shape=[shape(5, 8, SIDE), shape(4, 8, SIDE)],
        in_specs=[VMEM],
        out_specs=[VMEM] * 2,
        compiler_params=pltpu.CompilerParams(vmem_limit_bytes=16 << 20),
        cost_estimate=cost(0, 2 << 20),
    )(terrain)


def arrange_kernel(dest, strip0, strip1, strip2, strip3, ground_low, ground_high, low, high, west, south, east, north):
    for out in (west, south, east, north):
        out[...] = jnp.zeros_like(out)
    for k, strip in enumerate((strip0, strip1, strip2, strip3)):
        slot = landing_slot(dest, k)
        for side, (low_out, high_out) in enumerate(((west, east), (south, north))):
            row = pl.ds(side * 4 + slot, 1)
            for q in range(8):
                low[q, row] = strip[side, q : q + 1]
            for q in range(6):
                high[q, row] = strip[2 + side, q : q + 1]
            low_out[slot, 0:1] = strip[side, 0:1]
            low_out[slot, 1:2] = strip[side, 3:4]
            high_out[slot, 0:1] = strip[2 + side, 1:2]
            high_out[slot, 1:3] = strip[2 + side, 3:5]
    for b in range(BLOCKS):
        for side, (low_out, high_out) in enumerate(((west, east), (south, north))):
            sub = slice(side * 4 + b, side * 4 + b + 1)
            low_out[b, 2:3] = ground_low[0, sub]
            high_out[b, 3:4] = ground_high[1, sub]
            high_out[b, 4:5] = ground_high[3, sub]


def arrange(dest, strips, ground_low, ground_high):
    return pl.pallas_call(
        arrange_kernel,
        out_shape=[shape(8, 8, SIDE), shape(6, 8, SIDE)] + [shape(BLOCKS, 8, SIDE)] * 4,
        in_specs=[SMEM] + [VMEM] * 6,
        out_specs=[VMEM] * 6,
        cost_estimate=cost(0, 0),
    )(dest, *strips, ground_low, ground_high)


def pick(entry, own, other):
    near = own[jnp.clip(entry, 0, BLOCKS - 1)]
    far = other[jnp.clip(entry - BLOCKS, 0, BLOCKS - 1)]
    return jnp.where(entry >= BLOCKS, far, near)


def gather_rims(entries, own, other, rim_low, rim_high, has, low_count, high_count):
    for b in range(BLOCKS):
        for side in range(2):
            sub = slice(side * 4 + b, side * 4 + b + 1)
            entry = entries[0, b, 2 * side]
            alive = entry >= 0
            rows = jnp.where(alive, pick(entry, own[2 + side], other[2 + side]), 0.0)
            for q in range(low_count):
                rim_low[q, sub] = rows[q : q + 1]
            has[0, sub] = jnp.full((1, SIDE), jnp.where(alive, 1.0, 0.0), F32)
            entry = entries[0, b, 2 * side + 1]
            alive = entry >= 0
            rows = jnp.where(alive, pick(entry, own[side], other[side]), 0.0)
            for q in range(high_count):
                rim_high[q, sub] = rows[q : q + 1]
            has[1, sub] = jnp.full((1, SIDE), jnp.where(alive, 1.0, 0.0), F32)


def sides_swapped(x):
    return pltpu.roll(x, 4, 0)


def along_edge(h, z, rough, flow, spot, face_before, face_first, face_last):
    lane = lanes(8, SIDE)
    eta = h + z
    flux = face(
        eta, pltpu.roll(eta, SIDE - 1, 1), z, pltpu.roll(z, SIDE - 1, 1), rough,
        pltpu.roll(flow, 1, 1), flow, pltpu.roll(flow, SIDE - 1, 1),
    )
    here = slice(spot, spot + 1)
    flux = jnp.where(lane == 0, sides_swapped(face_first)[:, here], flux)
    flux = jnp.where(lane == SIDE - 1, sides_swapped(face_last)[:, here], flux)
    lower = jnp.where(lane == 0, sides_swapped(face_before)[:, here], pltpu.roll(flux, 1, 1))
    return lower - flux


def first_edges_kernel(
    entries, wet, normal_cell, tangent_cell, rates, low, high, ground_low, ground_high,
    own_w, own_s, own_e, own_n, oth_w, oth_s, oth_e, oth_n,
    faces, edge, rim_ground, west, south, east, north,
    rim_low, rim_high, has, wetness,
):
    gather_rims(
        entries, (own_w, own_s, own_e, own_n), (oth_w, oth_s, oth_e, oth_n), rim_low, rim_high, has, 5, 3
    )
    for b in range(BLOCKS):
        value = jnp.full((1, SIDE), wet[0, b].astype(F32), F32)
        wetness[b : b + 1] = value
        wetness[4 + b : 5 + b] = value
    hm, qmm, qm, zm, nm = (rim_low[q] for q in range(5))
    hp, qp, zp = (rim_high[q] for q in range(3))
    h0, h1, h2, q0, q1, q2, t0, t1 = (low[q] for q in range(8))
    z0, z1, z2, n0, n1 = (ground_low[q] for q in range(5))
    hy, hz, qx, qy, qz, tz = (high[q] for q in range(6))
    zy, zz, ny, nz = (ground_high[q] for q in range(4))
    face_m = face(hm + zm, h0 + z0, zm, z0, nm, qmm, qm, q0) * has[0]
    face_0 = face(h0 + z0, h1 + z1, z0, z1, n0, qm, q0, q1)
    face_1 = face(h1 + z1, h2 + z2, z1, z2, n1, q0, q1, q2)
    face_y = face(hy + zy, hz + zz, zy, zz, ny, qx, qy, qz)
    face_z = face(hz + zz, hp + zp, zz, zp, nz, qy, qz, qp) * has[1]
    lane = lanes(8, SIDE)
    spill = [jnp.zeros((8, SIDE), F32) for _ in range(3)]
    for p in range(RIVERS):
        here = lane == tangent_cell[:, p : p + 1]
        rate = jnp.where(here, rates[:, p : p + 1], 0.0)
        for i, place in enumerate((0, 1, SIDE - 1)):
            spill[i] = spill[i] + jnp.where(normal_cell[:, p : p + 1] == place, rate, 0.0)
    ratio = TIMESTEP / SPACING
    gain = TIMESTEP / (SPACING * SPACING)
    beside = (face_m, face_0, face_z)
    wets = wetness[...]
    new_0 = (h0 + ratio * (face_m - face_0 + along_edge(h0, z0, n0, t0, 0, *beside)) + gain * spill[0]) * wets
    new_1 = (h1 + ratio * (face_0 - face_1 + along_edge(h1, z1, n1, t1, 1, *beside)) + gain * spill[1]) * wets
    new_z = (hz + ratio * (face_y - face_z + along_edge(hz, zz, nz, tz, SIDE - 1, *beside)) + gain * spill[2]) * wets
    faces[0] = face_m
    faces[1] = face_0
    faces[2] = face_z
    rim_ground[0] = zm
    rim_ground[1] = nm
    rim_ground[2] = zp
    flow_0, flow_1, flow_y, flow_z = (f * wets for f in (face_0, face_1, face_y, face_z))
    for i, value in enumerate((new_0, new_1, flow_0, flow_1, new_z, flow_y, flow_z)):
        edge[i] = value
    for out in (west, south, east, north):
        out[...] = jnp.zeros_like(out)
    for b in range(BLOCKS):
        for side, (low_out, high_out) in enumerate(((west, east), (south, north))):
            sub = slice(side * 4 + b, side * 4 + b + 1)
            low_out[b, 0:1] = new_0[sub]
            low_out[b, 1:2] = flow_0[sub]
            high_out[b, 0:1] = new_z[sub]
            high_out[b, 1:2] = flow_y[sub]
            high_out[b, 2:3] = flow_z[sub]


def first_edges(entries, wet, normal_cell, tangent_cell, rates, low, high, ground, own, other):
    return pl.pallas_call(
        first_edges_kernel,
        out_shape=[shape(3, 8, SIDE), shape(7, 8, SIDE), shape(3, 8, SIDE)] + [shape(BLOCKS, 8, SIDE)] * 4,
        in_specs=[SMEM, SMEM] + [VMEM] * 15,
        out_specs=[VMEM] * 7,
        scratch_shapes=[
            pltpu.VMEM((5, 8, SIDE), F32),
            pltpu.VMEM((3, 8, SIDE), F32),
            pltpu.VMEM((2, 8, SIDE), F32),
            pltpu.VMEM((8, SIDE), F32),
        ],
        cost_estimate=cost(0, 0),
    )(entries, wet, normal_cell, tangent_cell, rates, low, high, *ground, *own, *other)


def second_edges_kernel(
    entries, faces, edge, rim_ground, ground_low, ground_high,
    own_w, own_s, own_e, own_n, oth_w, oth_s, oth_e, oth_n,
    columns, rows, rim_low, rim_high, has, stack,
):
    gather_rims(
        entries, (own_w, own_s, own_e, own_n), (oth_w, oth_s, oth_e, oth_n), rim_low, rim_high, has, 3, 2
    )
    hm, qmm, qm = (rim_low[q] for q in range(3))
    hp, qp = (rim_high[q] for q in range(2))
    zm, nm, zp = (rim_ground[q] for q in range(3))
    h0, h1, q0, q1, hz, qy, qz = (edge[q] for q in range(7))
    z0, z1, n0 = ground_low[0], ground_low[1], ground_low[3]
    zz, nz = ground_high[1], ground_high[3]
    face_m = face(hm + zm, h0 + z0, zm, z0, nm, qmm, qm, q0) * has[0]
    face_0 = face(h0 + z0, h1 + z1, z0, z1, n0, qm, q0, q1)
    face_z = face(hz + zz, hp + zp, zz, zp, nz, qy, qz, qp) * has[1]
    every = (faces[0], faces[1], faces[2], face_m, face_0, face_z)
    stack[...] = jnp.zeros_like(stack)
    rows[...] = jnp.zeros_like(rows)
    for b in range(BLOCKS):
        for i, value in enumerate(every):
            stack[b * 8 + i : b * 8 + i + 1] = value[b : b + 1]
            rows[b, i : i + 1] = value[4 + b : 5 + b]
    turned = stack[...].T
    columns[0] = turned
    for b in range(1, BLOCKS):
        columns[b] = pltpu.roll(turned, HALF - 8 * b, 1)


def second_edges(entries, faces, edge, rim_ground, ground, own, other):
    return pl.pallas_call(
        second_edges_kernel,
        out_shape=[shape(BLOCKS, SIDE, HALF), shape(BLOCKS, 8, SIDE)],
        in_specs=[SMEM] + [VMEM] * 13,
        out_specs=[VMEM] * 2,
        scratch_shapes=[
            pltpu.VMEM((3, 8, SIDE), F32),
            pltpu.VMEM((2, 8, SIDE), F32),
            pltpu.VMEM((2, 8, SIDE), F32),
            pltpu.VMEM((HALF, SIDE), F32),
        ],
        cost_estimate=cost(0, 0),
    )(entries, faces, edge, rim_ground, *ground, *own, *other)


def block_step(now, ground, spill, columns, rows, base, wetness, write):
    ratio = TIMESTEP / SPACING
    lane = lanes(ROWS, SIDE)
    sub = lax.broadcasted_iota(jnp.int32, (ROWS, SIDE), 0)

    def chunk(i, below):
        first = i * ROWS

        def at(ref, field, shift):
            return ref[field, pl.ds(first + (PAD + shift), ROWS), :]

        h, qx, qy = at(now, 0, 0), at(now, 1, 0), at(now, 2, 0)
        z, rough = at(ground, 0, 0), at(ground, 1, 0)
        eta = h + z
        flux_x = face(
            eta, pltpu.roll(eta, SIDE - 1, 1), z, pltpu.roll(z, SIDE - 1, 1), rough,
            pltpu.roll(qx, 1, 1), qx, pltpu.roll(qx, SIDE - 1, 1),
        )
        edge = columns[pl.ds(first, ROWS), :]
        flux_x = jnp.where(lane == 0, edge[:, base + 1 : base + 2], flux_x)
        flux_x = jnp.where(lane == SIDE - 1, edge[:, base + 2 : base + 3], flux_x)
        flux_w = jnp.where(lane == 0, edge[:, base : base + 1], pltpu.roll(flux_x, 1, 1))
        z_up = at(ground, 0, 1)
        flux_y = face(eta, at(now, 0, 1) + z_up, z, z_up, rough, at(now, 2, -1), qy, at(now, 2, 1))
        row = sub + first
        flux_y = jnp.where(row == 0, rows[base + 1 : base + 2], flux_y)
        flux_y = jnp.where(row == SIDE - 1, rows[base + 2 : base + 3], flux_y)
        flux_s = jnp.where(sub == 0, below, pltpu.roll(flux_y, 1, 0))
        depth = h + ratio * (flux_w - flux_x + flux_s - flux_y) + spill[pl.ds(first, ROWS), :]
        write(first, depth * wetness, flux_x * wetness, flux_y * wetness)
        return flux_y[ROWS - 1 : ROWS]

    below = rows[base : base + 1]
    for i in range(SIDE // ROWS):
        below = chunk(i, below)


def block_kernel(
    shift, dest, wet, cells, rates, state, terrain, columns, rows, *refs
):
    out, now, then, ground, column, row, spill, done, sems = refs[-9:]
    slot = landing_slot(dest, shift)
    if shift == 0:
        source = state.at[0, leaving_slot(dest, 0)]
    else:
        source = state
    inner = pl.ds(PAD, SIDE)
    copies = [
        pltpu.make_async_copy(source, now.at[:, inner], sems.at[0]),
        pltpu.make_async_copy(terrain.at[0, slot], ground.at[:, inner], sems.at[1]),
        pltpu.make_async_copy(columns.at[slot], column, sems.at[2]),
        pltpu.make_async_copy(rows.at[slot], row, sems.at[3]),
    ]
    for copy in copies:
        copy.start()
    gain = TIMESTEP / (SPACING * SPACING)
    spill[...] = jnp.zeros_like(spill)
    lane = lanes(1, SIDE)
    for p in range(RIVERS):
        cell = cells[0, slot, p]
        at = pl.ds(lax.div(cell, SIDE), 1)
        spill[at] = spill[at] + jnp.where(lane == lax.rem(cell, SIDE), gain * rates[0, slot, p], 0.0)
    wetness = wet[0, slot].astype(F32)
    for copy in copies:
        copy.wait()

    def keep(first, *fields):
        for f, value in enumerate(fields):
            then[f, pl.ds(first + PAD, ROWS), :] = value

    def finish(first, *fields):
        for f, value in enumerate(fields):
            done[f, pl.ds(first, ROWS), :] = value

    block_step(now, ground, spill, column, row, 0, wetness, keep)
    block_step(then, ground, spill, column, row, 3, wetness, finish)
    last = pltpu.make_async_copy(done, out.at[0, slot], sems.at[4])
    last.start()
    last.wait()


def run_block(shift, dest, wet, cells, rates, state, terrain, columns, rows, out):
    args = [dest, wet, cells, rates, state, terrain, columns, rows]
    specs = [SMEM] * 4 + [ANY] * 4
    aliases = {}
    if out is not None:
        aliases = {len(args): 0}
        args.append(out)
        specs.append(ANY)
    return pl.pallas_call(
        functools.partial(block_kernel, shift),
        out_shape=shape(1, BLOCKS, 3, SIDE, SIDE),
        in_specs=specs,
        out_specs=ANY,
        input_output_aliases=aliases,
        scratch_shapes=[
            pltpu.VMEM((3, SIDE + 2 * PAD, SIDE), F32),
            pltpu.VMEM((3, SIDE + 2 * PAD, SIDE), F32),
            pltpu.VMEM((2, SIDE + 2 * PAD, SIDE), F32),
            pltpu.VMEM((SIDE, HALF), F32),
            pltpu.VMEM((8, SIDE), F32),
            pltpu.VMEM((SIDE, SIDE), F32),
            pltpu.VMEM((3, SIDE, SIDE), F32),
            pltpu.SemaphoreType.DMA((5,)),
        ],
        compiler_params=pltpu.CompilerParams(vmem_limit_bytes=16 << 20),
        cost_estimate=cost(0, 0),
    )(*args)


def passed_along(x, axis, by):
    devices = lax.axis_size(axis)
    return lax.ppermute(x, axis, [(i, (i + by) % devices) for i in range(devices)])


def beside(packs):
    west, south, east, north = packs
    return (
        passed_along(west, "tile", -1),
        passed_along(south, "grp", -1),
        passed_along(east, "tile", 1),
        passed_along(north, "grp", 1),
    )


def body(flood_state, terrain, destination, wet_mask, neighbours, inflow_cells, inflow_rates):
    *outgoing, strip0, strip1, strip2, strip3 = prepare(destination, flood_state)
    strips = [strip0] + [passed_along(s, "tile", k) for k, s in ((1, strip1), (2, strip2), (3, strip3))]
    arrived = {k: passed_along(outgoing[k - 1], "tile", k) for k in SHIFTS}
    ground = ground_strips(terrain)
    low, high, *own = arrange(destination, strips, *ground)
    columns_of = jnp.bitwise_and(inflow_cells[0], SIDE - 1)
    rows_of = jnp.right_shift(inflow_cells[0], 8)
    normal_cell = jnp.concatenate([columns_of, rows_of])
    tangent_cell = jnp.concatenate([rows_of, columns_of])
    rates = jnp.concatenate([inflow_rates[0], inflow_rates[0]])
    faces, edge, rim_ground, *own2 = first_edges(
        neighbours, wet_mask, normal_cell, tangent_cell, rates, low, high, ground, own, beside(own)
    )
    columns, rows = second_edges(neighbours, faces, edge, rim_ground, ground, own2, beside(own2))
    out = None
    for k in (0,) + SHIFTS:
        state = arrived[k] if k else flood_state
        out = run_block(k, destination, wet_mask, inflow_cells, inflow_rates, state, terrain, columns, rows, out)
    return out


def solution(mesh):
    in_specs = (
        P("grp", "tile", None, None, None),
        P("grp", "tile", None, None, None),
        P("grp", None),
        P("grp", "tile"),
        P("grp", "tile", None),
        P("grp", "tile", None),
        P("grp", "tile", None),
    )
    out_specs = P("grp", "tile", None, None, None)
    return jax.shard_map(body, mesh=mesh, in_specs=in_specs, out_specs=out_specs, check_vma=False)
```

```python
import functools

import jax
import jax.numpy as jnp
from jax import lax
from jax.experimental import pallas as pl
from jax.experimental.pallas import tpu as pltpu
from jax.sharding import PartitionSpec as P

F32 = jnp.float32
GRAVITY = 9.81
SPACING = 10.0
TIMESTEP = 0.2
CENTRE_WEIGHT = 0.7
DEPTH_FLOOR = 0.1
SIDE = 256
HALF = 128
BLOCKS = 4
RIVERS = 16
ROWS = 64
GAIN = TIMESTEP / (SPACING * SPACING)
RATIO = TIMESTEP / SPACING

ANY = pl.BlockSpec(memory_space=pl.ANY)
VMEM = pl.BlockSpec(memory_space=pltpu.VMEM)
SMEM = pl.BlockSpec(memory_space=pltpu.SMEM)
HBM = pl.BlockSpec(memory_space=pltpu.HBM)
RING = 4
W_SHIFTS = (3, 1)
X_SHIFTS = (1, 3)


def shape(*dims):
    return jax.ShapeDtypeStruct(dims, F32)


def cost(flops, bytes_accessed):
    return pl.CostEstimate(flops=flops, bytes_accessed=bytes_accessed, transcendentals=0)


def face(eta_l, eta_r, z_l, z_r, rough, flow_left, flow_mid, flow_right):
    depth = jnp.maximum(eta_l, eta_r) - jnp.maximum(z_l, z_r)
    floored = jnp.maximum(depth, DEPTH_FLOOR)
    blended = CENTRE_WEIGHT * flow_mid + 0.5 * (1.0 - CENTRE_WEIGHT) * (flow_left + flow_right)
    slope = (GRAVITY * TIMESTEP / SPACING) * depth * (eta_r - eta_l)
    friction = 1.0 + (GRAVITY * TIMESTEP) * rough * rough * jnp.abs(flow_mid) * jnp.exp(
        (-7.0 / 3.0) * jnp.log(floored)
    )
    return (blended - slope) / friction


def core():
    return lax.rem(lax.axis_index("tile"), 2)


def params(mib):
    return pltpu.CompilerParams(vmem_limit_bytes=mib << 20)


def tile_offset(dest_ref, tile, slot):
    tiles = lax.axis_size("tile")
    return lax.rem(lax.div(dest_ref[0, tile * BLOCKS + slot], BLOCKS) - tile + tiles, tiles)


def leaving_slot(dest_ref, shift):
    me = lax.axis_index("tile")
    slot = jnp.int32(0)
    for j in range(1, BLOCKS):
        slot = jnp.where(tile_offset(dest_ref, me, j) == shift, j, slot)
    return slot


def landing_slot(dest_ref, shift, back=0):
    tiles = lax.axis_size("tile")
    sender = lax.rem(lax.axis_index("tile") - shift - back + 2 * tiles, tiles)
    slot = jnp.int32(0)
    for j in range(BLOCKS):
        place = lax.rem(dest_ref[0, sender * BLOCKS + j], BLOCKS)
        slot = jnp.where(tile_offset(dest_ref, sender, j) == shift, place, slot)
    return slot


def lanes(rows, columns):
    return lax.broadcasted_iota(jnp.int32, (rows, columns), 1)


def prepare_kernel(
    dest, state, terrain,
    own, block_a, block_w, block_x, low, high, pack0, pack1, pack2, pack3, pack4, pack_back, sems,
):
    slots = [leaving_slot(dest, k) for k in range(BLOCKS)]
    first_core = core() == 0
    slot_w = jnp.where(first_core, slots[1], slots[3])
    slot_x = jnp.where(first_core, slots[3], slots[1])
    held = (block_w, block_a, block_x, own)
    loads = [
        pltpu.make_async_copy(state.at[0, slot], ref, sems.at[i])
        for i, (slot, ref) in enumerate(zip((slot_w, slots[2], slot_x, slots[0]), held))
    ]
    for load in loads:
        load.start()
    lane = lanes(SIDE, HALF)

    def strips(ref, write):
        west = [ref[f, :, :HALF] for f in range(3)]
        east = [ref[f, :, HALF:] for f in range(3)]
        packed = jnp.where(lane < 3, west[0], pltpu.roll(west[1], 3, 1))
        packed = jnp.where(lane < 6, packed, pltpu.roll(west[2], 6, 1))
        packed = jnp.where(lane < 8, packed, pltpu.roll(east[0], 10, 1))
        packed = jnp.where(lane < 10, packed, pltpu.roll(east[1], 13, 1))
        packed = jnp.where(lane < 13, packed, pltpu.roll(east[2], 14, 1))
        turned = packed.T
        south = jnp.concatenate([ref[0, 0:3], ref[2, 0:3], ref[1, 0:2]])
        north = jnp.concatenate(
            [ref[0, SIDE - 2 : SIDE], ref[2, SIDE - 3 : SIDE], ref[1, SIDE - 1 : SIDE], jnp.zeros((2, SIDE), F32)]
        )
        write(turned[0:8], south, turned[8:16], north)

    strip_out = (pack0, pack1, pack2, pack3)
    west_out = (pack_back.at[0], pack0.at[4], pack1.at[5], pack2.at[5])
    east_out = (pack1.at[4], pack2.at[4], pack3.at[4], pack4.at[0])

    def write(k, west, south, east, north):
        for i, value in enumerate((west, south, east, north)):
            strip_out[k][i] = value
        west_out[k][...] = west
        east_out[k][...] = east

    def write_by_core(first, second):
        def both(*values):
            pl.when(first_core)(lambda: write(first, *values))
            pl.when(jnp.logical_not(first_core))(lambda: write(second, *values))

        return both

    for b in range(BLOCKS):
        west = [terrain[0, b, f, :, :HALF] for f in range(2)]
        east = [terrain[0, b, f, :, HALF:] for f in range(2)]
        packed = jnp.where(lane < 3, west[0], pltpu.roll(west[1], 3, 1))
        packed = jnp.where(lane < 5, packed, pltpu.roll(east[0], 7, 1))
        packed = jnp.where(lane < 7, packed, pltpu.roll(east[1], 9, 1))
        turned = packed.T
        for q in range(5):
            low[q, b : b + 1] = turned[q : q + 1]
        for q in range(4):
            high[q, b : b + 1] = turned[5 + q : 6 + q]
        for q in range(3):
            low[q, 4 + b : 5 + b] = terrain[0, b, 0, q : q + 1]
        for q in range(2):
            low[3 + q, 4 + b : 5 + b] = terrain[0, b, 1, q : q + 1]
            high[q, 4 + b : 5 + b] = terrain[0, b, 0, SIDE - 2 + q : SIDE - 1 + q]
            high[2 + q, 4 + b : 5 + b] = terrain[0, b, 1, SIDE - 2 + q : SIDE - 1 + q]
    pack1[6, 0:4] = high[1, 0:4]
    pack1[6, 4:8] = high[3, 0:4]
    pack_back[1] = low[0]
    writers = (write_by_core(1, 3), functools.partial(write, 2), write_by_core(3, 1), functools.partial(write, 0))
    for load, ref, write_out in zip(loads, held, writers):
        load.wait()
        strips(ref, write_out)


def prepare(dest, state, terrain):
    packs = [shape(count, 8, SIDE) for count in (5, 7, 6, 5, 1, 2)]
    return pl.pallas_call(
        prepare_kernel,
        out_shape=[shape(3, SIDE, SIDE)] * 4 + [shape(5, 8, SIDE), shape(4, 8, SIDE)] + packs,
        in_specs=[SMEM, HBM, VMEM],
        out_specs=[VMEM] * 12,
        scratch_shapes=[pltpu.SemaphoreType.DMA((BLOCKS,))],
        compiler_params=params(12),
        cost_estimate=cost(0, 3 << 20),
    )(dest, pltpu.with_memory_space_constraint(state, pltpu.HBM), terrain)


def gate_kernel(count, *refs):
    del count, refs


def gate(values, keys):
    count = len(values)
    return pl.pallas_call(
        functools.partial(gate_kernel, count),
        out_shape=[jax.ShapeDtypeStruct(v.shape, v.dtype) for v in values],
        in_specs=[ANY] * (count + len(keys)),
        out_specs=[ANY] * count,
        input_output_aliases={i: i for i in range(count)},
        compiler_params=params(1),
        cost_estimate=cost(0, 0),
    )(*values, *keys)


def arrange_kernel(
    dest, pack0, pack1, pack2, pack3, pack4, pack_back, ground_low, ground_high,
    low, high, west, south, east, north, other_west, other_east,
):
    for out in (west, south, east, north, other_west, other_east):
        out[...] = jnp.zeros_like(out)
    strips = (pack0, pack1, pack2, pack3)
    west_in = (pack_back.at[0], pack0.at[4], pack1.at[5], pack2.at[5])
    east_in = (pack1.at[4], pack2.at[4], pack3.at[4], pack4.at[0])
    for k in range(BLOCKS):
        strip = strips[k]
        slot = landing_slot(dest, k)
        for side, (low_out, high_out) in enumerate(((west, east), (south, north))):
            row = pl.ds(side * 4 + slot, 1)
            for q in range(8):
                low[q, row] = strip[side, q : q + 1]
            for q in range(6):
                high[q, row] = strip[2 + side, q : q + 1]
            low_out[slot, 0:1] = strip[side, 0:1]
            low_out[slot, 1:2] = strip[side, 3:4]
            high_out[slot, 0:1] = strip[2 + side, 1:2]
            high_out[slot, 1:3] = strip[2 + side, 3:5]
        slot = landing_slot(dest, k, 1)
        other_east[slot, 0:1] = east_in[k][1:2]
        other_east[slot, 1:3] = east_in[k][3:5]
        slot = landing_slot(dest, k, -1)
        other_west[slot, 0:1] = west_in[k][0:1]
        other_west[slot, 1:2] = west_in[k][3:4]
    for b in range(BLOCKS):
        for side, (low_out, high_out) in enumerate(((west, east), (south, north))):
            sub = slice(side * 4 + b, side * 4 + b + 1)
            low_out[b, 2:3] = ground_low[0, sub]
            high_out[b, 3:4] = ground_high[1, sub]
            high_out[b, 4:5] = ground_high[3, sub]
        other_east[b, 3:4] = pack1[6, b : b + 1]
        other_east[b, 4:5] = pack1[6, 4 + b : 5 + b]
        other_west[b, 2:3] = pack_back[1, b : b + 1]


def arrange(dest, packs, ground):
    return pl.pallas_call(
        arrange_kernel,
        out_shape=[shape(8, 8, SIDE), shape(6, 8, SIDE)] + [shape(BLOCKS, 8, SIDE)] * 6,
        in_specs=[SMEM] + [VMEM] * 8,
        out_specs=[VMEM] * 8,
        compiler_params=params(4),
        cost_estimate=cost(0, 0),
    )(dest, *packs, *ground)


def pick(entry, own, other):
    near = own[jnp.clip(entry, 0, BLOCKS - 1)]
    far = other[jnp.clip(entry - BLOCKS, 0, BLOCKS - 1)]
    return jnp.where(entry >= BLOCKS, far, near)


def gather_rims(entries, own, other, rim_low, rim_high, has, low_count, high_count):
    for b in range(BLOCKS):
        for side in range(2):
            sub = slice(side * 4 + b, side * 4 + b + 1)
            entry = entries[0, b, 2 * side]
            alive = entry >= 0
            rows = jnp.where(alive, pick(entry, own[2 + side], other[2 + side]), 0.0)
            for q in range(low_count):
                rim_low[q, sub] = rows[q : q + 1]
            has[0, sub] = jnp.full((1, SIDE), jnp.where(alive, 1.0, 0.0), F32)
            entry = entries[0, b, 2 * side + 1]
            alive = entry >= 0
            rows = jnp.where(alive, pick(entry, own[side], other[side]), 0.0)
            for q in range(high_count):
                rim_high[q, sub] = rows[q : q + 1]
            has[1, sub] = jnp.full((1, SIDE), jnp.where(alive, 1.0, 0.0), F32)


def sides_swapped(x):
    return pltpu.roll(x, 4, 0)


def along_edge(h, z, rough, flow, spot, face_before, face_first, face_last):
    lane = lanes(8, SIDE)
    eta = h + z
    flux = face(
        eta, pltpu.roll(eta, SIDE - 1, 1), z, pltpu.roll(z, SIDE - 1, 1), rough,
        pltpu.roll(flow, 1, 1), flow, pltpu.roll(flow, SIDE - 1, 1),
    )
    here = slice(spot, spot + 1)
    flux = jnp.where(lane == 0, sides_swapped(face_first)[:, here], flux)
    flux = jnp.where(lane == SIDE - 1, sides_swapped(face_last)[:, here], flux)
    lower = jnp.where(lane == 0, sides_swapped(face_before)[:, here], pltpu.roll(flux, 1, 1))
    return lower - flux


def first_edges_kernel(
    entries, wet, edge_spill, low, high, ground_low, ground_high,
    own_w, own_s, own_e, own_n, oth_w, oth_s, oth_e, oth_n,
    faces, edge, rim_ground, west, south, east, north,
    rim_low, rim_high, has, wetness,
):
    gather_rims(
        entries, (own_w, own_s, own_e, own_n), (oth_w, oth_s, oth_e, oth_n), rim_low, rim_high, has, 5, 3
    )
    for b in range(BLOCKS):
        value = jnp.full((1, SIDE), wet[0, b].astype(F32), F32)
        wetness[b : b + 1] = value
        wetness[4 + b : 5 + b] = value
    hm, qmm, qm, zm, nm = (rim_low[q] for q in range(5))
    hp, qp, zp = (rim_high[q] for q in range(3))
    h0, h1, h2, q0, q1, q2, t0, t1 = (low[q] for q in range(8))
    z0, z1, z2, n0, n1 = (ground_low[q] for q in range(5))
    hy, hz, qx, qy, qz, tz = (high[q] for q in range(6))
    zy, zz, ny, nz = (ground_high[q] for q in range(4))
    face_m = face(hm + zm, h0 + z0, zm, z0, nm, qmm, qm, q0) * has[0]
    face_0 = face(h0 + z0, h1 + z1, z0, z1, n0, qm, q0, q1)
    face_1 = face(h1 + z1, h2 + z2, z1, z2, n1, q0, q1, q2)
    face_y = face(hy + zy, hz + zz, zy, zz, ny, qx, qy, qz)
    face_z = face(hz + zz, hp + zp, zz, zp, nz, qy, qz, qp) * has[1]
    beside = (face_m, face_0, face_z)
    wets = wetness[...]
    new_0 = (h0 + RATIO * (face_m - face_0 + along_edge(h0, z0, n0, t0, 0, *beside)) + edge_spill[0]) * wets
    new_1 = (h1 + RATIO * (face_0 - face_1 + along_edge(h1, z1, n1, t1, 1, *beside)) + edge_spill[1]) * wets
    new_z = (hz + RATIO * (face_y - face_z + along_edge(hz, zz, nz, tz, SIDE - 1, *beside)) + edge_spill[2]) * wets
    faces[0] = face_m
    faces[1] = face_0
    faces[2] = face_z
    rim_ground[0] = zm
    rim_ground[1] = nm
    rim_ground[2] = zp
    flow_0, flow_1, flow_y, flow_z = (f * wets for f in (face_0, face_1, face_y, face_z))
    for i, value in enumerate((new_0, new_1, flow_0, flow_1, new_z, flow_y, flow_z)):
        edge[i] = value
    for out in (west, south, east, north):
        out[...] = jnp.zeros_like(out)
    for b in range(BLOCKS):
        for side, (low_out, high_out) in enumerate(((west, east), (south, north))):
            sub = slice(side * 4 + b, side * 4 + b + 1)
            low_out[b, 0:1] = new_0[sub]
            low_out[b, 1:2] = flow_0[sub]
            high_out[b, 0:1] = new_z[sub]
            high_out[b, 1:2] = flow_y[sub]
            high_out[b, 2:3] = flow_z[sub]


def first_edges(entries, wet, edge_spill, low, high, ground, own, other):
    return pl.pallas_call(
        first_edges_kernel,
        out_shape=[shape(3, 8, SIDE), shape(7, 8, SIDE), shape(3, 8, SIDE)] + [shape(BLOCKS, 8, SIDE)] * 4,
        in_specs=[SMEM, SMEM] + [VMEM] * 13,
        out_specs=[VMEM] * 7,
        scratch_shapes=[
            pltpu.VMEM((5, 8, SIDE), F32),
            pltpu.VMEM((3, 8, SIDE), F32),
            pltpu.VMEM((2, 8, SIDE), F32),
            pltpu.VMEM((8, SIDE), F32),
        ],
        compiler_params=params(4),
        cost_estimate=cost(0, 0),
    )(entries, wet, edge_spill, low, high, *ground, *own, *other)


def second_edges_kernel(
    entries, faces, edge, rim_ground, ground_low, ground_high,
    own_w, own_s, own_e, own_n, oth_w, oth_s, oth_e, oth_n,
    columns, rows, rim_low, rim_high, has, stack,
):
    gather_rims(
        entries, (own_w, own_s, own_e, own_n), (oth_w, oth_s, oth_e, oth_n), rim_low, rim_high, has, 3, 2
    )
    hm, qmm, qm = (rim_low[q] for q in range(3))
    hp, qp = (rim_high[q] for q in range(2))
    zm, nm, zp = (rim_ground[q] for q in range(3))
    h0, h1, q0, q1, hz, qy, qz = (edge[q] for q in range(7))
    z0, z1, n0 = ground_low[0], ground_low[1], ground_low[3]
    zz, nz = ground_high[1], ground_high[3]
    face_m = face(hm + zm, h0 + z0, zm, z0, nm, qmm, qm, q0) * has[0]
    face_0 = face(h0 + z0, h1 + z1, z0, z1, n0, qm, q0, q1)
    face_z = face(hz + zz, hp + zp, zz, zp, nz, qy, qz, qp) * has[1]
    every = (faces[0], faces[1], faces[2], face_m, face_0, face_z)
    stack[...] = jnp.zeros_like(stack)
    rows[...] = jnp.zeros_like(rows)
    for b in range(BLOCKS):
        for i, value in enumerate(every):
            stack[b * 8 + i : b * 8 + i + 1] = value[b : b + 1]
            rows[b, i : i + 1] = value[4 + b : 5 + b]
    turned = stack[...].T
    columns[0] = turned
    for b in range(1, BLOCKS):
        columns[b] = pltpu.roll(turned, HALF - 8 * b, 1)


def second_edges(entries, faces, edge, rim_ground, ground, own, other):
    return pl.pallas_call(
        second_edges_kernel,
        out_shape=[shape(BLOCKS, SIDE, HALF), shape(BLOCKS, 8, SIDE)],
        in_specs=[SMEM] + [VMEM] * 13,
        out_specs=[VMEM] * 2,
        scratch_shapes=[
            pltpu.VMEM((3, 8, SIDE), F32),
            pltpu.VMEM((2, 8, SIDE), F32),
            pltpu.VMEM((2, 8, SIDE), F32),
            pltpu.VMEM((HALF, SIDE), F32),
        ],
        compiler_params=params(4),
        cost_estimate=cost(0, 0),
    )(entries, faces, edge, rim_ground, *ground, *own, *other)


def inflow_kernel(cells, rates, spill, edge_spill):
    spill[...] = jnp.zeros_like(spill)
    edge_spill[...] = jnp.zeros_like(edge_spill)
    lane = lanes(1, SIDE)
    for b in range(BLOCKS):

        def point(p, carry, b=b):
            cell = cells[0, b, p]
            row = lax.div(cell, SIDE)
            column = lax.rem(cell, SIDE)
            rate = GAIN * rates[0, b, p]
            at_column = jnp.where(lane == column, rate, 0.0)
            at_row = jnp.where(lane == row, rate, 0.0)
            line = pl.ds(row, 1)
            spill[b, line] = spill[b, line] + at_column
            for i, place in enumerate((0, 1, SIDE - 1)):
                edge_spill[i, b : b + 1] += jnp.where(column == place, at_row, 0.0)
                edge_spill[i, 4 + b : 5 + b] += jnp.where(row == place, at_column, 0.0)
            return carry

        lax.fori_loop(0, RIVERS, point, 0)


def lay_inflow(cells, rates):
    return pl.pallas_call(
        inflow_kernel,
        out_shape=[shape(BLOCKS, SIDE, SIDE), shape(3, 8, SIDE)],
        in_specs=[SMEM, SMEM],
        out_specs=[VMEM] * 2,
        compiler_params=params(4),
        cost_estimate=cost(0, 1 << 20),
    )(cells, rates)


def block_step(now, ground, spill, columns, rows, base, wetness, write):
    lane = lanes(ROWS, SIDE)
    sub = lax.broadcasted_iota(jnp.int32, (ROWS, SIDE), 0)

    def at(load, field, first, shift):
        if 0 <= first + shift <= SIDE - ROWS:
            return load(field, pl.ds(first + shift, ROWS))
        return pltpu.roll(load(field, pl.ds(first, ROWS)), -shift % ROWS, 0)

    below = rows(base)
    for first in range(0, SIDE, ROWS):
        h, qx, qy = (at(now, f, first, 0) for f in range(3))
        z, rough = (at(ground, f, first, 0) for f in range(2))
        eta = h + z
        flux_x = face(
            eta, pltpu.roll(eta, SIDE - 1, 1), z, pltpu.roll(z, SIDE - 1, 1), rough,
            pltpu.roll(qx, 1, 1), qx, pltpu.roll(qx, SIDE - 1, 1),
        )
        edge = columns(pl.ds(first, ROWS))
        flux_x = jnp.where(lane == 0, edge[:, base + 1 : base + 2], flux_x)
        flux_x = jnp.where(lane == SIDE - 1, edge[:, base + 2 : base + 3], flux_x)
        flux_w = jnp.where(lane == 0, edge[:, base : base + 1], pltpu.roll(flux_x, 1, 1))
        z_up = at(ground, 0, first, 1)
        flux_y = face(
            eta, at(now, 0, first, 1) + z_up, z, z_up, rough, at(now, 2, first, -1), qy, at(now, 2, first, 1)
        )
        if first == 0:
            flux_y = jnp.where(sub == 0, rows(base + 1), flux_y)
        if first == SIDE - ROWS:
            flux_y = jnp.where(sub == ROWS - 1, rows(base + 2), flux_y)
        flux_s = jnp.where(sub == 0, below, pltpu.roll(flux_y, 1, 0))
        below = flux_y[ROWS - 1 : ROWS]
        depth = h + RATIO * (flux_w - flux_x + flux_s - flux_y) + spill(pl.ds(first, ROWS))
        write(first, depth * wetness, flux_x * wetness, flux_y * wetness)


def block_kernel(shifts, dest, wet, terrain, columns, rows, spill, *refs):
    out, then, done, sems = refs[-4:]
    shift = jnp.where(core() == 0, *shifts)
    slot = landing_slot(dest, shift)
    wetness = wet[0, slot].astype(F32)
    state = refs[0]
    if len(shifts) == 2 and shifts == W_SHIFTS:
        for here, ref in enumerate(refs[:2]):

            @pl.when(core() == 1 - here)
            def _(ref=ref):
                copy = pltpu.make_async_copy(ref, done, sems.at[0])
                copy.start()
                copy.wait()

        state = done
    copies = []

    def ground(field, at):
        return terrain[0, slot, field, at]

    def keep(first, *fields):
        for f, value in enumerate(fields):
            then[f, first : first + ROWS] = value

    def finish(first, *fields):
        for f, value in enumerate(fields):
            done[f, first : first + ROWS] = value
        lines = pl.ds(first, ROWS)
        copies.append(pltpu.make_async_copy(done.at[:, lines], out.at[0, slot, :, lines], sems.at[len(copies)]))
        copies[-1].start()

    shared = (
        lambda at: spill[slot, at],
        lambda at: columns[slot, at],
        lambda q: rows[slot, q : q + 1],
    )
    block_step(lambda f, at: state[f, at], ground, *shared, 0, wetness, keep)
    block_step(lambda f, at: then[f, at], ground, *shared, 3, wetness, finish)
    for copy in copies:
        copy.wait()


def run_block(shifts, dest, wet, terrain, columns, rows, spill, states, out):
    args = [dest, wet, terrain, columns, rows, spill, *states]
    specs = [SMEM] * 2 + [VMEM] * 4 + ([VMEM] if len(states) == 1 else [ANY] * 2)
    aliases = {}
    if out is not None:
        aliases = {len(args): 0}
        args.append(out)
        specs.append(ANY)
    return pl.pallas_call(
        functools.partial(block_kernel, shifts),
        out_shape=shape(1, BLOCKS, 3, SIDE, SIDE),
        in_specs=specs,
        out_specs=ANY,
        input_output_aliases=aliases,
        scratch_shapes=[
            pltpu.VMEM((3, SIDE, SIDE), F32),
            pltpu.VMEM((3, SIDE, SIDE), F32),
            pltpu.SemaphoreType.DMA((SIDE // ROWS,)),
        ],
        compiler_params=params(16),
        cost_estimate=cost(0, 0),
    )(*args)


def passed_along(x, axis, by, wrap=True):
    devices = lax.axis_size(axis)
    return lax.ppermute(x, axis, [(i, (i + by) % devices) for i in range(devices)])


def passed_to(x, target):
    devices = lax.axis_size("tile")
    pairs = [(i, target(i // 2, i % 2)) for i in range(devices)]
    return lax.ppermute(x, "tile", [(i, t % devices) for i, t in pairs if t is not None])


def back_one(chip):
    return chip // RING * RING + (chip - 1) % RING


def first_leg(chip, at):
    return 2 * chip + 1 if at == 0 else 2 * back_one(chip)


def second_leg(chip, at):
    sender = chip // RING * RING + (chip + 1) % RING
    return 2 * (sender + 2) if at == 0 else None


def next_chip_swapped(chip, at):
    return 2 * (chip + 1) + 1 - at


def body(flood_state, terrain, destination, wet_mask, neighbours, inflow_cells, inflow_rates):
    own, block_a, block_w, block_x, *rest = prepare(destination, flood_state, terrain)
    ground, packs = rest[:2], rest[2:]
    packs = [packs[0]] + [passed_along(p, "tile", d) for d, p in zip((1, 2, 3, 4, -1), packs[1:])]
    block_a, block_w = gate((block_a, block_w), packs[1:])
    block_a = passed_along(block_a, "tile", 2)
    block_w = passed_to(block_w, first_leg)
    spill, edge_spill = lay_inflow(inflow_cells, inflow_rates)
    low, high, west, south, east, north, other_west, other_east = arrange(destination, packs, ground)
    others = (other_west, passed_along(south, "grp", -1), other_east, passed_along(north, "grp", 1))
    faces, edge, rim_ground, west, south, east, north = first_edges(
        neighbours, wet_mask, edge_spill, low, high, ground, (west, south, east, north), others
    )
    others = (
        passed_along(west, "tile", -1),
        passed_along(south, "grp", -1),
        passed_along(east, "tile", 1),
        passed_along(north, "grp", 1),
    )
    block_x, block_w = gate((block_x, block_w), (others[0], others[2], block_a))
    relayed = passed_to(block_w, second_leg)
    block_x = passed_to(block_x, next_chip_swapped)
    columns, rows = second_edges(neighbours, faces, edge, rim_ground, ground, (west, south, east, north), others)
    out = None
    for shifts, states in (
        ((0, 0), (own,)),
        ((2, 2), (block_a,)),
        (W_SHIFTS, (block_w, relayed)),
        (X_SHIFTS, (block_x,)),
    ):
        out = run_block(shifts, destination, wet_mask, terrain, columns, rows, spill, states, out)
    return out


def solution(mesh):
    in_specs = (
        P("grp", "tile", None, None, None),
        P("grp", "tile", None, None, None),
        P("grp", None),
        P("grp", "tile"),
        P("grp", "tile", None),
        P("grp", "tile", None),
        P("grp", "tile", None),
    )
    out_specs = P("grp", "tile", None, None, None)
    return jax.shard_map(body, mesh=mesh, in_specs=in_specs, out_specs=out_specs, check_vma=False)
```

```python
import functools

import jax
import jax.numpy as jnp
from jax import lax
from jax.experimental import pallas as pl
from jax.experimental.pallas import tpu as pltpu
from jax.sharding import PartitionSpec as P

F32 = jnp.float32
GRAVITY = 9.81
SPACING = 10.0
TIMESTEP = 0.2
CENTRE_WEIGHT = 0.7
DEPTH_FLOOR = 0.1
SIDE = 256
HALF = 128
BLOCKS = 4
RIVERS = 16
ROWS = 64
GAIN = TIMESTEP / (SPACING * SPACING)
RATIO = TIMESTEP / SPACING

ANY = pl.BlockSpec(memory_space=pl.ANY)
VMEM = pl.BlockSpec(memory_space=pltpu.VMEM)
SMEM = pl.BlockSpec(memory_space=pltpu.SMEM)
HBM = pl.BlockSpec(memory_space=pltpu.HBM)
RING = 4
A_SHIFTS = (2, 2)
W_SHIFTS = (3, 1)
X_SHIFTS = (1, 3)


def shape(*dims):
    return jax.ShapeDtypeStruct(dims, F32)


def cost(flops, bytes_accessed):
    return pl.CostEstimate(flops=flops, bytes_accessed=bytes_accessed, transcendentals=0)


def face(eta_l, eta_r, z_l, z_r, rough, flow_left, flow_mid, flow_right):
    depth = jnp.maximum(eta_l, eta_r) - jnp.maximum(z_l, z_r)
    floored = jnp.maximum(depth, DEPTH_FLOOR)
    blended = CENTRE_WEIGHT * flow_mid + 0.5 * (1.0 - CENTRE_WEIGHT) * (flow_left + flow_right)
    slope = (GRAVITY * TIMESTEP / SPACING) * depth * (eta_r - eta_l)
    friction = 1.0 + (GRAVITY * TIMESTEP) * rough * rough * jnp.abs(flow_mid) * jnp.exp(
        (-7.0 / 3.0) * jnp.log(floored)
    )
    return (blended - slope) / friction


def core():
    return lax.rem(lax.axis_index("tile"), 2)


def params(mib):
    return pltpu.CompilerParams(vmem_limit_bytes=mib << 20)


def tile_offset(dest_ref, tile, slot):
    tiles = lax.axis_size("tile")
    return lax.rem(lax.div(dest_ref[0, tile * BLOCKS + slot], BLOCKS) - tile + tiles, tiles)


def leaving_slot(dest_ref, shift):
    me = lax.axis_index("tile")
    slot = jnp.int32(0)
    for j in range(1, BLOCKS):
        slot = jnp.where(tile_offset(dest_ref, me, j) == shift, j, slot)
    return slot


def landing_slot(dest_ref, shift, back=0):
    tiles = lax.axis_size("tile")
    sender = lax.rem(lax.axis_index("tile") - shift - back + 2 * tiles, tiles)
    slot = jnp.int32(0)
    for j in range(BLOCKS):
        place = lax.rem(dest_ref[0, sender * BLOCKS + j], BLOCKS)
        slot = jnp.where(tile_offset(dest_ref, sender, j) == shift, place, slot)
    return slot


def lanes(rows, columns):
    return lax.broadcasted_iota(jnp.int32, (rows, columns), 1)


MIDDLE = SIDE // 2


def in_hbm(x):
    return pltpu.with_memory_space_constraint(x, pltpu.HBM)


def pick_kernel(dest, state, first, second, sems):
    slot = leaving_slot(dest, 2)
    loads = [
        pltpu.make_async_copy(state.at[0, slot, :, pl.ds(i * MIDDLE, MIDDLE)], ref, sems.at[i])
        for i, ref in enumerate((first, second))
    ]
    for load in loads:
        load.start()
    for load in loads:
        load.wait()


def pick_a(dest, state):
    return pl.pallas_call(
        pick_kernel,
        out_shape=[shape(3, MIDDLE, SIDE)] * 2,
        in_specs=[SMEM, HBM],
        out_specs=[VMEM] * 2,
        scratch_shapes=[pltpu.SemaphoreType.DMA((2,))],
        compiler_params=params(4),
        cost_estimate=cost(0, 0),
    )(dest, state)


def prepare_kernel(
    dest, state, a_low, a_high, ground_in,
    own, block_w, block_x, low, high, pack0, pack1, pack2, pack3, pack4, pack_back, terrain, sems,
):
    slots = [leaving_slot(dest, k) for k in range(BLOCKS)]
    first_core = core() == 0
    slot_w = jnp.where(first_core, slots[1], slots[3])
    slot_x = jnp.where(first_core, slots[3], slots[1])
    held = (block_w, block_x, own)
    loads = [pltpu.make_async_copy(ground_in, terrain, sems.at[3])]
    for i, (slot, ref) in enumerate(zip((slot_w, slot_x, slots[0]), held)):
        loads.append(pltpu.make_async_copy(state.at[0, slot], ref, sems.at[i]))
    for load in loads:
        load.start()
    lane = lanes(SIDE, HALF)

    def strips(low_half, high_half, write):
        def side(columns):
            parts = [[half[f, :, columns] for half in (low_half, high_half)] for f in range(3)]
            return [jnp.concatenate(part) for part in parts]

        west = side(slice(0, HALF))
        east = side(slice(HALF, SIDE))
        packed = jnp.where(lane < 3, west[0], pltpu.roll(west[1], 3, 1))
        packed = jnp.where(lane < 6, packed, pltpu.roll(west[2], 6, 1))
        packed = jnp.where(lane < 8, packed, pltpu.roll(east[0], 10, 1))
        packed = jnp.where(lane < 10, packed, pltpu.roll(east[1], 13, 1))
        packed = jnp.where(lane < 13, packed, pltpu.roll(east[2], 14, 1))
        turned = packed.T
        south = jnp.concatenate([low_half[0, 0:3], low_half[2, 0:3], low_half[1, 0:2]])
        north = jnp.concatenate(
            [
                high_half[0, MIDDLE - 2 : MIDDLE],
                high_half[2, MIDDLE - 3 : MIDDLE],
                high_half[1, MIDDLE - 1 : MIDDLE],
                jnp.zeros((2, SIDE), F32),
            ]
        )
        write(turned[0:8], south, turned[8:16], north)

    strip_out = (pack0, pack1, pack2, pack3)
    west_out = (pack_back.at[0], pack0.at[4], pack1.at[5], pack2.at[5])
    east_out = (pack1.at[4], pack2.at[4], pack3.at[4], pack4.at[0])

    def write(k, west, south, east, north):
        for i, value in enumerate((west, south, east, north)):
            strip_out[k][i] = value
        west_out[k][...] = west
        east_out[k][...] = east

    def write_by_core(first, second):
        def both(*values):
            pl.when(first_core)(lambda: write(first, *values))
            pl.when(jnp.logical_not(first_core))(lambda: write(second, *values))

        return both

    strips(a_low, a_high, functools.partial(write, 2))
    loads[0].wait()
    for b in range(BLOCKS):
        west = [terrain[0, b, f, :, :HALF] for f in range(2)]
        east = [terrain[0, b, f, :, HALF:] for f in range(2)]
        packed = jnp.where(lane < 3, west[0], pltpu.roll(west[1], 3, 1))
        packed = jnp.where(lane < 5, packed, pltpu.roll(east[0], 7, 1))
        packed = jnp.where(lane < 7, packed, pltpu.roll(east[1], 9, 1))
        turned = packed.T
        for q in range(5):
            low[q, b : b + 1] = turned[q : q + 1]
        for q in range(4):
            high[q, b : b + 1] = turned[5 + q : 6 + q]
        for q in range(3):
            low[q, 4 + b : 5 + b] = terrain[0, b, 0, q : q + 1]
        for q in range(2):
            low[3 + q, 4 + b : 5 + b] = terrain[0, b, 1, q : q + 1]
            high[q, 4 + b : 5 + b] = terrain[0, b, 0, SIDE - 2 + q : SIDE - 1 + q]
            high[2 + q, 4 + b : 5 + b] = terrain[0, b, 1, SIDE - 2 + q : SIDE - 1 + q]
    pack1[6, 0:4] = high[1, 0:4]
    pack1[6, 4:8] = high[3, 0:4]
    pack_back[1] = low[0]
    writers = (write_by_core(1, 3), write_by_core(3, 1), functools.partial(write, 0))
    for load, ref, write_out in zip(loads[1:], held, writers):
        load.wait()
        strips(ref.at[:, pl.ds(0, MIDDLE)], ref.at[:, pl.ds(MIDDLE, MIDDLE)], write_out)


def prepare(dest, state, a_low, a_high, terrain):
    packs = [shape(count, 8, SIDE) for count in (5, 7, 6, 5, 1, 2)]
    return pl.pallas_call(
        prepare_kernel,
        out_shape=[shape(3, SIDE, SIDE)] * 3 + [shape(5, 8, SIDE), shape(4, 8, SIDE)] + packs,
        in_specs=[SMEM, HBM, VMEM, VMEM, HBM],
        out_specs=[VMEM] * 11,
        scratch_shapes=[
            pltpu.VMEM((1, BLOCKS, 2, SIDE, SIDE), F32),
            pltpu.SemaphoreType.DMA((BLOCKS,)),
        ],
        compiler_params=params(12),
        cost_estimate=cost(0, 0),
    )(dest, state, a_low, a_high, terrain)


def gate_kernel(count, *refs):
    del count, refs


def gate(values, keys):
    count = len(values)
    return pl.pallas_call(
        functools.partial(gate_kernel, count),
        out_shape=[jax.ShapeDtypeStruct(v.shape, v.dtype) for v in values],
        in_specs=[ANY] * (count + len(keys)),
        out_specs=[ANY] * count,
        input_output_aliases={i: i for i in range(count)},
        compiler_params=params(1),
        cost_estimate=cost(0, 0),
    )(*values, *keys)


def arrange_kernel(
    dest, pack0, pack1, pack2, pack3, pack4, pack_back, ground_low, ground_high,
    low, high, west, south, east, north, other_west, other_east,
):
    for out in (west, south, east, north, other_west, other_east):
        out[...] = jnp.zeros_like(out)
    strips = (pack0, pack1, pack2, pack3)
    west_in = (pack_back.at[0], pack0.at[4], pack1.at[5], pack2.at[5])
    east_in = (pack1.at[4], pack2.at[4], pack3.at[4], pack4.at[0])
    for k in range(BLOCKS):
        strip = strips[k]
        slot = landing_slot(dest, k)
        for side, (low_out, high_out) in enumerate(((west, east), (south, north))):
            row = pl.ds(side * 4 + slot, 1)
            for q in range(8):
                low[q, row] = strip[side, q : q + 1]
            for q in range(6):
                high[q, row] = strip[2 + side, q : q + 1]
            low_out[slot, 0:1] = strip[side, 0:1]
            low_out[slot, 1:2] = strip[side, 3:4]
            high_out[slot, 0:1] = strip[2 + side, 1:2]
            high_out[slot, 1:3] = strip[2 + side, 3:5]
        slot = landing_slot(dest, k, 1)
        other_east[slot, 0:1] = east_in[k][1:2]
        other_east[slot, 1:3] = east_in[k][3:5]
        slot = landing_slot(dest, k, -1)
        other_west[slot, 0:1] = west_in[k][0:1]
        other_west[slot, 1:2] = west_in[k][3:4]
    for b in range(BLOCKS):
        for side, (low_out, high_out) in enumerate(((west, east), (south, north))):
            sub = slice(side * 4 + b, side * 4 + b + 1)
            low_out[b, 2:3] = ground_low[0, sub]
            high_out[b, 3:4] = ground_high[1, sub]
            high_out[b, 4:5] = ground_high[3, sub]
        other_east[b, 3:4] = pack1[6, b : b + 1]
        other_east[b, 4:5] = pack1[6, 4 + b : 5 + b]
        other_west[b, 2:3] = pack_back[1, b : b + 1]


def arrange(dest, packs, ground):
    return pl.pallas_call(
        arrange_kernel,
        out_shape=[shape(8, 8, SIDE), shape(6, 8, SIDE)] + [shape(BLOCKS, 8, SIDE)] * 6,
        in_specs=[SMEM] + [VMEM] * 8,
        out_specs=[VMEM] * 8,
        compiler_params=params(4),
        cost_estimate=cost(0, 0),
    )(dest, *packs, *ground)


def pick(entry, own, other):
    near = own[jnp.clip(entry, 0, BLOCKS - 1)]
    far = other[jnp.clip(entry - BLOCKS, 0, BLOCKS - 1)]
    return jnp.where(entry >= BLOCKS, far, near)


def gather_rims(entries, own, other, rim_low, rim_high, has, low_count, high_count):
    for b in range(BLOCKS):
        for side in range(2):
            sub = slice(side * 4 + b, side * 4 + b + 1)
            entry = entries[0, b, 2 * side]
            alive = entry >= 0
            rows = jnp.where(alive, pick(entry, own[2 + side], other[2 + side]), 0.0)
            for q in range(low_count):
                rim_low[q, sub] = rows[q : q + 1]
            has[0, sub] = jnp.full((1, SIDE), jnp.where(alive, 1.0, 0.0), F32)
            entry = entries[0, b, 2 * side + 1]
            alive = entry >= 0
            rows = jnp.where(alive, pick(entry, own[side], other[side]), 0.0)
            for q in range(high_count):
                rim_high[q, sub] = rows[q : q + 1]
            has[1, sub] = jnp.full((1, SIDE), jnp.where(alive, 1.0, 0.0), F32)


def sides_swapped(x):
    return pltpu.roll(x, 4, 0)


def along_edge(h, z, rough, flow, spot, face_before, face_first, face_last):
    lane = lanes(8, SIDE)
    eta = h + z
    flux = face(
        eta, pltpu.roll(eta, SIDE - 1, 1), z, pltpu.roll(z, SIDE - 1, 1), rough,
        pltpu.roll(flow, 1, 1), flow, pltpu.roll(flow, SIDE - 1, 1),
    )
    here = slice(spot, spot + 1)
    flux = jnp.where(lane == 0, sides_swapped(face_first)[:, here], flux)
    flux = jnp.where(lane == SIDE - 1, sides_swapped(face_last)[:, here], flux)
    lower = jnp.where(lane == 0, sides_swapped(face_before)[:, here], pltpu.roll(flux, 1, 1))
    return lower - flux


def first_edges_kernel(
    entries, wet, edge_spill, low, high, ground_low, ground_high,
    own_w, own_s, own_e, own_n, oth_w, oth_s, oth_e, oth_n,
    faces, edge, rim_ground, west, south, east, north,
    rim_low, rim_high, has, wetness,
):
    gather_rims(
        entries, (own_w, own_s, own_e, own_n), (oth_w, oth_s, oth_e, oth_n), rim_low, rim_high, has, 5, 3
    )
    for b in range(BLOCKS):
        value = jnp.full((1, SIDE), wet[0, b].astype(F32), F32)
        wetness[b : b + 1] = value
        wetness[4 + b : 5 + b] = value
    hm, qmm, qm, zm, nm = (rim_low[q] for q in range(5))
    hp, qp, zp = (rim_high[q] for q in range(3))
    h0, h1, h2, q0, q1, q2, t0, t1 = (low[q] for q in range(8))
    z0, z1, z2, n0, n1 = (ground_low[q] for q in range(5))
    hy, hz, qx, qy, qz, tz = (high[q] for q in range(6))
    zy, zz, ny, nz = (ground_high[q] for q in range(4))
    face_m = face(hm + zm, h0 + z0, zm, z0, nm, qmm, qm, q0) * has[0]
    face_0 = face(h0 + z0, h1 + z1, z0, z1, n0, qm, q0, q1)
    face_1 = face(h1 + z1, h2 + z2, z1, z2, n1, q0, q1, q2)
    face_y = face(hy + zy, hz + zz, zy, zz, ny, qx, qy, qz)
    face_z = face(hz + zz, hp + zp, zz, zp, nz, qy, qz, qp) * has[1]
    beside = (face_m, face_0, face_z)
    wets = wetness[...]
    new_0 = (h0 + RATIO * (face_m - face_0 + along_edge(h0, z0, n0, t0, 0, *beside)) + edge_spill[0]) * wets
    new_1 = (h1 + RATIO * (face_0 - face_1 + along_edge(h1, z1, n1, t1, 1, *beside)) + edge_spill[1]) * wets
    new_z = (hz + RATIO * (face_y - face_z + along_edge(hz, zz, nz, tz, SIDE - 1, *beside)) + edge_spill[2]) * wets
    faces[0] = face_m
    faces[1] = face_0
    faces[2] = face_z
    rim_ground[0] = zm
    rim_ground[1] = nm
    rim_ground[2] = zp
    flow_0, flow_1, flow_y, flow_z = (f * wets for f in (face_0, face_1, face_y, face_z))
    for i, value in enumerate((new_0, new_1, flow_0, flow_1, new_z, flow_y, flow_z)):
        edge[i] = value
    for out in (west, south, east, north):
        out[...] = jnp.zeros_like(out)
    for b in range(BLOCKS):
        for side, (low_out, high_out) in enumerate(((west, east), (south, north))):
            sub = slice(side * 4 + b, side * 4 + b + 1)
            low_out[b, 0:1] = new_0[sub]
            low_out[b, 1:2] = flow_0[sub]
            high_out[b, 0:1] = new_z[sub]
            high_out[b, 1:2] = flow_y[sub]
            high_out[b, 2:3] = flow_z[sub]


def first_edges(entries, wet, edge_spill, low, high, ground, own, other):
    return pl.pallas_call(
        first_edges_kernel,
        out_shape=[shape(3, 8, SIDE), shape(7, 8, SIDE), shape(3, 8, SIDE)] + [shape(BLOCKS, 8, SIDE)] * 4,
        in_specs=[SMEM, SMEM] + [VMEM] * 13,
        out_specs=[VMEM] * 7,
        scratch_shapes=[
            pltpu.VMEM((5, 8, SIDE), F32),
            pltpu.VMEM((3, 8, SIDE), F32),
            pltpu.VMEM((2, 8, SIDE), F32),
            pltpu.VMEM((8, SIDE), F32),
        ],
        compiler_params=params(4),
        cost_estimate=cost(0, 0),
    )(entries, wet, edge_spill, low, high, *ground, *own, *other)


def second_edges_kernel(
    entries, faces, edge, rim_ground, ground_low, ground_high,
    own_w, own_s, own_e, own_n, oth_w, oth_s, oth_e, oth_n,
    columns, rows, rim_low, rim_high, has, stack,
):
    gather_rims(
        entries, (own_w, own_s, own_e, own_n), (oth_w, oth_s, oth_e, oth_n), rim_low, rim_high, has, 3, 2
    )
    hm, qmm, qm = (rim_low[q] for q in range(3))
    hp, qp = (rim_high[q] for q in range(2))
    zm, nm, zp = (rim_ground[q] for q in range(3))
    h0, h1, q0, q1, hz, qy, qz = (edge[q] for q in range(7))
    z0, z1, n0 = ground_low[0], ground_low[1], ground_low[3]
    zz, nz = ground_high[1], ground_high[3]
    face_m = face(hm + zm, h0 + z0, zm, z0, nm, qmm, qm, q0) * has[0]
    face_0 = face(h0 + z0, h1 + z1, z0, z1, n0, qm, q0, q1)
    face_z = face(hz + zz, hp + zp, zz, zp, nz, qy, qz, qp) * has[1]
    every = (faces[0], faces[1], faces[2], face_m, face_0, face_z)
    stack[...] = jnp.zeros_like(stack)
    rows[...] = jnp.zeros_like(rows)
    for b in range(BLOCKS):
        for i, value in enumerate(every):
            stack[b * 8 + i : b * 8 + i + 1] = value[b : b + 1]
            rows[b, i : i + 1] = value[4 + b : 5 + b]
    turned = stack[...].T
    columns[0] = turned
    for b in range(1, BLOCKS):
        columns[b] = pltpu.roll(turned, HALF - 8 * b, 1)


def second_edges(entries, faces, edge, rim_ground, ground, own, other):
    return pl.pallas_call(
        second_edges_kernel,
        out_shape=[shape(BLOCKS, SIDE, HALF), shape(BLOCKS, 8, SIDE)],
        in_specs=[SMEM] + [VMEM] * 13,
        out_specs=[VMEM] * 2,
        scratch_shapes=[
            pltpu.VMEM((3, 8, SIDE), F32),
            pltpu.VMEM((2, 8, SIDE), F32),
            pltpu.VMEM((2, 8, SIDE), F32),
            pltpu.VMEM((HALF, SIDE), F32),
        ],
        compiler_params=params(4),
        cost_estimate=cost(0, 0),
    )(entries, faces, edge, rim_ground, *ground, *own, *other)


def inflow_kernel(cells, rates, spill, edge_spill):
    spill[...] = jnp.zeros_like(spill)
    edge_spill[...] = jnp.zeros_like(edge_spill)
    lane = lanes(1, SIDE)
    for b in range(BLOCKS):

        def point(p, carry, b=b):
            cell = cells[0, b, p]
            row = lax.div(cell, SIDE)
            column = lax.rem(cell, SIDE)
            rate = GAIN * rates[0, b, p]
            at_column = jnp.where(lane == column, rate, 0.0)
            at_row = jnp.where(lane == row, rate, 0.0)
            line = pl.ds(row, 1)
            spill[b, line] = spill[b, line] + at_column
            for i, place in enumerate((0, 1, SIDE - 1)):
                edge_spill[i, b : b + 1] += jnp.where(column == place, at_row, 0.0)
                edge_spill[i, 4 + b : 5 + b] += jnp.where(row == place, at_column, 0.0)
            return carry

        lax.fori_loop(0, RIVERS, point, 0)


def lay_inflow(cells, rates):
    return pl.pallas_call(
        inflow_kernel,
        out_shape=[shape(BLOCKS, SIDE, SIDE), shape(3, 8, SIDE)],
        in_specs=[SMEM, SMEM],
        out_specs=[VMEM] * 2,
        compiler_params=params(4),
        cost_estimate=cost(0, 0),
    )(cells, rates)


def block_step(now, ground, spill, columns, rows, base, wetness, write):
    lane = lanes(ROWS, SIDE)
    sub = lax.broadcasted_iota(jnp.int32, (ROWS, SIDE), 0)

    def at(load, field, first, shift):
        if 0 <= first + shift <= SIDE - ROWS:
            return load(field, first + shift)
        return pltpu.roll(load(field, first), -shift % ROWS, 0)

    below = rows(base)
    for first in range(0, SIDE, ROWS):
        h, qx, qy = (at(now, f, first, 0) for f in range(3))
        z, rough = (at(ground, f, first, 0) for f in range(2))
        eta = h + z
        flux_x = face(
            eta, pltpu.roll(eta, SIDE - 1, 1), z, pltpu.roll(z, SIDE - 1, 1), rough,
            pltpu.roll(qx, 1, 1), qx, pltpu.roll(qx, SIDE - 1, 1),
        )
        edge = columns(pl.ds(first, ROWS))
        flux_x = jnp.where(lane == 0, edge[:, base + 1 : base + 2], flux_x)
        flux_x = jnp.where(lane == SIDE - 1, edge[:, base + 2 : base + 3], flux_x)
        flux_w = jnp.where(lane == 0, edge[:, base : base + 1], pltpu.roll(flux_x, 1, 1))
        z_up = at(ground, 0, first, 1)
        flux_y = face(
            eta, at(now, 0, first, 1) + z_up, z, z_up, rough, at(now, 2, first, -1), qy, at(now, 2, first, 1)
        )
        if first == 0:
            flux_y = jnp.where(sub == 0, rows(base + 1), flux_y)
        if first == SIDE - ROWS:
            flux_y = jnp.where(sub == ROWS - 1, rows(base + 2), flux_y)
        flux_s = jnp.where(sub == 0, below, pltpu.roll(flux_y, 1, 0))
        below = flux_y[ROWS - 1 : ROWS]
        depth = h + RATIO * (flux_w - flux_x + flux_s - flux_y) + spill(pl.ds(first, ROWS))
        write(first, depth * wetness, flux_x * wetness, flux_y * wetness)


def block_kernel(shifts, dest, wet, terrain, columns, rows, spill, *refs):
    out, then, done, sems = refs[-4:]
    shift = jnp.where(core() == 0, *shifts)
    slot = landing_slot(dest, shift)
    wetness = wet[0, slot].astype(F32)
    if shifts == W_SHIFTS:
        for here, ref in enumerate(refs[:2]):

            @pl.when(core() == 1 - here)
            def _(ref=ref):
                copy = pltpu.make_async_copy(ref, done, sems.at[0])
                copy.start()
                copy.wait()

        parts = (done,)
    elif shifts == A_SHIFTS:
        parts = refs[:2]
    else:
        parts = refs[:1]
    copies = []

    def now(field, first):
        if len(parts) == 1:
            return parts[0][field, first : first + ROWS]
        if first + ROWS <= MIDDLE:
            return parts[0][field, first : first + ROWS]
        if first >= MIDDLE:
            return parts[1][field, first - MIDDLE : first - MIDDLE + ROWS]
        return jnp.concatenate([parts[0][field, first:MIDDLE], parts[1][field, 0 : first + ROWS - MIDDLE]])

    def ground(field, first):
        return terrain[0, slot, field, first : first + ROWS]

    def keep(first, *fields):
        for f, value in enumerate(fields):
            then[f, first : first + ROWS] = value

    def finish(first, *fields):
        for f, value in enumerate(fields):
            done[f, first : first + ROWS] = value
        lines = pl.ds(first, ROWS)
        copies.append(pltpu.make_async_copy(done.at[:, lines], out.at[0, slot, :, lines], sems.at[len(copies)]))
        copies[-1].start()

    shared = (
        lambda at: spill[slot, at],
        lambda at: columns[slot, at],
        lambda q: rows[slot, q : q + 1],
    )
    block_step(now, ground, *shared, 0, wetness, keep)
    block_step(lambda f, first: then[f, first : first + ROWS], ground, *shared, 3, wetness, finish)
    for copy in copies:
        copy.wait()


def run_block(shifts, dest, wet, terrain, columns, rows, spill, states, out):
    args = [dest, wet, terrain, columns, rows, spill, *states]
    specs = [SMEM] * 2 + [VMEM] * 4 + [ANY if shifts == W_SHIFTS else VMEM] * len(states)
    aliases = {}
    if out is not None:
        aliases = {len(args): 0}
        args.append(out)
        specs.append(ANY)
    return pl.pallas_call(
        functools.partial(block_kernel, shifts),
        out_shape=shape(1, BLOCKS, 3, SIDE, SIDE),
        in_specs=specs,
        out_specs=ANY,
        input_output_aliases=aliases,
        scratch_shapes=[
            pltpu.VMEM((3, SIDE, SIDE), F32),
            pltpu.VMEM((3, SIDE, SIDE), F32),
            pltpu.SemaphoreType.DMA((SIDE // ROWS,)),
        ],
        compiler_params=params(16),
        cost_estimate=cost(0, 0),
    )(*args)


def passed_along(x, axis, by, wrap=True):
    devices = lax.axis_size(axis)
    return lax.ppermute(x, axis, [(i, (i + by) % devices) for i in range(devices)])


def passed_to(x, target):
    devices = lax.axis_size("tile")
    pairs = [(i, target(i // 2, i % 2)) for i in range(devices)]
    return lax.ppermute(x, "tile", [(i, t % devices) for i, t in pairs if t is not None])


def back_one(chip):
    return chip // RING * RING + (chip - 1) % RING


def first_leg(chip, at):
    return 2 * chip + 1 if at == 0 else 2 * back_one(chip)


def second_leg(chip, at):
    sender = chip // RING * RING + (chip + 1) % RING
    return 2 * (sender + 2) if at == 0 else None


def next_chip_swapped(chip, at):
    return 2 * (chip + 1) + 1 - at


def body(flood_state, terrain, destination, wet_mask, neighbours, inflow_cells, inflow_rates):
    dest, state = in_hbm(destination), in_hbm(flood_state)
    a_low, a_high = pick_a(dest, state)
    arrived_low = passed_along(a_low, "tile", 2)
    own, block_w, block_x, *rest = prepare(dest, state, a_low, a_high, in_hbm(terrain))
    ground, packs = rest[:2], rest[2:]
    packs = [packs[0]] + [passed_along(p, "tile", d) for d, p in zip((1, 2, 3, 4, -1), packs[1:])]
    a_high, block_w = gate((a_high, block_w), (*packs[1:], arrived_low))
    arrived_high = passed_along(a_high, "tile", 2)
    block_w = passed_to(block_w, first_leg)
    spill, edge_spill = lay_inflow(inflow_cells, inflow_rates)
    low, high, west, south, east, north, other_west, other_east = arrange(destination, packs, ground)
    others = (other_west, passed_along(south, "grp", -1), other_east, passed_along(north, "grp", 1))
    faces, edge, rim_ground, west, south, east, north = first_edges(
        neighbours, wet_mask, edge_spill, low, high, ground, (west, south, east, north), others
    )
    others = (
        passed_along(west, "tile", -1),
        passed_along(south, "grp", -1),
        passed_along(east, "tile", 1),
        passed_along(north, "grp", 1),
    )
    block_x, block_w = gate((block_x, block_w), (*others, arrived_high))
    relayed = passed_to(block_w, second_leg)
    block_x = passed_to(block_x, next_chip_swapped)
    columns, rows = second_edges(neighbours, faces, edge, rim_ground, ground, (west, south, east, north), others)
    out = None
    for shifts, states in (
        ((0, 0), (own,)),
        (A_SHIFTS, (arrived_low, arrived_high)),
        (W_SHIFTS, (block_w, relayed)),
        (X_SHIFTS, (block_x,)),
    ):
        out = run_block(shifts, destination, wet_mask, terrain, columns, rows, spill, states, out)
    return out


def solution(mesh):
    in_specs = (
        P("grp", "tile", None, None, None),
        P("grp", "tile", None, None, None),
        P("grp", None),
        P("grp", "tile"),
        P("grp", "tile", None),
        P("grp", "tile", None),
        P("grp", "tile", None),
    )
    out_specs = P("grp", "tile", None, None, None)
    return jax.shard_map(body, mesh=mesh, in_specs=in_specs, out_specs=out_specs, check_vma=False)
```

```python
import functools

import jax
import jax.numpy as jnp
from jax import lax
from jax.experimental import pallas as pl
from jax.experimental.pallas import tpu as pltpu
from jax.sharding import PartitionSpec as P

F32 = jnp.float32
GRAVITY = 9.81
SPACING = 10.0
TIMESTEP = 0.2
CENTRE_WEIGHT = 0.7
DEPTH_FLOOR = 0.1
SIDE = 256
HALF = 128
BLOCKS = 4
RIVERS = 16
ROWS = 64
GAIN = TIMESTEP / (SPACING * SPACING)
RATIO = TIMESTEP / SPACING

ANY = pl.BlockSpec(memory_space=pl.ANY)
VMEM = pl.BlockSpec(memory_space=pltpu.VMEM)
SMEM = pl.BlockSpec(memory_space=pltpu.SMEM)
HBM = pl.BlockSpec(memory_space=pltpu.HBM)
RING = 4
A_SHIFTS = (2, 2)
W_SHIFTS = (3, 1)
X_SHIFTS = (1, 3)


def shape(*dims):
    return jax.ShapeDtypeStruct(dims, F32)


def cost(flops, bytes_accessed):
    return pl.CostEstimate(flops=flops, bytes_accessed=bytes_accessed, transcendentals=0)


def face(eta_l, eta_r, z_l, z_r, rough, flow_left, flow_mid, flow_right):
    depth = jnp.maximum(eta_l, eta_r) - jnp.maximum(z_l, z_r)
    floored = jnp.maximum(depth, DEPTH_FLOOR)
    blended = CENTRE_WEIGHT * flow_mid + 0.5 * (1.0 - CENTRE_WEIGHT) * (flow_left + flow_right)
    slope = (GRAVITY * TIMESTEP / SPACING) * depth * (eta_r - eta_l)
    friction = 1.0 + (GRAVITY * TIMESTEP) * rough * rough * jnp.abs(flow_mid) * jnp.exp(
        (-7.0 / 3.0) * jnp.log(floored)
    )
    return (blended - slope) / friction


def core():
    return lax.rem(lax.axis_index("tile"), 2)


def params(mib):
    return pltpu.CompilerParams(vmem_limit_bytes=mib << 20)


def tile_offset(dest_ref, tile, slot):
    tiles = lax.axis_size("tile")
    return lax.rem(lax.div(dest_ref[0, tile * BLOCKS + slot], BLOCKS) - tile + tiles, tiles)


def leaving_slot(dest_ref, shift):
    me = lax.axis_index("tile")
    slot = jnp.int32(0)
    for j in range(1, BLOCKS):
        slot = jnp.where(tile_offset(dest_ref, me, j) == shift, j, slot)
    return slot


def landing_slot(dest_ref, shift, back=0):
    tiles = lax.axis_size("tile")
    sender = lax.rem(lax.axis_index("tile") - shift - back + 2 * tiles, tiles)
    slot = jnp.int32(0)
    for j in range(BLOCKS):
        place = lax.rem(dest_ref[0, sender * BLOCKS + j], BLOCKS)
        slot = jnp.where(tile_offset(dest_ref, sender, j) == shift, place, slot)
    return slot


def lanes(rows, columns):
    return lax.broadcasted_iota(jnp.int32, (rows, columns), 1)


CUT = 64


def in_hbm(x):
    return pltpu.with_memory_space_constraint(x, pltpu.HBM)


def pick_kernel(dest, state, first, second, sems):
    slot = leaving_slot(dest, 2)
    loads = [
        pltpu.make_async_copy(state.at[0, slot, :, rows], ref, sems.at[i])
        for i, (rows, ref) in enumerate(((pl.ds(0, CUT), first), (pl.ds(CUT, SIDE - CUT), second)))
    ]
    for load in loads:
        load.start()
    for load in loads:
        load.wait()


def pick_a(dest, state):
    return pl.pallas_call(
        pick_kernel,
        out_shape=[shape(3, CUT, SIDE), shape(3, SIDE - CUT, SIDE)],
        in_specs=[SMEM, HBM],
        out_specs=[VMEM] * 2,
        scratch_shapes=[pltpu.SemaphoreType.DMA((2,))],
        compiler_params=params(4),
        cost_estimate=cost(0, 0),
    )(dest, state)


def prepare_kernel(
    dest, state, a_low, a_high, ground_in,
    own, block_w, block_x, low, high, pack0, pack1, pack2, pack3, pack4, pack_back, terrain, sems,
):
    slots = [leaving_slot(dest, k) for k in range(BLOCKS)]
    first_core = core() == 0
    slot_w = jnp.where(first_core, slots[1], slots[3])
    slot_x = jnp.where(first_core, slots[3], slots[1])
    held = (block_w, block_x, own)
    loads = [pltpu.make_async_copy(ground_in, terrain, sems.at[3])]
    for i, (slot, ref) in enumerate(zip((slot_w, slot_x, slots[0]), held)):
        loads.append(pltpu.make_async_copy(state.at[0, slot], ref, sems.at[i]))
    for load in loads:
        load.start()
    lane = lanes(SIDE, HALF)

    def strips(first_part, second_part, write):
        def side(columns):
            parts = [[half[f, :, columns] for half in (first_part, second_part)] for f in range(3)]
            return [jnp.concatenate(part) for part in parts]

        west = side(slice(0, HALF))
        east = side(slice(HALF, SIDE))
        packed = jnp.where(lane < 3, west[0], pltpu.roll(west[1], 3, 1))
        packed = jnp.where(lane < 6, packed, pltpu.roll(west[2], 6, 1))
        packed = jnp.where(lane < 8, packed, pltpu.roll(east[0], 10, 1))
        packed = jnp.where(lane < 10, packed, pltpu.roll(east[1], 13, 1))
        packed = jnp.where(lane < 13, packed, pltpu.roll(east[2], 14, 1))
        turned = packed.T
        south = jnp.concatenate([first_part[0, 0:3], first_part[2, 0:3], first_part[1, 0:2]])
        north = jnp.concatenate(
            [
                second_part[0, SIDE - CUT - 2 : SIDE - CUT],
                second_part[2, SIDE - CUT - 3 : SIDE - CUT],
                second_part[1, SIDE - CUT - 1 : SIDE - CUT],
                jnp.zeros((2, SIDE), F32),
            ]
        )
        write(turned[0:8], south, turned[8:16], north)

    strip_out = (pack0, pack1, pack2, pack3)
    west_out = (pack_back.at[0], pack0.at[4], pack1.at[5], pack2.at[5])
    east_out = (pack1.at[4], pack2.at[4], pack3.at[4], pack4.at[0])

    def write(k, west, south, east, north):
        for i, value in enumerate((west, south, east, north)):
            strip_out[k][i] = value
        west_out[k][...] = west
        east_out[k][...] = east

    def write_by_core(first, second):
        def both(*values):
            pl.when(first_core)(lambda: write(first, *values))
            pl.when(jnp.logical_not(first_core))(lambda: write(second, *values))

        return both

    strips(a_low, a_high, functools.partial(write, 2))
    loads[0].wait()
    for b in range(BLOCKS):
        west = [terrain[0, b, f, :, :HALF] for f in range(2)]
        east = [terrain[0, b, f, :, HALF:] for f in range(2)]
        packed = jnp.where(lane < 3, west[0], pltpu.roll(west[1], 3, 1))
        packed = jnp.where(lane < 5, packed, pltpu.roll(east[0], 7, 1))
        packed = jnp.where(lane < 7, packed, pltpu.roll(east[1], 9, 1))
        turned = packed.T
        for q in range(5):
            low[q, b : b + 1] = turned[q : q + 1]
        for q in range(4):
            high[q, b : b + 1] = turned[5 + q : 6 + q]
        for q in range(3):
            low[q, 4 + b : 5 + b] = terrain[0, b, 0, q : q + 1]
        for q in range(2):
            low[3 + q, 4 + b : 5 + b] = terrain[0, b, 1, q : q + 1]
            high[q, 4 + b : 5 + b] = terrain[0, b, 0, SIDE - 2 + q : SIDE - 1 + q]
            high[2 + q, 4 + b : 5 + b] = terrain[0, b, 1, SIDE - 2 + q : SIDE - 1 + q]
    pack1[6, 0:4] = high[1, 0:4]
    pack1[6, 4:8] = high[3, 0:4]
    pack_back[1] = low[0]
    writers = (write_by_core(1, 3), write_by_core(3, 1), functools.partial(write, 0))
    for load, ref, write_out in zip(loads[1:], held, writers):
        load.wait()
        strips(ref.at[:, pl.ds(0, CUT)], ref.at[:, pl.ds(CUT, SIDE - CUT)], write_out)


def prepare(dest, state, a_low, a_high, terrain):
    packs = [shape(count, 8, SIDE) for count in (5, 7, 6, 5, 1, 2)]
    return pl.pallas_call(
        prepare_kernel,
        out_shape=[shape(3, SIDE, SIDE)] * 3 + [shape(5, 8, SIDE), shape(4, 8, SIDE)] + packs,
        in_specs=[SMEM, HBM, VMEM, VMEM, HBM],
        out_specs=[VMEM] * 11,
        scratch_shapes=[
            pltpu.VMEM((1, BLOCKS, 2, SIDE, SIDE), F32),
            pltpu.SemaphoreType.DMA((BLOCKS,)),
        ],
        compiler_params=params(12),
        cost_estimate=cost(0, 0),
    )(dest, state, a_low, a_high, terrain)


def gate_kernel(count, *refs):
    del count, refs


def gate(values, keys):
    count = len(values)
    return pl.pallas_call(
        functools.partial(gate_kernel, count),
        out_shape=[jax.ShapeDtypeStruct(v.shape, v.dtype) for v in values],
        in_specs=[ANY] * (count + len(keys)),
        out_specs=[ANY] * count,
        input_output_aliases={i: i for i in range(count)},
        compiler_params=params(1),
        cost_estimate=cost(0, 0),
    )(*values, *keys)


def arrange_kernel(
    dest, pack0, pack1, pack2, pack3, pack4, pack_back, ground_low, ground_high,
    low, high, west, south, east, north, other_west, other_east,
):
    for out in (west, south, east, north, other_west, other_east):
        out[...] = jnp.zeros_like(out)
    strips = (pack0, pack1, pack2, pack3)
    west_in = (pack_back.at[0], pack0.at[4], pack1.at[5], pack2.at[5])
    east_in = (pack1.at[4], pack2.at[4], pack3.at[4], pack4.at[0])
    for k in range(BLOCKS):
        strip = strips[k]
        slot = landing_slot(dest, k)
        for side, (low_out, high_out) in enumerate(((west, east), (south, north))):
            row = pl.ds(side * 4 + slot, 1)
            for q in range(8):
                low[q, row] = strip[side, q : q + 1]
            for q in range(6):
                high[q, row] = strip[2 + side, q : q + 1]
            low_out[slot, 0:1] = strip[side, 0:1]
            low_out[slot, 1:2] = strip[side, 3:4]
            high_out[slot, 0:1] = strip[2 + side, 1:2]
            high_out[slot, 1:3] = strip[2 + side, 3:5]
        slot = landing_slot(dest, k, 1)
        other_east[slot, 0:1] = east_in[k][1:2]
        other_east[slot, 1:3] = east_in[k][3:5]
        slot = landing_slot(dest, k, -1)
        other_west[slot, 0:1] = west_in[k][0:1]
        other_west[slot, 1:2] = west_in[k][3:4]
    for b in range(BLOCKS):
        for side, (low_out, high_out) in enumerate(((west, east), (south, north))):
            sub = slice(side * 4 + b, side * 4 + b + 1)
            low_out[b, 2:3] = ground_low[0, sub]
            high_out[b, 3:4] = ground_high[1, sub]
            high_out[b, 4:5] = ground_high[3, sub]
        other_east[b, 3:4] = pack1[6, b : b + 1]
        other_east[b, 4:5] = pack1[6, 4 + b : 5 + b]
        other_west[b, 2:3] = pack_back[1, b : b + 1]


def arrange(dest, packs, ground):
    return pl.pallas_call(
        arrange_kernel,
        out_shape=[shape(8, 8, SIDE), shape(6, 8, SIDE)] + [shape(BLOCKS, 8, SIDE)] * 6,
        in_specs=[SMEM] + [VMEM] * 8,
        out_specs=[VMEM] * 8,
        compiler_params=params(4),
        cost_estimate=cost(0, 0),
    )(dest, *packs, *ground)


def pick(entry, own, other):
    near = own[jnp.clip(entry, 0, BLOCKS - 1)]
    far = other[jnp.clip(entry - BLOCKS, 0, BLOCKS - 1)]
    return jnp.where(entry >= BLOCKS, far, near)


def gather_rims(entries, own, other, rim_low, rim_high, has, low_count, high_count):
    for b in range(BLOCKS):
        for side in range(2):
            sub = slice(side * 4 + b, side * 4 + b + 1)
            entry = entries[0, b, 2 * side]
            alive = entry >= 0
            rows = jnp.where(alive, pick(entry, own[2 + side], other[2 + side]), 0.0)
            for q in range(low_count):
                rim_low[q, sub] = rows[q : q + 1]
            has[0, sub] = jnp.full((1, SIDE), jnp.where(alive, 1.0, 0.0), F32)
            entry = entries[0, b, 2 * side + 1]
            alive = entry >= 0
            rows = jnp.where(alive, pick(entry, own[side], other[side]), 0.0)
            for q in range(high_count):
                rim_high[q, sub] = rows[q : q + 1]
            has[1, sub] = jnp.full((1, SIDE), jnp.where(alive, 1.0, 0.0), F32)


def sides_swapped(x):
    return pltpu.roll(x, 4, 0)


def along_edge(h, z, rough, flow, spot, face_before, face_first, face_last):
    lane = lanes(8, SIDE)
    eta = h + z
    flux = face(
        eta, pltpu.roll(eta, SIDE - 1, 1), z, pltpu.roll(z, SIDE - 1, 1), rough,
        pltpu.roll(flow, 1, 1), flow, pltpu.roll(flow, SIDE - 1, 1),
    )
    here = slice(spot, spot + 1)
    flux = jnp.where(lane == 0, sides_swapped(face_first)[:, here], flux)
    flux = jnp.where(lane == SIDE - 1, sides_swapped(face_last)[:, here], flux)
    lower = jnp.where(lane == 0, sides_swapped(face_before)[:, here], pltpu.roll(flux, 1, 1))
    return lower - flux


def first_edges_kernel(
    entries, wet, edge_spill, key, low, high, ground_low, ground_high,
    own_w, own_s, own_e, own_n, oth_w, oth_s, oth_e, oth_n,
    faces, edge, rim_ground, west, south, east, north,
    rim_low, rim_high, has, wetness,
):
    gather_rims(
        entries, (own_w, own_s, own_e, own_n), (oth_w, oth_s, oth_e, oth_n), rim_low, rim_high, has, 5, 3
    )
    for b in range(BLOCKS):
        value = jnp.full((1, SIDE), wet[0, b].astype(F32), F32)
        wetness[b : b + 1] = value
        wetness[4 + b : 5 + b] = value
    hm, qmm, qm, zm, nm = (rim_low[q] for q in range(5))
    hp, qp, zp = (rim_high[q] for q in range(3))
    h0, h1, h2, q0, q1, q2, t0, t1 = (low[q] for q in range(8))
    z0, z1, z2, n0, n1 = (ground_low[q] for q in range(5))
    hy, hz, qx, qy, qz, tz = (high[q] for q in range(6))
    zy, zz, ny, nz = (ground_high[q] for q in range(4))
    face_m = face(hm + zm, h0 + z0, zm, z0, nm, qmm, qm, q0) * has[0]
    face_0 = face(h0 + z0, h1 + z1, z0, z1, n0, qm, q0, q1)
    face_1 = face(h1 + z1, h2 + z2, z1, z2, n1, q0, q1, q2)
    face_y = face(hy + zy, hz + zz, zy, zz, ny, qx, qy, qz)
    face_z = face(hz + zz, hp + zp, zz, zp, nz, qy, qz, qp) * has[1]
    beside = (face_m, face_0, face_z)
    wets = wetness[...]
    new_0 = (h0 + RATIO * (face_m - face_0 + along_edge(h0, z0, n0, t0, 0, *beside)) + edge_spill[0]) * wets
    new_1 = (h1 + RATIO * (face_0 - face_1 + along_edge(h1, z1, n1, t1, 1, *beside)) + edge_spill[1]) * wets
    new_z = (hz + RATIO * (face_y - face_z + along_edge(hz, zz, nz, tz, SIDE - 1, *beside)) + edge_spill[2]) * wets
    faces[0] = face_m
    faces[1] = face_0
    faces[2] = face_z
    rim_ground[0] = zm
    rim_ground[1] = nm
    rim_ground[2] = zp
    flow_0, flow_1, flow_y, flow_z = (f * wets for f in (face_0, face_1, face_y, face_z))
    for i, value in enumerate((new_0, new_1, flow_0, flow_1, new_z, flow_y, flow_z)):
        edge[i] = value
    for out in (west, south, east, north):
        out[...] = jnp.zeros_like(out)
    for b in range(BLOCKS):
        for side, (low_out, high_out) in enumerate(((west, east), (south, north))):
            sub = slice(side * 4 + b, side * 4 + b + 1)
            low_out[b, 0:1] = new_0[sub]
            low_out[b, 1:2] = flow_0[sub]
            high_out[b, 0:1] = new_z[sub]
            high_out[b, 1:2] = flow_y[sub]
            high_out[b, 2:3] = flow_z[sub]


def first_edges(entries, wet, edge_spill, key, low, high, ground, own, other):
    return pl.pallas_call(
        first_edges_kernel,
        out_shape=[shape(3, 8, SIDE), shape(7, 8, SIDE), shape(3, 8, SIDE)] + [shape(BLOCKS, 8, SIDE)] * 4,
        in_specs=[SMEM, SMEM, VMEM, ANY] + [VMEM] * 12,
        out_specs=[VMEM] * 7,
        scratch_shapes=[
            pltpu.VMEM((5, 8, SIDE), F32),
            pltpu.VMEM((3, 8, SIDE), F32),
            pltpu.VMEM((2, 8, SIDE), F32),
            pltpu.VMEM((8, SIDE), F32),
        ],
        compiler_params=params(4),
        cost_estimate=cost(0, 0),
    )(entries, wet, edge_spill, key, low, high, *ground, *own, *other)


def second_edges_kernel(
    entries, faces, edge, rim_ground, ground_low, ground_high,
    own_w, own_s, own_e, own_n, oth_w, oth_s, oth_e, oth_n,
    columns, rows, rim_low, rim_high, has, stack,
):
    gather_rims(
        entries, (own_w, own_s, own_e, own_n), (oth_w, oth_s, oth_e, oth_n), rim_low, rim_high, has, 3, 2
    )
    hm, qmm, qm = (rim_low[q] for q in range(3))
    hp, qp = (rim_high[q] for q in range(2))
    zm, nm, zp = (rim_ground[q] for q in range(3))
    h0, h1, q0, q1, hz, qy, qz = (edge[q] for q in range(7))
    z0, z1, n0 = ground_low[0], ground_low[1], ground_low[3]
    zz, nz = ground_high[1], ground_high[3]
    face_m = face(hm + zm, h0 + z0, zm, z0, nm, qmm, qm, q0) * has[0]
    face_0 = face(h0 + z0, h1 + z1, z0, z1, n0, qm, q0, q1)
    face_z = face(hz + zz, hp + zp, zz, zp, nz, qy, qz, qp) * has[1]
    every = (faces[0], faces[1], faces[2], face_m, face_0, face_z)
    stack[...] = jnp.zeros_like(stack)
    rows[...] = jnp.zeros_like(rows)
    for b in range(BLOCKS):
        for i, value in enumerate(every):
            stack[b * 8 + i : b * 8 + i + 1] = value[b : b + 1]
            rows[b, i : i + 1] = value[4 + b : 5 + b]
    turned = stack[...].T
    columns[0] = turned
    for b in range(1, BLOCKS):
        columns[b] = pltpu.roll(turned, HALF - 8 * b, 1)


def second_edges(entries, faces, edge, rim_ground, ground, own, other):
    return pl.pallas_call(
        second_edges_kernel,
        out_shape=[shape(BLOCKS, SIDE, HALF), shape(BLOCKS, 8, SIDE)],
        in_specs=[SMEM] + [VMEM] * 13,
        out_specs=[VMEM] * 2,
        scratch_shapes=[
            pltpu.VMEM((3, 8, SIDE), F32),
            pltpu.VMEM((2, 8, SIDE), F32),
            pltpu.VMEM((2, 8, SIDE), F32),
            pltpu.VMEM((HALF, SIDE), F32),
        ],
        compiler_params=params(4),
        cost_estimate=cost(0, 0),
    )(entries, faces, edge, rim_ground, *ground, *own, *other)


def inflow_kernel(cells, rates, spill, edge_spill):
    spill[...] = jnp.zeros_like(spill)
    edge_spill[...] = jnp.zeros_like(edge_spill)
    lane = lanes(1, SIDE)
    for b in range(BLOCKS):

        def point(p, carry, b=b):
            cell = cells[0, b, p]
            row = lax.div(cell, SIDE)
            column = lax.rem(cell, SIDE)
            rate = GAIN * rates[0, b, p]
            at_column = jnp.where(lane == column, rate, 0.0)
            at_row = jnp.where(lane == row, rate, 0.0)
            line = pl.ds(row, 1)
            spill[b, line] = spill[b, line] + at_column
            for i, place in enumerate((0, 1, SIDE - 1)):
                edge_spill[i, b : b + 1] += jnp.where(column == place, at_row, 0.0)
                edge_spill[i, 4 + b : 5 + b] += jnp.where(row == place, at_column, 0.0)
            return carry

        lax.fori_loop(0, RIVERS, point, 0)


def lay_inflow(cells, rates):
    return pl.pallas_call(
        inflow_kernel,
        out_shape=[shape(BLOCKS, SIDE, SIDE), shape(3, 8, SIDE)],
        in_specs=[SMEM, SMEM],
        out_specs=[VMEM] * 2,
        compiler_params=params(4),
        cost_estimate=cost(0, 0),
    )(cells, rates)


def block_step(now, ground, spill, columns, rows, base, wetness, write):
    lane = lanes(ROWS, SIDE)
    sub = lax.broadcasted_iota(jnp.int32, (ROWS, SIDE), 0)

    def at(load, field, first, shift):
        if 0 <= first + shift <= SIDE - ROWS:
            return load(field, first + shift)
        return pltpu.roll(load(field, first), -shift % ROWS, 0)

    below = rows(base)
    for first in range(0, SIDE, ROWS):
        h, qx, qy = (at(now, f, first, 0) for f in range(3))
        z, rough = (at(ground, f, first, 0) for f in range(2))
        eta = h + z
        flux_x = face(
            eta, pltpu.roll(eta, SIDE - 1, 1), z, pltpu.roll(z, SIDE - 1, 1), rough,
            pltpu.roll(qx, 1, 1), qx, pltpu.roll(qx, SIDE - 1, 1),
        )
        edge = columns(pl.ds(first, ROWS))
        flux_x = jnp.where(lane == 0, edge[:, base + 1 : base + 2], flux_x)
        flux_x = jnp.where(lane == SIDE - 1, edge[:, base + 2 : base + 3], flux_x)
        flux_w = jnp.where(lane == 0, edge[:, base : base + 1], pltpu.roll(flux_x, 1, 1))
        z_up = at(ground, 0, first, 1)
        flux_y = face(
            eta, at(now, 0, first, 1) + z_up, z, z_up, rough, at(now, 2, first, -1), qy, at(now, 2, first, 1)
        )
        if first == 0:
            flux_y = jnp.where(sub == 0, rows(base + 1), flux_y)
        if first == SIDE - ROWS:
            flux_y = jnp.where(sub == ROWS - 1, rows(base + 2), flux_y)
        flux_s = jnp.where(sub == 0, below, pltpu.roll(flux_y, 1, 0))
        below = flux_y[ROWS - 1 : ROWS]
        depth = h + RATIO * (flux_w - flux_x + flux_s - flux_y) + spill(pl.ds(first, ROWS))
        write(first, depth * wetness, flux_x * wetness, flux_y * wetness)


def block_kernel(shifts, dest, wet, terrain, columns, rows, spill, *refs):
    out, then, done, sems = refs[-4:]
    shift = jnp.where(core() == 0, *shifts)
    slot = landing_slot(dest, shift)
    wetness = wet[0, slot].astype(F32)
    if shifts == W_SHIFTS:
        for here, ref in enumerate(refs[:2]):

            @pl.when(core() == 1 - here)
            def _(ref=ref):
                copy = pltpu.make_async_copy(ref, done, sems.at[0])
                copy.start()
                copy.wait()

        parts = (done,)
    elif shifts == A_SHIFTS:
        parts = refs[:2]
    else:
        parts = refs[:1]
    copies = []

    def now(field, first):
        if len(parts) == 1:
            return parts[0][field, first : first + ROWS]
        if first + ROWS <= CUT:
            return parts[0][field, first : first + ROWS]
        if first >= CUT:
            return parts[1][field, first - CUT : first - CUT + ROWS]
        return jnp.concatenate([parts[0][field, first:CUT], parts[1][field, 0 : first + ROWS - CUT]])

    def ground(field, first):
        return terrain[0, slot, field, first : first + ROWS]

    def keep(first, *fields):
        for f, value in enumerate(fields):
            then[f, first : first + ROWS] = value

    def finish(first, *fields):
        for f, value in enumerate(fields):
            done[f, first : first + ROWS] = value
        lines = pl.ds(first, ROWS)
        copies.append(pltpu.make_async_copy(done.at[:, lines], out.at[0, slot, :, lines], sems.at[len(copies)]))
        copies[-1].start()

    shared = (
        lambda at: spill[slot, at],
        lambda at: columns[slot, at],
        lambda q: rows[slot, q : q + 1],
    )
    block_step(now, ground, *shared, 0, wetness, keep)
    block_step(lambda f, first: then[f, first : first + ROWS], ground, *shared, 3, wetness, finish)
    for copy in copies:
        copy.wait()


def run_block(shifts, dest, wet, terrain, columns, rows, spill, states, out):
    args = [dest, wet, terrain, columns, rows, spill, *states]
    specs = [SMEM] * 2 + [VMEM] * 4 + [ANY if shifts == W_SHIFTS else VMEM] * len(states)
    aliases = {}
    if out is not None:
        aliases = {len(args): 0}
        args.append(out)
        specs.append(ANY)
    return pl.pallas_call(
        functools.partial(block_kernel, shifts),
        out_shape=shape(1, BLOCKS, 3, SIDE, SIDE),
        in_specs=specs,
        out_specs=ANY,
        input_output_aliases=aliases,
        scratch_shapes=[
            pltpu.VMEM((3, SIDE, SIDE), F32),
            pltpu.VMEM((3, SIDE, SIDE), F32),
            pltpu.SemaphoreType.DMA((SIDE // ROWS,)),
        ],
        compiler_params=params(16),
        cost_estimate=cost(0, 0),
    )(*args)


def passed_along(x, axis, by, wrap=True):
    devices = lax.axis_size(axis)
    return lax.ppermute(x, axis, [(i, (i + by) % devices) for i in range(devices)])


def passed_to(x, target):
    devices = lax.axis_size("tile")
    pairs = [(i, target(i // 2, i % 2)) for i in range(devices)]
    return lax.ppermute(x, "tile", [(i, t % devices) for i, t in pairs if t is not None])


def back_one(chip):
    return chip // RING * RING + (chip - 1) % RING


def first_leg(chip, at):
    return 2 * chip + 1 if at == 0 else 2 * back_one(chip)


def second_leg(chip, at):
    sender = chip // RING * RING + (chip + 1) % RING
    return 2 * (sender + 2) if at == 0 else None


def next_chip_swapped(chip, at):
    return 2 * (chip + 1) + 1 - at


def body(flood_state, terrain, destination, wet_mask, neighbours, inflow_cells, inflow_rates):
    dest, state = in_hbm(destination), in_hbm(flood_state)
    a_low, a_high = pick_a(dest, state)
    arrived_low = passed_along(a_low, "tile", 2)
    own, block_w, block_x, *rest = prepare(dest, state, a_low, a_high, in_hbm(terrain))
    ground, packs = rest[:2], rest[2:]
    (packs[5],) = gate((packs[5],), (arrived_low,))
    packs = [packs[0]] + [passed_along(p, "tile", d) for d, p in zip((1, 2, 3, 4, -1), packs[1:])]
    block_x, block_w = gate((block_x, block_w), packs[1:])
    arrived_x = passed_to(block_x, next_chip_swapped)
    block_w = passed_to(block_w, first_leg)
    spill, edge_spill = lay_inflow(inflow_cells, inflow_rates)
    low, high, west, south, east, north, other_west, other_east = arrange(destination, packs, ground)
    others = (other_west, passed_along(south, "grp", -1), other_east, passed_along(north, "grp", 1))
    faces, edge, rim_ground, west, south, east, north = first_edges(
        neighbours, wet_mask, edge_spill, block_w, low, high, ground, (west, south, east, north), others
    )
    others = (
        passed_along(west, "tile", -1),
        passed_along(south, "grp", -1),
        passed_along(east, "tile", 1),
        passed_along(north, "grp", 1),
    )
    a_high, block_w = gate((a_high, block_w), (*others, arrived_x))
    arrived_high = passed_along(a_high, "tile", 2)
    relayed = passed_to(block_w, second_leg)
    columns, rows = second_edges(neighbours, faces, edge, rim_ground, ground, (west, south, east, north), others)
    out = None
    for shifts, states in (
        ((0, 0), (own,)),
        (X_SHIFTS, (arrived_x,)),
        (W_SHIFTS, (block_w, relayed)),
        (A_SHIFTS, (arrived_low, arrived_high)),
    ):
        out = run_block(shifts, destination, wet_mask, terrain, columns, rows, spill, states, out)
    return out


def solution(mesh):
    in_specs = (
        P("grp", "tile", None, None, None),
        P("grp", "tile", None, None, None),
        P("grp", None),
        P("grp", "tile"),
        P("grp", "tile", None),
        P("grp", "tile", None),
        P("grp", "tile", None),
    )
    out_specs = P("grp", "tile", None, None, None)
    return jax.shard_map(body, mesh=mesh, in_specs=in_specs, out_specs=out_specs, check_vma=False)
```

```python
import functools

import jax
import jax.numpy as jnp
from jax import lax
from jax.experimental import pallas as pl
from jax.experimental.pallas import tpu as pltpu
from jax.sharding import PartitionSpec as P

F32 = jnp.float32
GRAVITY = 9.81
SPACING = 10.0
TIMESTEP = 0.2
CENTRE_WEIGHT = 0.7
DEPTH_FLOOR = 0.1
SIDE = 256
HALF = 128
BLOCKS = 4
RIVERS = 16
ROWS = 64
GAIN = TIMESTEP / (SPACING * SPACING)
RATIO = TIMESTEP / SPACING

ANY = pl.BlockSpec(memory_space=pl.ANY)
VMEM = pl.BlockSpec(memory_space=pltpu.VMEM)
SMEM = pl.BlockSpec(memory_space=pltpu.SMEM)
HBM = pl.BlockSpec(memory_space=pltpu.HBM)
RING = 4
A_SHIFTS = (2, 2)
W_SHIFTS = (3, 1)
X_SHIFTS = (1, 3)


def shape(*dims):
    return jax.ShapeDtypeStruct(dims, F32)


def cost(flops, bytes_accessed):
    return pl.CostEstimate(flops=flops, bytes_accessed=bytes_accessed, transcendentals=0)


def face(eta_l, eta_r, z_l, z_r, rough, flow_left, flow_mid, flow_right):
    depth = jnp.maximum(eta_l, eta_r) - jnp.maximum(z_l, z_r)
    floored = jnp.maximum(depth, DEPTH_FLOOR)
    blended = CENTRE_WEIGHT * flow_mid + 0.5 * (1.0 - CENTRE_WEIGHT) * (flow_left + flow_right)
    slope = (GRAVITY * TIMESTEP / SPACING) * depth * (eta_r - eta_l)
    friction = 1.0 + (GRAVITY * TIMESTEP) * rough * rough * jnp.abs(flow_mid) * jnp.exp(
        (-7.0 / 3.0) * jnp.log(floored)
    )
    return (blended - slope) / friction


def core():
    return lax.rem(lax.axis_index("tile"), 2)


def params(mib):
    return pltpu.CompilerParams(vmem_limit_bytes=mib << 20)


def tile_offset(dest_ref, tile, slot):
    tiles = lax.axis_size("tile")
    return lax.rem(lax.div(dest_ref[0, tile * BLOCKS + slot], BLOCKS) - tile + tiles, tiles)


def leaving_slot(dest_ref, shift):
    me = lax.axis_index("tile")
    slot = jnp.int32(0)
    for j in range(1, BLOCKS):
        slot = jnp.where(tile_offset(dest_ref, me, j) == shift, j, slot)
    return slot


def landing_slot(dest_ref, shift, back=0):
    tiles = lax.axis_size("tile")
    sender = lax.rem(lax.axis_index("tile") - shift - back + 2 * tiles, tiles)
    slot = jnp.int32(0)
    for j in range(BLOCKS):
        place = lax.rem(dest_ref[0, sender * BLOCKS + j], BLOCKS)
        slot = jnp.where(tile_offset(dest_ref, sender, j) == shift, place, slot)
    return slot


def lanes(rows, columns):
    return lax.broadcasted_iota(jnp.int32, (rows, columns), 1)


def in_hbm(x):
    return pltpu.with_memory_space_constraint(x, pltpu.HBM)


def pick_kernel(dest, state, block_a, block_w, sems):
    slots = [leaving_slot(dest, k) for k in range(1, BLOCKS)]
    slot_w = jnp.where(core() == 0, slots[0], slots[2])
    loads = [
        pltpu.make_async_copy(state.at[0, slot], ref, sems.at[i])
        for i, (slot, ref) in enumerate(((slots[1], block_a), (slot_w, block_w)))
    ]
    for load in loads:
        load.start()
    for load in loads:
        load.wait()


def pick_early(dest, state):
    return pl.pallas_call(
        pick_kernel,
        out_shape=[shape(3, SIDE, SIDE)] * 2,
        in_specs=[SMEM, HBM],
        out_specs=[VMEM] * 2,
        scratch_shapes=[pltpu.SemaphoreType.DMA((2,))],
        compiler_params=params(4),
        cost_estimate=cost(0, 0),
    )(dest, state)


def prepare_kernel(
    dest, entries, state, block_a, block_w, ground_in, cells, rates,
    own, block_x, low, high, pack0, pack1, pack2, pack3, pack4, terrain, sems,
):
    slots = [leaving_slot(dest, k) for k in range(BLOCKS)]
    first_core = core() == 0
    slot_x = jnp.where(first_core, slots[3], slots[1])
    held = (block_x, own)
    loads = [pltpu.make_async_copy(ground_in, terrain, sems.at[3])]
    for i, (slot, ref) in enumerate(zip((slot_x, slots[0]), held)):
        loads.append(pltpu.make_async_copy(state.at[0, slot], ref, sems.at[i]))
    for load in loads:
        load.start()
    lane = lanes(SIDE, HALF)

    def strips(ref, write):
        west = [ref[f, :, :HALF] for f in range(3)]
        east = [ref[f, :, HALF:] for f in range(3)]
        packed = jnp.where(lane < 3, west[0], pltpu.roll(west[1], 3, 1))
        packed = jnp.where(lane < 6, packed, pltpu.roll(west[2], 6, 1))
        packed = jnp.where(lane < 8, packed, pltpu.roll(east[0], 10, 1))
        packed = jnp.where(lane < 10, packed, pltpu.roll(east[1], 13, 1))
        packed = jnp.where(lane < 13, packed, pltpu.roll(east[2], 14, 1))
        turned = packed.T
        south = jnp.concatenate([ref[0, 0:3], ref[2, 0:3], ref[1, 0:2]])
        north = jnp.concatenate(
            [ref[0, SIDE - 2 : SIDE], ref[2, SIDE - 3 : SIDE], ref[1, SIDE - 1 : SIDE], jnp.zeros((2, SIDE), F32)]
        )
        write(turned[0:8], south, turned[8:16], north)

    strip_out = (pack0, pack1, pack2, pack3)
    east_out = (pack1.at[4], pack2.at[4], pack3.at[4], pack4.at[0])

    def write(k, west, south, east, north):
        for i, value in enumerate((west, south, east, north)):
            strip_out[k][i] = value
        east_out[k][...] = east

    def write_by_core(first, second):
        def both(*values):
            pl.when(first_core)(lambda: write(first, *values))
            pl.when(jnp.logical_not(first_core))(lambda: write(second, *values))

        return both

    strips(block_a, functools.partial(write, 2))
    strips(block_w, write_by_core(1, 3))
    spill = jnp.zeros((BLOCKS, SIDE), F32)
    along = lanes(BLOCKS, SIDE)
    for p in range(RIVERS):
        cell = cells[0, :, p : p + 1]
        there = (along * SIDE + SIDE - 1) == cell
        spill = spill + jnp.where(there, GAIN * rates[0, :, p : p + 1], 0.0)
    loads[0].wait()
    for b in range(BLOCKS):
        west = [terrain[0, b, f, :, :HALF] for f in range(2)]
        east = [terrain[0, b, f, :, HALF:] for f in range(2)]
        packed = jnp.where(lane < 3, west[0], pltpu.roll(west[1], 3, 1))
        packed = jnp.where(lane < 5, packed, pltpu.roll(east[0], 7, 1))
        packed = jnp.where(lane < 7, packed, pltpu.roll(east[1], 9, 1))
        turned = packed.T
        for q in range(5):
            low[q, b : b + 1] = turned[q : q + 1]
        for q in range(4):
            high[q, b : b + 1] = turned[5 + q : 6 + q]
        for q in range(3):
            low[q, 4 + b : 5 + b] = terrain[0, b, 0, q : q + 1]
        for q in range(2):
            low[3 + q, 4 + b : 5 + b] = terrain[0, b, 1, q : q + 1]
            high[q, 4 + b : 5 + b] = terrain[0, b, 0, SIDE - 2 + q : SIDE - 1 + q]
            high[2 + q, 4 + b : 5 + b] = terrain[0, b, 1, SIDE - 2 + q : SIDE - 1 + q]
    for b in range(BLOCKS):
        for q in range(4):
            pack1[5 + b, q : q + 1] = high[q, b : b + 1]
        pack1[5 + b, 4:5] = spill[b : b + 1]
        for side in (2, 3):
            pack1[5 + b, 3 + side : 4 + side] = jnp.full((1, SIDE), entries[0, b, side].astype(F32), F32)
        pack1[5 + b, 7:8] = jnp.zeros((1, SIDE), F32)
    writers = (write_by_core(3, 1), functools.partial(write, 0))
    for load, ref, write_out in zip(loads[1:], held, writers):
        load.wait()
        strips(ref, write_out)


def prepare(dest, entries, state, block_a, block_w, terrain, cells, rates):
    packs = [shape(count, 8, SIDE) for count in (4, 9, 5, 5, 1)]
    return pl.pallas_call(
        prepare_kernel,
        out_shape=[shape(3, SIDE, SIDE)] * 2 + [shape(5, 8, SIDE), shape(4, 8, SIDE)] + packs,
        in_specs=[SMEM, SMEM, HBM, VMEM, VMEM, HBM, VMEM, VMEM],
        out_specs=[VMEM] * 9,
        scratch_shapes=[
            pltpu.VMEM((1, BLOCKS, 2, SIDE, SIDE), F32),
            pltpu.SemaphoreType.DMA((BLOCKS,)),
        ],
        compiler_params=params(12),
        cost_estimate=cost(0, 0),
    )(dest, entries, state, block_a, block_w, terrain, cells, rates)


def gate_kernel(count, *refs):
    del count, refs


def gate(values, keys):
    count = len(values)
    return pl.pallas_call(
        functools.partial(gate_kernel, count),
        out_shape=[jax.ShapeDtypeStruct(v.shape, v.dtype) for v in values],
        in_specs=[ANY] * (count + len(keys)),
        out_specs=[ANY] * count,
        input_output_aliases={i: i for i in range(count)},
        compiler_params=params(1),
        cost_estimate=cost(0, 0),
    )(*values, *keys)


def arrange_kernel(
    dest, pack0, pack1, pack2, pack3, pack4, ground_low, ground_high,
    low, high, west, east, south, north, far_east,
):
    for out in (west, east, south, north):
        out[...] = jnp.zeros_like(out)
    strips = (pack0, pack1, pack2, pack3)
    east_in = (pack1.at[4], pack2.at[4], pack3.at[4], pack4.at[0])
    for k in range(BLOCKS):
        strip = strips[k]
        slot = landing_slot(dest, k)
        for side, (low_out, high_out) in enumerate(((west, east), (south, north))):
            row = pl.ds(side * 4 + slot, 1)
            for q in range(8):
                low[q, row] = strip[side, q : q + 1]
            for q in range(6):
                high[q, row] = strip[2 + side, q : q + 1]
            low_out[slot, 0:1] = strip[side, 0:1]
            low_out[slot, 1:2] = strip[side, 3:4]
            high_out[slot, 0:1] = strip[2 + side, 1:2]
            high_out[slot, 1:3] = strip[2 + side, 3:5]
        slot = landing_slot(dest, k, 1)
        far_east[slot] = east_in[k][...]
        for out in (south, north):
            out[BLOCKS + slot, 0:1] = east_in[k][1:2]
            out[BLOCKS + slot, 1:2] = east_in[k][5:6]
    for b in range(BLOCKS):
        for side, (low_out, high_out) in enumerate(((west, east), (south, north))):
            sub = slice(side * 4 + b, side * 4 + b + 1)
            low_out[b, 2:3] = ground_low[0, sub]
            high_out[b, 3:4] = ground_high[1, sub]
            high_out[b, 4:5] = ground_high[3, sub]
        for out in (south, north):
            out[BLOCKS + b, 2:3] = pack1[5 + b, 1:2]
            out[BLOCKS + b, 3:4] = pack1[5 + b, 3:4]


def arrange(dest, packs, ground):
    rims = [shape(BLOCKS, 8, SIDE)] * 2 + [shape(2 * BLOCKS, 8, SIDE)] * 2 + [shape(BLOCKS, 8, SIDE)]
    return pl.pallas_call(
        arrange_kernel,
        out_shape=[shape(8, 8, SIDE), shape(6, 8, SIDE)] + rims,
        in_specs=[SMEM] + [VMEM] * 7,
        out_specs=[VMEM] * 7,
        compiler_params=params(4),
        cost_estimate=cost(0, 0),
    )(dest, *packs, *ground)


def pick(entry, own, other):
    near = own[jnp.clip(entry, 0, BLOCKS - 1)]
    far = other[jnp.clip(entry - BLOCKS, 0, BLOCKS - 1)]
    return jnp.where(entry >= BLOCKS, far, near)


def gather_rims(entries, own, other, rim_low, rim_high, has, low_count, high_count, from_west):
    for b in range(BLOCKS):
        for side in range(2):
            sub = slice(side * 4 + b, side * 4 + b + 1)
            entry = entries[0, b, 2 * side]
            alive = entry >= 0
            if side == 0:
                near = own[2][jnp.clip(entry, 0, BLOCKS - 1)]
                rows = jnp.where(entry >= BLOCKS, from_west(b, entry), near)
            else:
                rows = pick(entry, own[3], other[3])
            rows = jnp.where(alive, rows, 0.0)
            for q in range(low_count):
                rim_low[q, sub] = rows[q : q + 1]
            has[0, sub] = jnp.full((1, SIDE), jnp.where(alive, 1.0, 0.0), F32)
            entry = entries[0, b, 2 * side + 1]
            alive = entry >= 0
            rows = jnp.where(alive, pick(entry, own[side], other[side]), 0.0)
            for q in range(high_count):
                rim_high[q, sub] = rows[q : q + 1]
            has[1, sub] = jnp.full((1, SIDE), jnp.where(alive, 1.0, 0.0), F32)


def sides_swapped(x):
    return pltpu.roll(x, 4, 0)


def column(x, at):
    return x[:, at : at + 1]


def along_edge(h, z, rough, flow, face_before, face_first, face_last):
    lane = lanes(8, SIDE)
    eta = h + z
    flux = face(
        eta, pltpu.roll(eta, SIDE - 1, 1), z, pltpu.roll(z, SIDE - 1, 1), rough,
        pltpu.roll(flow, 1, 1), flow, pltpu.roll(flow, SIDE - 1, 1),
    )
    flux = jnp.where(lane == 0, face_first, flux)
    flux = jnp.where(lane == SIDE - 1, face_last, flux)
    lower = jnp.where(lane == 0, face_before, pltpu.roll(flux, 1, 1))
    return lower - flux


def west_device_edge(wide, ground_wide, corners_s, corners_n, face_last):
    hy, hz, qx, qy, qz, tz = (wide[q] for q in range(6))
    zy, zz, ny, nz, spill, entry_s, entry_n = (ground_wide[q] for q in range(7))
    face_y = face(hy + zy, hz + zz, zy, zz, ny, qx, qy, qz)

    def chosen(entry, corners, q):
        value = jnp.zeros((8, SIDE), F32)
        for j in range(2 * BLOCKS):
            value = jnp.where(entry == j, corners[q, j : j + 1], value)
        return value

    h_s, t_s, z_s, n_s = (chosen(entry_s, corners_s, q) for q in range(4))
    h_n, t_n, z_n = (chosen(entry_n, corners_n, q) for q in range(3))
    last = SIDE - 1
    has_s = jnp.where(column(entry_s, 0) >= 0.0, 1.0, 0.0)
    has_n = jnp.where(column(entry_n, 0) >= 0.0, 1.0, 0.0)
    eta = hz + zz
    eta_s, eta_n = h_s + z_s, h_n + z_n
    before = face(
        column(eta_s, last), column(eta, 0), column(z_s, last), column(zz, 0), column(n_s, last),
        column(t_s, last - 1), column(t_s, last), column(tz, 0),
    ) * has_s
    first = face(
        column(eta, 0), column(eta, 1), column(zz, 0), column(zz, 1), column(nz, 0),
        column(t_s, last), column(tz, 0), column(tz, 1),
    )
    final = face(
        column(eta, last), column(eta_n, 0), column(zz, last), column(z_n, 0), column(nz, last),
        column(tz, last - 1), column(tz, last), column(t_n, 0),
    ) * has_n
    depth = hz + RATIO * (face_y - face_last + along_edge(hz, zz, nz, tz, before, first, final)) + spill
    return depth, face_y


def first_edges_kernel(
    entries, wet, edge_spill, key, low, high, ground_low, ground_high,
    own_w, own_e, own_s, own_n, far_east, pack1, oth_w, oth_s, oth_n,
    faces, edge, rim_ground, wide_edge, west, south, east, north,
    rim_low, rim_high, has, wetness, wide, ground_wide, corners_s, corners_n,
):
    def from_west(b, entry):
        slot = jnp.clip(entry - BLOCKS, 0, BLOCKS - 1)
        state, ground = far_east[slot], pack1[5 + slot]
        for q in range(6):
            wide[q, b : b + 1] = state[q : q + 1]
        for q in range(7):
            ground_wide[q, b : b + 1] = ground[q : q + 1]
        return jnp.concatenate([state[1:2], state[3:5], ground[1:2], ground[3:4], jnp.zeros((3, SIDE), F32)])

    wide[...] = jnp.zeros_like(wide)
    ground_wide[...] = jnp.zeros_like(ground_wide)
    gather_rims(
        entries, (own_w, own_s, own_e, own_n), (oth_w, oth_s, None, oth_n), rim_low, rim_high, has, 5, 3, from_west
    )
    for j in range(BLOCKS):
        for corners, far in ((corners_s, oth_n), (corners_n, oth_s)):
            corners[0, j : j + 1] = far_east[j, 1:2]
            corners[1, j : j + 1] = far_east[j, 5:6]
            corners[2, j : j + 1] = pack1[5 + j, 1:2]
            corners[3, j : j + 1] = pack1[5 + j, 3:4]
            for q in range(4):
                corners[q, BLOCKS + j : BLOCKS + j + 1] = far[BLOCKS + j, q : q + 1]
    for b in range(BLOCKS):
        value = jnp.full((1, SIDE), wet[0, b].astype(F32), F32)
        wetness[b : b + 1] = value
        wetness[4 + b : 5 + b] = value
    hm, qmm, qm, zm, nm = (rim_low[q] for q in range(5))
    hp, qp, zp = (rim_high[q] for q in range(3))
    h0, h1, h2, q0, q1, q2, t0, t1 = (low[q] for q in range(8))
    z0, z1, z2, n0, n1 = (ground_low[q] for q in range(5))
    hy, hz, qx, qy, qz, tz = (high[q] for q in range(6))
    zy, zz, ny, nz = (ground_high[q] for q in range(4))
    face_m = face(hm + zm, h0 + z0, zm, z0, nm, qmm, qm, q0) * has[0]
    face_0 = face(h0 + z0, h1 + z1, z0, z1, n0, qm, q0, q1)
    face_1 = face(h1 + z1, h2 + z2, z1, z2, n1, q0, q1, q2)
    face_y = face(hy + zy, hz + zz, zy, zz, ny, qx, qy, qz)
    face_z = face(hz + zz, hp + zp, zz, zp, nz, qy, qz, qp) * has[1]
    swapped = [sides_swapped(f) for f in (face_m, face_0, face_z)]

    def beside(spot):
        return [column(f, spot) for f in swapped]

    wide_depth, wide_flow = west_device_edge(wide, ground_wide, corners_s, corners_n, face_m)
    for i, value in enumerate((wide_depth, wide_flow, face_m)):
        wide_edge[i] = value
    wets = wetness[...]
    new_0 = (h0 + RATIO * (face_m - face_0 + along_edge(h0, z0, n0, t0, *beside(0))) + edge_spill[0]) * wets
    new_1 = (h1 + RATIO * (face_0 - face_1 + along_edge(h1, z1, n1, t1, *beside(1))) + edge_spill[1]) * wets
    new_z = (hz + RATIO * (face_y - face_z + along_edge(hz, zz, nz, tz, *beside(SIDE - 1))) + edge_spill[2]) * wets
    faces[0] = face_m
    faces[1] = face_0
    faces[2] = face_z
    rim_ground[0] = zm
    rim_ground[1] = nm
    rim_ground[2] = zp
    flow_0, flow_1, flow_y, flow_z = (f * wets for f in (face_0, face_1, face_y, face_z))
    for i, value in enumerate((new_0, new_1, flow_0, flow_1, new_z, flow_y, flow_z)):
        edge[i] = value
    for out in (west, south, east, north):
        out[...] = jnp.zeros_like(out)
    for b in range(BLOCKS):
        for side, (low_out, high_out) in enumerate(((west, east), (south, north))):
            sub = slice(side * 4 + b, side * 4 + b + 1)
            low_out[b, 0:1] = new_0[sub]
            low_out[b, 1:2] = flow_0[sub]
            high_out[b, 0:1] = new_z[sub]
            high_out[b, 1:2] = flow_y[sub]
            high_out[b, 2:3] = flow_z[sub]


def first_edges(entries, wet, edge_spill, key, low, high, ground, own, far_east, pack1, other):
    return pl.pallas_call(
        first_edges_kernel,
        out_shape=[shape(3, 8, SIDE), shape(7, 8, SIDE), shape(3, 8, SIDE), shape(3, 8, SIDE)]
        + [shape(BLOCKS, 8, SIDE)] * 4,
        in_specs=[SMEM, SMEM, VMEM, ANY] + [VMEM] * 13,
        out_specs=[VMEM] * 8,
        scratch_shapes=[
            pltpu.VMEM((5, 8, SIDE), F32),
            pltpu.VMEM((3, 8, SIDE), F32),
            pltpu.VMEM((2, 8, SIDE), F32),
            pltpu.VMEM((8, SIDE), F32),
            pltpu.VMEM((6, 8, SIDE), F32),
            pltpu.VMEM((7, 8, SIDE), F32),
            pltpu.VMEM((4, 8, SIDE), F32),
            pltpu.VMEM((4, 8, SIDE), F32),
        ],
        compiler_params=params(4),
        cost_estimate=cost(0, 0),
    )(entries, wet, edge_spill, key, low, high, *ground, *own, far_east, pack1, *other)


def second_edges_kernel(
    entries, faces, edge, rim_ground, wide_edge, ground_low, ground_high,
    own_w, own_s, own_e, own_n, oth_w, oth_s, oth_n,
    columns, rows, rim_low, rim_high, has, stack,
):
    def from_west(b, entry):
        rows = [wide_edge[q, b : b + 1] for q in range(3)]
        return jnp.concatenate(rows + [jnp.zeros((5, SIDE), F32)])

    gather_rims(
        entries, (own_w, own_s, own_e, own_n), (oth_w, oth_s, None, oth_n), rim_low, rim_high, has, 3, 2, from_west
    )
    hm, qmm, qm = (rim_low[q] for q in range(3))
    hp, qp = (rim_high[q] for q in range(2))
    zm, nm, zp = (rim_ground[q] for q in range(3))
    h0, h1, q0, q1, hz, qy, qz = (edge[q] for q in range(7))
    z0, z1, n0 = ground_low[0], ground_low[1], ground_low[3]
    zz, nz = ground_high[1], ground_high[3]
    face_m = face(hm + zm, h0 + z0, zm, z0, nm, qmm, qm, q0) * has[0]
    face_0 = face(h0 + z0, h1 + z1, z0, z1, n0, qm, q0, q1)
    face_z = face(hz + zz, hp + zp, zz, zp, nz, qy, qz, qp) * has[1]
    every = (faces[0], faces[1], faces[2], face_m, face_0, face_z)
    stack[...] = jnp.zeros_like(stack)
    rows[...] = jnp.zeros_like(rows)
    for b in range(BLOCKS):
        for i, value in enumerate(every):
            stack[b * 8 + i : b * 8 + i + 1] = value[b : b + 1]
            rows[b, i : i + 1] = value[4 + b : 5 + b]
    turned = stack[...].T
    columns[0] = turned
    for b in range(1, BLOCKS):
        columns[b] = pltpu.roll(turned, HALF - 8 * b, 1)


def second_edges(entries, faces, edge, rim_ground, wide_edge, ground, own, other):
    return pl.pallas_call(
        second_edges_kernel,
        out_shape=[shape(BLOCKS, SIDE, HALF), shape(BLOCKS, 8, SIDE)],
        in_specs=[SMEM] + [VMEM] * 13,
        out_specs=[VMEM] * 2,
        scratch_shapes=[
            pltpu.VMEM((3, 8, SIDE), F32),
            pltpu.VMEM((2, 8, SIDE), F32),
            pltpu.VMEM((2, 8, SIDE), F32),
            pltpu.VMEM((HALF, SIDE), F32),
        ],
        compiler_params=params(4),
        cost_estimate=cost(0, 0),
    )(entries, faces, edge, rim_ground, wide_edge, *ground, *own, *other)


def inflow_kernel(cells, rates, spill, edge_spill):
    spill[...] = jnp.zeros_like(spill)
    edge_spill[...] = jnp.zeros_like(edge_spill)
    lane = lanes(1, SIDE)
    for b in range(BLOCKS):

        def point(p, carry, b=b):
            cell = cells[0, b, p]
            row = lax.div(cell, SIDE)
            column = lax.rem(cell, SIDE)
            rate = GAIN * rates[0, b, p]
            at_column = jnp.where(lane == column, rate, 0.0)
            at_row = jnp.where(lane == row, rate, 0.0)
            line = pl.ds(row, 1)
            spill[b, line] = spill[b, line] + at_column
            for i, place in enumerate((0, 1, SIDE - 1)):
                edge_spill[i, b : b + 1] += jnp.where(column == place, at_row, 0.0)
                edge_spill[i, 4 + b : 5 + b] += jnp.where(row == place, at_column, 0.0)
            return carry

        lax.fori_loop(0, RIVERS, point, 0)


def lay_inflow(cells, rates):
    return pl.pallas_call(
        inflow_kernel,
        out_shape=[shape(BLOCKS, SIDE, SIDE), shape(3, 8, SIDE)],
        in_specs=[SMEM, SMEM],
        out_specs=[VMEM] * 2,
        compiler_params=params(4),
        cost_estimate=cost(0, 0),
    )(cells, rates)


def block_step(now, ground, spill, columns, rows, base, wetness, write):
    lane = lanes(ROWS, SIDE)
    sub = lax.broadcasted_iota(jnp.int32, (ROWS, SIDE), 0)

    def at(load, field, first, shift):
        if 0 <= first + shift <= SIDE - ROWS:
            return load(field, first + shift)
        return pltpu.roll(load(field, first), -shift % ROWS, 0)

    below = rows(base)
    for first in range(0, SIDE, ROWS):
        h, qx, qy = (at(now, f, first, 0) for f in range(3))
        z, rough = (at(ground, f, first, 0) for f in range(2))
        eta = h + z
        flux_x = face(
            eta, pltpu.roll(eta, SIDE - 1, 1), z, pltpu.roll(z, SIDE - 1, 1), rough,
            pltpu.roll(qx, 1, 1), qx, pltpu.roll(qx, SIDE - 1, 1),
        )
        edge = columns(pl.ds(first, ROWS))
        flux_x = jnp.where(lane == 0, edge[:, base + 1 : base + 2], flux_x)
        flux_x = jnp.where(lane == SIDE - 1, edge[:, base + 2 : base + 3], flux_x)
        flux_w = jnp.where(lane == 0, edge[:, base : base + 1], pltpu.roll(flux_x, 1, 1))
        z_up = at(ground, 0, first, 1)
        flux_y = face(
            eta, at(now, 0, first, 1) + z_up, z, z_up, rough, at(now, 2, first, -1), qy, at(now, 2, first, 1)
        )
        if first == 0:
            flux_y = jnp.where(sub == 0, rows(base + 1), flux_y)
        if first == SIDE - ROWS:
            flux_y = jnp.where(sub == ROWS - 1, rows(base + 2), flux_y)
        flux_s = jnp.where(sub == 0, below, pltpu.roll(flux_y, 1, 0))
        below = flux_y[ROWS - 1 : ROWS]
        depth = h + RATIO * (flux_w - flux_x + flux_s - flux_y) + spill(pl.ds(first, ROWS))
        write(first, depth * wetness, flux_x * wetness, flux_y * wetness)


def block_kernel(shifts, dest, wet, terrain, columns, rows, spill, *refs):
    out, then, done, sems = refs[-4:]
    shift = jnp.where(core() == 0, *shifts)
    slot = landing_slot(dest, shift)
    wetness = wet[0, slot].astype(F32)
    if shifts == W_SHIFTS:
        for here, ref in enumerate(refs[:2]):

            @pl.when(core() == 1 - here)
            def _(ref=ref):
                copy = pltpu.make_async_copy(ref, done, sems.at[0])
                copy.start()
                copy.wait()

        state = done
    else:
        state = refs[0]
    copies = []

    def now(field, first):
        return state[field, first : first + ROWS]

    def ground(field, first):
        return terrain[0, slot, field, first : first + ROWS]

    def keep(first, *fields):
        for f, value in enumerate(fields):
            then[f, first : first + ROWS] = value

    def finish(first, *fields):
        for f, value in enumerate(fields):
            done[f, first : first + ROWS] = value
        lines = pl.ds(first, ROWS)
        copies.append(pltpu.make_async_copy(done.at[:, lines], out.at[0, slot, :, lines], sems.at[len(copies)]))
        copies[-1].start()

    shared = (
        lambda at: spill[slot, at],
        lambda at: columns[slot, at],
        lambda q: rows[slot, q : q + 1],
    )
    block_step(now, ground, *shared, 0, wetness, keep)
    block_step(lambda f, first: then[f, first : first + ROWS], ground, *shared, 3, wetness, finish)
    for copy in copies:
        copy.wait()


def run_block(shifts, dest, wet, terrain, columns, rows, spill, states, out):
    args = [dest, wet, terrain, columns, rows, spill, *states]
    specs = [SMEM] * 2 + [VMEM] * 4 + [ANY if shifts == W_SHIFTS else VMEM] * len(states)
    aliases = {}
    if out is not None:
        aliases = {len(args): 0}
        args.append(out)
        specs.append(ANY)
    return pl.pallas_call(
        functools.partial(block_kernel, shifts),
        out_shape=shape(1, BLOCKS, 3, SIDE, SIDE),
        in_specs=specs,
        out_specs=ANY,
        input_output_aliases=aliases,
        scratch_shapes=[
            pltpu.VMEM((3, SIDE, SIDE), F32),
            pltpu.VMEM((3, SIDE, SIDE), F32),
            pltpu.SemaphoreType.DMA((SIDE // ROWS,)),
        ],
        compiler_params=params(16),
        cost_estimate=cost(0, 0),
    )(*args)


def passed_along(x, axis, by, wrap=True):
    devices = lax.axis_size(axis)
    return lax.ppermute(x, axis, [(i, (i + by) % devices) for i in range(devices)])


def passed_to(x, target):
    devices = lax.axis_size("tile")
    pairs = [(i, target(i // 2, i % 2)) for i in range(devices)]
    return lax.ppermute(x, "tile", [(i, t % devices) for i, t in pairs if t is not None])


def back_one(chip):
    return chip // RING * RING + (chip - 1) % RING


def first_leg(chip, at):
    return 2 * chip + 1 if at == 0 else 2 * back_one(chip)


def second_leg(chip, at):
    sender = chip // RING * RING + (chip + 1) % RING
    return 2 * (sender + 2) if at == 0 else None


def next_chip_swapped(chip, at):
    return 2 * (chip + 1) + 1 - at


def body(flood_state, terrain, destination, wet_mask, neighbours, inflow_cells, inflow_rates):
    dest, state = in_hbm(destination), in_hbm(flood_state)
    block_a, block_w = pick_early(dest, state)
    arrived_a = passed_along(block_a, "tile", 2)
    arrived_w = passed_to(block_w, first_leg)
    own, block_x, ground_low, ground_high, *packs = prepare(
        dest, in_hbm(neighbours), state, block_a, block_w, in_hbm(terrain), in_hbm(inflow_cells), in_hbm(inflow_rates)
    )
    ground = (ground_low, ground_high)
    (packs[3],) = gate((packs[3],), (arrived_w,))
    packs = [packs[0]] + [passed_along(p, "tile", d) for d, p in zip((1, 2, 3, 4), packs[1:])]
    block_x, arrived_w = gate((block_x, arrived_w), (*packs[1:], arrived_a))
    arrived_x = passed_to(block_x, next_chip_swapped)
    relayed = passed_to(arrived_w, second_leg)
    spill, edge_spill = lay_inflow(inflow_cells, inflow_rates)
    low, high, west, east, south, north, far_east = arrange(destination, packs, ground)
    others = (passed_along(west, "tile", -1), passed_along(south, "grp", -1), passed_along(north, "grp", 1))
    faces, edge, rim_ground, wide_edge, west, south, east, north = first_edges(
        neighbours, wet_mask, edge_spill, relayed, low, high, ground,
        (west, east, south, north), far_east, packs[1], others,
    )
    others = (passed_along(west, "tile", -1), passed_along(south, "grp", -1), passed_along(north, "grp", 1))
    columns, rows = second_edges(
        neighbours, faces, edge, rim_ground, wide_edge, ground, (west, south, east, north), others
    )
    out = None
    for shifts, states in (
        ((0, 0), (own,)),
        (A_SHIFTS, (arrived_a,)),
        (W_SHIFTS, (arrived_w, relayed)),
        (X_SHIFTS, (arrived_x,)),
    ):
        out = run_block(shifts, destination, wet_mask, terrain, columns, rows, spill, states, out)
    return out


def solution(mesh):
    in_specs = (
        P("grp", "tile", None, None, None),
        P("grp", "tile", None, None, None),
        P("grp", None),
        P("grp", "tile"),
        P("grp", "tile", None),
        P("grp", "tile", None),
        P("grp", "tile", None),
    )
    out_specs = P("grp", "tile", None, None, None)
    return jax.shard_map(body, mesh=mesh, in_specs=in_specs, out_specs=out_specs, check_vma=False)
```

```python
import functools

import jax
import jax.numpy as jnp
from jax import lax
from jax.experimental import pallas as pl
from jax.experimental.pallas import tpu as pltpu
from jax.sharding import PartitionSpec as P

F32 = jnp.float32
GRAVITY = 9.81
SPACING = 10.0
TIMESTEP = 0.2
CENTRE_WEIGHT = 0.7
DEPTH_FLOOR = 0.1
SIDE = 256
HALF = 128
BLOCKS = 4
RIVERS = 16
ROWS = 64
GAIN = TIMESTEP / (SPACING * SPACING)
RATIO = TIMESTEP / SPACING

ANY = pl.BlockSpec(memory_space=pl.ANY)
VMEM = pl.BlockSpec(memory_space=pltpu.VMEM)
SMEM = pl.BlockSpec(memory_space=pltpu.SMEM)
HBM = pl.BlockSpec(memory_space=pltpu.HBM)
RING = 4
CUT = 96
A_SHIFTS = (2, 2)
W_SHIFTS = (3, 1)
X_SHIFTS = (1, 3)


def shape(*dims):
    return jax.ShapeDtypeStruct(dims, F32)


def cost(flops, bytes_accessed):
    return pl.CostEstimate(flops=flops, bytes_accessed=bytes_accessed, transcendentals=0)


def face(eta_l, eta_r, z_l, z_r, rough, flow_left, flow_mid, flow_right):
    depth = jnp.maximum(eta_l, eta_r) - jnp.maximum(z_l, z_r)
    floored = jnp.maximum(depth, DEPTH_FLOOR)
    blended = CENTRE_WEIGHT * flow_mid + 0.5 * (1.0 - CENTRE_WEIGHT) * (flow_left + flow_right)
    slope = (GRAVITY * TIMESTEP / SPACING) * depth * (eta_r - eta_l)
    friction = 1.0 + (GRAVITY * TIMESTEP) * rough * rough * jnp.abs(flow_mid) * jnp.exp(
        (-7.0 / 3.0) * jnp.log(floored)
    )
    return (blended - slope) / friction


def core():
    return lax.rem(lax.axis_index("tile"), 2)


def params(mib):
    return pltpu.CompilerParams(vmem_limit_bytes=mib << 20)


def tile_offset(dest_ref, tile, slot):
    tiles = lax.axis_size("tile")
    return lax.rem(lax.div(dest_ref[0, tile * BLOCKS + slot], BLOCKS) - tile + tiles, tiles)


def leaving_slot(dest_ref, shift):
    me = lax.axis_index("tile")
    slot = jnp.int32(0)
    for j in range(1, BLOCKS):
        slot = jnp.where(tile_offset(dest_ref, me, j) == shift, j, slot)
    return slot


def landing_slot(dest_ref, shift, back=0):
    tiles = lax.axis_size("tile")
    sender = lax.rem(lax.axis_index("tile") - shift - back + 2 * tiles, tiles)
    slot = jnp.int32(0)
    for j in range(BLOCKS):
        place = lax.rem(dest_ref[0, sender * BLOCKS + j], BLOCKS)
        slot = jnp.where(tile_offset(dest_ref, sender, j) == shift, place, slot)
    return slot


def lanes(rows, columns):
    return lax.broadcasted_iota(jnp.int32, (rows, columns), 1)


def in_hbm(x):
    return pltpu.with_memory_space_constraint(x, pltpu.HBM)


def pick_kernel(dest, state, a_low, a_high, block_w, sems):
    slots = [leaving_slot(dest, k) for k in range(1, BLOCKS)]
    slot_w = jnp.where(core() == 0, slots[0], slots[2])
    parts = (
        (state.at[0, slots[1], :, pl.ds(0, CUT)], a_low),
        (state.at[0, slots[1], :, pl.ds(CUT, SIDE - CUT)], a_high),
        (state.at[0, slot_w], block_w),
    )
    loads = [pltpu.make_async_copy(part, ref, sems.at[i]) for i, (part, ref) in enumerate(parts)]
    for load in loads:
        load.start()
    for load in loads:
        load.wait()


def pick_early(dest, state):
    return pl.pallas_call(
        pick_kernel,
        out_shape=[shape(3, CUT, SIDE), shape(3, SIDE - CUT, SIDE), shape(3, SIDE, SIDE)],
        in_specs=[SMEM, HBM],
        out_specs=[VMEM] * 3,
        scratch_shapes=[pltpu.SemaphoreType.DMA((3,))],
        compiler_params=params(4),
        cost_estimate=cost(0, 0),
    )(dest, state)


def prepare_kernel(
    dest, entries, state, a_low, a_high, block_w, ground_in, cells, rates,
    own, block_x, low, high, pack0, pack1, pack2, pack3, pack4, terrain, sems,
):
    slots = [leaving_slot(dest, k) for k in range(BLOCKS)]
    first_core = core() == 0
    slot_x = jnp.where(first_core, slots[3], slots[1])
    held = (block_x, own)
    loads = [pltpu.make_async_copy(ground_in, terrain, sems.at[3])]
    for i, (slot, ref) in enumerate(zip((slot_x, slots[0]), held)):
        loads.append(pltpu.make_async_copy(state.at[0, slot], ref, sems.at[i]))
    for load in loads:
        load.start()
    lane = lanes(SIDE, HALF)

    def strips(parts, write):
        ref, tail = parts[0], parts[-1]
        size = tail.shape[1]

        def half(columns):
            return [jnp.concatenate([part[f, :, columns] for part in parts]) for f in range(3)]

        west = half(slice(0, HALF))
        east = half(slice(HALF, SIDE))
        packed = jnp.where(lane < 3, west[0], pltpu.roll(west[1], 3, 1))
        packed = jnp.where(lane < 6, packed, pltpu.roll(west[2], 6, 1))
        packed = jnp.where(lane < 8, packed, pltpu.roll(east[0], 10, 1))
        packed = jnp.where(lane < 10, packed, pltpu.roll(east[1], 13, 1))
        packed = jnp.where(lane < 13, packed, pltpu.roll(east[2], 14, 1))
        turned = packed.T
        south = jnp.concatenate([ref[0, 0:3], ref[2, 0:3], ref[1, 0:2]])
        north = jnp.concatenate(
            [tail[0, size - 2 : size], tail[2, size - 3 : size], tail[1, size - 1 : size], jnp.zeros((2, SIDE), F32)]
        )
        write(turned[0:8], south, turned[8:16], north)

    strip_out = (pack0, pack1, pack2, pack3)
    east_out = (pack1.at[4], pack2.at[4], pack3.at[4], pack4.at[0])

    def write(k, west, south, east, north):
        for i, value in enumerate((west, south, east, north)):
            strip_out[k][i] = value
        east_out[k][...] = east

    def write_by_core(first, second):
        def both(*values):
            pl.when(first_core)(lambda: write(first, *values))
            pl.when(jnp.logical_not(first_core))(lambda: write(second, *values))

        return both

    strips((a_low, a_high), functools.partial(write, 2))
    strips((block_w,), write_by_core(1, 3))
    spill = jnp.zeros((BLOCKS, SIDE), F32)
    along = lanes(BLOCKS, SIDE)
    for p in range(RIVERS):
        cell = cells[0, :, p : p + 1]
        there = (along * SIDE + SIDE - 1) == cell
        spill = spill + jnp.where(there, GAIN * rates[0, :, p : p + 1], 0.0)
    loads[0].wait()
    for b in range(BLOCKS):
        west = [terrain[0, b, f, :, :HALF] for f in range(2)]
        east = [terrain[0, b, f, :, HALF:] for f in range(2)]
        packed = jnp.where(lane < 3, west[0], pltpu.roll(west[1], 3, 1))
        packed = jnp.where(lane < 5, packed, pltpu.roll(east[0], 7, 1))
        packed = jnp.where(lane < 7, packed, pltpu.roll(east[1], 9, 1))
        turned = packed.T
        for q in range(5):
            low[q, b : b + 1] = turned[q : q + 1]
        for q in range(4):
            high[q, b : b + 1] = turned[5 + q : 6 + q]
        for q in range(3):
            low[q, 4 + b : 5 + b] = terrain[0, b, 0, q : q + 1]
        for q in range(2):
            low[3 + q, 4 + b : 5 + b] = terrain[0, b, 1, q : q + 1]
            high[q, 4 + b : 5 + b] = terrain[0, b, 0, SIDE - 2 + q : SIDE - 1 + q]
            high[2 + q, 4 + b : 5 + b] = terrain[0, b, 1, SIDE - 2 + q : SIDE - 1 + q]
    for b in range(BLOCKS):
        for q in range(4):
            pack1[5 + b, q : q + 1] = high[q, b : b + 1]
        pack1[5 + b, 4:5] = spill[b : b + 1]
        for side in (2, 3):
            pack1[5 + b, 3 + side : 4 + side] = jnp.full((1, SIDE), entries[0, b, side].astype(F32), F32)
        pack1[5 + b, 7:8] = jnp.zeros((1, SIDE), F32)
    writers = (write_by_core(3, 1), functools.partial(write, 0))
    for load, ref, write_out in zip(loads[1:], held, writers):
        load.wait()
        strips((ref,), write_out)


def prepare(dest, entries, state, a_low, a_high, block_w, terrain, cells, rates):
    packs = [shape(count, 8, SIDE) for count in (4, 9, 5, 5, 1)]
    return pl.pallas_call(
        prepare_kernel,
        out_shape=[shape(3, SIDE, SIDE)] * 2 + [shape(5, 8, SIDE), shape(4, 8, SIDE)] + packs,
        in_specs=[SMEM, SMEM, HBM, VMEM, VMEM, VMEM, HBM, VMEM, VMEM],
        out_specs=[VMEM] * 9,
        scratch_shapes=[
            pltpu.VMEM((1, BLOCKS, 2, SIDE, SIDE), F32),
            pltpu.SemaphoreType.DMA((BLOCKS,)),
        ],
        compiler_params=params(12),
        cost_estimate=cost(0, 0),
    )(dest, entries, state, a_low, a_high, block_w, terrain, cells, rates)


def gate_kernel(count, *refs):
    del count, refs


def gate(values, keys):
    count = len(values)
    return pl.pallas_call(
        functools.partial(gate_kernel, count),
        out_shape=[jax.ShapeDtypeStruct(v.shape, v.dtype) for v in values],
        in_specs=[ANY] * (count + len(keys)),
        out_specs=[ANY] * count,
        input_output_aliases={i: i for i in range(count)},
        compiler_params=params(1),
        cost_estimate=cost(0, 0),
    )(*values, *keys)


def arrange_kernel(
    dest, pack0, pack1, pack2, pack3, pack4, ground_low, ground_high,
    low, high, west, east, south, north, far_east,
):
    for out in (west, east, south, north):
        out[...] = jnp.zeros_like(out)
    strips = (pack0, pack1, pack2, pack3)
    east_in = (pack1.at[4], pack2.at[4], pack3.at[4], pack4.at[0])
    for k in range(BLOCKS):
        strip = strips[k]
        slot = landing_slot(dest, k)
        for side, (low_out, high_out) in enumerate(((west, east), (south, north))):
            row = pl.ds(side * 4 + slot, 1)
            for q in range(8):
                low[q, row] = strip[side, q : q + 1]
            for q in range(6):
                high[q, row] = strip[2 + side, q : q + 1]
            low_out[slot, 0:1] = strip[side, 0:1]
            low_out[slot, 1:2] = strip[side, 3:4]
            high_out[slot, 0:1] = strip[2 + side, 1:2]
            high_out[slot, 1:3] = strip[2 + side, 3:5]
        slot = landing_slot(dest, k, 1)
        far_east[slot] = east_in[k][...]
        for out in (south, north):
            out[BLOCKS + slot, 0:1] = east_in[k][1:2]
            out[BLOCKS + slot, 1:2] = east_in[k][5:6]
    for b in range(BLOCKS):
        for side, (low_out, high_out) in enumerate(((west, east), (south, north))):
            sub = slice(side * 4 + b, side * 4 + b + 1)
            low_out[b, 2:3] = ground_low[0, sub]
            high_out[b, 3:4] = ground_high[1, sub]
            high_out[b, 4:5] = ground_high[3, sub]
        for out in (south, north):
            out[BLOCKS + b, 2:3] = pack1[5 + b, 1:2]
            out[BLOCKS + b, 3:4] = pack1[5 + b, 3:4]


def arrange(dest, packs, ground):
    rims = [shape(BLOCKS, 8, SIDE)] * 2 + [shape(2 * BLOCKS, 8, SIDE)] * 2 + [shape(BLOCKS, 8, SIDE)]
    return pl.pallas_call(
        arrange_kernel,
        out_shape=[shape(8, 8, SIDE), shape(6, 8, SIDE)] + rims,
        in_specs=[SMEM] + [VMEM] * 7,
        out_specs=[VMEM] * 7,
        compiler_params=params(4),
        cost_estimate=cost(0, 0),
    )(dest, *packs, *ground)


def pick(entry, own, other):
    near = own[jnp.clip(entry, 0, BLOCKS - 1)]
    far = other[jnp.clip(entry - BLOCKS, 0, BLOCKS - 1)]
    return jnp.where(entry >= BLOCKS, far, near)


def gather_rims(entries, own, other, rim_low, rim_high, has, low_count, high_count, from_west):
    for b in range(BLOCKS):
        for side in range(2):
            sub = slice(side * 4 + b, side * 4 + b + 1)
            entry = entries[0, b, 2 * side]
            alive = entry >= 0
            if side == 0:
                near = own[2][jnp.clip(entry, 0, BLOCKS - 1)]
                rows = jnp.where(entry >= BLOCKS, from_west(b, entry), near)
            else:
                rows = pick(entry, own[3], other[3])
            rows = jnp.where(alive, rows, 0.0)
            for q in range(low_count):
                rim_low[q, sub] = rows[q : q + 1]
            has[0, sub] = jnp.full((1, SIDE), jnp.where(alive, 1.0, 0.0), F32)
            entry = entries[0, b, 2 * side + 1]
            alive = entry >= 0
            rows = jnp.where(alive, pick(entry, own[side], other[side]), 0.0)
            for q in range(high_count):
                rim_high[q, sub] = rows[q : q + 1]
            has[1, sub] = jnp.full((1, SIDE), jnp.where(alive, 1.0, 0.0), F32)


def sides_swapped(x):
    return pltpu.roll(x, 4, 0)


def column(x, at):
    return x[:, at : at + 1]


def along_edge(h, z, rough, flow, face_before, face_first, face_last):
    lane = lanes(8, SIDE)
    eta = h + z
    flux = face(
        eta, pltpu.roll(eta, SIDE - 1, 1), z, pltpu.roll(z, SIDE - 1, 1), rough,
        pltpu.roll(flow, 1, 1), flow, pltpu.roll(flow, SIDE - 1, 1),
    )
    flux = jnp.where(lane == 0, face_first, flux)
    flux = jnp.where(lane == SIDE - 1, face_last, flux)
    lower = jnp.where(lane == 0, face_before, pltpu.roll(flux, 1, 1))
    return lower - flux


def west_device_edge(wide, ground_wide, corners_s, corners_n, face_last):
    hy, hz, qx, qy, qz, tz = (wide[q] for q in range(6))
    zy, zz, ny, nz, spill, entry_s, entry_n = (ground_wide[q] for q in range(7))
    face_y = face(hy + zy, hz + zz, zy, zz, ny, qx, qy, qz)

    def chosen(entry, corners, q):
        value = jnp.zeros((8, SIDE), F32)
        for j in range(2 * BLOCKS):
            value = jnp.where(entry == j, corners[q, j : j + 1], value)
        return value

    h_s, t_s, z_s, n_s = (chosen(entry_s, corners_s, q) for q in range(4))
    h_n, t_n, z_n = (chosen(entry_n, corners_n, q) for q in range(3))
    last = SIDE - 1
    has_s = jnp.where(column(entry_s, 0) >= 0.0, 1.0, 0.0)
    has_n = jnp.where(column(entry_n, 0) >= 0.0, 1.0, 0.0)
    eta = hz + zz
    eta_s, eta_n = h_s + z_s, h_n + z_n
    before = face(
        column(eta_s, last), column(eta, 0), column(z_s, last), column(zz, 0), column(n_s, last),
        column(t_s, last - 1), column(t_s, last), column(tz, 0),
    ) * has_s
    first = face(
        column(eta, 0), column(eta, 1), column(zz, 0), column(zz, 1), column(nz, 0),
        column(t_s, last), column(tz, 0), column(tz, 1),
    )
    final = face(
        column(eta, last), column(eta_n, 0), column(zz, last), column(z_n, 0), column(nz, last),
        column(tz, last - 1), column(tz, last), column(t_n, 0),
    ) * has_n
    depth = hz + RATIO * (face_y - face_last + along_edge(hz, zz, nz, tz, before, first, final)) + spill
    return depth, face_y


def first_edges_kernel(
    entries, wet, edge_spill, key, low, high, ground_low, ground_high,
    own_w, own_e, own_s, own_n, far_east, pack1, oth_w, oth_s, oth_n,
    faces, edge, rim_ground, wide_edge, west, south, east, north,
    rim_low, rim_high, has, wetness, wide, ground_wide, corners_s, corners_n,
):
    def from_west(b, entry):
        slot = jnp.clip(entry - BLOCKS, 0, BLOCKS - 1)
        state, ground = far_east[slot], pack1[5 + slot]
        for q in range(6):
            wide[q, b : b + 1] = state[q : q + 1]
        for q in range(7):
            ground_wide[q, b : b + 1] = ground[q : q + 1]
        return jnp.concatenate([state[1:2], state[3:5], ground[1:2], ground[3:4], jnp.zeros((3, SIDE), F32)])

    wide[...] = jnp.zeros_like(wide)
    ground_wide[...] = jnp.zeros_like(ground_wide)
    gather_rims(
        entries, (own_w, own_s, own_e, own_n), (oth_w, oth_s, None, oth_n), rim_low, rim_high, has, 5, 3, from_west
    )
    for j in range(BLOCKS):
        for corners, far in ((corners_s, oth_n), (corners_n, oth_s)):
            corners[0, j : j + 1] = far_east[j, 1:2]
            corners[1, j : j + 1] = far_east[j, 5:6]
            corners[2, j : j + 1] = pack1[5 + j, 1:2]
            corners[3, j : j + 1] = pack1[5 + j, 3:4]
            for q in range(4):
                corners[q, BLOCKS + j : BLOCKS + j + 1] = far[BLOCKS + j, q : q + 1]
    for b in range(BLOCKS):
        value = jnp.full((1, SIDE), wet[0, b].astype(F32), F32)
        wetness[b : b + 1] = value
        wetness[4 + b : 5 + b] = value
    hm, qmm, qm, zm, nm = (rim_low[q] for q in range(5))
    hp, qp, zp = (rim_high[q] for q in range(3))
    h0, h1, h2, q0, q1, q2, t0, t1 = (low[q] for q in range(8))
    z0, z1, z2, n0, n1 = (ground_low[q] for q in range(5))
    hy, hz, qx, qy, qz, tz = (high[q] for q in range(6))
    zy, zz, ny, nz = (ground_high[q] for q in range(4))
    face_m = face(hm + zm, h0 + z0, zm, z0, nm, qmm, qm, q0) * has[0]
    face_0 = face(h0 + z0, h1 + z1, z0, z1, n0, qm, q0, q1)
    face_1 = face(h1 + z1, h2 + z2, z1, z2, n1, q0, q1, q2)
    face_y = face(hy + zy, hz + zz, zy, zz, ny, qx, qy, qz)
    face_z = face(hz + zz, hp + zp, zz, zp, nz, qy, qz, qp) * has[1]
    swapped = [sides_swapped(f) for f in (face_m, face_0, face_z)]

    def beside(spot):
        return [column(f, spot) for f in swapped]

    wide_depth, wide_flow = west_device_edge(wide, ground_wide, corners_s, corners_n, face_m)
    for i, value in enumerate((wide_depth, wide_flow, face_m)):
        wide_edge[i] = value
    wets = wetness[...]
    new_0 = (h0 + RATIO * (face_m - face_0 + along_edge(h0, z0, n0, t0, *beside(0))) + edge_spill[0]) * wets
    new_1 = (h1 + RATIO * (face_0 - face_1 + along_edge(h1, z1, n1, t1, *beside(1))) + edge_spill[1]) * wets
    new_z = (hz + RATIO * (face_y - face_z + along_edge(hz, zz, nz, tz, *beside(SIDE - 1))) + edge_spill[2]) * wets
    faces[0] = face_m
    faces[1] = face_0
    faces[2] = face_z
    rim_ground[0] = zm
    rim_ground[1] = nm
    rim_ground[2] = zp
    flow_0, flow_1, flow_y, flow_z = (f * wets for f in (face_0, face_1, face_y, face_z))
    for i, value in enumerate((new_0, new_1, flow_0, flow_1, new_z, flow_y, flow_z)):
        edge[i] = value
    for out in (west, south, east, north):
        out[...] = jnp.zeros_like(out)
    for b in range(BLOCKS):
        for side, (low_out, high_out) in enumerate(((west, east), (south, north))):
            sub = slice(side * 4 + b, side * 4 + b + 1)
            low_out[b, 0:1] = new_0[sub]
            low_out[b, 1:2] = flow_0[sub]
            high_out[b, 0:1] = new_z[sub]
            high_out[b, 1:2] = flow_y[sub]
            high_out[b, 2:3] = flow_z[sub]


def first_edges(entries, wet, edge_spill, key, low, high, ground, own, far_east, pack1, other):
    return pl.pallas_call(
        first_edges_kernel,
        out_shape=[shape(3, 8, SIDE), shape(7, 8, SIDE), shape(3, 8, SIDE), shape(3, 8, SIDE)]
        + [shape(BLOCKS, 8, SIDE)] * 4,
        in_specs=[SMEM, SMEM, VMEM, ANY] + [VMEM] * 13,
        out_specs=[VMEM] * 8,
        scratch_shapes=[
            pltpu.VMEM((5, 8, SIDE), F32),
            pltpu.VMEM((3, 8, SIDE), F32),
            pltpu.VMEM((2, 8, SIDE), F32),
            pltpu.VMEM((8, SIDE), F32),
            pltpu.VMEM((6, 8, SIDE), F32),
            pltpu.VMEM((7, 8, SIDE), F32),
            pltpu.VMEM((4, 8, SIDE), F32),
            pltpu.VMEM((4, 8, SIDE), F32),
        ],
        compiler_params=params(4),
        cost_estimate=cost(0, 0),
    )(entries, wet, edge_spill, key, low, high, *ground, *own, far_east, pack1, *other)


def second_edges_kernel(
    entries, faces, edge, rim_ground, wide_edge, ground_low, ground_high,
    own_w, own_s, own_e, own_n, oth_w, oth_s, oth_n,
    columns, rows, rim_low, rim_high, has, stack,
):
    def from_west(b, entry):
        rows = [wide_edge[q, b : b + 1] for q in range(3)]
        return jnp.concatenate(rows + [jnp.zeros((5, SIDE), F32)])

    gather_rims(
        entries, (own_w, own_s, own_e, own_n), (oth_w, oth_s, None, oth_n), rim_low, rim_high, has, 3, 2, from_west
    )
    hm, qmm, qm = (rim_low[q] for q in range(3))
    hp, qp = (rim_high[q] for q in range(2))
    zm, nm, zp = (rim_ground[q] for q in range(3))
    h0, h1, q0, q1, hz, qy, qz = (edge[q] for q in range(7))
    z0, z1, n0 = ground_low[0], ground_low[1], ground_low[3]
    zz, nz = ground_high[1], ground_high[3]
    face_m = face(hm + zm, h0 + z0, zm, z0, nm, qmm, qm, q0) * has[0]
    face_0 = face(h0 + z0, h1 + z1, z0, z1, n0, qm, q0, q1)
    face_z = face(hz + zz, hp + zp, zz, zp, nz, qy, qz, qp) * has[1]
    every = (faces[0], faces[1], faces[2], face_m, face_0, face_z)
    stack[...] = jnp.zeros_like(stack)
    rows[...] = jnp.zeros_like(rows)
    for b in range(BLOCKS):
        for i, value in enumerate(every):
            stack[b * 8 + i : b * 8 + i + 1] = value[b : b + 1]
            rows[b, i : i + 1] = value[4 + b : 5 + b]
    turned = stack[...].T
    columns[0] = turned
    for b in range(1, BLOCKS):
        columns[b] = pltpu.roll(turned, HALF - 8 * b, 1)


def second_edges(entries, faces, edge, rim_ground, wide_edge, ground, own, other):
    return pl.pallas_call(
        second_edges_kernel,
        out_shape=[shape(BLOCKS, SIDE, HALF), shape(BLOCKS, 8, SIDE)],
        in_specs=[SMEM] + [VMEM] * 13,
        out_specs=[VMEM] * 2,
        scratch_shapes=[
            pltpu.VMEM((3, 8, SIDE), F32),
            pltpu.VMEM((2, 8, SIDE), F32),
            pltpu.VMEM((2, 8, SIDE), F32),
            pltpu.VMEM((HALF, SIDE), F32),
        ],
        compiler_params=params(4),
        cost_estimate=cost(0, 0),
    )(entries, faces, edge, rim_ground, wide_edge, *ground, *own, *other)


def inflow_kernel(cells, rates, spill, edge_spill):
    spill[...] = jnp.zeros_like(spill)
    edge_spill[...] = jnp.zeros_like(edge_spill)
    lane = lanes(1, SIDE)
    for b in range(BLOCKS):

        def point(p, carry, b=b):
            cell = cells[0, b, p]
            row = lax.div(cell, SIDE)
            column = lax.rem(cell, SIDE)
            rate = GAIN * rates[0, b, p]
            at_column = jnp.where(lane == column, rate, 0.0)
            at_row = jnp.where(lane == row, rate, 0.0)
            line = pl.ds(row, 1)
            spill[b, line] = spill[b, line] + at_column
            for i, place in enumerate((0, 1, SIDE - 1)):
                edge_spill[i, b : b + 1] += jnp.where(column == place, at_row, 0.0)
                edge_spill[i, 4 + b : 5 + b] += jnp.where(row == place, at_column, 0.0)
            return carry

        lax.fori_loop(0, RIVERS, point, 0)


def lay_inflow(cells, rates):
    return pl.pallas_call(
        inflow_kernel,
        out_shape=[shape(BLOCKS, SIDE, SIDE), shape(3, 8, SIDE)],
        in_specs=[SMEM, SMEM],
        out_specs=[VMEM] * 2,
        compiler_params=params(4),
        cost_estimate=cost(0, 0),
    )(cells, rates)


def block_step(now, ground, spill, columns, rows, base, wetness, write):
    lane = lanes(ROWS, SIDE)
    sub = lax.broadcasted_iota(jnp.int32, (ROWS, SIDE), 0)

    def at(load, field, first, shift):
        if 0 <= first + shift <= SIDE - ROWS:
            return load(field, first + shift)
        return pltpu.roll(load(field, first), -shift % ROWS, 0)

    below = rows(base)
    for first in range(0, SIDE, ROWS):
        h, qx, qy = (at(now, f, first, 0) for f in range(3))
        z, rough = (at(ground, f, first, 0) for f in range(2))
        eta = h + z
        flux_x = face(
            eta, pltpu.roll(eta, SIDE - 1, 1), z, pltpu.roll(z, SIDE - 1, 1), rough,
            pltpu.roll(qx, 1, 1), qx, pltpu.roll(qx, SIDE - 1, 1),
        )
        edge = columns(pl.ds(first, ROWS))
        flux_x = jnp.where(lane == 0, edge[:, base + 1 : base + 2], flux_x)
        flux_x = jnp.where(lane == SIDE - 1, edge[:, base + 2 : base + 3], flux_x)
        flux_w = jnp.where(lane == 0, edge[:, base : base + 1], pltpu.roll(flux_x, 1, 1))
        z_up = at(ground, 0, first, 1)
        flux_y = face(
            eta, at(now, 0, first, 1) + z_up, z, z_up, rough, at(now, 2, first, -1), qy, at(now, 2, first, 1)
        )
        if first == 0:
            flux_y = jnp.where(sub == 0, rows(base + 1), flux_y)
        if first == SIDE - ROWS:
            flux_y = jnp.where(sub == ROWS - 1, rows(base + 2), flux_y)
        flux_s = jnp.where(sub == 0, below, pltpu.roll(flux_y, 1, 0))
        below = flux_y[ROWS - 1 : ROWS]
        depth = h + RATIO * (flux_w - flux_x + flux_s - flux_y) + spill(pl.ds(first, ROWS))
        write(first, depth * wetness, flux_x * wetness, flux_y * wetness)


def block_kernel(shifts, dest, wet, terrain, columns, rows, spill, *refs):
    out, then, done, sems = refs[-4:]
    shift = jnp.where(core() == 0, *shifts)
    slot = landing_slot(dest, shift)
    wetness = wet[0, slot].astype(F32)
    if shifts == W_SHIFTS:
        for here, ref in enumerate(refs[:2]):

            @pl.when(core() == 1 - here)
            def _(ref=ref):
                copy = pltpu.make_async_copy(ref, done, sems.at[0])
                copy.start()
                copy.wait()

        state = done
    else:
        state = refs[0]
    copies = []

    def now(field, first):
        if shifts != A_SHIFTS:
            return state[field, first : first + ROWS]
        if first + ROWS <= CUT:
            return refs[0][field, first : first + ROWS]
        if first >= CUT:
            return refs[1][field, first - CUT : first - CUT + ROWS]
        return jnp.concatenate([refs[0][field, first:CUT], refs[1][field, 0 : first + ROWS - CUT]])

    def ground(field, first):
        return terrain[0, slot, field, first : first + ROWS]

    def keep(first, *fields):
        for f, value in enumerate(fields):
            then[f, first : first + ROWS] = value

    def finish(first, *fields):
        for f, value in enumerate(fields):
            done[f, first : first + ROWS] = value
        lines = pl.ds(first, ROWS)
        copies.append(pltpu.make_async_copy(done.at[:, lines], out.at[0, slot, :, lines], sems.at[len(copies)]))
        copies[-1].start()

    shared = (
        lambda at: spill[slot, at],
        lambda at: columns[slot, at],
        lambda q: rows[slot, q : q + 1],
    )
    block_step(now, ground, *shared, 0, wetness, keep)
    block_step(lambda f, first: then[f, first : first + ROWS], ground, *shared, 3, wetness, finish)
    for copy in copies:
        copy.wait()


def run_block(shifts, dest, wet, terrain, columns, rows, spill, states, out):
    args = [dest, wet, terrain, columns, rows, spill, *states]
    specs = [SMEM] * 2 + [VMEM] * 4 + [ANY if shifts == W_SHIFTS else VMEM] * len(states)
    aliases = {}
    if out is not None:
        aliases = {len(args): 0}
        args.append(out)
        specs.append(ANY)
    return pl.pallas_call(
        functools.partial(block_kernel, shifts),
        out_shape=shape(1, BLOCKS, 3, SIDE, SIDE),
        in_specs=specs,
        out_specs=ANY,
        input_output_aliases=aliases,
        scratch_shapes=[
            pltpu.VMEM((3, SIDE, SIDE), F32),
            pltpu.VMEM((3, SIDE, SIDE), F32),
            pltpu.SemaphoreType.DMA((SIDE // ROWS,)),
        ],
        compiler_params=params(16),
        cost_estimate=cost(0, 0),
    )(*args)


def passed_along(x, axis, by, wrap=True):
    devices = lax.axis_size(axis)
    return lax.ppermute(x, axis, [(i, (i + by) % devices) for i in range(devices)])


def passed_to(x, target):
    devices = lax.axis_size("tile")
    pairs = [(i, target(i // 2, i % 2)) for i in range(devices)]
    return lax.ppermute(x, "tile", [(i, t % devices) for i, t in pairs if t is not None])


def back_one(chip):
    return chip // RING * RING + (chip - 1) % RING


def first_leg(chip, at):
    return 2 * chip + 1 if at == 0 else 2 * back_one(chip)


def second_leg(chip, at):
    sender = chip // RING * RING + (chip + 1) % RING
    return 2 * (sender + 2) if at == 0 else None


def next_chip_swapped(chip, at):
    return 2 * (chip + 1) + 1 - at


def body(flood_state, terrain, destination, wet_mask, neighbours, inflow_cells, inflow_rates):
    dest, state = in_hbm(destination), in_hbm(flood_state)
    a_low, a_high, block_w = pick_early(dest, state)
    arrived_low = passed_along(a_low, "tile", 2)
    arrived_w = passed_to(block_w, first_leg)
    own, block_x, ground_low, ground_high, *packs = prepare(
        dest, in_hbm(neighbours), state, a_low, a_high, block_w,
        in_hbm(terrain), in_hbm(inflow_cells), in_hbm(inflow_rates),
    )
    ground = (ground_low, ground_high)
    (packs[1],) = gate((packs[1],), (arrived_low, ))
    (arrived_w,) = gate((arrived_w,), (arrived_low,))
    packs = [packs[0]] + [passed_along(p, "tile", d) for d, p in zip((1, 2, 3, 4), packs[1:])]
    a_high, block_x = gate((a_high, block_x), packs[1:])
    arrived_high = passed_along(a_high, "tile", 2)
    arrived_x = passed_to(block_x, next_chip_swapped)
    relayed = passed_to(arrived_w, second_leg)
    spill, edge_spill = lay_inflow(inflow_cells, inflow_rates)
    low, high, west, east, south, north, far_east = arrange(destination, packs, ground)
    others = (passed_along(west, "tile", -1), passed_along(south, "grp", -1), passed_along(north, "grp", 1))
    faces, edge, rim_ground, wide_edge, west, south, east, north = first_edges(
        neighbours, wet_mask, edge_spill, relayed, low, high, ground,
        (west, east, south, north), far_east, packs[1], others,
    )
    others = (passed_along(west, "tile", -1), passed_along(south, "grp", -1), passed_along(north, "grp", 1))
    columns, rows = second_edges(
        neighbours, faces, edge, rim_ground, wide_edge, ground, (west, south, east, north), others
    )
    out = None
    for shifts, states in (
        ((0, 0), (own,)),
        (W_SHIFTS, (arrived_w, relayed)),
        (X_SHIFTS, (arrived_x,)),
        (A_SHIFTS, (arrived_low, arrived_high)),
    ):
        out = run_block(shifts, destination, wet_mask, terrain, columns, rows, spill, states, out)
    return out


def solution(mesh):
    in_specs = (
        P("grp", "tile", None, None, None),
        P("grp", "tile", None, None, None),
        P("grp", None),
        P("grp", "tile"),
        P("grp", "tile", None),
        P("grp", "tile", None),
        P("grp", "tile", None),
    )
    out_specs = P("grp", "tile", None, None, None)
    return jax.shard_map(body, mesh=mesh, in_specs=in_specs, out_specs=out_specs, check_vma=False)
```

```python
import functools

import jax
import jax.numpy as jnp
from jax import lax
from jax.experimental import pallas as pl
from jax.experimental.pallas import tpu as pltpu
from jax.sharding import PartitionSpec as P

F32 = jnp.float32
GRAVITY = 9.81
SPACING = 10.0
TIMESTEP = 0.2
CENTRE_WEIGHT = 0.7
DEPTH_FLOOR = 0.1
SIDE = 256
HALF = 128
BLOCKS = 4
RIVERS = 16
ROWS = 64
GAIN = TIMESTEP / (SPACING * SPACING)
RATIO = TIMESTEP / SPACING

ANY = pl.BlockSpec(memory_space=pl.ANY)
VMEM = pl.BlockSpec(memory_space=pltpu.VMEM)
SMEM = pl.BlockSpec(memory_space=pltpu.SMEM)
HBM = pl.BlockSpec(memory_space=pltpu.HBM)
RING = 4
CUT = 128
A_SHIFTS = (2, 2)
W_SHIFTS = (3, 1)
X_SHIFTS = (1, 3)


def shape(*dims):
    return jax.ShapeDtypeStruct(dims, F32)


def cost(flops, bytes_accessed):
    return pl.CostEstimate(flops=flops, bytes_accessed=bytes_accessed, transcendentals=0)


def face(eta_l, eta_r, z_l, z_r, rough, flow_left, flow_mid, flow_right):
    depth = jnp.maximum(eta_l, eta_r) - jnp.maximum(z_l, z_r)
    floored = jnp.maximum(depth, DEPTH_FLOOR)
    blended = CENTRE_WEIGHT * flow_mid + 0.5 * (1.0 - CENTRE_WEIGHT) * (flow_left + flow_right)
    slope = (GRAVITY * TIMESTEP / SPACING) * depth * (eta_r - eta_l)
    friction = 1.0 + (GRAVITY * TIMESTEP) * rough * rough * jnp.abs(flow_mid) * jnp.exp(
        (-7.0 / 3.0) * jnp.log(floored)
    )
    return (blended - slope) / friction


def core():
    return lax.rem(lax.axis_index("tile"), 2)


def params(mib):
    return pltpu.CompilerParams(vmem_limit_bytes=mib << 20)


def tile_offset(dest_ref, tile, slot):
    tiles = lax.axis_size("tile")
    return lax.rem(lax.div(dest_ref[0, tile * BLOCKS + slot], BLOCKS) - tile + tiles, tiles)


def leaving_slot(dest_ref, shift):
    me = lax.axis_index("tile")
    slot = jnp.int32(0)
    for j in range(1, BLOCKS):
        slot = jnp.where(tile_offset(dest_ref, me, j) == shift, j, slot)
    return slot


def landing_slot(dest_ref, shift, back=0):
    tiles = lax.axis_size("tile")
    sender = lax.rem(lax.axis_index("tile") - shift - back + 2 * tiles, tiles)
    slot = jnp.int32(0)
    for j in range(BLOCKS):
        place = lax.rem(dest_ref[0, sender * BLOCKS + j], BLOCKS)
        slot = jnp.where(tile_offset(dest_ref, sender, j) == shift, place, slot)
    return slot


def lanes(rows, columns):
    return lax.broadcasted_iota(jnp.int32, (rows, columns), 1)


def in_hbm(x):
    return pltpu.with_memory_space_constraint(x, pltpu.HBM)


def pick_kernel(dest, state, a_low, a_high, sems):
    slot = leaving_slot(dest, 2)
    parts = (
        (state.at[0, slot, :, pl.ds(0, CUT)], a_low),
        (state.at[0, slot, :, pl.ds(CUT, SIDE - CUT)], a_high),
    )
    loads = [pltpu.make_async_copy(part, ref, sems.at[i]) for i, (part, ref) in enumerate(parts)]
    for load in loads:
        load.start()
    for load in loads:
        load.wait()


def pick_early(dest, state):
    return pl.pallas_call(
        pick_kernel,
        out_shape=[shape(3, CUT, SIDE), shape(3, SIDE - CUT, SIDE)],
        in_specs=[SMEM, HBM],
        out_specs=[VMEM] * 2,
        scratch_shapes=[pltpu.SemaphoreType.DMA((2,))],
        compiler_params=params(4),
        cost_estimate=cost(0, 0),
    )(dest, state)


def prepare_kernel(
    dest, entries, state, a_low, a_high, ground_in, cells, rates,
    own, block_w, block_x, low, high, pack0, pack1, pack2, pack3, pack4, pack_back, terrain, sems,
):
    slots = [leaving_slot(dest, k) for k in range(BLOCKS)]
    first_core = core() == 0
    slot_w = jnp.where(first_core, slots[1], slots[3])
    slot_x = jnp.where(first_core, slots[3], slots[1])
    held = (block_w, block_x, own)
    loads = [pltpu.make_async_copy(ground_in, terrain, sems.at[3])]
    for i, (slot, ref) in enumerate(zip((slot_w, slot_x, slots[0]), held)):
        loads.append(pltpu.make_async_copy(state.at[0, slot], ref, sems.at[i]))
    for load in loads:
        load.start()
    lane = lanes(SIDE, HALF)

    def strips(parts, write):
        ref, tail = parts[0], parts[-1]
        size = tail.shape[1]

        def half(columns):
            return [jnp.concatenate([part[f, :, columns] for part in parts]) for f in range(3)]

        west = half(slice(0, HALF))
        east = half(slice(HALF, SIDE))
        packed = jnp.where(lane < 3, west[0], pltpu.roll(west[1], 3, 1))
        packed = jnp.where(lane < 6, packed, pltpu.roll(west[2], 6, 1))
        packed = jnp.where(lane < 8, packed, pltpu.roll(east[0], 10, 1))
        packed = jnp.where(lane < 10, packed, pltpu.roll(east[1], 13, 1))
        packed = jnp.where(lane < 13, packed, pltpu.roll(east[2], 14, 1))
        turned = packed.T
        south = jnp.concatenate([ref[0, 0:3], ref[2, 0:3], ref[1, 0:2]])
        north = jnp.concatenate(
            [tail[0, size - 2 : size], tail[2, size - 3 : size], tail[1, size - 1 : size], jnp.zeros((2, SIDE), F32)]
        )
        write(turned[0:8], south, turned[8:16], north)

    strip_out = (pack0, pack1, pack2, pack3)
    west_out = (pack_back.at[0], pack0.at[4], pack1.at[5], pack2.at[5])
    east_out = (pack1.at[4], pack2.at[4], pack3.at[4], pack4.at[0])

    def write(k, west, south, east, north):
        for i, value in enumerate((west, south, east, north)):
            strip_out[k][i] = value
        east_out[k][...] = east
        west_out[k][...] = west

    def write_by_core(first, second):
        def both(*values):
            pl.when(first_core)(lambda: write(first, *values))
            pl.when(jnp.logical_not(first_core))(lambda: write(second, *values))

        return both

    strips((a_low, a_high), functools.partial(write, 2))
    along = lanes(BLOCKS, SIDE)
    spills = [jnp.zeros((BLOCKS, SIDE), F32) for _ in range(2)]
    for p in range(RIVERS):
        cell = cells[0, :, p : p + 1] - along * SIDE
        rate = GAIN * rates[0, :, p : p + 1]
        for i, place in enumerate((0, SIDE - 1)):
            spills[i] = spills[i] + jnp.where(cell == place, rate, 0.0)
    loads[0].wait()
    for b in range(BLOCKS):
        west = [terrain[0, b, f, :, :HALF] for f in range(2)]
        east = [terrain[0, b, f, :, HALF:] for f in range(2)]
        packed = jnp.where(lane < 3, west[0], pltpu.roll(west[1], 3, 1))
        packed = jnp.where(lane < 5, packed, pltpu.roll(east[0], 7, 1))
        packed = jnp.where(lane < 7, packed, pltpu.roll(east[1], 9, 1))
        turned = packed.T
        for q in range(5):
            low[q, b : b + 1] = turned[q : q + 1]
        for q in range(4):
            high[q, b : b + 1] = turned[5 + q : 6 + q]
        for q in range(3):
            low[q, 4 + b : 5 + b] = terrain[0, b, 0, q : q + 1]
        for q in range(2):
            low[3 + q, 4 + b : 5 + b] = terrain[0, b, 1, q : q + 1]
            high[q, 4 + b : 5 + b] = terrain[0, b, 0, SIDE - 2 + q : SIDE - 1 + q]
            high[2 + q, 4 + b : 5 + b] = terrain[0, b, 1, SIDE - 2 + q : SIDE - 1 + q]
    for b in range(BLOCKS):
        line = slice(b, b + 1)
        links = [jnp.full((1, SIDE), entries[0, b, side].astype(F32), F32) for side in (2, 3)]
        blank = [jnp.zeros((1, SIDE), F32)]
        pack1[6 + b] = jnp.concatenate([high[q, line] for q in range(4)] + [spills[1][line]] + links + blank)
        pack_back[1 + b] = jnp.concatenate(
            [low[0, line], low[1, line], low[3, line], spills[0][line]] + links + blank * 2
        )
    writers = (write_by_core(1, 3), write_by_core(3, 1), functools.partial(write, 0))
    for load, ref, write_out in zip(loads[1:], held, writers):
        load.wait()
        strips((ref,), write_out)


def prepare(dest, entries, state, a_low, a_high, terrain, cells, rates):
    packs = [shape(count, 8, SIDE) for count in (5, 10, 6, 5, 1, 5)]
    return pl.pallas_call(
        prepare_kernel,
        out_shape=[shape(3, SIDE, SIDE)] * 3 + [shape(5, 8, SIDE), shape(4, 8, SIDE)] + packs,
        in_specs=[SMEM, SMEM, HBM, VMEM, VMEM, HBM, VMEM, VMEM],
        out_specs=[VMEM] * 11,
        scratch_shapes=[
            pltpu.VMEM((1, BLOCKS, 2, SIDE, SIDE), F32),
            pltpu.SemaphoreType.DMA((BLOCKS,)),
        ],
        compiler_params=params(12),
        cost_estimate=cost(0, 0),
    )(dest, entries, state, a_low, a_high, terrain, cells, rates)


def gate_kernel(count, *refs):
    del count, refs


def gate(values, keys):
    count = len(values)
    return pl.pallas_call(
        functools.partial(gate_kernel, count),
        out_shape=[jax.ShapeDtypeStruct(v.shape, v.dtype) for v in values],
        in_specs=[ANY] * (count + len(keys)),
        out_specs=[ANY] * count,
        input_output_aliases={i: i for i in range(count)},
        compiler_params=params(1),
        cost_estimate=cost(0, 0),
    )(*values, *keys)


def sides_swapped(x):
    return pltpu.roll(x, 4, 0)


def column(x, at):
    return x[:, at : at + 1]


def put_rim(entry, sub, near_state, near_fixed, far_state, far_fixed, wide, has):
    near = jnp.clip(entry, 0, BLOCKS - 1)
    far = jnp.clip(entry - BLOCKS, 0, BLOCKS - 1)
    alive = entry >= 0
    for i, (close, distant) in enumerate(((near_state, far_state), (near_fixed, far_fixed))):
        rows = jnp.where(entry >= BLOCKS, distant(far), close(near))
        rows = jnp.where(alive, rows, 0.0)
        for q in range(8):
            wide[8 * i + q, sub : sub + 1] = rows[q : q + 1]
    has[sub : sub + 1] = jnp.full((1, SIDE), jnp.where(alive, 1.0, 0.0), F32)


def faces_low(low, ground_low, wide):
    h0, h1, h2, q0, q1, q2 = (low[q] for q in range(6))
    z0, z1, z2, n0, n1 = (ground_low[q] for q in range(5))
    hm, qmm, qm, zm, nm = (wide[q] for q in (1, 3, 4, 9, 11))
    return (
        face(hm + zm, h0 + z0, zm, z0, nm, qmm, qm, q0),
        face(h0 + z0, h1 + z1, z0, z1, n0, qm, q0, q1),
        face(h1 + z1, h2 + z2, z1, z2, n1, q0, q1, q2),
    )


def faces_high(high, ground_high, wide):
    hy, hz, qx, qy, qz = (high[q] for q in range(5))
    zy, zz, ny, nz = (ground_high[q] for q in range(4))
    hp, qp, zp = (wide[q] for q in (0, 3, 8))
    return (
        face(hy + zy, hz + zz, zy, zz, ny, qx, qy, qz),
        face(hz + zz, hp + zp, zz, zp, nz, qy, qz, qp),
    )


def arrange_kernel(
    dest, entries, pack0, pack1, pack2, pack3, pack4, pack_back, ground_low, ground_high, edge_spill,
    low, high, wide_low, wide_high, has_low, has_high, far_east, far_west, to_south, to_north,
    west, east,
):
    for out in (low, high, wide_low, wide_high, has_low, has_high):
        out[...] = jnp.zeros_like(out)
    strips = (pack0, pack1, pack2, pack3)
    west_in = (pack_back.at[0], pack0.at[4], pack1.at[5], pack2.at[5])
    east_in = (pack1.at[4], pack2.at[4], pack3.at[4], pack4.at[0])
    for k in range(BLOCKS):
        strip = strips[k]
        slot = landing_slot(dest, k)
        for side in range(2):
            row = pl.ds(side * 4 + slot, 1)
            for q in range(8):
                low[q, row] = strip[side, q : q + 1]
            for q in range(6):
                high[q, row] = strip[2 + side, q : q + 1]
        for i, out in enumerate((west, to_south, east, to_north)):
            out[slot] = strip[i]
        slot = landing_slot(dest, k, 1)
        far_east[slot] = east_in[k][...]
        slot = landing_slot(dest, k, -1)
        far_west[slot] = west_in[k][...]

    def fixed_low(slot):
        row = pl.ds(slot, 1)
        rows = [ground_low[0, row], ground_low[1, row], ground_low[3, row]]
        return jnp.concatenate(rows + [jnp.zeros((5, SIDE), F32)])

    def fixed_high(slot):
        row = pl.ds(slot, 1)
        return jnp.concatenate([ground_high[q, row] for q in range(4)] + [jnp.zeros((4, SIDE), F32)])

    for b in range(BLOCKS):
        put_rim(
            entries[0, b, 0], b, lambda s: east[s], fixed_high,
            lambda s: far_east[s], lambda s: pack1[6 + s], wide_low, has_low,
        )
        put_rim(
            entries[0, b, 1], b, lambda s: west[s], fixed_low,
            lambda s: far_west[s], lambda s: pack_back[1 + s], wide_high, has_high,
        )
    face_m, face_0, _ = faces_low(low, ground_low, wide_low)
    _, face_z = faces_high(high, ground_high, wide_high)
    face_m = face_m * has_low[...]
    face_z = face_z * has_high[...]
    for b in range(BLOCKS):
        sub = slice(4 + b, 5 + b)
        beside = [f[b : b + 1] for f in (face_m, face_0, face_z)]
        blank = [jnp.zeros((1, SIDE), F32)]
        to_north[4 + b] = jnp.concatenate([ground_high[q, sub] for q in range(4)] + [edge_spill[2, sub]] + beside)
        to_south[4 + b] = jnp.concatenate(
            [ground_low[0, sub], ground_low[1, sub], ground_low[3, sub], edge_spill[0, sub]] + beside + blank
        )
        passed = jnp.concatenate(
            [
                far_east[b, 1:2], far_east[b, 5:6], pack1[6 + b, 1:2], pack1[6 + b, 3:4],
                far_west[b, 0:1], far_west[b, 6:7], pack_back[1 + b, 0:1], pack_back[1 + b, 2:3],
            ]
        )
        to_north[8 + b] = passed
        to_south[8 + b] = passed


def arrange(dest, entries, packs, ground, edge_spill):
    outs = [(8, 8), (6, 8), (16, 8), (16, 8), (8,), (8,), (BLOCKS, 8), (BLOCKS, 8), (3 * BLOCKS, 8), (3 * BLOCKS, 8)]
    return pl.pallas_call(
        arrange_kernel,
        out_shape=[shape(*dims, SIDE) for dims in outs],
        in_specs=[SMEM] * 2 + [VMEM] * 9,
        out_specs=[VMEM] * len(outs),
        scratch_shapes=[pltpu.VMEM((BLOCKS, 8, SIDE), F32)] * 2,
        compiler_params=params(4),
        cost_estimate=cost(0, 0),
    )(dest, entries, *packs, *ground, edge_spill)


def along_edge(h, z, rough, flow, face_before, face_first, face_last):
    lane = lanes(8, SIDE)
    eta = h + z
    flux = face(
        eta, pltpu.roll(eta, SIDE - 1, 1), z, pltpu.roll(z, SIDE - 1, 1), rough,
        pltpu.roll(flow, 1, 1), flow, pltpu.roll(flow, SIDE - 1, 1),
    )
    flux = jnp.where(lane == 0, face_first, flux)
    flux = jnp.where(lane == SIDE - 1, face_last, flux)
    lower = jnp.where(lane == 0, face_before, pltpu.roll(flux, 1, 1))
    return lower - flux


def corner_faces(h, z, rough, flow, entry_s, entry_n, corners_s, corners_n):
    def chosen(entry, corners, q):
        value = jnp.zeros((8, SIDE), F32)
        for j in range(2 * BLOCKS):
            value = jnp.where(entry == j, corners[q][j : j + 1], value)
        return value

    h_s, t_s, z_s, n_s = (chosen(entry_s, corners_s, q) for q in range(4))
    h_n, t_n, z_n = (chosen(entry_n, corners_n, q) for q in range(3))
    last = SIDE - 1
    has_s = jnp.where(column(entry_s, 0) >= 0.0, 1.0, 0.0)
    has_n = jnp.where(column(entry_n, 0) >= 0.0, 1.0, 0.0)
    eta, eta_s, eta_n = h + z, h_s + z_s, h_n + z_n
    before = face(
        column(eta_s, last), column(eta, 0), column(z_s, last), column(z, 0), column(n_s, last),
        column(t_s, last - 1), column(t_s, last), column(flow, 0),
    ) * has_s
    first = face(
        column(eta, 0), column(eta, 1), column(z, 0), column(z, 1), column(rough, 0),
        column(t_s, last), column(flow, 0), column(flow, 1),
    )
    final = face(
        column(eta, last), column(eta_n, 0), column(z, last), column(z_n, 0), column(rough, last),
        column(flow, last - 1), column(flow, last), column(t_n, 0),
    ) * has_n
    return before, first, final


def edges_kernel(
    entries, wet, edge_spill, low, high, ground_low, ground_high, wide_low_in, wide_high_in, has_low_in, has_high_in,
    far_east, far_west, pack1, pack_back, to_south, to_north, from_north, from_south,
    columns, rows,
    wide_low, wide_high, has_low, has_high, wetness, edge, rim_low, rim_high, corners, stack,
):
    wide_low[...] = wide_low_in[...]
    wide_high[...] = wide_high_in[...]
    has_low[...] = has_low_in[...]
    has_high[...] = has_high_in[...]
    for b in range(BLOCKS):
        value = jnp.full((1, SIDE), wet[0, b].astype(F32), F32)
        wetness[b : b + 1] = value
        wetness[4 + b : 5 + b] = value
        for entry, near, far, wide, has in (
            (entries[0, b, 2], to_north, from_south, wide_low, has_low),
            (entries[0, b, 3], to_south, from_north, wide_high, has_high),
        ):
            put_rim(
                entry, 4 + b, lambda s, r=near: r[s], lambda s, r=near: r[BLOCKS + s],
                lambda s, r=far: r[s], lambda s, r=far: r[BLOCKS + s], wide, has,
            )
    for j in range(BLOCKS):
        near = slice(j, j + 1)
        far = slice(BLOCKS + j, BLOCKS + j + 1)
        for q, row in enumerate(
            (
                far_east[j, 1:2], far_east[j, 5:6], pack1[6 + j, 1:2], pack1[6 + j, 3:4],
                far_west[j, 0:1], far_west[j, 6:7], pack_back[1 + j, 0:1], pack_back[1 + j, 2:3],
            )
        ):
            for i, passed in enumerate((from_south, from_north)):
                corners[i, q, near] = row
                corners[i, q, far] = passed[2 * BLOCKS + j, q : q + 1]

    def seen(i, first):
        return [corners[i, first + q] for q in range(4)]

    h0, h1, h2, q0, q1, q2, t0, t1 = (low[q] for q in range(8))
    z0, z1, z2, n0, n1 = (ground_low[q] for q in range(5))
    hy, hz, qx, qy, qz, tz = (high[q] for q in range(6))
    zy, zz, ny, nz = (ground_high[q] for q in range(4))
    face_m, face_0, face_1 = faces_low(low, ground_low, wide_low)
    face_y, face_z = faces_high(high, ground_high, wide_high)
    face_m = face_m * has_low[...]
    face_z = face_z * has_high[...]
    swapped = [sides_swapped(f) for f in (face_m, face_0, face_z)]

    def beside(spot):
        return [column(f, spot) for f in swapped]

    wets = wetness[...]
    last = SIDE - 1
    new_0 = (h0 + RATIO * (face_m - face_0 + along_edge(h0, z0, n0, t0, *beside(0))) + edge_spill[0]) * wets
    new_1 = (h1 + RATIO * (face_0 - face_1 + along_edge(h1, z1, n1, t1, *beside(1))) + edge_spill[1]) * wets
    new_z = (hz + RATIO * (face_y - face_z + along_edge(hz, zz, nz, tz, *beside(last))) + edge_spill[2]) * wets
    flow_0, flow_1, flow_y, flow_z = (f * wets for f in (face_0, face_1, face_y, face_z))
    for i, value in enumerate((new_z, flow_y, flow_z, new_0, flow_0)):
        edge[i] = value

    sides = lax.broadcasted_iota(jnp.int32, (8, 1), 0) < 4
    ghy, ghz, gqx, gqy, gqz, gtz = (wide_low[q] for q in range(6))
    gzy, gzz, gny, gnz, gspill = (wide_low[8 + q] for q in range(5))
    across = corner_faces(ghz, gzz, gnz, gtz, wide_low[13], wide_low[14], seen(0, 0), seen(1, 0))
    given = [column(wide_low[13 + q], last) for q in range(3)]
    ends = [jnp.where(sides, a, g) for a, g in zip(across, given)]
    far_face = face(ghy + gzy, ghz + gzz, gzy, gzz, gny, gqx, gqy, gqz)
    far_low = (
        ghz + RATIO * (far_face - face_m + along_edge(ghz, gzz, gnz, gtz, *ends)) + gspill,
        far_face,
        face_m,
    )
    gh0, gh1, gq0, gq1, gt0 = (wide_high[q] for q in (0, 1, 3, 4, 6))
    gz0, gz1, gn0, gspill = (wide_high[8 + q] for q in range(4))
    across = corner_faces(gh0, gz0, gn0, gt0, wide_high[12], wide_high[13], seen(0, 4), seen(1, 4))
    given = [column(wide_high[12 + q], 0) for q in range(3)]
    ends = [jnp.where(sides, a, g) for a, g in zip(across, given)]
    far_face = face(gh0 + gz0, gh1 + gz1, gz0, gz1, gn0, qz, gq0, gq1)
    far_high = (
        gh0 + RATIO * (face_z - far_face + along_edge(gh0, gz0, gn0, gt0, *ends)) + gspill,
        far_face,
    )
    for rim, far_rows, first, group in ((rim_low, far_low, 0, 0), (rim_high, far_high, 3, 1)):
        for q, far_row in enumerate(far_rows):
            rim[q] = far_row
        for b in range(BLOCKS):
            for side in range(2):
                entry = entries[0, b, 2 * side + group]
                sub = slice(side * 4 + b, side * 4 + b + 1)
                near = pl.ds(side * 4 + jnp.clip(entry, 0, BLOCKS - 1), 1)
                for q in range(len(far_rows)):
                    row = jnp.where(entry >= BLOCKS, rim[q, sub], edge[first + q, near])
                    rim[q, sub] = jnp.where(entry >= 0, row, 0.0)

    hm, qmm, qm = (rim_low[q] for q in range(3))
    hp, qp = (rim_high[q] for q in range(2))
    zm, nm, zp = wide_low[9], wide_low[11], wide_high[8]
    next_m = face(hm + zm, new_0 + z0, zm, z0, nm, qmm, qm, flow_0) * has_low[...]
    next_0 = face(new_0 + z0, new_1 + z1, z0, z1, n0, qm, flow_0, flow_1)
    next_z = face(new_z + zz, hp + zp, zz, zp, nz, flow_y, flow_z, qp) * has_high[...]
    stack[...] = jnp.zeros_like(stack)
    rows[...] = jnp.zeros_like(rows)
    for b in range(BLOCKS):
        for i, value in enumerate((face_m, face_0, face_z, next_m, next_0, next_z)):
            stack[b * 8 + i : b * 8 + i + 1] = value[b : b + 1]
            rows[b, i : i + 1] = value[4 + b : 5 + b]
    turned = stack[...].T
    columns[0] = turned
    for b in range(1, BLOCKS):
        columns[b] = pltpu.roll(turned, HALF - 8 * b, 1)


def edge_faces(entries, wet, *arrays):
    return pl.pallas_call(
        edges_kernel,
        out_shape=[shape(BLOCKS, SIDE, HALF), shape(BLOCKS, 8, SIDE)],
        in_specs=[SMEM] * 2 + [VMEM] * len(arrays),
        out_specs=[VMEM] * 2,
        scratch_shapes=[
            pltpu.VMEM((16, 8, SIDE), F32),
            pltpu.VMEM((16, 8, SIDE), F32),
            pltpu.VMEM((8, SIDE), F32),
            pltpu.VMEM((8, SIDE), F32),
            pltpu.VMEM((8, SIDE), F32),
            pltpu.VMEM((5, 8, SIDE), F32),
            pltpu.VMEM((3, 8, SIDE), F32),
            pltpu.VMEM((2, 8, SIDE), F32),
            pltpu.VMEM((2, 8, 8, SIDE), F32),
            pltpu.VMEM((HALF, SIDE), F32),
        ],
        compiler_params=params(6),
        cost_estimate=cost(0, 0),
    )(entries, wet, *arrays)


def inflow_kernel(cells, rates, spill, edge_spill):
    spill[...] = jnp.zeros_like(spill)
    edge_spill[...] = jnp.zeros_like(edge_spill)
    lane = lanes(1, SIDE)
    for b in range(BLOCKS):

        def point(p, carry, b=b):
            cell = cells[0, b, p]
            row = lax.div(cell, SIDE)
            column = lax.rem(cell, SIDE)
            rate = GAIN * rates[0, b, p]
            at_column = jnp.where(lane == column, rate, 0.0)
            at_row = jnp.where(lane == row, rate, 0.0)
            line = pl.ds(row, 1)
            spill[b, line] = spill[b, line] + at_column
            for i, place in enumerate((0, 1, SIDE - 1)):
                edge_spill[i, b : b + 1] += jnp.where(column == place, at_row, 0.0)
                edge_spill[i, 4 + b : 5 + b] += jnp.where(row == place, at_column, 0.0)
            return carry

        lax.fori_loop(0, RIVERS, point, 0)


def lay_inflow(cells, rates):
    return pl.pallas_call(
        inflow_kernel,
        out_shape=[shape(BLOCKS, SIDE, SIDE), shape(3, 8, SIDE)],
        in_specs=[SMEM, SMEM],
        out_specs=[VMEM] * 2,
        compiler_params=params(4),
        cost_estimate=cost(0, 0),
    )(cells, rates)


def block_step(now, ground, spill, columns, rows, base, wetness, write):
    lane = lanes(ROWS, SIDE)
    sub = lax.broadcasted_iota(jnp.int32, (ROWS, SIDE), 0)

    def at(load, field, first, shift):
        if 0 <= first + shift <= SIDE - ROWS:
            return load(field, first + shift)
        return pltpu.roll(load(field, first), -shift % ROWS, 0)

    below = rows(base)
    for first in range(0, SIDE, ROWS):
        h, qx, qy = (at(now, f, first, 0) for f in range(3))
        z, rough = (at(ground, f, first, 0) for f in range(2))
        eta = h + z
        flux_x = face(
            eta, pltpu.roll(eta, SIDE - 1, 1), z, pltpu.roll(z, SIDE - 1, 1), rough,
            pltpu.roll(qx, 1, 1), qx, pltpu.roll(qx, SIDE - 1, 1),
        )
        edge = columns(pl.ds(first, ROWS))
        flux_x = jnp.where(lane == 0, edge[:, base + 1 : base + 2], flux_x)
        flux_x = jnp.where(lane == SIDE - 1, edge[:, base + 2 : base + 3], flux_x)
        flux_w = jnp.where(lane == 0, edge[:, base : base + 1], pltpu.roll(flux_x, 1, 1))
        z_up = at(ground, 0, first, 1)
        flux_y = face(
            eta, at(now, 0, first, 1) + z_up, z, z_up, rough, at(now, 2, first, -1), qy, at(now, 2, first, 1)
        )
        if first == 0:
            flux_y = jnp.where(sub == 0, rows(base + 1), flux_y)
        if first == SIDE - ROWS:
            flux_y = jnp.where(sub == ROWS - 1, rows(base + 2), flux_y)
        flux_s = jnp.where(sub == 0, below, pltpu.roll(flux_y, 1, 0))
        below = flux_y[ROWS - 1 : ROWS]
        depth = h + RATIO * (flux_w - flux_x + flux_s - flux_y) + spill(pl.ds(first, ROWS))
        write(first, depth * wetness, flux_x * wetness, flux_y * wetness)


def block_kernel(shifts, dest, wet, terrain, columns, rows, spill, *refs):
    out, then, done, sems = refs[-4:]
    shift = jnp.where(core() == 0, *shifts)
    slot = landing_slot(dest, shift)
    wetness = wet[0, slot].astype(F32)
    if shifts == W_SHIFTS:
        for here, ref in enumerate(refs[:2]):

            @pl.when(core() == 1 - here)
            def _(ref=ref):
                copy = pltpu.make_async_copy(ref, done, sems.at[0])
                copy.start()
                copy.wait()

        state = done
    else:
        state = refs[0]
    copies = []

    def now(field, first):
        if shifts != A_SHIFTS:
            return state[field, first : first + ROWS]
        if first + ROWS <= CUT:
            return refs[0][field, first : first + ROWS]
        if first >= CUT:
            return refs[1][field, first - CUT : first - CUT + ROWS]
        return jnp.concatenate([refs[0][field, first:CUT], refs[1][field, 0 : first + ROWS - CUT]])

    def ground(field, first):
        return terrain[0, slot, field, first : first + ROWS]

    def keep(first, *fields):
        for f, value in enumerate(fields):
            then[f, first : first + ROWS] = value

    def finish(first, *fields):
        for f, value in enumerate(fields):
            done[f, first : first + ROWS] = value
        lines = pl.ds(first, ROWS)
        copies.append(pltpu.make_async_copy(done.at[:, lines], out.at[0, slot, :, lines], sems.at[len(copies)]))
        copies[-1].start()

    shared = (
        lambda at: spill[slot, at],
        lambda at: columns[slot, at],
        lambda q: rows[slot, q : q + 1],
    )
    block_step(now, ground, *shared, 0, wetness, keep)
    block_step(lambda f, first: then[f, first : first + ROWS], ground, *shared, 3, wetness, finish)
    for copy in copies:
        copy.wait()


def run_block(shifts, dest, wet, terrain, columns, rows, spill, states, out):
    args = [dest, wet, terrain, columns, rows, spill, *states]
    specs = [SMEM] * 2 + [VMEM] * 4 + [ANY if shifts == W_SHIFTS else VMEM] * len(states)
    aliases = {}
    if out is not None:
        aliases = {len(args): 0}
        args.append(out)
        specs.append(ANY)
    return pl.pallas_call(
        functools.partial(block_kernel, shifts),
        out_shape=shape(1, BLOCKS, 3, SIDE, SIDE),
        in_specs=specs,
        out_specs=ANY,
        input_output_aliases=aliases,
        scratch_shapes=[
            pltpu.VMEM((3, SIDE, SIDE), F32),
            pltpu.VMEM((3, SIDE, SIDE), F32),
            pltpu.SemaphoreType.DMA((SIDE // ROWS,)),
        ],
        compiler_params=params(16),
        cost_estimate=cost(0, 0),
    )(*args)


def passed_along(x, axis, by, wrap=True):
    devices = lax.axis_size(axis)
    return lax.ppermute(x, axis, [(i, (i + by) % devices) for i in range(devices)])


def passed_to(x, target):
    devices = lax.axis_size("tile")
    pairs = [(i, target(i // 2, i % 2)) for i in range(devices)]
    return lax.ppermute(x, "tile", [(i, t % devices) for i, t in pairs if t is not None])


def back_one(chip):
    return chip // RING * RING + (chip - 1) % RING


def first_leg(chip, at):
    return 2 * chip + 1 if at == 0 else 2 * back_one(chip)


def second_leg(chip, at):
    sender = chip // RING * RING + (chip + 1) % RING
    return 2 * (sender + 2) if at == 0 else None


def next_chip_swapped(chip, at):
    return 2 * (chip + 1) + 1 - at


def body(flood_state, terrain, destination, wet_mask, neighbours, inflow_cells, inflow_rates):
    dest, state = in_hbm(destination), in_hbm(flood_state)
    a_low, a_high = pick_early(dest, state)
    arrived_low = passed_along(a_low, "tile", 2)
    own, block_w, block_x, ground_low, ground_high, *packs = prepare(
        dest, in_hbm(neighbours), state, a_low, a_high,
        in_hbm(terrain), in_hbm(inflow_cells), in_hbm(inflow_rates),
    )
    ground = (ground_low, ground_high)
    spill, edge_spill = lay_inflow(inflow_cells, inflow_rates)
    (packs[5],) = gate((packs[5],), (arrived_low,))
    packs = [packs[0]] + [passed_along(p, "tile", d) for d, p in zip((1, 2, 3, 4, -1), packs[1:])]
    a_high, block_x, block_w = gate((a_high, block_x, block_w), packs[1:])
    arrived_high = passed_along(a_high, "tile", 2)
    arrived_x = passed_to(block_x, next_chip_swapped)
    arrived_w = passed_to(block_w, first_leg)
    low, high, wide_low, wide_high, has_low, has_high, far_east, far_west, to_south, to_north = arrange(
        destination, neighbours, packs, ground, edge_spill
    )
    from_north = passed_along(to_south, "grp", -1)
    from_south = passed_along(to_north, "grp", 1)
    (arrived_w,) = gate((arrived_w,), (from_north, from_south, arrived_high))
    relayed = passed_to(arrived_w, second_leg)
    columns, rows = edge_faces(
        neighbours, wet_mask, edge_spill, low, high, *ground, wide_low, wide_high, has_low, has_high,
        far_east, far_west, packs[1], packs[5], to_south, to_north, from_north, from_south,
    )
    out = None
    for shifts, states in (
        ((0, 0), (own,)),
        (W_SHIFTS, (arrived_w, relayed)),
        (X_SHIFTS, (arrived_x,)),
        (A_SHIFTS, (arrived_low, arrived_high)),
    ):
        out = run_block(shifts, destination, wet_mask, terrain, columns, rows, spill, states, out)
    return out


def solution(mesh):
    in_specs = (
        P("grp", "tile", None, None, None),
        P("grp", "tile", None, None, None),
        P("grp", None),
        P("grp", "tile"),
        P("grp", "tile", None),
        P("grp", "tile", None),
        P("grp", "tile", None),
    )
    out_specs = P("grp", "tile", None, None, None)
    return jax.shard_map(body, mesh=mesh, in_specs=in_specs, out_specs=out_specs, check_vma=False)
```

```python
import functools

import jax
import jax.numpy as jnp
from jax import lax
from jax.experimental import pallas as pl
from jax.experimental.pallas import tpu as pltpu
from jax.sharding import PartitionSpec as P

F32 = jnp.float32
GRAVITY = 9.81
SPACING = 10.0
TIMESTEP = 0.2
CENTRE_WEIGHT = 0.7
DEPTH_FLOOR = 0.1
SIDE = 256
HALF = 128
BLOCKS = 4
RIVERS = 16
ROWS = 64
GAIN = TIMESTEP / (SPACING * SPACING)
RATIO = TIMESTEP / SPACING

ANY = pl.BlockSpec(memory_space=pl.ANY)
VMEM = pl.BlockSpec(memory_space=pltpu.VMEM)
SMEM = pl.BlockSpec(memory_space=pltpu.SMEM)
HBM = pl.BlockSpec(memory_space=pltpu.HBM)
RING = 4
CUT = 64
OWN_SHIFTS = (0, 0)
A_SHIFTS = (2, 2)
W_SHIFTS = (3, 1)
X_SHIFTS = (1, 3)


def shape(*dims):
    return jax.ShapeDtypeStruct(dims, F32)


def cost(flops, bytes_accessed):
    return pl.CostEstimate(flops=flops, bytes_accessed=bytes_accessed, transcendentals=0)


def face(eta_l, eta_r, z_l, z_r, rough, flow_left, flow_mid, flow_right):
    depth = jnp.maximum(eta_l, eta_r) - jnp.maximum(z_l, z_r)
    floored = jnp.maximum(depth, DEPTH_FLOOR)
    blended = CENTRE_WEIGHT * flow_mid + 0.5 * (1.0 - CENTRE_WEIGHT) * (flow_left + flow_right)
    slope = (GRAVITY * TIMESTEP / SPACING) * depth * (eta_r - eta_l)
    friction = 1.0 + (GRAVITY * TIMESTEP) * rough * rough * jnp.abs(flow_mid) * jnp.exp(
        (-7.0 / 3.0) * jnp.log(floored)
    )
    return (blended - slope) / friction


def core():
    return lax.rem(lax.axis_index("tile"), 2)


def params(mib):
    return pltpu.CompilerParams(vmem_limit_bytes=mib << 20)


def tile_offset(dest_ref, tile, slot):
    tiles = lax.axis_size("tile")
    return lax.rem(lax.div(dest_ref[0, tile * BLOCKS + slot], BLOCKS) - tile + tiles, tiles)


def leaving_slot(dest_ref, shift):
    me = lax.axis_index("tile")
    slot = jnp.int32(0)
    for j in range(1, BLOCKS):
        slot = jnp.where(tile_offset(dest_ref, me, j) == shift, j, slot)
    return slot


def landing_slot(dest_ref, shift, back=0):
    tiles = lax.axis_size("tile")
    sender = lax.rem(lax.axis_index("tile") - shift - back + 2 * tiles, tiles)
    slot = jnp.int32(0)
    for j in range(BLOCKS):
        place = lax.rem(dest_ref[0, sender * BLOCKS + j], BLOCKS)
        slot = jnp.where(tile_offset(dest_ref, sender, j) == shift, place, slot)
    return slot


def lanes(rows, columns):
    return lax.broadcasted_iota(jnp.int32, (rows, columns), 1)


def in_hbm(x):
    return pltpu.with_memory_space_constraint(x, pltpu.HBM)


def pick_kernel(dest, state, a_low, a_high, sems):
    slot = leaving_slot(dest, 2)
    parts = (
        (state.at[0, slot, :, pl.ds(0, CUT)], a_low),
        (state.at[0, slot, :, pl.ds(CUT, SIDE - CUT)], a_high),
    )
    loads = [pltpu.make_async_copy(part, ref, sems.at[i]) for i, (part, ref) in enumerate(parts)]
    for load in loads:
        load.start()
    for load in loads:
        load.wait()


def pick_early(dest, state):
    return pl.pallas_call(
        pick_kernel,
        out_shape=[shape(3, CUT, SIDE), shape(3, SIDE - CUT, SIDE)],
        in_specs=[SMEM, HBM],
        out_specs=[VMEM] * 2,
        scratch_shapes=[pltpu.SemaphoreType.DMA((2,))],
        compiler_params=params(4),
        cost_estimate=cost(0, 0),
    )(dest, state)


def prepare_kernel(
    dest, entries, state, a_low, a_high, ground_in, cells, rates,
    own, block_w, block_x, low, high, pack0, pack1, pack2, pack3, pack4, pack_back, terrain, sems,
):
    slots = [leaving_slot(dest, k) for k in range(BLOCKS)]
    first_core = core() == 0
    slot_w = jnp.where(first_core, slots[1], slots[3])
    slot_x = jnp.where(first_core, slots[3], slots[1])
    held = (block_w, block_x, own)
    loads = [pltpu.make_async_copy(ground_in, terrain, sems.at[3])]
    for i, (slot, ref) in enumerate(zip((slot_w, slot_x, slots[0]), held)):
        loads.append(pltpu.make_async_copy(state.at[0, slot], ref, sems.at[i]))
    for load in loads:
        load.start()
    lane = lanes(SIDE, HALF)

    def strips(parts, write):
        ref, tail = parts[0], parts[-1]
        size = tail.shape[1]

        def half(columns):
            return [jnp.concatenate([part[f, :, columns] for part in parts]) for f in range(3)]

        west = half(slice(0, HALF))
        east = half(slice(HALF, SIDE))
        packed = jnp.where(lane < 3, west[0], pltpu.roll(west[1], 3, 1))
        packed = jnp.where(lane < 6, packed, pltpu.roll(west[2], 6, 1))
        packed = jnp.where(lane < 8, packed, pltpu.roll(east[0], 10, 1))
        packed = jnp.where(lane < 10, packed, pltpu.roll(east[1], 13, 1))
        packed = jnp.where(lane < 13, packed, pltpu.roll(east[2], 14, 1))
        turned = packed.T
        south = jnp.concatenate([ref[0, 0:3], ref[2, 0:3], ref[1, 0:2]])
        north = jnp.concatenate(
            [tail[0, size - 2 : size], tail[2, size - 3 : size], tail[1, size - 1 : size], jnp.zeros((2, SIDE), F32)]
        )
        write(turned[0:8], south, turned[8:16], north)

    strip_out = (pack0, pack1, pack2, pack3)
    west_out = (pack_back.at[0], pack0.at[4], pack1.at[5], pack2.at[5])
    east_out = (pack1.at[4], pack2.at[4], pack3.at[4], pack4.at[0])

    def write(k, west, south, east, north):
        for i, value in enumerate((west, south, east, north)):
            strip_out[k][i] = value
        east_out[k][...] = east
        west_out[k][...] = west

    def write_by_core(first, second):
        def both(*values):
            pl.when(first_core)(lambda: write(first, *values))
            pl.when(jnp.logical_not(first_core))(lambda: write(second, *values))

        return both

    strips((a_low, a_high), functools.partial(write, 2))
    along = lanes(BLOCKS, SIDE)
    spills = [jnp.zeros((BLOCKS, SIDE), F32) for _ in range(2)]
    for p in range(RIVERS):
        cell = cells[0, :, p : p + 1] - along * SIDE
        rate = GAIN * rates[0, :, p : p + 1]
        for i, place in enumerate((0, SIDE - 1)):
            spills[i] = spills[i] + jnp.where(cell == place, rate, 0.0)
    loads[0].wait()
    for b in range(BLOCKS):
        west = [terrain[0, b, f, :, :HALF] for f in range(2)]
        east = [terrain[0, b, f, :, HALF:] for f in range(2)]
        packed = jnp.where(lane < 3, west[0], pltpu.roll(west[1], 3, 1))
        packed = jnp.where(lane < 5, packed, pltpu.roll(east[0], 7, 1))
        packed = jnp.where(lane < 7, packed, pltpu.roll(east[1], 9, 1))
        turned = packed.T
        for q in range(5):
            low[q, b : b + 1] = turned[q : q + 1]
        for q in range(4):
            high[q, b : b + 1] = turned[5 + q : 6 + q]
        for q in range(3):
            low[q, 4 + b : 5 + b] = terrain[0, b, 0, q : q + 1]
        for q in range(2):
            low[3 + q, 4 + b : 5 + b] = terrain[0, b, 1, q : q + 1]
            high[q, 4 + b : 5 + b] = terrain[0, b, 0, SIDE - 2 + q : SIDE - 1 + q]
            high[2 + q, 4 + b : 5 + b] = terrain[0, b, 1, SIDE - 2 + q : SIDE - 1 + q]
    for b in range(BLOCKS):
        line = slice(b, b + 1)
        links = [jnp.full((1, SIDE), entries[0, b, side].astype(F32), F32) for side in (2, 3)]
        blank = [jnp.zeros((1, SIDE), F32)]
        pack1[6 + b] = jnp.concatenate([high[q, line] for q in range(4)] + [spills[1][line]] + links + blank)
        pack_back[1 + b] = jnp.concatenate(
            [low[0, line], low[1, line], low[3, line], spills[0][line]] + links + blank * 2
        )
    writers = (write_by_core(1, 3), write_by_core(3, 1), functools.partial(write, 0))
    for load, ref, write_out in zip(loads[1:], held, writers):
        load.wait()
        strips((ref,), write_out)


def prepare(dest, entries, state, a_low, a_high, terrain, cells, rates):
    packs = [shape(count, 8, SIDE) for count in (5, 10, 6, 5, 1, 5)]
    return pl.pallas_call(
        prepare_kernel,
        out_shape=[shape(3, SIDE, SIDE)] * 3 + [shape(5, 8, SIDE), shape(4, 8, SIDE)] + packs,
        in_specs=[SMEM, SMEM, HBM, VMEM, VMEM, HBM, VMEM, VMEM],
        out_specs=[VMEM] * 11,
        scratch_shapes=[
            pltpu.VMEM((1, BLOCKS, 2, SIDE, SIDE), F32),
            pltpu.SemaphoreType.DMA((BLOCKS,)),
        ],
        compiler_params=params(12),
        cost_estimate=cost(0, 0),
    )(dest, entries, state, a_low, a_high, terrain, cells, rates)


def gate_kernel(count, *refs):
    del count, refs


def gate(values, keys):
    count = len(values)
    return pl.pallas_call(
        functools.partial(gate_kernel, count),
        out_shape=[jax.ShapeDtypeStruct(v.shape, v.dtype) for v in values],
        in_specs=[ANY] * (count + len(keys)),
        out_specs=[ANY] * count,
        input_output_aliases={i: i for i in range(count)},
        compiler_params=params(1),
        cost_estimate=cost(0, 0),
    )(*values, *keys)


def sides_swapped(x):
    return pltpu.roll(x, 4, 0)


def column(x, at):
    return x[:, at : at + 1]


def put_rim(entry, sub, near_state, near_fixed, far_state, far_fixed, wide, has):
    near = jnp.clip(entry, 0, BLOCKS - 1)
    far = jnp.clip(entry - BLOCKS, 0, BLOCKS - 1)
    alive = entry >= 0
    for i, (close, distant) in enumerate(((near_state, far_state), (near_fixed, far_fixed))):
        rows = jnp.where(entry >= BLOCKS, distant(far), close(near))
        rows = jnp.where(alive, rows, 0.0)
        for q in range(8):
            wide[8 * i + q, sub : sub + 1] = rows[q : q + 1]
    has[sub : sub + 1] = jnp.full((1, SIDE), jnp.where(alive, 1.0, 0.0), F32)


def faces_low(low, ground_low, wide):
    h0, h1, h2, q0, q1, q2 = (low[q] for q in range(6))
    z0, z1, z2, n0, n1 = (ground_low[q] for q in range(5))
    hm, qmm, qm, zm, nm = (wide[q] for q in (1, 3, 4, 9, 11))
    return (
        face(hm + zm, h0 + z0, zm, z0, nm, qmm, qm, q0),
        face(h0 + z0, h1 + z1, z0, z1, n0, qm, q0, q1),
        face(h1 + z1, h2 + z2, z1, z2, n1, q0, q1, q2),
    )


def faces_high(high, ground_high, wide):
    hy, hz, qx, qy, qz = (high[q] for q in range(5))
    zy, zz, ny, nz = (ground_high[q] for q in range(4))
    hp, qp, zp = (wide[q] for q in (0, 3, 8))
    return (
        face(hy + zy, hz + zz, zy, zz, ny, qx, qy, qz),
        face(hz + zz, hp + zp, zz, zp, nz, qy, qz, qp),
    )


def arrange_kernel(
    dest, entries, pack0, pack1, pack2, pack3, pack4, pack_back, ground_low, ground_high, edge_spill,
    low, high, wide_low, wide_high, has_low, has_high, far_east, far_west, to_south, to_north,
    west, east,
):
    for out in (low, high, wide_low, wide_high, has_low, has_high):
        out[...] = jnp.zeros_like(out)
    strips = (pack0, pack1, pack2, pack3)
    west_in = (pack_back.at[0], pack0.at[4], pack1.at[5], pack2.at[5])
    east_in = (pack1.at[4], pack2.at[4], pack3.at[4], pack4.at[0])
    for k in range(BLOCKS):
        strip = strips[k]
        slot = landing_slot(dest, k)
        for side in range(2):
            row = pl.ds(side * 4 + slot, 1)
            for q in range(8):
                low[q, row] = strip[side, q : q + 1]
            for q in range(6):
                high[q, row] = strip[2 + side, q : q + 1]
        for i, out in enumerate((west, to_south, east, to_north)):
            out[slot] = strip[i]
        slot = landing_slot(dest, k, 1)
        far_east[slot] = east_in[k][...]
        slot = landing_slot(dest, k, -1)
        far_west[slot] = west_in[k][...]

    def fixed_low(slot):
        row = pl.ds(slot, 1)
        rows = [ground_low[0, row], ground_low[1, row], ground_low[3, row]]
        return jnp.concatenate(rows + [jnp.zeros((5, SIDE), F32)])

    def fixed_high(slot):
        row = pl.ds(slot, 1)
        return jnp.concatenate([ground_high[q, row] for q in range(4)] + [jnp.zeros((4, SIDE), F32)])

    for b in range(BLOCKS):
        put_rim(
            entries[0, b, 0], b, lambda s: east[s], fixed_high,
            lambda s: far_east[s], lambda s: pack1[6 + s], wide_low, has_low,
        )
        put_rim(
            entries[0, b, 1], b, lambda s: west[s], fixed_low,
            lambda s: far_west[s], lambda s: pack_back[1 + s], wide_high, has_high,
        )
    face_m, face_0, _ = faces_low(low, ground_low, wide_low)
    _, face_z = faces_high(high, ground_high, wide_high)
    face_m = face_m * has_low[...]
    face_z = face_z * has_high[...]
    for b in range(BLOCKS):
        sub = slice(4 + b, 5 + b)
        beside = [f[b : b + 1] for f in (face_m, face_0, face_z)]
        blank = [jnp.zeros((1, SIDE), F32)]
        to_north[4 + b] = jnp.concatenate([ground_high[q, sub] for q in range(4)] + [edge_spill[2, sub]] + beside)
        to_south[4 + b] = jnp.concatenate(
            [ground_low[0, sub], ground_low[1, sub], ground_low[3, sub], edge_spill[0, sub]] + beside + blank
        )
        passed = jnp.concatenate(
            [
                far_east[b, 1:2], far_east[b, 5:6], pack1[6 + b, 1:2], pack1[6 + b, 3:4],
                far_west[b, 0:1], far_west[b, 6:7], pack_back[1 + b, 0:1], pack_back[1 + b, 2:3],
            ]
        )
        to_north[8 + b] = passed
        to_south[8 + b] = passed


def arrange(dest, entries, packs, ground, edge_spill):
    outs = [(8, 8), (6, 8), (16, 8), (16, 8), (8,), (8,), (BLOCKS, 8), (BLOCKS, 8), (3 * BLOCKS, 8), (3 * BLOCKS, 8)]
    return pl.pallas_call(
        arrange_kernel,
        out_shape=[shape(*dims, SIDE) for dims in outs],
        in_specs=[SMEM] * 2 + [VMEM] * 9,
        out_specs=[VMEM] * len(outs),
        scratch_shapes=[pltpu.VMEM((BLOCKS, 8, SIDE), F32)] * 2,
        compiler_params=params(4),
        cost_estimate=cost(0, 0),
    )(dest, entries, *packs, *ground, edge_spill)


def along_edge(h, z, rough, flow, face_before, face_first, face_last):
    lane = lanes(8, SIDE)
    eta = h + z
    flux = face(
        eta, pltpu.roll(eta, SIDE - 1, 1), z, pltpu.roll(z, SIDE - 1, 1), rough,
        pltpu.roll(flow, 1, 1), flow, pltpu.roll(flow, SIDE - 1, 1),
    )
    flux = jnp.where(lane == 0, face_first, flux)
    flux = jnp.where(lane == SIDE - 1, face_last, flux)
    lower = jnp.where(lane == 0, face_before, pltpu.roll(flux, 1, 1))
    return lower - flux


def corner_faces(h, z, rough, flow, entry_s, entry_n, corners_s, corners_n):
    def chosen(entry, corners, q):
        value = jnp.zeros((8, SIDE), F32)
        for j in range(2 * BLOCKS):
            value = jnp.where(entry == j, corners[q][j : j + 1], value)
        return value

    h_s, t_s, z_s, n_s = (chosen(entry_s, corners_s, q) for q in range(4))
    h_n, t_n, z_n = (chosen(entry_n, corners_n, q) for q in range(3))
    last = SIDE - 1
    has_s = jnp.where(column(entry_s, 0) >= 0.0, 1.0, 0.0)
    has_n = jnp.where(column(entry_n, 0) >= 0.0, 1.0, 0.0)
    eta, eta_s, eta_n = h + z, h_s + z_s, h_n + z_n
    before = face(
        column(eta_s, last), column(eta, 0), column(z_s, last), column(z, 0), column(n_s, last),
        column(t_s, last - 1), column(t_s, last), column(flow, 0),
    ) * has_s
    first = face(
        column(eta, 0), column(eta, 1), column(z, 0), column(z, 1), column(rough, 0),
        column(t_s, last), column(flow, 0), column(flow, 1),
    )
    final = face(
        column(eta, last), column(eta_n, 0), column(z, last), column(z_n, 0), column(rough, last),
        column(flow, last - 1), column(flow, last), column(t_n, 0),
    ) * has_n
    return before, first, final


def edges_kernel(
    entries, wet, edge_spill, low, high, ground_low, ground_high, wide_low_in, wide_high_in, has_low_in, has_high_in,
    far_east, far_west, pack1, pack_back, to_south, to_north, from_north, from_south,
    columns, rows,
    wide_low, wide_high, has_low, has_high, wetness, edge, rim_low, rim_high, corners, stack,
):
    wide_low[...] = wide_low_in[...]
    wide_high[...] = wide_high_in[...]
    has_low[...] = has_low_in[...]
    has_high[...] = has_high_in[...]
    for b in range(BLOCKS):
        value = jnp.full((1, SIDE), wet[0, b].astype(F32), F32)
        wetness[b : b + 1] = value
        wetness[4 + b : 5 + b] = value
        for entry, near, far, wide, has in (
            (entries[0, b, 2], to_north, from_south, wide_low, has_low),
            (entries[0, b, 3], to_south, from_north, wide_high, has_high),
        ):
            put_rim(
                entry, 4 + b, lambda s, r=near: r[s], lambda s, r=near: r[BLOCKS + s],
                lambda s, r=far: r[s], lambda s, r=far: r[BLOCKS + s], wide, has,
            )
    for j in range(BLOCKS):
        near = slice(j, j + 1)
        far = slice(BLOCKS + j, BLOCKS + j + 1)
        for q, row in enumerate(
            (
                far_east[j, 1:2], far_east[j, 5:6], pack1[6 + j, 1:2], pack1[6 + j, 3:4],
                far_west[j, 0:1], far_west[j, 6:7], pack_back[1 + j, 0:1], pack_back[1 + j, 2:3],
            )
        ):
            for i, passed in enumerate((from_south, from_north)):
                corners[i, q, near] = row
                corners[i, q, far] = passed[2 * BLOCKS + j, q : q + 1]

    def seen(i, first):
        return [corners[i, first + q] for q in range(4)]

    h0, h1, h2, q0, q1, q2, t0, t1 = (low[q] for q in range(8))
    z0, z1, z2, n0, n1 = (ground_low[q] for q in range(5))
    hy, hz, qx, qy, qz, tz = (high[q] for q in range(6))
    zy, zz, ny, nz = (ground_high[q] for q in range(4))
    face_m, face_0, face_1 = faces_low(low, ground_low, wide_low)
    face_y, face_z = faces_high(high, ground_high, wide_high)
    face_m = face_m * has_low[...]
    face_z = face_z * has_high[...]
    swapped = [sides_swapped(f) for f in (face_m, face_0, face_z)]

    def beside(spot):
        return [column(f, spot) for f in swapped]

    wets = wetness[...]
    last = SIDE - 1
    new_0 = (h0 + RATIO * (face_m - face_0 + along_edge(h0, z0, n0, t0, *beside(0))) + edge_spill[0]) * wets
    new_1 = (h1 + RATIO * (face_0 - face_1 + along_edge(h1, z1, n1, t1, *beside(1))) + edge_spill[1]) * wets
    new_z = (hz + RATIO * (face_y - face_z + along_edge(hz, zz, nz, tz, *beside(last))) + edge_spill[2]) * wets
    flow_0, flow_1, flow_y, flow_z = (f * wets for f in (face_0, face_1, face_y, face_z))
    for i, value in enumerate((new_z, flow_y, flow_z, new_0, flow_0)):
        edge[i] = value

    sides = lax.broadcasted_iota(jnp.int32, (8, 1), 0) < 4
    ghy, ghz, gqx, gqy, gqz, gtz = (wide_low[q] for q in range(6))
    gzy, gzz, gny, gnz, gspill = (wide_low[8 + q] for q in range(5))
    across = corner_faces(ghz, gzz, gnz, gtz, wide_low[13], wide_low[14], seen(0, 0), seen(1, 0))
    given = [column(wide_low[13 + q], last) for q in range(3)]
    ends = [jnp.where(sides, a, g) for a, g in zip(across, given)]
    far_face = face(ghy + gzy, ghz + gzz, gzy, gzz, gny, gqx, gqy, gqz)
    far_low = (
        ghz + RATIO * (far_face - face_m + along_edge(ghz, gzz, gnz, gtz, *ends)) + gspill,
        far_face,
        face_m,
    )
    gh0, gh1, gq0, gq1, gt0 = (wide_high[q] for q in (0, 1, 3, 4, 6))
    gz0, gz1, gn0, gspill = (wide_high[8 + q] for q in range(4))
    across = corner_faces(gh0, gz0, gn0, gt0, wide_high[12], wide_high[13], seen(0, 4), seen(1, 4))
    given = [column(wide_high[12 + q], 0) for q in range(3)]
    ends = [jnp.where(sides, a, g) for a, g in zip(across, given)]
    far_face = face(gh0 + gz0, gh1 + gz1, gz0, gz1, gn0, qz, gq0, gq1)
    far_high = (
        gh0 + RATIO * (face_z - far_face + along_edge(gh0, gz0, gn0, gt0, *ends)) + gspill,
        far_face,
    )
    for rim, far_rows, first, group in ((rim_low, far_low, 0, 0), (rim_high, far_high, 3, 1)):
        for q, far_row in enumerate(far_rows):
            rim[q] = far_row
        for b in range(BLOCKS):
            for side in range(2):
                entry = entries[0, b, 2 * side + group]
                sub = slice(side * 4 + b, side * 4 + b + 1)
                near = pl.ds(side * 4 + jnp.clip(entry, 0, BLOCKS - 1), 1)
                for q in range(len(far_rows)):
                    row = jnp.where(entry >= BLOCKS, rim[q, sub], edge[first + q, near])
                    rim[q, sub] = jnp.where(entry >= 0, row, 0.0)

    hm, qmm, qm = (rim_low[q] for q in range(3))
    hp, qp = (rim_high[q] for q in range(2))
    zm, nm, zp = wide_low[9], wide_low[11], wide_high[8]
    next_m = face(hm + zm, new_0 + z0, zm, z0, nm, qmm, qm, flow_0) * has_low[...]
    next_0 = face(new_0 + z0, new_1 + z1, z0, z1, n0, qm, flow_0, flow_1)
    next_z = face(new_z + zz, hp + zp, zz, zp, nz, flow_y, flow_z, qp) * has_high[...]
    stack[...] = jnp.zeros_like(stack)
    rows[...] = jnp.zeros_like(rows)
    for b in range(BLOCKS):
        for i, value in enumerate((face_m, face_0, face_z, next_m, next_0, next_z)):
            stack[b * 8 + i : b * 8 + i + 1] = value[b : b + 1]
            rows[b, i : i + 1] = value[4 + b : 5 + b]
    turned = stack[...].T
    columns[0] = turned
    for b in range(1, BLOCKS):
        columns[b] = pltpu.roll(turned, HALF - 8 * b, 1)


def inflow_kernel(cells, rates, spill, edge_spill):
    spill[...] = jnp.zeros_like(spill)
    edge_spill[...] = jnp.zeros_like(edge_spill)
    lane = lanes(1, SIDE)
    for b in range(BLOCKS):

        def point(p, carry, b=b):
            cell = cells[0, b, p]
            row = lax.div(cell, SIDE)
            column = lax.rem(cell, SIDE)
            rate = GAIN * rates[0, b, p]
            at_column = jnp.where(lane == column, rate, 0.0)
            at_row = jnp.where(lane == row, rate, 0.0)
            line = pl.ds(row, 1)
            spill[b, line] = spill[b, line] + at_column
            for i, place in enumerate((0, 1, SIDE - 1)):
                edge_spill[i, b : b + 1] += jnp.where(column == place, at_row, 0.0)
                edge_spill[i, 4 + b : 5 + b] += jnp.where(row == place, at_column, 0.0)
            return carry

        lax.fori_loop(0, RIVERS, point, 0)


def lay_inflow(cells, rates):
    return pl.pallas_call(
        inflow_kernel,
        out_shape=[shape(BLOCKS, SIDE, SIDE), shape(3, 8, SIDE)],
        in_specs=[SMEM, SMEM],
        out_specs=[VMEM] * 2,
        compiler_params=params(4),
        cost_estimate=cost(0, 0),
    )(cells, rates)


def block_step(now, ground, spill, columns, rows, base, wetness, write):
    lane = lanes(ROWS, SIDE)
    sub = lax.broadcasted_iota(jnp.int32, (ROWS, SIDE), 0)

    def at(load, field, first, shift):
        if 0 <= first + shift <= SIDE - ROWS:
            return load(field, first + shift)
        return pltpu.roll(load(field, first), -shift % ROWS, 0)

    below = rows(base)
    for first in range(0, SIDE, ROWS):
        h, qx, qy = (at(now, f, first, 0) for f in range(3))
        z, rough = (at(ground, f, first, 0) for f in range(2))
        eta = h + z
        flux_x = face(
            eta, pltpu.roll(eta, SIDE - 1, 1), z, pltpu.roll(z, SIDE - 1, 1), rough,
            pltpu.roll(qx, 1, 1), qx, pltpu.roll(qx, SIDE - 1, 1),
        )
        edge = columns(pl.ds(first, ROWS))
        flux_x = jnp.where(lane == 0, edge[:, base + 1 : base + 2], flux_x)
        flux_x = jnp.where(lane == SIDE - 1, edge[:, base + 2 : base + 3], flux_x)
        flux_w = jnp.where(lane == 0, edge[:, base : base + 1], pltpu.roll(flux_x, 1, 1))
        z_up = at(ground, 0, first, 1)
        flux_y = face(
            eta, at(now, 0, first, 1) + z_up, z, z_up, rough, at(now, 2, first, -1), qy, at(now, 2, first, 1)
        )
        if first == 0:
            flux_y = jnp.where(sub == 0, rows(base + 1), flux_y)
        if first == SIDE - ROWS:
            flux_y = jnp.where(sub == ROWS - 1, rows(base + 2), flux_y)
        flux_s = jnp.where(sub == 0, below, pltpu.roll(flux_y, 1, 0))
        below = flux_y[ROWS - 1 : ROWS]
        depth = h + RATIO * (flux_w - flux_x + flux_s - flux_y) + spill(pl.ds(first, ROWS))
        write(first, depth * wetness, flux_x * wetness, flux_y * wetness)


def block(shifts, dest, wet, terrain, columns, rows, spill, states, out, then, done, sems):
    slot = landing_slot(dest, jnp.where(core() == 0, *shifts))
    wetness = wet[0, slot].astype(F32)
    state = states[0]
    if shifts == W_SHIFTS:
        for here, ref in enumerate(states):

            @pl.when(core() == 1 - here)
            def _(ref=ref):
                copy = pltpu.make_async_copy(ref, done, sems.at[0])
                copy.start()
                copy.wait()

        state = done
    copies = []

    def now(field, first):
        if shifts != A_SHIFTS:
            return state[field, first : first + ROWS]
        if first + ROWS <= CUT:
            return states[0][field, first : first + ROWS]
        if first >= CUT:
            return states[1][field, first - CUT : first - CUT + ROWS]
        return jnp.concatenate([states[0][field, first:CUT], states[1][field, 0 : first + ROWS - CUT]])

    def ground(field, first):
        return terrain[0, slot, field, first : first + ROWS]

    def keep(first, *fields):
        for f, value in enumerate(fields):
            then[f, first : first + ROWS] = value

    def finish(first, *fields):
        for f, value in enumerate(fields):
            done[f, first : first + ROWS] = value
        lines = pl.ds(first, ROWS)
        copies.append(pltpu.make_async_copy(done.at[:, lines], out.at[0, slot, :, lines], sems.at[len(copies)]))
        copies[-1].start()

    shared = (
        lambda at: spill[slot, at],
        lambda at: columns[slot, at],
        lambda q: rows[slot, q : q + 1],
    )
    block_step(now, ground, *shared, 0, wetness, keep)
    block_step(lambda f, first: then[f, first : first + ROWS], ground, *shared, 3, wetness, finish)
    return copies


EDGE_INPUTS = 19
EDGE_SCRATCH = 10


def block_scratch():
    return [pltpu.VMEM((3, SIDE, SIDE), F32)] * 3 + [pltpu.SemaphoreType.DMA((SIDE // ROWS,))] * 2


def early_kernel(dest, *refs):
    ins, refs = refs[:EDGE_INPUTS], refs[EDGE_INPUTS:]
    terrain, spill, own, a_low, a_high, out, columns, rows = refs[:8]
    edge_scratch, (then, done1, done2, sems1, sems2) = refs[8 : 8 + EDGE_SCRATCH], refs[8 + EDGE_SCRATCH :]
    edges_kernel(*ins, columns, rows, *edge_scratch)
    shared = (dest, ins[1], terrain, columns, rows, spill)
    copies = block(OWN_SHIFTS, *shared, (own,), out, then, done1, sems1)
    copies += block(A_SHIFTS, *shared, (a_low, a_high), out, then, done2, sems2)
    for copy in copies:
        copy.wait()


def early_blocks(dest, edge_inputs, terrain, spill, own, a_low, a_high):
    return pl.pallas_call(
        early_kernel,
        out_shape=[shape(1, BLOCKS, 3, SIDE, SIDE), shape(BLOCKS, SIDE, HALF), shape(BLOCKS, 8, SIDE)],
        in_specs=[SMEM] * 3 + [VMEM] * (EDGE_INPUTS - 2 + 5),
        out_specs=[HBM, VMEM, VMEM],
        scratch_shapes=[
            pltpu.VMEM((16, 8, SIDE), F32),
            pltpu.VMEM((16, 8, SIDE), F32),
            pltpu.VMEM((8, SIDE), F32),
            pltpu.VMEM((8, SIDE), F32),
            pltpu.VMEM((8, SIDE), F32),
            pltpu.VMEM((5, 8, SIDE), F32),
            pltpu.VMEM((3, 8, SIDE), F32),
            pltpu.VMEM((2, 8, SIDE), F32),
            pltpu.VMEM((2, 8, 8, SIDE), F32),
            pltpu.VMEM((HALF, SIDE), F32),
        ]
        + block_scratch(),
        compiler_params=params(16),
        cost_estimate=cost(0, 0),
    )(dest, *edge_inputs, terrain, spill, own, a_low, a_high)


def late_kernel(dest, wet, terrain, columns, rows, spill, arrived_w, relayed, arrived_x, _, out, *scratch):
    then, done1, done2, sems1, sems2 = scratch
    shared = (dest, wet, terrain, columns, rows, spill)
    copies = block(W_SHIFTS, *shared, (arrived_w, relayed), out, then, done1, sems1)
    copies += block(X_SHIFTS, *shared, (arrived_x,), out, then, done2, sems2)
    for copy in copies:
        copy.wait()


def late_blocks(dest, wet, terrain, columns, rows, spill, arrived_w, relayed, arrived_x, out):
    return pl.pallas_call(
        late_kernel,
        out_shape=shape(1, BLOCKS, 3, SIDE, SIDE),
        in_specs=[SMEM] * 2 + [VMEM] * 4 + [ANY] * 2 + [VMEM, HBM],
        out_specs=HBM,
        input_output_aliases={9: 0},
        scratch_shapes=block_scratch(),
        compiler_params=params(16),
        cost_estimate=cost(0, 0),
    )(dest, wet, terrain, columns, rows, spill, arrived_w, relayed, arrived_x, out)


def passed_along(x, axis, by, wrap=True):
    devices = lax.axis_size(axis)
    return lax.ppermute(x, axis, [(i, (i + by) % devices) for i in range(devices)])


def passed_to(x, target):
    devices = lax.axis_size("tile")
    pairs = [(i, target(i // 2, i % 2)) for i in range(devices)]
    return lax.ppermute(x, "tile", [(i, t % devices) for i, t in pairs if t is not None])


def back_one(chip):
    return chip // RING * RING + (chip - 1) % RING


def first_leg(chip, at):
    return 2 * chip + 1 if at == 0 else 2 * back_one(chip)


def second_leg(chip, at):
    sender = chip // RING * RING + (chip + 1) % RING
    return 2 * (sender + 2) if at == 0 else None


def next_chip_swapped(chip, at):
    return 2 * (chip + 1) + 1 - at


def body(flood_state, terrain, destination, wet_mask, neighbours, inflow_cells, inflow_rates):
    dest, state = in_hbm(destination), in_hbm(flood_state)
    a_low, a_high = pick_early(dest, state)
    arrived_low = passed_along(a_low, "tile", 2)
    own, block_w, block_x, ground_low, ground_high, *packs = prepare(
        dest, in_hbm(neighbours), state, a_low, a_high,
        in_hbm(terrain), in_hbm(inflow_cells), in_hbm(inflow_rates),
    )
    ground = (ground_low, ground_high)
    spill, edge_spill = lay_inflow(inflow_cells, inflow_rates)
    (packs[5],) = gate((packs[5],), (arrived_low,))
    packs = [packs[0]] + [passed_along(p, "tile", d) for d, p in zip((1, 2, 3, 4, -1), packs[1:])]
    a_high, block_x, block_w = gate((a_high, block_x, block_w), packs[1:])
    arrived_high = passed_along(a_high, "tile", 2)
    arrived_x = passed_to(block_x, next_chip_swapped)
    arrived_w = passed_to(block_w, first_leg)
    low, high, wide_low, wide_high, has_low, has_high, far_east, far_west, to_south, to_north = arrange(
        destination, neighbours, packs, ground, edge_spill
    )
    from_north = passed_along(to_south, "grp", -1)
    from_south = passed_along(to_north, "grp", 1)
    (arrived_w,) = gate((arrived_w,), (from_north, from_south, arrived_high))
    relayed = passed_to(arrived_w, second_leg)
    edge_inputs = (
        neighbours, wet_mask, edge_spill, low, high, *ground, wide_low, wide_high, has_low, has_high,
        far_east, far_west, packs[1], packs[5], to_south, to_north, from_north, from_south,
    )
    out, columns, rows = early_blocks(destination, edge_inputs, terrain, spill, own, arrived_low, arrived_high)
    return late_blocks(destination, wet_mask, terrain, columns, rows, spill, arrived_w, relayed, arrived_x, out)


def solution(mesh):
    in_specs = (
        P("grp", "tile", None, None, None),
        P("grp", "tile", None, None, None),
        P("grp", None),
        P("grp", "tile"),
        P("grp", "tile", None),
        P("grp", "tile", None),
        P("grp", "tile", None),
    )
    out_specs = P("grp", "tile", None, None, None)
    return jax.shard_map(body, mesh=mesh, in_specs=in_specs, out_specs=out_specs, check_vma=False)
```

```python
import functools

import jax
import jax.numpy as jnp
from jax import lax
from jax.experimental import pallas as pl
from jax.experimental.pallas import tpu as pltpu
from jax.sharding import PartitionSpec as P

F32 = jnp.float32
GRAVITY = 9.81
SPACING = 10.0
TIMESTEP = 0.2
CENTRE_WEIGHT = 0.7
DEPTH_FLOOR = 0.1
SIDE = 256
HALF = 128
BLOCKS = 4
RIVERS = 16
ROWS = 64
GAIN = TIMESTEP / (SPACING * SPACING)
RATIO = TIMESTEP / SPACING

ANY = pl.BlockSpec(memory_space=pl.ANY)
VMEM = pl.BlockSpec(memory_space=pltpu.VMEM)
SMEM = pl.BlockSpec(memory_space=pltpu.SMEM)
HBM = pl.BlockSpec(memory_space=pltpu.HBM)
RING = 4
OWN_SHIFTS = (0, 0)
A_SHIFTS = (2, 2)
W_SHIFTS = (3, 1)
X_SHIFTS = (1, 3)


def shape(*dims):
    return jax.ShapeDtypeStruct(dims, F32)


def cost(flops, bytes_accessed):
    return pl.CostEstimate(flops=flops, bytes_accessed=bytes_accessed, transcendentals=0)


def face(eta_l, eta_r, z_l, z_r, rough, flow_left, flow_mid, flow_right):
    depth = jnp.maximum(eta_l, eta_r) - jnp.maximum(z_l, z_r)
    floored = jnp.maximum(depth, DEPTH_FLOOR)
    blended = CENTRE_WEIGHT * flow_mid + 0.5 * (1.0 - CENTRE_WEIGHT) * (flow_left + flow_right)
    slope = (GRAVITY * TIMESTEP / SPACING) * depth * (eta_r - eta_l)
    friction = 1.0 + (GRAVITY * TIMESTEP) * rough * rough * jnp.abs(flow_mid) * jnp.exp(
        (-7.0 / 3.0) * jnp.log(floored)
    )
    return (blended - slope) / friction


def core():
    return lax.rem(lax.axis_index("tile"), 2)


def params(mib):
    return pltpu.CompilerParams(vmem_limit_bytes=mib << 20)


def tile_offset(dest_ref, tile, slot):
    tiles = lax.axis_size("tile")
    return lax.rem(lax.div(dest_ref[0, tile * BLOCKS + slot], BLOCKS) - tile + tiles, tiles)


def leaving_slot(dest_ref, shift):
    me = lax.axis_index("tile")
    slot = jnp.int32(0)
    for j in range(1, BLOCKS):
        slot = jnp.where(tile_offset(dest_ref, me, j) == shift, j, slot)
    return slot


def landing_slot(dest_ref, shift, back=0):
    tiles = lax.axis_size("tile")
    sender = lax.rem(lax.axis_index("tile") - shift - back + 2 * tiles, tiles)
    slot = jnp.int32(0)
    for j in range(BLOCKS):
        place = lax.rem(dest_ref[0, sender * BLOCKS + j], BLOCKS)
        slot = jnp.where(tile_offset(dest_ref, sender, j) == shift, place, slot)
    return slot


def lanes(rows, columns):
    return lax.broadcasted_iota(jnp.int32, (rows, columns), 1)


def in_hbm(x):
    return pltpu.with_memory_space_constraint(x, pltpu.HBM)


def pick_kernel(dest, state, block_a, block_w, sems):
    slots = [leaving_slot(dest, k) for k in range(1, BLOCKS)]
    slot_w = jnp.where(core() == 0, slots[0], slots[2])
    loads = [
        pltpu.make_async_copy(state.at[0, slot], ref, sems.at[i])
        for i, (slot, ref) in enumerate(((slots[1], block_a), (slot_w, block_w)))
    ]
    for load in loads:
        load.start()
    for load in loads:
        load.wait()


def pick_early(dest, state):
    return pl.pallas_call(
        pick_kernel,
        out_shape=[shape(3, SIDE, SIDE)] * 2,
        in_specs=[SMEM, HBM],
        out_specs=[VMEM] * 2,
        scratch_shapes=[pltpu.SemaphoreType.DMA((2,))],
        compiler_params=params(4),
        cost_estimate=cost(0, 0),
    )(dest, state)


def prepare_kernel(
    dest, entries, state, block_a, block_w, ground_in, cells, rates,
    own, block_x, low, high, pack0, pack1, pack2, pack3, pack4, pack_back, terrain, sems,
):
    slots = [leaving_slot(dest, k) for k in range(BLOCKS)]
    first_core = core() == 0
    slot_x = jnp.where(first_core, slots[3], slots[1])
    held = (block_x, own)
    loads = [pltpu.make_async_copy(ground_in, terrain, sems.at[3])]
    for i, (slot, ref) in enumerate(zip((slot_x, slots[0]), held)):
        loads.append(pltpu.make_async_copy(state.at[0, slot], ref, sems.at[i]))
    for load in loads:
        load.start()
    lane = lanes(SIDE, HALF)

    def strips(ref, write):
        west = [ref[f, :, :HALF] for f in range(3)]
        east = [ref[f, :, HALF:] for f in range(3)]
        packed = jnp.where(lane < 3, west[0], pltpu.roll(west[1], 3, 1))
        packed = jnp.where(lane < 6, packed, pltpu.roll(west[2], 6, 1))
        packed = jnp.where(lane < 8, packed, pltpu.roll(east[0], 10, 1))
        packed = jnp.where(lane < 10, packed, pltpu.roll(east[1], 13, 1))
        packed = jnp.where(lane < 13, packed, pltpu.roll(east[2], 14, 1))
        turned = packed.T
        south = jnp.concatenate([ref[0, 0:3], ref[2, 0:3], ref[1, 0:2]])
        north = jnp.concatenate(
            [ref[0, SIDE - 2 : SIDE], ref[2, SIDE - 3 : SIDE], ref[1, SIDE - 1 : SIDE], jnp.zeros((2, SIDE), F32)]
        )
        write(turned[0:8], south, turned[8:16], north)

    strip_out = (pack0, pack1, pack2, pack3)
    west_out = (pack_back.at[0], pack0.at[4], pack1.at[5], pack2.at[5])
    east_out = (pack1.at[4], pack2.at[4], pack3.at[4], pack4.at[0])

    def write(k, west, south, east, north):
        for i, value in enumerate((west, south, east, north)):
            strip_out[k][i] = value
        east_out[k][...] = east
        west_out[k][...] = west

    def write_by_core(first, second):
        def both(*values):
            pl.when(first_core)(lambda: write(first, *values))
            pl.when(jnp.logical_not(first_core))(lambda: write(second, *values))

        return both

    strips(block_a, functools.partial(write, 2))
    strips(block_w, write_by_core(1, 3))
    along = lanes(BLOCKS, SIDE)
    spills = [jnp.zeros((BLOCKS, SIDE), F32) for _ in range(2)]
    for p in range(RIVERS):
        cell = cells[0, :, p : p + 1] - along * SIDE
        rate = GAIN * rates[0, :, p : p + 1]
        for i, place in enumerate((0, SIDE - 1)):
            spills[i] = spills[i] + jnp.where(cell == place, rate, 0.0)
    loads[0].wait()
    for b in range(BLOCKS):
        west = [terrain[0, b, f, :, :HALF] for f in range(2)]
        east = [terrain[0, b, f, :, HALF:] for f in range(2)]
        packed = jnp.where(lane < 3, west[0], pltpu.roll(west[1], 3, 1))
        packed = jnp.where(lane < 5, packed, pltpu.roll(east[0], 7, 1))
        packed = jnp.where(lane < 7, packed, pltpu.roll(east[1], 9, 1))
        turned = packed.T
        for q in range(5):
            low[q, b : b + 1] = turned[q : q + 1]
        for q in range(4):
            high[q, b : b + 1] = turned[5 + q : 6 + q]
        for q in range(3):
            low[q, 4 + b : 5 + b] = terrain[0, b, 0, q : q + 1]
        for q in range(2):
            low[3 + q, 4 + b : 5 + b] = terrain[0, b, 1, q : q + 1]
            high[q, 4 + b : 5 + b] = terrain[0, b, 0, SIDE - 2 + q : SIDE - 1 + q]
            high[2 + q, 4 + b : 5 + b] = terrain[0, b, 1, SIDE - 2 + q : SIDE - 1 + q]
    for b in range(BLOCKS):
        line = slice(b, b + 1)
        links = [jnp.full((1, SIDE), entries[0, b, side].astype(F32), F32) for side in (2, 3)]
        blank = [jnp.zeros((1, SIDE), F32)]
        pack1[6 + b] = jnp.concatenate([high[q, line] for q in range(4)] + [spills[1][line]] + links + blank)
        pack_back[1 + b] = jnp.concatenate(
            [low[0, line], low[1, line], low[3, line], spills[0][line]] + links + blank * 2
        )
    writers = (write_by_core(3, 1), functools.partial(write, 0))
    for load, ref, write_out in zip(loads[1:], held, writers):
        load.wait()
        strips(ref, write_out)


def prepare(dest, entries, state, block_a, block_w, terrain, cells, rates):
    packs = [shape(count, 8, SIDE) for count in (5, 10, 6, 5, 1, 5)]
    return pl.pallas_call(
        prepare_kernel,
        out_shape=[shape(3, SIDE, SIDE)] * 2 + [shape(5, 8, SIDE), shape(4, 8, SIDE)] + packs,
        in_specs=[SMEM, SMEM, HBM, VMEM, VMEM, HBM, VMEM, VMEM],
        out_specs=[VMEM] * 10,
        scratch_shapes=[
            pltpu.VMEM((1, BLOCKS, 2, SIDE, SIDE), F32),
            pltpu.SemaphoreType.DMA((BLOCKS,)),
        ],
        compiler_params=params(12),
        cost_estimate=cost(0, 0),
    )(dest, entries, state, block_a, block_w, terrain, cells, rates)


def gate_kernel(count, *refs):
    del count, refs


def gate(values, keys):
    count = len(values)
    return pl.pallas_call(
        functools.partial(gate_kernel, count),
        out_shape=[jax.ShapeDtypeStruct(v.shape, v.dtype) for v in values],
        in_specs=[ANY] * (count + len(keys)),
        out_specs=[ANY] * count,
        input_output_aliases={i: i for i in range(count)},
        compiler_params=params(1),
        cost_estimate=cost(0, 0),
    )(*values, *keys)


def sides_swapped(x):
    return pltpu.roll(x, 4, 0)


def column(x, at):
    return x[:, at : at + 1]


def put_rim(entry, sub, near_state, near_fixed, far_state, far_fixed, wide, has):
    near = jnp.clip(entry, 0, BLOCKS - 1)
    far = jnp.clip(entry - BLOCKS, 0, BLOCKS - 1)
    alive = entry >= 0
    for i, (close, distant) in enumerate(((near_state, far_state), (near_fixed, far_fixed))):
        rows = jnp.where(entry >= BLOCKS, distant(far), close(near))
        rows = jnp.where(alive, rows, 0.0)
        for q in range(8):
            wide[8 * i + q, sub : sub + 1] = rows[q : q + 1]
    has[sub : sub + 1] = jnp.full((1, SIDE), jnp.where(alive, 1.0, 0.0), F32)


def faces_low(low, ground_low, wide):
    h0, h1, h2, q0, q1, q2 = (low[q] for q in range(6))
    z0, z1, z2, n0, n1 = (ground_low[q] for q in range(5))
    hm, qmm, qm, zm, nm = (wide[q] for q in (1, 3, 4, 9, 11))
    return (
        face(hm + zm, h0 + z0, zm, z0, nm, qmm, qm, q0),
        face(h0 + z0, h1 + z1, z0, z1, n0, qm, q0, q1),
        face(h1 + z1, h2 + z2, z1, z2, n1, q0, q1, q2),
    )


def faces_high(high, ground_high, wide):
    hy, hz, qx, qy, qz = (high[q] for q in range(5))
    zy, zz, ny, nz = (ground_high[q] for q in range(4))
    hp, qp, zp = (wide[q] for q in (0, 3, 8))
    return (
        face(hy + zy, hz + zz, zy, zz, ny, qx, qy, qz),
        face(hz + zz, hp + zp, zz, zp, nz, qy, qz, qp),
    )


def arrange_kernel(
    dest, entries, pack0, pack1, pack2, pack3, pack4, pack_back, ground_low, ground_high, edge_spill,
    low, high, wide_low, wide_high, has_low, has_high, far_east, far_west, to_south, to_north,
    west, east,
):
    for out in (low, high, wide_low, wide_high, has_low, has_high):
        out[...] = jnp.zeros_like(out)
    strips = (pack0, pack1, pack2, pack3)
    west_in = (pack_back.at[0], pack0.at[4], pack1.at[5], pack2.at[5])
    east_in = (pack1.at[4], pack2.at[4], pack3.at[4], pack4.at[0])
    for k in range(BLOCKS):
        strip = strips[k]
        slot = landing_slot(dest, k)
        for side in range(2):
            row = pl.ds(side * 4 + slot, 1)
            for q in range(8):
                low[q, row] = strip[side, q : q + 1]
            for q in range(6):
                high[q, row] = strip[2 + side, q : q + 1]
        for i, out in enumerate((west, to_south, east, to_north)):
            out[slot] = strip[i]
        slot = landing_slot(dest, k, 1)
        far_east[slot] = east_in[k][...]
        slot = landing_slot(dest, k, -1)
        far_west[slot] = west_in[k][...]

    def fixed_low(slot):
        row = pl.ds(slot, 1)
        rows = [ground_low[0, row], ground_low[1, row], ground_low[3, row]]
        return jnp.concatenate(rows + [jnp.zeros((5, SIDE), F32)])

    def fixed_high(slot):
        row = pl.ds(slot, 1)
        return jnp.concatenate([ground_high[q, row] for q in range(4)] + [jnp.zeros((4, SIDE), F32)])

    for b in range(BLOCKS):
        put_rim(
            entries[0, b, 0], b, lambda s: east[s], fixed_high,
            lambda s: far_east[s], lambda s: pack1[6 + s], wide_low, has_low,
        )
        put_rim(
            entries[0, b, 1], b, lambda s: west[s], fixed_low,
            lambda s: far_west[s], lambda s: pack_back[1 + s], wide_high, has_high,
        )
    face_m, face_0, _ = faces_low(low, ground_low, wide_low)
    _, face_z = faces_high(high, ground_high, wide_high)
    face_m = face_m * has_low[...]
    face_z = face_z * has_high[...]
    for b in range(BLOCKS):
        sub = slice(4 + b, 5 + b)
        beside = [f[b : b + 1] for f in (face_m, face_0, face_z)]
        blank = [jnp.zeros((1, SIDE), F32)]
        to_north[4 + b] = jnp.concatenate([ground_high[q, sub] for q in range(4)] + [edge_spill[2, sub]] + beside)
        to_south[4 + b] = jnp.concatenate(
            [ground_low[0, sub], ground_low[1, sub], ground_low[3, sub], edge_spill[0, sub]] + beside + blank
        )
        passed = jnp.concatenate(
            [
                far_east[b, 1:2], far_east[b, 5:6], pack1[6 + b, 1:2], pack1[6 + b, 3:4],
                far_west[b, 0:1], far_west[b, 6:7], pack_back[1 + b, 0:1], pack_back[1 + b, 2:3],
            ]
        )
        to_north[8 + b] = passed
        to_south[8 + b] = passed


def arrange(dest, entries, packs, ground, edge_spill):
    outs = [(8, 8), (6, 8), (16, 8), (16, 8), (8,), (8,), (BLOCKS, 8), (BLOCKS, 8), (3 * BLOCKS, 8), (3 * BLOCKS, 8)]
    return pl.pallas_call(
        arrange_kernel,
        out_shape=[shape(*dims, SIDE) for dims in outs],
        in_specs=[SMEM] * 2 + [VMEM] * 9,
        out_specs=[VMEM] * len(outs),
        scratch_shapes=[pltpu.VMEM((BLOCKS, 8, SIDE), F32)] * 2,
        compiler_params=params(4),
        cost_estimate=cost(0, 0),
    )(dest, entries, *packs, *ground, edge_spill)


def along_edge(h, z, rough, flow, face_before, face_first, face_last):
    lane = lanes(8, SIDE)
    eta = h + z
    flux = face(
        eta, pltpu.roll(eta, SIDE - 1, 1), z, pltpu.roll(z, SIDE - 1, 1), rough,
        pltpu.roll(flow, 1, 1), flow, pltpu.roll(flow, SIDE - 1, 1),
    )
    flux = jnp.where(lane == 0, face_first, flux)
    flux = jnp.where(lane == SIDE - 1, face_last, flux)
    lower = jnp.where(lane == 0, face_before, pltpu.roll(flux, 1, 1))
    return lower - flux


def corner_faces(h, z, rough, flow, entry_s, entry_n, corners_s, corners_n):
    def chosen(entry, corners, q):
        value = jnp.zeros((8, SIDE), F32)
        for j in range(2 * BLOCKS):
            value = jnp.where(entry == j, corners[q][j : j + 1], value)
        return value

    h_s, t_s, z_s, n_s = (chosen(entry_s, corners_s, q) for q in range(4))
    h_n, t_n, z_n = (chosen(entry_n, corners_n, q) for q in range(3))
    last = SIDE - 1
    has_s = jnp.where(column(entry_s, 0) >= 0.0, 1.0, 0.0)
    has_n = jnp.where(column(entry_n, 0) >= 0.0, 1.0, 0.0)
    eta, eta_s, eta_n = h + z, h_s + z_s, h_n + z_n
    before = face(
        column(eta_s, last), column(eta, 0), column(z_s, last), column(z, 0), column(n_s, last),
        column(t_s, last - 1), column(t_s, last), column(flow, 0),
    ) * has_s
    first = face(
        column(eta, 0), column(eta, 1), column(z, 0), column(z, 1), column(rough, 0),
        column(t_s, last), column(flow, 0), column(flow, 1),
    )
    final = face(
        column(eta, last), column(eta_n, 0), column(z, last), column(z_n, 0), column(rough, last),
        column(flow, last - 1), column(flow, last), column(t_n, 0),
    ) * has_n
    return before, first, final


def edges_kernel(
    entries, wet, edge_spill, low, high, ground_low, ground_high, wide_low_in, wide_high_in, has_low_in, has_high_in,
    far_east, far_west, pack1, pack_back, to_south, to_north, from_north, from_south,
    columns, rows,
    wide_low, wide_high, has_low, has_high, wetness, edge, rim_low, rim_high, corners, stack,
):
    wide_low[...] = wide_low_in[...]
    wide_high[...] = wide_high_in[...]
    has_low[...] = has_low_in[...]
    has_high[...] = has_high_in[...]
    for b in range(BLOCKS):
        value = jnp.full((1, SIDE), wet[0, b].astype(F32), F32)
        wetness[b : b + 1] = value
        wetness[4 + b : 5 + b] = value
        for entry, near, far, wide, has in (
            (entries[0, b, 2], to_north, from_south, wide_low, has_low),
            (entries[0, b, 3], to_south, from_north, wide_high, has_high),
        ):
            put_rim(
                entry, 4 + b, lambda s, r=near: r[s], lambda s, r=near: r[BLOCKS + s],
                lambda s, r=far: r[s], lambda s, r=far: r[BLOCKS + s], wide, has,
            )
    for j in range(BLOCKS):
        near = slice(j, j + 1)
        far = slice(BLOCKS + j, BLOCKS + j + 1)
        for q, row in enumerate(
            (
                far_east[j, 1:2], far_east[j, 5:6], pack1[6 + j, 1:2], pack1[6 + j, 3:4],
                far_west[j, 0:1], far_west[j, 6:7], pack_back[1 + j, 0:1], pack_back[1 + j, 2:3],
            )
        ):
            for i, passed in enumerate((from_south, from_north)):
                corners[i, q, near] = row
                corners[i, q, far] = passed[2 * BLOCKS + j, q : q + 1]

    def seen(i, first):
        return [corners[i, first + q] for q in range(4)]

    h0, h1, h2, q0, q1, q2, t0, t1 = (low[q] for q in range(8))
    z0, z1, z2, n0, n1 = (ground_low[q] for q in range(5))
    hy, hz, qx, qy, qz, tz = (high[q] for q in range(6))
    zy, zz, ny, nz = (ground_high[q] for q in range(4))
    face_m, face_0, face_1 = faces_low(low, ground_low, wide_low)
    face_y, face_z = faces_high(high, ground_high, wide_high)
    face_m = face_m * has_low[...]
    face_z = face_z * has_high[...]
    swapped = [sides_swapped(f) for f in (face_m, face_0, face_z)]

    def beside(spot):
        return [column(f, spot) for f in swapped]

    wets = wetness[...]
    last = SIDE - 1
    new_0 = (h0 + RATIO * (face_m - face_0 + along_edge(h0, z0, n0, t0, *beside(0))) + edge_spill[0]) * wets
    new_1 = (h1 + RATIO * (face_0 - face_1 + along_edge(h1, z1, n1, t1, *beside(1))) + edge_spill[1]) * wets
    new_z = (hz + RATIO * (face_y - face_z + along_edge(hz, zz, nz, tz, *beside(last))) + edge_spill[2]) * wets
    flow_0, flow_1, flow_y, flow_z = (f * wets for f in (face_0, face_1, face_y, face_z))
    for i, value in enumerate((new_z, flow_y, flow_z, new_0, flow_0)):
        edge[i] = value

    sides = lax.broadcasted_iota(jnp.int32, (8, 1), 0) < 4
    ghy, ghz, gqx, gqy, gqz, gtz = (wide_low[q] for q in range(6))
    gzy, gzz, gny, gnz, gspill = (wide_low[8 + q] for q in range(5))
    across = corner_faces(ghz, gzz, gnz, gtz, wide_low[13], wide_low[14], seen(0, 0), seen(1, 0))
    given = [column(wide_low[13 + q], last) for q in range(3)]
    ends = [jnp.where(sides, a, g) for a, g in zip(across, given)]
    far_face = face(ghy + gzy, ghz + gzz, gzy, gzz, gny, gqx, gqy, gqz)
    far_low = (
        ghz + RATIO * (far_face - face_m + along_edge(ghz, gzz, gnz, gtz, *ends)) + gspill,
        far_face,
        face_m,
    )
    gh0, gh1, gq0, gq1, gt0 = (wide_high[q] for q in (0, 1, 3, 4, 6))
    gz0, gz1, gn0, gspill = (wide_high[8 + q] for q in range(4))
    across = corner_faces(gh0, gz0, gn0, gt0, wide_high[12], wide_high[13], seen(0, 4), seen(1, 4))
    given = [column(wide_high[12 + q], 0) for q in range(3)]
    ends = [jnp.where(sides, a, g) for a, g in zip(across, given)]
    far_face = face(gh0 + gz0, gh1 + gz1, gz0, gz1, gn0, qz, gq0, gq1)
    far_high = (
        gh0 + RATIO * (face_z - far_face + along_edge(gh0, gz0, gn0, gt0, *ends)) + gspill,
        far_face,
    )
    for rim, far_rows, first, group in ((rim_low, far_low, 0, 0), (rim_high, far_high, 3, 1)):
        for q, far_row in enumerate(far_rows):
            rim[q] = far_row
        for b in range(BLOCKS):
            for side in range(2):
                entry = entries[0, b, 2 * side + group]
                sub = slice(side * 4 + b, side * 4 + b + 1)
                near = pl.ds(side * 4 + jnp.clip(entry, 0, BLOCKS - 1), 1)
                for q in range(len(far_rows)):
                    row = jnp.where(entry >= BLOCKS, rim[q, sub], edge[first + q, near])
                    rim[q, sub] = jnp.where(entry >= 0, row, 0.0)

    hm, qmm, qm = (rim_low[q] for q in range(3))
    hp, qp = (rim_high[q] for q in range(2))
    zm, nm, zp = wide_low[9], wide_low[11], wide_high[8]
    next_m = face(hm + zm, new_0 + z0, zm, z0, nm, qmm, qm, flow_0) * has_low[...]
    next_0 = face(new_0 + z0, new_1 + z1, z0, z1, n0, qm, flow_0, flow_1)
    next_z = face(new_z + zz, hp + zp, zz, zp, nz, flow_y, flow_z, qp) * has_high[...]
    stack[...] = jnp.zeros_like(stack)
    rows[...] = jnp.zeros_like(rows)
    for b in range(BLOCKS):
        for i, value in enumerate((face_m, face_0, face_z, next_m, next_0, next_z)):
            stack[b * 8 + i : b * 8 + i + 1] = value[b : b + 1]
            rows[b, i : i + 1] = value[4 + b : 5 + b]
    turned = stack[...].T
    columns[0] = turned
    for b in range(1, BLOCKS):
        columns[b] = pltpu.roll(turned, HALF - 8 * b, 1)


def inflow_kernel(cells, rates, spill, edge_spill):
    spill[...] = jnp.zeros_like(spill)
    edge_spill[...] = jnp.zeros_like(edge_spill)
    lane = lanes(1, SIDE)
    for b in range(BLOCKS):

        def point(p, carry, b=b):
            cell = cells[0, b, p]
            row = lax.div(cell, SIDE)
            column = lax.rem(cell, SIDE)
            rate = GAIN * rates[0, b, p]
            at_column = jnp.where(lane == column, rate, 0.0)
            at_row = jnp.where(lane == row, rate, 0.0)
            line = pl.ds(row, 1)
            spill[b, line] = spill[b, line] + at_column
            for i, place in enumerate((0, 1, SIDE - 1)):
                edge_spill[i, b : b + 1] += jnp.where(column == place, at_row, 0.0)
                edge_spill[i, 4 + b : 5 + b] += jnp.where(row == place, at_column, 0.0)
            return carry

        lax.fori_loop(0, RIVERS, point, 0)


def lay_inflow(cells, rates):
    return pl.pallas_call(
        inflow_kernel,
        out_shape=[shape(BLOCKS, SIDE, SIDE), shape(3, 8, SIDE)],
        in_specs=[SMEM, SMEM],
        out_specs=[VMEM] * 2,
        compiler_params=params(4),
        cost_estimate=cost(0, 0),
    )(cells, rates)


def block_step(now, ground, spill, columns, rows, base, wetness, write):
    lane = lanes(ROWS, SIDE)
    sub = lax.broadcasted_iota(jnp.int32, (ROWS, SIDE), 0)

    def at(load, field, first, shift):
        if 0 <= first + shift <= SIDE - ROWS:
            return load(field, first + shift)
        return pltpu.roll(load(field, first), -shift % ROWS, 0)

    below = rows(base)
    for first in range(0, SIDE, ROWS):
        h, qx, qy = (at(now, f, first, 0) for f in range(3))
        z, rough = (at(ground, f, first, 0) for f in range(2))
        eta = h + z
        flux_x = face(
            eta, pltpu.roll(eta, SIDE - 1, 1), z, pltpu.roll(z, SIDE - 1, 1), rough,
            pltpu.roll(qx, 1, 1), qx, pltpu.roll(qx, SIDE - 1, 1),
        )
        edge = columns(pl.ds(first, ROWS))
        flux_x = jnp.where(lane == 0, edge[:, base + 1 : base + 2], flux_x)
        flux_x = jnp.where(lane == SIDE - 1, edge[:, base + 2 : base + 3], flux_x)
        flux_w = jnp.where(lane == 0, edge[:, base : base + 1], pltpu.roll(flux_x, 1, 1))
        z_up = at(ground, 0, first, 1)
        flux_y = face(
            eta, at(now, 0, first, 1) + z_up, z, z_up, rough, at(now, 2, first, -1), qy, at(now, 2, first, 1)
        )
        if first == 0:
            flux_y = jnp.where(sub == 0, rows(base + 1), flux_y)
        if first == SIDE - ROWS:
            flux_y = jnp.where(sub == ROWS - 1, rows(base + 2), flux_y)
        flux_s = jnp.where(sub == 0, below, pltpu.roll(flux_y, 1, 0))
        below = flux_y[ROWS - 1 : ROWS]
        depth = h + RATIO * (flux_w - flux_x + flux_s - flux_y) + spill(pl.ds(first, ROWS))
        write(first, depth * wetness, flux_x * wetness, flux_y * wetness)


def block(shifts, dest, wet, terrain, columns, rows, spill, states, out, then, done, sems):
    slot = landing_slot(dest, jnp.where(core() == 0, *shifts))
    wetness = wet[0, slot].astype(F32)
    state = states[0]
    if shifts == W_SHIFTS:
        for here, ref in enumerate(states):

            @pl.when(core() == 1 - here)
            def _(ref=ref):
                copy = pltpu.make_async_copy(ref, done, sems.at[0])
                copy.start()
                copy.wait()

        state = done
    copies = []

    def now(field, first):
        return state[field, first : first + ROWS]

    def ground(field, first):
        return terrain[0, slot, field, first : first + ROWS]

    def keep(first, *fields):
        for f, value in enumerate(fields):
            then[f, first : first + ROWS] = value

    def finish(first, *fields):
        for f, value in enumerate(fields):
            done[f, first : first + ROWS] = value
        lines = pl.ds(first, ROWS)
        copies.append(pltpu.make_async_copy(done.at[:, lines], out.at[0, slot, :, lines], sems.at[len(copies)]))
        copies[-1].start()

    shared = (
        lambda at: spill[slot, at],
        lambda at: columns[slot, at],
        lambda q: rows[slot, q : q + 1],
    )
    block_step(now, ground, *shared, 0, wetness, keep)
    block_step(lambda f, first: then[f, first : first + ROWS], ground, *shared, 3, wetness, finish)
    return copies


EDGE_INPUTS = 19
EDGE_SCRATCH = 10


def block_scratch():
    return [pltpu.VMEM((3, SIDE, SIDE), F32)] * 3 + [pltpu.SemaphoreType.DMA((SIDE // ROWS,))] * 2


def early_kernel(dest, *refs):
    ins, refs = refs[:EDGE_INPUTS], refs[EDGE_INPUTS:]
    terrain, spill, own, arrived_a, arrived_w, relayed, out, columns, rows = refs[:9]
    edge_scratch, (then, done1, done2, sems1, sems2) = refs[9 : 9 + EDGE_SCRATCH], refs[9 + EDGE_SCRATCH :]
    edges_kernel(*ins, columns, rows, *edge_scratch)
    shared = (dest, ins[1], terrain, columns, rows, spill)
    copies = block(OWN_SHIFTS, *shared, (own,), out, then, done1, sems1)
    later = block(A_SHIFTS, *shared, (arrived_a,), out, then, done2, sems2)
    for copy in copies:
        copy.wait()
    later += block(W_SHIFTS, *shared, (arrived_w, relayed), out, then, done1, sems1)
    for copy in later:
        copy.wait()


def early_blocks(dest, edge_inputs, terrain, spill, own, arrived_a, arrived_w, relayed):
    return pl.pallas_call(
        early_kernel,
        out_shape=[shape(1, BLOCKS, 3, SIDE, SIDE), shape(BLOCKS, SIDE, HALF), shape(BLOCKS, 8, SIDE)],
        in_specs=[SMEM] * 3 + [VMEM] * (EDGE_INPUTS - 2 + 4) + [ANY] * 2,
        out_specs=[HBM, VMEM, VMEM],
        scratch_shapes=[
            pltpu.VMEM((16, 8, SIDE), F32),
            pltpu.VMEM((16, 8, SIDE), F32),
            pltpu.VMEM((8, SIDE), F32),
            pltpu.VMEM((8, SIDE), F32),
            pltpu.VMEM((8, SIDE), F32),
            pltpu.VMEM((5, 8, SIDE), F32),
            pltpu.VMEM((3, 8, SIDE), F32),
            pltpu.VMEM((2, 8, SIDE), F32),
            pltpu.VMEM((2, 8, 8, SIDE), F32),
            pltpu.VMEM((HALF, SIDE), F32),
        ]
        + block_scratch(),
        compiler_params=params(16),
        cost_estimate=cost(0, 0),
    )(dest, *edge_inputs, terrain, spill, own, arrived_a, arrived_w, relayed)


def late_kernel(dest, wet, terrain, columns, rows, spill, arrived_x, _, out, then, done, sems):
    shared = (dest, wet, terrain, columns, rows, spill)
    for copy in block(X_SHIFTS, *shared, (arrived_x,), out, then, done, sems):
        copy.wait()


def late_blocks(dest, wet, terrain, columns, rows, spill, arrived_x, out):
    return pl.pallas_call(
        late_kernel,
        out_shape=shape(1, BLOCKS, 3, SIDE, SIDE),
        in_specs=[SMEM] * 2 + [VMEM] * 5 + [HBM],
        out_specs=HBM,
        input_output_aliases={7: 0},
        scratch_shapes=[pltpu.VMEM((3, SIDE, SIDE), F32)] * 2 + [pltpu.SemaphoreType.DMA((SIDE // ROWS,))],
        compiler_params=params(16),
        cost_estimate=cost(0, 0),
    )(dest, wet, terrain, columns, rows, spill, arrived_x, out)


def passed_along(x, axis, by, wrap=True):
    devices = lax.axis_size(axis)
    return lax.ppermute(x, axis, [(i, (i + by) % devices) for i in range(devices)])


def passed_to(x, target):
    devices = lax.axis_size("tile")
    pairs = [(i, target(i // 2, i % 2)) for i in range(devices)]
    return lax.ppermute(x, "tile", [(i, t % devices) for i, t in pairs if t is not None])


def back_one(chip):
    return chip // RING * RING + (chip - 1) % RING


def first_leg(chip, at):
    return 2 * chip + 1 if at == 0 else 2 * back_one(chip)


def second_leg(chip, at):
    sender = chip // RING * RING + (chip + 1) % RING
    return 2 * (sender + 2) if at == 0 else None


def next_chip_swapped(chip, at):
    return 2 * (chip + 1) + 1 - at


def body(flood_state, terrain, destination, wet_mask, neighbours, inflow_cells, inflow_rates):
    dest, state = in_hbm(destination), in_hbm(flood_state)
    block_a, block_w = pick_early(dest, state)
    arrived_a = passed_along(block_a, "tile", 2)
    arrived_w = passed_to(block_w, first_leg)
    own, block_x, ground_low, ground_high, *packs = prepare(
        dest, in_hbm(neighbours), state, block_a, block_w,
        in_hbm(terrain), in_hbm(inflow_cells), in_hbm(inflow_rates),
    )
    ground = (ground_low, ground_high)
    spill, edge_spill = lay_inflow(inflow_cells, inflow_rates)
    packs[5] = passed_along(packs[5], "tile", -1)
    packs[1:3] = [passed_along(packs[d], "tile", d) for d in (1, 2)]
    packs[3], packs[4], arrived_w = gate((packs[3], packs[4], arrived_w), (packs[5], edge_spill))
    packs[3:5] = [passed_along(packs[d], "tile", d) for d in (3, 4)]
    block_x, arrived_w = gate((block_x, arrived_w), (*packs[1:5], arrived_a))
    arrived_x = passed_to(block_x, next_chip_swapped)
    relayed = passed_to(arrived_w, second_leg)
    low, high, wide_low, wide_high, has_low, has_high, far_east, far_west, to_south, to_north = arrange(
        destination, neighbours, packs, ground, edge_spill
    )
    from_north = passed_along(to_south, "grp", -1)
    from_south = passed_along(to_north, "grp", 1)
    edge_inputs = (
        neighbours, wet_mask, edge_spill, low, high, *ground, wide_low, wide_high, has_low, has_high,
        far_east, far_west, packs[1], packs[5], to_south, to_north, from_north, from_south,
    )
    out, columns, rows = early_blocks(
        destination, edge_inputs, terrain, spill, own, arrived_a, arrived_w, relayed
    )
    return late_blocks(destination, wet_mask, terrain, columns, rows, spill, arrived_x, out)


def solution(mesh):
    in_specs = (
        P("grp", "tile", None, None, None),
        P("grp", "tile", None, None, None),
        P("grp", None),
        P("grp", "tile"),
        P("grp", "tile", None),
        P("grp", "tile", None),
        P("grp", "tile", None),
    )
    out_specs = P("grp", "tile", None, None, None)
    return jax.shard_map(body, mesh=mesh, in_specs=in_specs, out_specs=out_specs, check_vma=False)
```

```python
import functools

import jax
import jax.numpy as jnp
from jax import lax
from jax.experimental import pallas as pl
from jax.experimental.pallas import tpu as pltpu
from jax.sharding import PartitionSpec as P

F32 = jnp.float32
GRAVITY = 9.81
SPACING = 10.0
TIMESTEP = 0.2
CENTRE_WEIGHT = 0.7
DEPTH_FLOOR = 0.1
SIDE = 256
HALF = 128
BLOCKS = 4
RIVERS = 16
ROWS = 64
GAIN = TIMESTEP / (SPACING * SPACING)
RATIO = TIMESTEP / SPACING

ANY = pl.BlockSpec(memory_space=pl.ANY)
VMEM = pl.BlockSpec(memory_space=pltpu.VMEM)
SMEM = pl.BlockSpec(memory_space=pltpu.SMEM)
HBM = pl.BlockSpec(memory_space=pltpu.HBM)
RING = 4
OWN_SHIFTS = (0, 0)
A_SHIFTS = (2, 2)
W_SHIFTS = (3, 1)
X_SHIFTS = (1, 3)


def shape(*dims):
    return jax.ShapeDtypeStruct(dims, F32)


def cost(flops, bytes_accessed):
    return pl.CostEstimate(flops=flops, bytes_accessed=bytes_accessed, transcendentals=0)


def face(eta_l, eta_r, z_l, z_r, rough, flow_left, flow_mid, flow_right):
    depth = jnp.maximum(eta_l, eta_r) - jnp.maximum(z_l, z_r)
    floored = jnp.maximum(depth, DEPTH_FLOOR)
    blended = CENTRE_WEIGHT * flow_mid + 0.5 * (1.0 - CENTRE_WEIGHT) * (flow_left + flow_right)
    slope = (GRAVITY * TIMESTEP / SPACING) * depth * (eta_r - eta_l)
    friction = 1.0 + (GRAVITY * TIMESTEP) * rough * rough * jnp.abs(flow_mid) * jnp.exp(
        (-7.0 / 3.0) * jnp.log(floored)
    )
    return (blended - slope) / friction


def core():
    return lax.rem(lax.axis_index("tile"), 2)


def params(mib):
    return pltpu.CompilerParams(vmem_limit_bytes=mib << 20)


def tile_offset(dest_ref, tile, slot):
    tiles = lax.axis_size("tile")
    return lax.rem(lax.div(dest_ref[0, tile * BLOCKS + slot], BLOCKS) - tile + tiles, tiles)


def leaving_slot(dest_ref, shift):
    me = lax.axis_index("tile")
    slot = jnp.int32(0)
    for j in range(1, BLOCKS):
        slot = jnp.where(tile_offset(dest_ref, me, j) == shift, j, slot)
    return slot


def landing_slot(dest_ref, shift, back=0):
    tiles = lax.axis_size("tile")
    sender = lax.rem(lax.axis_index("tile") - shift - back + 2 * tiles, tiles)
    slot = jnp.int32(0)
    for j in range(BLOCKS):
        place = lax.rem(dest_ref[0, sender * BLOCKS + j], BLOCKS)
        slot = jnp.where(tile_offset(dest_ref, sender, j) == shift, place, slot)
    return slot


def lanes(rows, columns):
    return lax.broadcasted_iota(jnp.int32, (rows, columns), 1)


def in_hbm(x):
    return pltpu.with_memory_space_constraint(x, pltpu.HBM)


def pick_kernel(dest, state, block_a, block_w, sems):
    slots = [leaving_slot(dest, k) for k in range(1, BLOCKS)]
    slot_w = jnp.where(core() == 0, slots[0], slots[2])
    loads = [
        pltpu.make_async_copy(state.at[0, slot], ref, sems.at[i])
        for i, (slot, ref) in enumerate(((slots[1], block_a), (slot_w, block_w)))
    ]
    for load in loads:
        load.start()
    for load in loads:
        load.wait()


def pick_early(dest, state):
    return pl.pallas_call(
        pick_kernel,
        out_shape=[shape(3, SIDE, SIDE)] * 2,
        in_specs=[SMEM, HBM],
        out_specs=[VMEM] * 2,
        scratch_shapes=[pltpu.SemaphoreType.DMA((2,))],
        compiler_params=params(4),
        cost_estimate=cost(0, 0),
    )(dest, state)


def prepare_kernel(
    dest, entries, state, block_a, block_w, ground_in, cells, rates,
    own, block_x, low, high, pack0, pack1, pack2, pack3, pack4, pack_back, terrain, sems,
):
    slots = [leaving_slot(dest, k) for k in range(BLOCKS)]
    first_core = core() == 0
    slot_x = jnp.where(first_core, slots[3], slots[1])
    held = (block_x, own)
    loads = [pltpu.make_async_copy(ground_in, terrain, sems.at[3])]
    for i, (slot, ref) in enumerate(zip((slot_x, slots[0]), held)):
        loads.append(pltpu.make_async_copy(state.at[0, slot], ref, sems.at[i]))
    for load in loads:
        load.start()
    lane = lanes(SIDE, HALF)

    def strips(ref, write):
        west = [ref[f, :, :HALF] for f in range(3)]
        east = [ref[f, :, HALF:] for f in range(3)]
        packed = jnp.where(lane < 3, west[0], pltpu.roll(west[1], 3, 1))
        packed = jnp.where(lane < 6, packed, pltpu.roll(west[2], 6, 1))
        packed = jnp.where(lane < 8, packed, pltpu.roll(east[0], 10, 1))
        packed = jnp.where(lane < 10, packed, pltpu.roll(east[1], 13, 1))
        packed = jnp.where(lane < 13, packed, pltpu.roll(east[2], 14, 1))
        turned = packed.T
        south = jnp.concatenate([ref[0, 0:3], ref[2, 0:3], ref[1, 0:2]])
        north = jnp.concatenate(
            [ref[0, SIDE - 2 : SIDE], ref[2, SIDE - 3 : SIDE], ref[1, SIDE - 1 : SIDE], jnp.zeros((2, SIDE), F32)]
        )
        write(turned[0:8], south, turned[8:16], north)

    strip_out = (pack0, pack1, pack2, pack3)
    west_out = (pack_back.at[0], pack0.at[4], pack1.at[5], pack2.at[5])
    east_out = (pack1.at[4], pack2.at[4], pack3.at[4], pack4.at[0])

    def write(k, west, south, east, north):
        for i, value in enumerate((west, south, east, north)):
            strip_out[k][i] = value
        east_out[k][...] = east
        west_out[k][...] = west

    def write_by_core(first, second):
        def both(*values):
            pl.when(first_core)(lambda: write(first, *values))
            pl.when(jnp.logical_not(first_core))(lambda: write(second, *values))

        return both

    strips(block_a, functools.partial(write, 2))
    strips(block_w, write_by_core(1, 3))
    along = lanes(BLOCKS, SIDE)
    spills = [jnp.zeros((BLOCKS, SIDE), F32) for _ in range(2)]
    for p in range(RIVERS):
        cell = cells[0, :, p : p + 1] - along * SIDE
        rate = GAIN * rates[0, :, p : p + 1]
        for i, place in enumerate((0, SIDE - 1)):
            spills[i] = spills[i] + jnp.where(cell == place, rate, 0.0)
    loads[0].wait()
    for b in range(BLOCKS):
        west = [terrain[0, b, f, :, :HALF] for f in range(2)]
        east = [terrain[0, b, f, :, HALF:] for f in range(2)]
        packed = jnp.where(lane < 3, west[0], pltpu.roll(west[1], 3, 1))
        packed = jnp.where(lane < 5, packed, pltpu.roll(east[0], 7, 1))
        packed = jnp.where(lane < 7, packed, pltpu.roll(east[1], 9, 1))
        turned = packed.T
        for q in range(5):
            low[q, b : b + 1] = turned[q : q + 1]
        for q in range(4):
            high[q, b : b + 1] = turned[5 + q : 6 + q]
        for q in range(3):
            low[q, 4 + b : 5 + b] = terrain[0, b, 0, q : q + 1]
        for q in range(2):
            low[3 + q, 4 + b : 5 + b] = terrain[0, b, 1, q : q + 1]
            high[q, 4 + b : 5 + b] = terrain[0, b, 0, SIDE - 2 + q : SIDE - 1 + q]
            high[2 + q, 4 + b : 5 + b] = terrain[0, b, 1, SIDE - 2 + q : SIDE - 1 + q]
    for b in range(BLOCKS):
        line = slice(b, b + 1)
        links = [jnp.full((1, SIDE), entries[0, b, side].astype(F32), F32) for side in (2, 3)]
        blank = [jnp.zeros((1, SIDE), F32)]
        pack1[6 + b] = jnp.concatenate([high[q, line] for q in range(4)] + [spills[1][line]] + links + blank)
        pack_back[1 + b] = jnp.concatenate(
            [low[0, line], low[1, line], low[3, line], spills[0][line]] + links + blank * 2
        )
    writers = (write_by_core(3, 1), functools.partial(write, 0))
    for load, ref, write_out in zip(loads[1:], held, writers):
        load.wait()
        strips(ref, write_out)


def prepare(dest, entries, state, block_a, block_w, terrain, cells, rates):
    packs = [shape(count, 8, SIDE) for count in (5, 10, 6, 5, 1, 5)]
    return pl.pallas_call(
        prepare_kernel,
        out_shape=[shape(3, SIDE, SIDE)] * 2 + [shape(5, 8, SIDE), shape(4, 8, SIDE)] + packs,
        in_specs=[SMEM, SMEM, HBM, VMEM, VMEM, HBM, VMEM, VMEM],
        out_specs=[VMEM] * 10,
        scratch_shapes=[
            pltpu.VMEM((1, BLOCKS, 2, SIDE, SIDE), F32),
            pltpu.SemaphoreType.DMA((BLOCKS,)),
        ],
        compiler_params=params(12),
        cost_estimate=cost(0, 0),
    )(dest, entries, state, block_a, block_w, terrain, cells, rates)


def gate_kernel(count, *refs):
    del count, refs


def gate(values, keys):
    count = len(values)
    return pl.pallas_call(
        functools.partial(gate_kernel, count),
        out_shape=[jax.ShapeDtypeStruct(v.shape, v.dtype) for v in values],
        in_specs=[ANY] * (count + len(keys)),
        out_specs=[ANY] * count,
        input_output_aliases={i: i for i in range(count)},
        compiler_params=params(1),
        cost_estimate=cost(0, 0),
    )(*values, *keys)


def sides_swapped(x):
    return pltpu.roll(x, 4, 0)


def column(x, at):
    return x[:, at : at + 1]


def put_rim(entry, sub, near_state, near_fixed, far_state, far_fixed, wide, has):
    near = jnp.clip(entry, 0, BLOCKS - 1)
    far = jnp.clip(entry - BLOCKS, 0, BLOCKS - 1)
    alive = entry >= 0
    for i, (close, distant) in enumerate(((near_state, far_state), (near_fixed, far_fixed))):
        rows = jnp.where(entry >= BLOCKS, distant(far), close(near))
        rows = jnp.where(alive, rows, 0.0)
        for q in range(8):
            wide[8 * i + q, sub : sub + 1] = rows[q : q + 1]
    has[sub : sub + 1] = jnp.full((1, SIDE), jnp.where(alive, 1.0, 0.0), F32)


def faces_low(low, ground_low, wide):
    h0, h1, h2, q0, q1, q2 = (low[q] for q in range(6))
    z0, z1, z2, n0, n1 = (ground_low[q] for q in range(5))
    hm, qmm, qm, zm, nm = (wide[q] for q in (1, 3, 4, 9, 11))
    return (
        face(hm + zm, h0 + z0, zm, z0, nm, qmm, qm, q0),
        face(h0 + z0, h1 + z1, z0, z1, n0, qm, q0, q1),
        face(h1 + z1, h2 + z2, z1, z2, n1, q0, q1, q2),
    )


def faces_high(high, ground_high, wide):
    hy, hz, qx, qy, qz = (high[q] for q in range(5))
    zy, zz, ny, nz = (ground_high[q] for q in range(4))
    hp, qp, zp = (wide[q] for q in (0, 3, 8))
    return (
        face(hy + zy, hz + zz, zy, zz, ny, qx, qy, qz),
        face(hz + zz, hp + zp, zz, zp, nz, qy, qz, qp),
    )


def arrange_kernel(
    dest, entries, pack0, pack1, pack2, pack3, pack4, pack_back, ground_low, ground_high, edge_spill, _key, _,
    _relay, low, high, wide_low, wide_high, has_low, has_high, far_east, far_west, to_south, to_north,
    west, east,
):
    for out in (low, high, wide_low, wide_high, has_low, has_high):
        out[...] = jnp.zeros_like(out)
    strips = (pack0, pack1, pack2, pack3)
    west_in = (pack_back.at[0], pack0.at[4], pack1.at[5], pack2.at[5])
    east_in = (pack1.at[4], pack2.at[4], pack3.at[4], pack4.at[0])
    for k in range(BLOCKS):
        strip = strips[k]
        slot = landing_slot(dest, k)
        for side in range(2):
            row = pl.ds(side * 4 + slot, 1)
            for q in range(8):
                low[q, row] = strip[side, q : q + 1]
            for q in range(6):
                high[q, row] = strip[2 + side, q : q + 1]
        for i, out in enumerate((west, to_south, east, to_north)):
            out[slot] = strip[i]
        slot = landing_slot(dest, k, 1)
        far_east[slot] = east_in[k][...]
        slot = landing_slot(dest, k, -1)
        far_west[slot] = west_in[k][...]

    def fixed_low(slot):
        row = pl.ds(slot, 1)
        rows = [ground_low[0, row], ground_low[1, row], ground_low[3, row]]
        return jnp.concatenate(rows + [jnp.zeros((5, SIDE), F32)])

    def fixed_high(slot):
        row = pl.ds(slot, 1)
        return jnp.concatenate([ground_high[q, row] for q in range(4)] + [jnp.zeros((4, SIDE), F32)])

    for b in range(BLOCKS):
        put_rim(
            entries[0, b, 0], b, lambda s: east[s], fixed_high,
            lambda s: far_east[s], lambda s: pack1[6 + s], wide_low, has_low,
        )
        put_rim(
            entries[0, b, 1], b, lambda s: west[s], fixed_low,
            lambda s: far_west[s], lambda s: pack_back[1 + s], wide_high, has_high,
        )
    face_m, face_0, _ = faces_low(low, ground_low, wide_low)
    _, face_z = faces_high(high, ground_high, wide_high)
    face_m = face_m * has_low[...]
    face_z = face_z * has_high[...]
    for b in range(BLOCKS):
        sub = slice(4 + b, 5 + b)
        beside = [f[b : b + 1] for f in (face_m, face_0, face_z)]
        blank = [jnp.zeros((1, SIDE), F32)]
        to_north[4 + b] = jnp.concatenate([ground_high[q, sub] for q in range(4)] + [edge_spill[2, sub]] + beside)
        to_south[4 + b] = jnp.concatenate(
            [ground_low[0, sub], ground_low[1, sub], ground_low[3, sub], edge_spill[0, sub]] + beside + blank
        )
        passed = jnp.concatenate(
            [
                far_east[b, 1:2], far_east[b, 5:6], pack1[6 + b, 1:2], pack1[6 + b, 3:4],
                far_west[b, 0:1], far_west[b, 6:7], pack_back[1 + b, 0:1], pack_back[1 + b, 2:3],
            ]
        )
        to_north[8 + b] = passed
        to_south[8 + b] = passed


def arrange(dest, entries, packs, ground, edge_spill, key, relay):
    outs = [(8, 8), (6, 8), (16, 8), (16, 8), (8,), (8,), (BLOCKS, 8), (BLOCKS, 8), (3 * BLOCKS, 8), (3 * BLOCKS, 8)]
    return pl.pallas_call(
        arrange_kernel,
        out_shape=[shape(3, SIDE, SIDE)] + [shape(*dims, SIDE) for dims in outs],
        in_specs=[SMEM] * 2 + [VMEM] * 9 + [ANY] * 2,
        out_specs=[ANY] + [VMEM] * len(outs),
        input_output_aliases={12: 0},
        scratch_shapes=[pltpu.VMEM((BLOCKS, 8, SIDE), F32)] * 2,
        compiler_params=params(4),
        cost_estimate=cost(0, 0),
    )(dest, entries, *packs, *ground, edge_spill, key, relay)


def along_edge(h, z, rough, flow, face_before, face_first, face_last):
    lane = lanes(8, SIDE)
    eta = h + z
    flux = face(
        eta, pltpu.roll(eta, SIDE - 1, 1), z, pltpu.roll(z, SIDE - 1, 1), rough,
        pltpu.roll(flow, 1, 1), flow, pltpu.roll(flow, SIDE - 1, 1),
    )
    flux = jnp.where(lane == 0, face_first, flux)
    flux = jnp.where(lane == SIDE - 1, face_last, flux)
    lower = jnp.where(lane == 0, face_before, pltpu.roll(flux, 1, 1))
    return lower - flux


def corner_faces(h, z, rough, flow, entry_s, entry_n, corners_s, corners_n):
    def chosen(entry, corners, q):
        value = jnp.zeros((8, SIDE), F32)
        for j in range(2 * BLOCKS):
            value = jnp.where(entry == j, corners[q][j : j + 1], value)
        return value

    h_s, t_s, z_s, n_s = (chosen(entry_s, corners_s, q) for q in range(4))
    h_n, t_n, z_n = (chosen(entry_n, corners_n, q) for q in range(3))
    last = SIDE - 1
    has_s = jnp.where(column(entry_s, 0) >= 0.0, 1.0, 0.0)
    has_n = jnp.where(column(entry_n, 0) >= 0.0, 1.0, 0.0)
    eta, eta_s, eta_n = h + z, h_s + z_s, h_n + z_n
    before = face(
        column(eta_s, last), column(eta, 0), column(z_s, last), column(z, 0), column(n_s, last),
        column(t_s, last - 1), column(t_s, last), column(flow, 0),
    ) * has_s
    first = face(
        column(eta, 0), column(eta, 1), column(z, 0), column(z, 1), column(rough, 0),
        column(t_s, last), column(flow, 0), column(flow, 1),
    )
    final = face(
        column(eta, last), column(eta_n, 0), column(z, last), column(z_n, 0), column(rough, last),
        column(flow, last - 1), column(flow, last), column(t_n, 0),
    ) * has_n
    return before, first, final


def edges_kernel(
    entries, wet, edge_spill, low, high, ground_low, ground_high, wide_low_in, wide_high_in, has_low_in, has_high_in,
    far_east, far_west, pack1, pack_back, to_south, to_north, from_north, from_south,
    columns, rows,
    wide_low, wide_high, has_low, has_high, wetness, edge, rim_low, rim_high, corners, stack,
):
    wide_low[...] = wide_low_in[...]
    wide_high[...] = wide_high_in[...]
    has_low[...] = has_low_in[...]
    has_high[...] = has_high_in[...]
    for b in range(BLOCKS):
        value = jnp.full((1, SIDE), wet[0, b].astype(F32), F32)
        wetness[b : b + 1] = value
        wetness[4 + b : 5 + b] = value
        for entry, near, far, wide, has in (
            (entries[0, b, 2], to_north, from_south, wide_low, has_low),
            (entries[0, b, 3], to_south, from_north, wide_high, has_high),
        ):
            put_rim(
                entry, 4 + b, lambda s, r=near: r[s], lambda s, r=near: r[BLOCKS + s],
                lambda s, r=far: r[s], lambda s, r=far: r[BLOCKS + s], wide, has,
            )
    for j in range(BLOCKS):
        near = slice(j, j + 1)
        far = slice(BLOCKS + j, BLOCKS + j + 1)
        for q, row in enumerate(
            (
                far_east[j, 1:2], far_east[j, 5:6], pack1[6 + j, 1:2], pack1[6 + j, 3:4],
                far_west[j, 0:1], far_west[j, 6:7], pack_back[1 + j, 0:1], pack_back[1 + j, 2:3],
            )
        ):
            for i, passed in enumerate((from_south, from_north)):
                corners[i, q, near] = row
                corners[i, q, far] = passed[2 * BLOCKS + j, q : q + 1]

    def seen(i, first):
        return [corners[i, first + q] for q in range(4)]

    h0, h1, h2, q0, q1, q2, t0, t1 = (low[q] for q in range(8))
    z0, z1, z2, n0, n1 = (ground_low[q] for q in range(5))
    hy, hz, qx, qy, qz, tz = (high[q] for q in range(6))
    zy, zz, ny, nz = (ground_high[q] for q in range(4))
    face_m, face_0, face_1 = faces_low(low, ground_low, wide_low)
    face_y, face_z = faces_high(high, ground_high, wide_high)
    face_m = face_m * has_low[...]
    face_z = face_z * has_high[...]
    swapped = [sides_swapped(f) for f in (face_m, face_0, face_z)]

    def beside(spot):
        return [column(f, spot) for f in swapped]

    wets = wetness[...]
    last = SIDE - 1
    new_0 = (h0 + RATIO * (face_m - face_0 + along_edge(h0, z0, n0, t0, *beside(0))) + edge_spill[0]) * wets
    new_1 = (h1 + RATIO * (face_0 - face_1 + along_edge(h1, z1, n1, t1, *beside(1))) + edge_spill[1]) * wets
    new_z = (hz + RATIO * (face_y - face_z + along_edge(hz, zz, nz, tz, *beside(last))) + edge_spill[2]) * wets
    flow_0, flow_1, flow_y, flow_z = (f * wets for f in (face_0, face_1, face_y, face_z))
    for i, value in enumerate((new_z, flow_y, flow_z, new_0, flow_0)):
        edge[i] = value

    sides = lax.broadcasted_iota(jnp.int32, (8, 1), 0) < 4
    ghy, ghz, gqx, gqy, gqz, gtz = (wide_low[q] for q in range(6))
    gzy, gzz, gny, gnz, gspill = (wide_low[8 + q] for q in range(5))
    across = corner_faces(ghz, gzz, gnz, gtz, wide_low[13], wide_low[14], seen(0, 0), seen(1, 0))
    given = [column(wide_low[13 + q], last) for q in range(3)]
    ends = [jnp.where(sides, a, g) for a, g in zip(across, given)]
    far_face = face(ghy + gzy, ghz + gzz, gzy, gzz, gny, gqx, gqy, gqz)
    far_low = (
        ghz + RATIO * (far_face - face_m + along_edge(ghz, gzz, gnz, gtz, *ends)) + gspill,
        far_face,
        face_m,
    )
    gh0, gh1, gq0, gq1, gt0 = (wide_high[q] for q in (0, 1, 3, 4, 6))
    gz0, gz1, gn0, gspill = (wide_high[8 + q] for q in range(4))
    across = corner_faces(gh0, gz0, gn0, gt0, wide_high[12], wide_high[13], seen(0, 4), seen(1, 4))
    given = [column(wide_high[12 + q], 0) for q in range(3)]
    ends = [jnp.where(sides, a, g) for a, g in zip(across, given)]
    far_face = face(gh0 + gz0, gh1 + gz1, gz0, gz1, gn0, qz, gq0, gq1)
    far_high = (
        gh0 + RATIO * (face_z - far_face + along_edge(gh0, gz0, gn0, gt0, *ends)) + gspill,
        far_face,
    )
    for rim, far_rows, first, group in ((rim_low, far_low, 0, 0), (rim_high, far_high, 3, 1)):
        for q, far_row in enumerate(far_rows):
            rim[q] = far_row
        for b in range(BLOCKS):
            for side in range(2):
                entry = entries[0, b, 2 * side + group]
                sub = slice(side * 4 + b, side * 4 + b + 1)
                near = pl.ds(side * 4 + jnp.clip(entry, 0, BLOCKS - 1), 1)
                for q in range(len(far_rows)):
                    row = jnp.where(entry >= BLOCKS, rim[q, sub], edge[first + q, near])
                    rim[q, sub] = jnp.where(entry >= 0, row, 0.0)

    hm, qmm, qm = (rim_low[q] for q in range(3))
    hp, qp = (rim_high[q] for q in range(2))
    zm, nm, zp = wide_low[9], wide_low[11], wide_high[8]
    next_m = face(hm + zm, new_0 + z0, zm, z0, nm, qmm, qm, flow_0) * has_low[...]
    next_0 = face(new_0 + z0, new_1 + z1, z0, z1, n0, qm, flow_0, flow_1)
    next_z = face(new_z + zz, hp + zp, zz, zp, nz, flow_y, flow_z, qp) * has_high[...]
    stack[...] = jnp.zeros_like(stack)
    rows[...] = jnp.zeros_like(rows)
    for b in range(BLOCKS):
        for i, value in enumerate((face_m, face_0, face_z, next_m, next_0, next_z)):
            stack[b * 8 + i : b * 8 + i + 1] = value[b : b + 1]
            rows[b, i : i + 1] = value[4 + b : 5 + b]
    turned = stack[...].T
    columns[0] = turned
    for b in range(1, BLOCKS):
        columns[b] = pltpu.roll(turned, HALF - 8 * b, 1)


def inflow_kernel(cells, rates, spill, edge_spill):
    spill[...] = jnp.zeros_like(spill)
    edge_spill[...] = jnp.zeros_like(edge_spill)
    lane = lanes(1, SIDE)
    for b in range(BLOCKS):

        def point(p, carry, b=b):
            cell = cells[0, b, p]
            row = lax.div(cell, SIDE)
            column = lax.rem(cell, SIDE)
            rate = GAIN * rates[0, b, p]
            at_column = jnp.where(lane == column, rate, 0.0)
            at_row = jnp.where(lane == row, rate, 0.0)
            line = pl.ds(row, 1)
            spill[b, line] = spill[b, line] + at_column
            for i, place in enumerate((0, 1, SIDE - 1)):
                edge_spill[i, b : b + 1] += jnp.where(column == place, at_row, 0.0)
                edge_spill[i, 4 + b : 5 + b] += jnp.where(row == place, at_column, 0.0)
            return carry

        lax.fori_loop(0, RIVERS, point, 0)


def lay_inflow(cells, rates):
    return pl.pallas_call(
        inflow_kernel,
        out_shape=[shape(BLOCKS, SIDE, SIDE), shape(3, 8, SIDE)],
        in_specs=[SMEM, SMEM],
        out_specs=[VMEM] * 2,
        compiler_params=params(4),
        cost_estimate=cost(0, 0),
    )(cells, rates)


def block_step(now, ground, spill, columns, rows, base, wetness, write):
    lane = lanes(ROWS, SIDE)
    sub = lax.broadcasted_iota(jnp.int32, (ROWS, SIDE), 0)

    def at(load, field, first, shift):
        if 0 <= first + shift <= SIDE - ROWS:
            return load(field, first + shift)
        return pltpu.roll(load(field, first), -shift % ROWS, 0)

    below = rows(base)
    for first in range(0, SIDE, ROWS):
        h, qx, qy = (at(now, f, first, 0) for f in range(3))
        z, rough = (at(ground, f, first, 0) for f in range(2))
        eta = h + z
        flux_x = face(
            eta, pltpu.roll(eta, SIDE - 1, 1), z, pltpu.roll(z, SIDE - 1, 1), rough,
            pltpu.roll(qx, 1, 1), qx, pltpu.roll(qx, SIDE - 1, 1),
        )
        edge = columns(pl.ds(first, ROWS))
        flux_x = jnp.where(lane == 0, edge[:, base + 1 : base + 2], flux_x)
        flux_x = jnp.where(lane == SIDE - 1, edge[:, base + 2 : base + 3], flux_x)
        flux_w = jnp.where(lane == 0, edge[:, base : base + 1], pltpu.roll(flux_x, 1, 1))
        z_up = at(ground, 0, first, 1)
        flux_y = face(
            eta, at(now, 0, first, 1) + z_up, z, z_up, rough, at(now, 2, first, -1), qy, at(now, 2, first, 1)
        )
        if first == 0:
            flux_y = jnp.where(sub == 0, rows(base + 1), flux_y)
        if first == SIDE - ROWS:
            flux_y = jnp.where(sub == ROWS - 1, rows(base + 2), flux_y)
        flux_s = jnp.where(sub == 0, below, pltpu.roll(flux_y, 1, 0))
        below = flux_y[ROWS - 1 : ROWS]
        depth = h + RATIO * (flux_w - flux_x + flux_s - flux_y) + spill(pl.ds(first, ROWS))
        write(first, depth * wetness, flux_x * wetness, flux_y * wetness)


def block(shifts, dest, wet, terrain, columns, rows, spill, states, out, then, done, sems):
    slot = landing_slot(dest, jnp.where(core() == 0, *shifts))
    wetness = wet[0, slot].astype(F32)
    state = states[0]
    if shifts == W_SHIFTS:
        for here, ref in enumerate(states):

            @pl.when(core() == 1 - here)
            def _(ref=ref):
                copy = pltpu.make_async_copy(ref, done, sems.at[0])
                copy.start()
                copy.wait()

        state = done
    copies = []

    def now(field, first):
        return state[field, first : first + ROWS]

    def ground(field, first):
        return terrain[0, slot, field, first : first + ROWS]

    def keep(first, *fields):
        for f, value in enumerate(fields):
            then[f, first : first + ROWS] = value

    def finish(first, *fields):
        for f, value in enumerate(fields):
            done[f, first : first + ROWS] = value
        lines = pl.ds(first, ROWS)
        copies.append(pltpu.make_async_copy(done.at[:, lines], out.at[0, slot, :, lines], sems.at[len(copies)]))
        copies[-1].start()

    shared = (
        lambda at: spill[slot, at],
        lambda at: columns[slot, at],
        lambda q: rows[slot, q : q + 1],
    )
    block_step(now, ground, *shared, 0, wetness, keep)
    block_step(lambda f, first: then[f, first : first + ROWS], ground, *shared, 3, wetness, finish)
    return copies


EDGE_INPUTS = 19
EDGE_SCRATCH = 10


def block_scratch():
    return [pltpu.VMEM((3, SIDE, SIDE), F32)] * 3 + [pltpu.SemaphoreType.DMA((SIDE // ROWS,))] * 2


def blocks_kernel(dest, *refs):
    ins, refs = refs[:EDGE_INPUTS], refs[EDGE_INPUTS:]
    terrain, spill, own, arrived_a, arrived_x, arrived_w, relayed, out = refs[:8]
    edge_scratch, (columns, rows, then, done1, done2, sems1, sems2) = refs[8 : 8 + EDGE_SCRATCH], refs[8 + EDGE_SCRATCH :]
    edges_kernel(*ins, columns, rows, *edge_scratch)
    shared = (dest, ins[1], terrain, columns, rows, spill)
    copies = block(OWN_SHIFTS, *shared, (own,), out, then, done1, sems1)
    later = block(A_SHIFTS, *shared, (arrived_a,), out, then, done2, sems2)
    for copy in copies:
        copy.wait()
    copies = block(W_SHIFTS, *shared, (arrived_w, relayed), out, then, done1, sems1)
    for copy in later:
        copy.wait()
    copies += block(X_SHIFTS, *shared, (arrived_x,), out, then, done2, sems2)
    for copy in copies:
        copy.wait()


def all_blocks(dest, edge_inputs, terrain, spill, own, arrived_a, arrived_x, arrived_w, relayed):
    return pl.pallas_call(
        blocks_kernel,
        out_shape=shape(1, BLOCKS, 3, SIDE, SIDE),
        in_specs=[SMEM] * 3 + [VMEM] * (EDGE_INPUTS - 2 + 5) + [ANY] * 2,
        out_specs=HBM,
        scratch_shapes=[
            pltpu.VMEM((16, 8, SIDE), F32),
            pltpu.VMEM((16, 8, SIDE), F32),
            pltpu.VMEM((8, SIDE), F32),
            pltpu.VMEM((8, SIDE), F32),
            pltpu.VMEM((8, SIDE), F32),
            pltpu.VMEM((5, 8, SIDE), F32),
            pltpu.VMEM((3, 8, SIDE), F32),
            pltpu.VMEM((2, 8, SIDE), F32),
            pltpu.VMEM((2, 8, 8, SIDE), F32),
            pltpu.VMEM((HALF, SIDE), F32),
            pltpu.VMEM((BLOCKS, SIDE, HALF), F32),
            pltpu.VMEM((BLOCKS, 8, SIDE), F32),
        ]
        + block_scratch(),
        compiler_params=params(16),
        cost_estimate=cost(0, 0),
    )(dest, *edge_inputs, terrain, spill, own, arrived_a, arrived_x, arrived_w, relayed)


def passed_along(x, axis, by, wrap=True):
    devices = lax.axis_size(axis)
    return lax.ppermute(x, axis, [(i, (i + by) % devices) for i in range(devices)])


def passed_to(x, target):
    devices = lax.axis_size("tile")
    pairs = [(i, target(i // 2, i % 2)) for i in range(devices)]
    return lax.ppermute(x, "tile", [(i, t % devices) for i, t in pairs if t is not None])


def back_one(chip):
    return chip // RING * RING + (chip - 1) % RING


def first_leg(chip, at):
    return 2 * chip + 1 if at == 0 else 2 * back_one(chip)


def second_leg(chip, at):
    sender = chip // RING * RING + (chip + 1) % RING
    return 2 * (sender + 2) if at == 0 else None


def next_chip_swapped(chip, at):
    return 2 * (chip + 1) + 1 - at


def body(flood_state, terrain, destination, wet_mask, neighbours, inflow_cells, inflow_rates):
    dest, state = in_hbm(destination), in_hbm(flood_state)
    block_a, block_w = pick_early(dest, state)
    arrived_a = passed_along(block_a, "tile", 2)
    arrived_w = passed_to(block_w, first_leg)
    own, block_x, ground_low, ground_high, *packs = prepare(
        dest, in_hbm(neighbours), state, block_a, block_w,
        in_hbm(terrain), in_hbm(inflow_cells), in_hbm(inflow_rates),
    )
    ground = (ground_low, ground_high)
    spill, edge_spill = lay_inflow(inflow_cells, inflow_rates)
    packs[5] = passed_along(packs[5], "tile", -1)
    packs[1:3] = [passed_along(packs[d], "tile", d) for d in (1, 2)]
    packs[3], packs[4], arrived_w = gate((packs[3], packs[4], arrived_w), (packs[5], edge_spill))
    packs[3:5] = [passed_along(packs[d], "tile", d) for d in (3, 4)]
    (block_x,) = gate((block_x,), (arrived_a,))
    arrived_x = passed_to(block_x, next_chip_swapped)
    arrived_w, low, high, wide_low, wide_high, has_low, has_high, far_east, far_west, to_south, to_north = arrange(
        destination, neighbours, packs, ground, edge_spill, arrived_a, arrived_w
    )
    relayed = passed_to(arrived_w, second_leg)
    from_north = passed_along(to_south, "grp", -1)
    from_south = passed_along(to_north, "grp", 1)
    edge_inputs = (
        neighbours, wet_mask, edge_spill, low, high, *ground, wide_low, wide_high, has_low, has_high,
        far_east, far_west, packs[1], packs[5], to_south, to_north, from_north, from_south,
    )
    return all_blocks(
        destination, edge_inputs, terrain, spill, own, arrived_a, arrived_x, arrived_w, relayed
    )


def solution(mesh):
    in_specs = (
        P("grp", "tile", None, None, None),
        P("grp", "tile", None, None, None),
        P("grp", None),
        P("grp", "tile"),
        P("grp", "tile", None),
        P("grp", "tile", None),
        P("grp", "tile", None),
    )
    out_specs = P("grp", "tile", None, None, None)
    return jax.shard_map(body, mesh=mesh, in_specs=in_specs, out_specs=out_specs, check_vma=False)
```

```python
import functools

import jax
import jax.numpy as jnp
from jax import lax
from jax.experimental import pallas as pl
from jax.experimental.pallas import tpu as pltpu
from jax.sharding import PartitionSpec as P

F32 = jnp.float32
GRAVITY = 9.81
SPACING = 10.0
TIMESTEP = 0.2
CENTRE_WEIGHT = 0.7
DEPTH_FLOOR = 0.1
SIDE = 256
HALF = 128
BLOCKS = 4
RIVERS = 16
ROWS = 64
GAIN = TIMESTEP / (SPACING * SPACING)
RATIO = TIMESTEP / SPACING

ANY = pl.BlockSpec(memory_space=pl.ANY)
VMEM = pl.BlockSpec(memory_space=pltpu.VMEM)
SMEM = pl.BlockSpec(memory_space=pltpu.SMEM)
HBM = pl.BlockSpec(memory_space=pltpu.HBM)
RING = 4
OWN_SHIFTS = (0, 0)
A_SHIFTS = (2, 2)
W_SHIFTS = (3, 1)
X_SHIFTS = (1, 3)


def shape(*dims):
    return jax.ShapeDtypeStruct(dims, F32)


def cost(flops, bytes_accessed):
    return pl.CostEstimate(flops=flops, bytes_accessed=bytes_accessed, transcendentals=0)


def face(eta_l, eta_r, z_l, z_r, rough, flow_left, flow_mid, flow_right):
    depth = jnp.maximum(eta_l, eta_r) - jnp.maximum(z_l, z_r)
    floored = jnp.maximum(depth, DEPTH_FLOOR)
    blended = CENTRE_WEIGHT * flow_mid + 0.5 * (1.0 - CENTRE_WEIGHT) * (flow_left + flow_right)
    slope = (GRAVITY * TIMESTEP / SPACING) * depth * (eta_r - eta_l)
    friction = 1.0 + (GRAVITY * TIMESTEP) * rough * rough * jnp.abs(flow_mid) * jnp.exp(
        (-7.0 / 3.0) * jnp.log(floored)
    )
    return (blended - slope) / friction


def core():
    return lax.rem(lax.axis_index("tile"), 2)


def params(mib):
    return pltpu.CompilerParams(vmem_limit_bytes=mib << 20)


def tile_offset(dest_ref, tile, slot):
    tiles = lax.axis_size("tile")
    return lax.rem(lax.div(dest_ref[0, tile * BLOCKS + slot], BLOCKS) - tile + tiles, tiles)


def leaving_slot(dest_ref, shift):
    me = lax.axis_index("tile")
    slot = jnp.int32(0)
    for j in range(1, BLOCKS):
        slot = jnp.where(tile_offset(dest_ref, me, j) == shift, j, slot)
    return slot


def landing_slot(dest_ref, shift, back=0):
    tiles = lax.axis_size("tile")
    sender = lax.rem(lax.axis_index("tile") - shift - back + 2 * tiles, tiles)
    slot = jnp.int32(0)
    for j in range(BLOCKS):
        place = lax.rem(dest_ref[0, sender * BLOCKS + j], BLOCKS)
        slot = jnp.where(tile_offset(dest_ref, sender, j) == shift, place, slot)
    return slot


def lanes(rows, columns):
    return lax.broadcasted_iota(jnp.int32, (rows, columns), 1)


def in_hbm(x):
    return pltpu.with_memory_space_constraint(x, pltpu.HBM)


def pick_kernel(dest, state, block_a, block_w, sems):
    slots = [leaving_slot(dest, k) for k in range(1, BLOCKS)]
    slot_w = jnp.where(core() == 0, slots[0], slots[2])
    loads = [
        pltpu.make_async_copy(state.at[0, slot], ref, sems.at[i])
        for i, (slot, ref) in enumerate(((slots[1], block_a), (slot_w, block_w)))
    ]
    for load in loads:
        load.start()
    for load in loads:
        load.wait()


def pick_early(dest, state):
    return pl.pallas_call(
        pick_kernel,
        out_shape=[shape(3, SIDE, SIDE)] * 2,
        in_specs=[SMEM, HBM],
        out_specs=[VMEM] * 2,
        scratch_shapes=[pltpu.SemaphoreType.DMA((2,))],
        compiler_params=params(4),
        cost_estimate=cost(0, 0),
    )(dest, state)


def prepare_kernel(
    dest, entries, state, block_a, block_w, ground_in, cells, rates,
    own, block_x, low, high, pack0, pack1, pack2, pack3, pack4, pack_back, terrain, sems,
):
    slots = [leaving_slot(dest, k) for k in range(BLOCKS)]
    first_core = core() == 0
    slot_x = jnp.where(first_core, slots[3], slots[1])
    held = (block_x, own)
    loads = [pltpu.make_async_copy(ground_in, terrain, sems.at[3])]
    for i, (slot, ref) in enumerate(zip((slot_x, slots[0]), held)):
        loads.append(pltpu.make_async_copy(state.at[0, slot], ref, sems.at[i]))
    for load in loads:
        load.start()
    lane = lanes(SIDE, HALF)

    def strips(ref, write):
        west = [ref[f, :, :HALF] for f in range(3)]
        east = [ref[f, :, HALF:] for f in range(3)]
        packed = jnp.where(lane < 3, west[0], pltpu.roll(west[1], 3, 1))
        packed = jnp.where(lane < 6, packed, pltpu.roll(west[2], 6, 1))
        packed = jnp.where(lane < 8, packed, pltpu.roll(east[0], 10, 1))
        packed = jnp.where(lane < 10, packed, pltpu.roll(east[1], 13, 1))
        packed = jnp.where(lane < 13, packed, pltpu.roll(east[2], 14, 1))
        turned = packed.T
        south = jnp.concatenate([ref[0, 0:3], ref[2, 0:3], ref[1, 0:2]])
        north = jnp.concatenate(
            [ref[0, SIDE - 2 : SIDE], ref[2, SIDE - 3 : SIDE], ref[1, SIDE - 1 : SIDE], jnp.zeros((2, SIDE), F32)]
        )
        write(turned[0:8], south, turned[8:16], north)

    strip_out = (pack0, pack1, pack2, pack3)
    west_out = (pack_back.at[0], pack0.at[4], pack1.at[5], pack2.at[5])
    east_out = (pack1.at[4], pack2.at[4], pack3.at[4], pack4.at[0])

    def write(k, west, south, east, north):
        for i, value in enumerate((west, south, east, north)):
            strip_out[k][i] = value
        east_out[k][...] = east
        west_out[k][...] = west

    def write_by_core(first, second):
        def both(*values):
            pl.when(first_core)(lambda: write(first, *values))
            pl.when(jnp.logical_not(first_core))(lambda: write(second, *values))

        return both

    strips(block_a, functools.partial(write, 2))
    strips(block_w, write_by_core(1, 3))
    along = lanes(BLOCKS, SIDE)
    spills = [jnp.zeros((BLOCKS, SIDE), F32) for _ in range(2)]
    for p in range(RIVERS):
        cell = cells[0, :, p : p + 1] - along * SIDE
        rate = GAIN * rates[0, :, p : p + 1]
        for i, place in enumerate((0, SIDE - 1)):
            spills[i] = spills[i] + jnp.where(cell == place, rate, 0.0)
    loads[0].wait()
    for b in range(BLOCKS):
        west = [terrain[0, b, f, :, :HALF] for f in range(2)]
        east = [terrain[0, b, f, :, HALF:] for f in range(2)]
        packed = jnp.where(lane < 3, west[0], pltpu.roll(west[1], 3, 1))
        packed = jnp.where(lane < 5, packed, pltpu.roll(east[0], 7, 1))
        packed = jnp.where(lane < 7, packed, pltpu.roll(east[1], 9, 1))
        turned = packed.T
        for q in range(5):
            low[q, b : b + 1] = turned[q : q + 1]
        for q in range(4):
            high[q, b : b + 1] = turned[5 + q : 6 + q]
        for q in range(3):
            low[q, 4 + b : 5 + b] = terrain[0, b, 0, q : q + 1]
        for q in range(2):
            low[3 + q, 4 + b : 5 + b] = terrain[0, b, 1, q : q + 1]
            high[q, 4 + b : 5 + b] = terrain[0, b, 0, SIDE - 2 + q : SIDE - 1 + q]
            high[2 + q, 4 + b : 5 + b] = terrain[0, b, 1, SIDE - 2 + q : SIDE - 1 + q]
    for b in range(BLOCKS):
        line = slice(b, b + 1)
        links = [jnp.full((1, SIDE), entries[0, b, side].astype(F32), F32) for side in (2, 3)]
        blank = [jnp.zeros((1, SIDE), F32)]
        pack1[6 + b] = jnp.concatenate([high[q, line] for q in range(4)] + [spills[1][line]] + links + blank)
        pack_back[1 + b] = jnp.concatenate(
            [low[0, line], low[1, line], low[3, line], spills[0][line]] + links + blank * 2
        )
    writers = (write_by_core(3, 1), functools.partial(write, 0))
    for load, ref, write_out in zip(loads[1:], held, writers):
        load.wait()
        strips(ref, write_out)


def prepare(dest, entries, state, block_a, block_w, terrain, cells, rates):
    packs = [shape(count, 8, SIDE) for count in (5, 10, 6, 5, 1, 5)]
    return pl.pallas_call(
        prepare_kernel,
        out_shape=[shape(3, SIDE, SIDE)] * 2 + [shape(5, 8, SIDE), shape(4, 8, SIDE)] + packs,
        in_specs=[SMEM, SMEM, HBM, VMEM, VMEM, HBM, VMEM, VMEM],
        out_specs=[VMEM] * 10,
        scratch_shapes=[
            pltpu.VMEM((1, BLOCKS, 2, SIDE, SIDE), F32),
            pltpu.SemaphoreType.DMA((BLOCKS,)),
        ],
        compiler_params=params(12),
        cost_estimate=cost(0, 0),
    )(dest, entries, state, block_a, block_w, terrain, cells, rates)


def gate_kernel(count, *refs):
    del count, refs


def gate(values, keys):
    count = len(values)
    return pl.pallas_call(
        functools.partial(gate_kernel, count),
        out_shape=[jax.ShapeDtypeStruct(v.shape, v.dtype) for v in values],
        in_specs=[ANY] * (count + len(keys)),
        out_specs=[ANY] * count,
        input_output_aliases={i: i for i in range(count)},
        compiler_params=params(1),
        cost_estimate=cost(0, 0),
    )(*values, *keys)


def sides_swapped(x):
    return pltpu.roll(x, 4, 0)


def column(x, at):
    return x[:, at : at + 1]


def put_rim(entry, sub, near_state, near_fixed, far_state, far_fixed, wide, has):
    near = jnp.clip(entry, 0, BLOCKS - 1)
    far = jnp.clip(entry - BLOCKS, 0, BLOCKS - 1)
    alive = entry >= 0
    for i, (close, distant) in enumerate(((near_state, far_state), (near_fixed, far_fixed))):
        rows = jnp.where(entry >= BLOCKS, distant(far), close(near))
        rows = jnp.where(alive, rows, 0.0)
        for q in range(8):
            wide[8 * i + q, sub : sub + 1] = rows[q : q + 1]
    has[sub : sub + 1] = jnp.full((1, SIDE), jnp.where(alive, 1.0, 0.0), F32)


def faces_low(low, ground_low, wide):
    h0, h1, h2, q0, q1, q2 = (low[q] for q in range(6))
    z0, z1, z2, n0, n1 = (ground_low[q] for q in range(5))
    hm, qmm, qm, zm, nm = (wide[q] for q in (1, 3, 4, 9, 11))
    return (
        face(hm + zm, h0 + z0, zm, z0, nm, qmm, qm, q0),
        face(h0 + z0, h1 + z1, z0, z1, n0, qm, q0, q1),
        face(h1 + z1, h2 + z2, z1, z2, n1, q0, q1, q2),
    )


def faces_high(high, ground_high, wide):
    hy, hz, qx, qy, qz = (high[q] for q in range(5))
    zy, zz, ny, nz = (ground_high[q] for q in range(4))
    hp, qp, zp = (wide[q] for q in (0, 3, 8))
    return (
        face(hy + zy, hz + zz, zy, zz, ny, qx, qy, qz),
        face(hz + zz, hp + zp, zz, zp, nz, qy, qz, qp),
    )


def arrange_kernel(
    dest, entries, pack0, pack1, pack2, pack3, pack4, pack_back, ground_low, ground_high, edge_spill, _key, _,
    _relay, low, high, wide_low, wide_high, has_low, has_high, far_east, far_west, to_south, to_north,
    west, east,
):
    for out in (low, high, wide_low, wide_high, has_low, has_high):
        out[...] = jnp.zeros_like(out)
    strips = (pack0, pack1, pack2, pack3)
    west_in = (pack_back.at[0], pack0.at[4], pack1.at[5], pack2.at[5])
    east_in = (pack1.at[4], pack2.at[4], pack3.at[4], pack4.at[0])
    for k in range(BLOCKS):
        strip = strips[k]
        slot = landing_slot(dest, k)
        for side in range(2):
            row = pl.ds(side * 4 + slot, 1)
            for q in range(8):
                low[q, row] = strip[side, q : q + 1]
            for q in range(6):
                high[q, row] = strip[2 + side, q : q + 1]
        for i, out in enumerate((west, to_south, east, to_north)):
            out[slot] = strip[i]
        slot = landing_slot(dest, k, 1)
        far_east[slot] = east_in[k][...]
        slot = landing_slot(dest, k, -1)
        far_west[slot] = west_in[k][...]

    def fixed_low(slot):
        row = pl.ds(slot, 1)
        rows = [ground_low[0, row], ground_low[1, row], ground_low[3, row]]
        return jnp.concatenate(rows + [jnp.zeros((5, SIDE), F32)])

    def fixed_high(slot):
        row = pl.ds(slot, 1)
        return jnp.concatenate([ground_high[q, row] for q in range(4)] + [jnp.zeros((4, SIDE), F32)])

    for b in range(BLOCKS):
        put_rim(
            entries[0, b, 0], b, lambda s: east[s], fixed_high,
            lambda s: far_east[s], lambda s: pack1[6 + s], wide_low, has_low,
        )
        put_rim(
            entries[0, b, 1], b, lambda s: west[s], fixed_low,
            lambda s: far_west[s], lambda s: pack_back[1 + s], wide_high, has_high,
        )
    face_m, face_0, _ = faces_low(low, ground_low, wide_low)
    _, face_z = faces_high(high, ground_high, wide_high)
    face_m = face_m * has_low[...]
    face_z = face_z * has_high[...]
    for b in range(BLOCKS):
        sub = slice(4 + b, 5 + b)
        beside = [f[b : b + 1] for f in (face_m, face_0, face_z)]
        blank = [jnp.zeros((1, SIDE), F32)]
        to_north[4 + b] = jnp.concatenate([ground_high[q, sub] for q in range(4)] + [edge_spill[2, sub]] + beside)
        to_south[4 + b] = jnp.concatenate(
            [ground_low[0, sub], ground_low[1, sub], ground_low[3, sub], edge_spill[0, sub]] + beside + blank
        )
        passed = jnp.concatenate(
            [
                far_east[b, 1:2], far_east[b, 5:6], pack1[6 + b, 1:2], pack1[6 + b, 3:4],
                far_west[b, 0:1], far_west[b, 6:7], pack_back[1 + b, 0:1], pack_back[1 + b, 2:3],
            ]
        )
        to_north[8 + b] = passed
        to_south[8 + b] = passed


def arrange(dest, entries, packs, ground, edge_spill, key, relay):
    outs = [(8, 8), (6, 8), (16, 8), (16, 8), (8,), (8,), (BLOCKS, 8), (BLOCKS, 8), (3 * BLOCKS, 8), (3 * BLOCKS, 8)]
    return pl.pallas_call(
        arrange_kernel,
        out_shape=[shape(3, SIDE, SIDE)] + [shape(*dims, SIDE) for dims in outs],
        in_specs=[SMEM] * 2 + [VMEM] * 9 + [ANY] * 2,
        out_specs=[ANY] + [VMEM] * len(outs),
        input_output_aliases={12: 0},
        scratch_shapes=[pltpu.VMEM((BLOCKS, 8, SIDE), F32)] * 2,
        compiler_params=params(4),
        cost_estimate=cost(0, 0),
    )(dest, entries, *packs, *ground, edge_spill, key, relay)


def along_edge(h, z, rough, flow, face_before, face_first, face_last):
    lane = lanes(8, SIDE)
    eta = h + z
    flux = face(
        eta, pltpu.roll(eta, SIDE - 1, 1), z, pltpu.roll(z, SIDE - 1, 1), rough,
        pltpu.roll(flow, 1, 1), flow, pltpu.roll(flow, SIDE - 1, 1),
    )
    flux = jnp.where(lane == 0, face_first, flux)
    flux = jnp.where(lane == SIDE - 1, face_last, flux)
    lower = jnp.where(lane == 0, face_before, pltpu.roll(flux, 1, 1))
    return lower - flux


def corner_faces(h, z, rough, flow, entry_s, entry_n, corners_s, corners_n):
    def chosen(entry, corners, q):
        value = jnp.zeros((8, SIDE), F32)
        for j in range(2 * BLOCKS):
            value = jnp.where(entry == j, corners[q][j : j + 1], value)
        return value

    h_s, t_s, z_s, n_s = (chosen(entry_s, corners_s, q) for q in range(4))
    h_n, t_n, z_n = (chosen(entry_n, corners_n, q) for q in range(3))
    last = SIDE - 1
    has_s = jnp.where(column(entry_s, 0) >= 0.0, 1.0, 0.0)
    has_n = jnp.where(column(entry_n, 0) >= 0.0, 1.0, 0.0)
    eta, eta_s, eta_n = h + z, h_s + z_s, h_n + z_n
    before = face(
        column(eta_s, last), column(eta, 0), column(z_s, last), column(z, 0), column(n_s, last),
        column(t_s, last - 1), column(t_s, last), column(flow, 0),
    ) * has_s
    first = face(
        column(eta, 0), column(eta, 1), column(z, 0), column(z, 1), column(rough, 0),
        column(t_s, last), column(flow, 0), column(flow, 1),
    )
    final = face(
        column(eta, last), column(eta_n, 0), column(z, last), column(z_n, 0), column(rough, last),
        column(flow, last - 1), column(flow, last), column(t_n, 0),
    ) * has_n
    return before, first, final


def edges_kernel(
    entries, wet, edge_spill, low, high, ground_low, ground_high, wide_low_in, wide_high_in, has_low_in, has_high_in,
    far_east, far_west, pack1, pack_back, to_south, to_north, from_north, from_south,
    columns, rows,
    wide_low, wide_high, has_low, has_high, wetness, edge, rim_low, rim_high, corners, stack,
):
    wide_low[...] = wide_low_in[...]
    wide_high[...] = wide_high_in[...]
    has_low[...] = has_low_in[...]
    has_high[...] = has_high_in[...]
    for b in range(BLOCKS):
        value = jnp.full((1, SIDE), wet[0, b].astype(F32), F32)
        wetness[b : b + 1] = value
        wetness[4 + b : 5 + b] = value
        for entry, near, far, wide, has in (
            (entries[0, b, 2], to_north, from_south, wide_low, has_low),
            (entries[0, b, 3], to_south, from_north, wide_high, has_high),
        ):
            put_rim(
                entry, 4 + b, lambda s, r=near: r[s], lambda s, r=near: r[BLOCKS + s],
                lambda s, r=far: r[s], lambda s, r=far: r[BLOCKS + s], wide, has,
            )
    for j in range(BLOCKS):
        near = slice(j, j + 1)
        far = slice(BLOCKS + j, BLOCKS + j + 1)
        for q, row in enumerate(
            (
                far_east[j, 1:2], far_east[j, 5:6], pack1[6 + j, 1:2], pack1[6 + j, 3:4],
                far_west[j, 0:1], far_west[j, 6:7], pack_back[1 + j, 0:1], pack_back[1 + j, 2:3],
            )
        ):
            for i, passed in enumerate((from_south, from_north)):
                corners[i, q, near] = row
                corners[i, q, far] = passed[2 * BLOCKS + j, q : q + 1]

    def seen(i, first):
        return [corners[i, first + q] for q in range(4)]

    h0, h1, h2, q0, q1, q2, t0, t1 = (low[q] for q in range(8))
    z0, z1, z2, n0, n1 = (ground_low[q] for q in range(5))
    hy, hz, qx, qy, qz, tz = (high[q] for q in range(6))
    zy, zz, ny, nz = (ground_high[q] for q in range(4))
    face_m, face_0, face_1 = faces_low(low, ground_low, wide_low)
    face_y, face_z = faces_high(high, ground_high, wide_high)
    face_m = face_m * has_low[...]
    face_z = face_z * has_high[...]
    swapped = [sides_swapped(f) for f in (face_m, face_0, face_z)]

    def beside(spot):
        return [column(f, spot) for f in swapped]

    wets = wetness[...]
    last = SIDE - 1
    new_0 = (h0 + RATIO * (face_m - face_0 + along_edge(h0, z0, n0, t0, *beside(0))) + edge_spill[0]) * wets
    new_1 = (h1 + RATIO * (face_0 - face_1 + along_edge(h1, z1, n1, t1, *beside(1))) + edge_spill[1]) * wets
    new_z = (hz + RATIO * (face_y - face_z + along_edge(hz, zz, nz, tz, *beside(last))) + edge_spill[2]) * wets
    flow_0, flow_1, flow_y, flow_z = (f * wets for f in (face_0, face_1, face_y, face_z))
    for i, value in enumerate((new_z, flow_y, flow_z, new_0, flow_0)):
        edge[i] = value

    sides = lax.broadcasted_iota(jnp.int32, (8, 1), 0) < 4
    ghy, ghz, gqx, gqy, gqz, gtz = (wide_low[q] for q in range(6))
    gzy, gzz, gny, gnz, gspill = (wide_low[8 + q] for q in range(5))
    across = corner_faces(ghz, gzz, gnz, gtz, wide_low[13], wide_low[14], seen(0, 0), seen(1, 0))
    given = [column(wide_low[13 + q], last) for q in range(3)]
    ends = [jnp.where(sides, a, g) for a, g in zip(across, given)]
    far_face = face(ghy + gzy, ghz + gzz, gzy, gzz, gny, gqx, gqy, gqz)
    far_low = (
        ghz + RATIO * (far_face - face_m + along_edge(ghz, gzz, gnz, gtz, *ends)) + gspill,
        far_face,
        face_m,
    )
    gh0, gh1, gq0, gq1, gt0 = (wide_high[q] for q in (0, 1, 3, 4, 6))
    gz0, gz1, gn0, gspill = (wide_high[8 + q] for q in range(4))
    across = corner_faces(gh0, gz0, gn0, gt0, wide_high[12], wide_high[13], seen(0, 4), seen(1, 4))
    given = [column(wide_high[12 + q], 0) for q in range(3)]
    ends = [jnp.where(sides, a, g) for a, g in zip(across, given)]
    far_face = face(gh0 + gz0, gh1 + gz1, gz0, gz1, gn0, qz, gq0, gq1)
    far_high = (
        gh0 + RATIO * (face_z - far_face + along_edge(gh0, gz0, gn0, gt0, *ends)) + gspill,
        far_face,
    )
    for rim, far_rows, first, group in ((rim_low, far_low, 0, 0), (rim_high, far_high, 3, 1)):
        for q, far_row in enumerate(far_rows):
            rim[q] = far_row
        for b in range(BLOCKS):
            for side in range(2):
                entry = entries[0, b, 2 * side + group]
                sub = slice(side * 4 + b, side * 4 + b + 1)
                near = pl.ds(side * 4 + jnp.clip(entry, 0, BLOCKS - 1), 1)
                for q in range(len(far_rows)):
                    row = jnp.where(entry >= BLOCKS, rim[q, sub], edge[first + q, near])
                    rim[q, sub] = jnp.where(entry >= 0, row, 0.0)

    hm, qmm, qm = (rim_low[q] for q in range(3))
    hp, qp = (rim_high[q] for q in range(2))
    zm, nm, zp = wide_low[9], wide_low[11], wide_high[8]
    next_m = face(hm + zm, new_0 + z0, zm, z0, nm, qmm, qm, flow_0) * has_low[...]
    next_0 = face(new_0 + z0, new_1 + z1, z0, z1, n0, qm, flow_0, flow_1)
    next_z = face(new_z + zz, hp + zp, zz, zp, nz, flow_y, flow_z, qp) * has_high[...]
    stack[...] = jnp.zeros_like(stack)
    rows[...] = jnp.zeros_like(rows)
    for b in range(BLOCKS):
        for i, value in enumerate((face_m, face_0, face_z, next_m, next_0, next_z)):
            stack[b * 8 + i : b * 8 + i + 1] = value[b : b + 1]
            rows[b, i : i + 1] = value[4 + b : 5 + b]
    turned = stack[...].T
    columns[0] = turned
    for b in range(1, BLOCKS):
        columns[b] = pltpu.roll(turned, HALF - 8 * b, 1)


def inflow_kernel(cells, rates, spill, edge_spill):
    spill[...] = jnp.zeros_like(spill)
    edge_spill[...] = jnp.zeros_like(edge_spill)
    lane = lanes(1, SIDE)
    for b in range(BLOCKS):

        def point(p, carry, b=b):
            cell = cells[0, b, p]
            row = lax.div(cell, SIDE)
            column = lax.rem(cell, SIDE)
            rate = GAIN * rates[0, b, p]
            at_column = jnp.where(lane == column, rate, 0.0)
            at_row = jnp.where(lane == row, rate, 0.0)
            line = pl.ds(row, 1)
            spill[b, line] = spill[b, line] + at_column
            for i, place in enumerate((0, 1, SIDE - 1)):
                edge_spill[i, b : b + 1] += jnp.where(column == place, at_row, 0.0)
                edge_spill[i, 4 + b : 5 + b] += jnp.where(row == place, at_column, 0.0)
            return carry

        lax.fori_loop(0, RIVERS, point, 0)


def lay_inflow(cells, rates):
    return pl.pallas_call(
        inflow_kernel,
        out_shape=[shape(BLOCKS, SIDE, SIDE), shape(3, 8, SIDE)],
        in_specs=[SMEM, SMEM],
        out_specs=[VMEM] * 2,
        compiler_params=params(4),
        cost_estimate=cost(0, 0),
    )(cells, rates)


def block_step(now, ground, spill, columns, rows, base, wetness, write):
    lane = lanes(ROWS, SIDE)
    sub = lax.broadcasted_iota(jnp.int32, (ROWS, SIDE), 0)

    def at(load, field, first, shift):
        if 0 <= first + shift <= SIDE - ROWS:
            return load(field, first + shift)
        return pltpu.roll(load(field, first), -shift % ROWS, 0)

    below = rows(base)
    for first in range(0, SIDE, ROWS):
        h, qx, qy = (at(now, f, first, 0) for f in range(3))
        z, rough = (at(ground, f, first, 0) for f in range(2))
        eta = h + z
        flux_x = face(
            eta, pltpu.roll(eta, SIDE - 1, 1), z, pltpu.roll(z, SIDE - 1, 1), rough,
            pltpu.roll(qx, 1, 1), qx, pltpu.roll(qx, SIDE - 1, 1),
        )
        edge = columns(pl.ds(first, ROWS))
        flux_x = jnp.where(lane == 0, edge[:, base + 1 : base + 2], flux_x)
        flux_x = jnp.where(lane == SIDE - 1, edge[:, base + 2 : base + 3], flux_x)
        flux_w = jnp.where(lane == 0, edge[:, base : base + 1], pltpu.roll(flux_x, 1, 1))
        z_up = at(ground, 0, first, 1)
        flux_y = face(
            eta, at(now, 0, first, 1) + z_up, z, z_up, rough, at(now, 2, first, -1), qy, at(now, 2, first, 1)
        )
        if first == 0:
            flux_y = jnp.where(sub == 0, rows(base + 1), flux_y)
        if first == SIDE - ROWS:
            flux_y = jnp.where(sub == ROWS - 1, rows(base + 2), flux_y)
        flux_s = jnp.where(sub == 0, below, pltpu.roll(flux_y, 1, 0))
        below = flux_y[ROWS - 1 : ROWS]
        depth = h + RATIO * (flux_w - flux_x + flux_s - flux_y) + spill(pl.ds(first, ROWS))
        write(first, depth * wetness, flux_x * wetness, flux_y * wetness)


def block(shifts, dest, wet, terrain, columns, rows, spill, states, out, then, done, sems):
    slot = landing_slot(dest, jnp.where(core() == 0, *shifts))
    wetness = wet[0, slot].astype(F32)
    state = states[0]
    if shifts == W_SHIFTS:
        for here, ref in enumerate(states):

            @pl.when(core() == 1 - here)
            def _(ref=ref):
                copy = pltpu.make_async_copy(ref, done, sems.at[0])
                copy.start()
                copy.wait()

        state = done
    copies = []

    def now(field, first):
        return state[field, first : first + ROWS]

    def ground(field, first):
        return terrain[0, slot, field, first : first + ROWS]

    def keep(first, *fields):
        for f, value in enumerate(fields):
            then[f, first : first + ROWS] = value

    def finish(first, *fields):
        for f, value in enumerate(fields):
            done[f, first : first + ROWS] = value
        lines = pl.ds(first, ROWS)
        copies.append(pltpu.make_async_copy(done.at[:, lines], out.at[0, slot, :, lines], sems.at[len(copies)]))
        copies[-1].start()

    shared = (
        lambda at: spill[slot, at],
        lambda at: columns[slot, at],
        lambda q: rows[slot, q : q + 1],
    )
    block_step(now, ground, *shared, 0, wetness, keep)
    block_step(lambda f, first: then[f, first : first + ROWS], ground, *shared, 3, wetness, finish)
    return copies


EDGE_INPUTS = 19
EDGE_SCRATCH = 10


def block_scratch():
    return [pltpu.VMEM((3, SIDE, SIDE), F32)] * 3 + [pltpu.SemaphoreType.DMA((SIDE // ROWS,))] * 2


def blocks_kernel(dest, *refs):
    ins, refs = refs[:EDGE_INPUTS], refs[EDGE_INPUTS:]
    terrain, spill, own, arrived_a, arrived_x, arrived_w, relayed, out = refs[:8]
    edge_scratch, (columns, rows, then, done1, done2, sems1, sems2) = refs[8 : 8 + EDGE_SCRATCH], refs[8 + EDGE_SCRATCH :]
    edges_kernel(*ins, columns, rows, *edge_scratch)
    shared = (dest, ins[1], terrain, columns, rows, spill)
    copies = block(OWN_SHIFTS, *shared, (own,), out, then, done1, sems1)
    later = block(A_SHIFTS, *shared, (arrived_a,), out, then, done2, sems2)
    for copy in copies:
        copy.wait()
    copies = block(W_SHIFTS, *shared, (arrived_w, relayed), out, then, done1, sems1)
    for copy in later:
        copy.wait()
    copies += block(X_SHIFTS, *shared, (arrived_x,), out, then, done2, sems2)
    for copy in copies:
        copy.wait()


def all_blocks(dest, edge_inputs, terrain, spill, own, arrived_a, arrived_x, arrived_w, relayed):
    return pl.pallas_call(
        blocks_kernel,
        out_shape=shape(1, BLOCKS, 3, SIDE, SIDE),
        in_specs=[SMEM] * 3 + [VMEM] * (EDGE_INPUTS - 2 + 5) + [ANY] * 2,
        out_specs=HBM,
        scratch_shapes=[
            pltpu.VMEM((16, 8, SIDE), F32),
            pltpu.VMEM((16, 8, SIDE), F32),
            pltpu.VMEM((8, SIDE), F32),
            pltpu.VMEM((8, SIDE), F32),
            pltpu.VMEM((8, SIDE), F32),
            pltpu.VMEM((5, 8, SIDE), F32),
            pltpu.VMEM((3, 8, SIDE), F32),
            pltpu.VMEM((2, 8, SIDE), F32),
            pltpu.VMEM((2, 8, 8, SIDE), F32),
            pltpu.VMEM((HALF, SIDE), F32),
            pltpu.VMEM((BLOCKS, SIDE, HALF), F32),
            pltpu.VMEM((BLOCKS, 8, SIDE), F32),
        ]
        + block_scratch(),
        compiler_params=params(16),
        cost_estimate=cost(0, 0),
    )(dest, *edge_inputs, terrain, spill, own, arrived_a, arrived_x, arrived_w, relayed)


def passed_along(x, axis, by, wrap=True):
    devices = lax.axis_size(axis)
    return lax.ppermute(x, axis, [(i, (i + by) % devices) for i in range(devices)])


def passed_to(x, target):
    devices = lax.axis_size("tile")
    pairs = [(i, target(i // 2, i % 2)) for i in range(devices)]
    return lax.ppermute(x, "tile", [(i, t % devices) for i, t in pairs if t is not None])


def back_one(chip):
    return chip // RING * RING + (chip - 1) % RING


def first_leg(chip, at):
    return 2 * chip + 1 if at == 0 else 2 * back_one(chip)


def second_leg(chip, at):
    sender = chip // RING * RING + (chip + 1) % RING
    return 2 * (sender + 2) if at == 0 else None


def next_chip_swapped(chip, at):
    return 2 * (chip + 1) + 1 - at


def body(flood_state, terrain, destination, wet_mask, neighbours, inflow_cells, inflow_rates):
    dest, state = in_hbm(destination), in_hbm(flood_state)
    block_a, block_w = pick_early(dest, state)
    arrived_a = passed_along(block_a, "tile", 2)
    arrived_w = passed_to(block_w, first_leg)
    own, block_x, ground_low, ground_high, *packs = prepare(
        dest, in_hbm(neighbours), state, block_a, block_w,
        in_hbm(terrain), in_hbm(inflow_cells), in_hbm(inflow_rates),
    )
    ground = (ground_low, ground_high)
    spill, edge_spill = lay_inflow(inflow_cells, inflow_rates)
    packs[5] = passed_along(packs[5], "tile", -1)
    packs[1:3] = [passed_along(packs[d], "tile", d) for d in (1, 2)]
    (packs[3],) = gate((packs[3],), (packs[5], edge_spill))
    packs[3] = passed_along(packs[3], "tile", 3)
    (packs[4],) = gate((packs[4],), (arrived_a,))
    packs[4] = passed_along(packs[4], "tile", 4)
    block_x, arrived_w = gate((block_x, arrived_w), (arrived_a,))
    arrived_x = passed_to(block_x, next_chip_swapped)
    arrived_w, low, high, wide_low, wide_high, has_low, has_high, far_east, far_west, to_south, to_north = arrange(
        destination, neighbours, packs, ground, edge_spill, arrived_a, arrived_w
    )
    relayed = passed_to(arrived_w, second_leg)
    from_north = passed_along(to_south, "grp", -1)
    from_south = passed_along(to_north, "grp", 1)
    edge_inputs = (
        neighbours, wet_mask, edge_spill, low, high, *ground, wide_low, wide_high, has_low, has_high,
        far_east, far_west, packs[1], packs[5], to_south, to_north, from_north, from_south,
    )
    return all_blocks(
        destination, edge_inputs, terrain, spill, own, arrived_a, arrived_x, arrived_w, relayed
    )


def solution(mesh):
    in_specs = (
        P("grp", "tile", None, None, None),
        P("grp", "tile", None, None, None),
        P("grp", None),
        P("grp", "tile"),
        P("grp", "tile", None),
        P("grp", "tile", None),
        P("grp", "tile", None),
    )
    out_specs = P("grp", "tile", None, None, None)
    return jax.shard_map(body, mesh=mesh, in_specs=in_specs, out_specs=out_specs, check_vma=False)
```

```python
import functools

import jax
import jax.numpy as jnp
from jax import lax
from jax.experimental import pallas as pl
from jax.experimental.pallas import tpu as pltpu
from jax.sharding import PartitionSpec as P

F32 = jnp.float32
GRAVITY = 9.81
SPACING = 10.0
TIMESTEP = 0.2
CENTRE_WEIGHT = 0.7
DEPTH_FLOOR = 0.1
SIDE = 256
HALF = 128
BLOCKS = 4
RIVERS = 16
ROWS = 64
GAIN = TIMESTEP / (SPACING * SPACING)
RATIO = TIMESTEP / SPACING

ANY = pl.BlockSpec(memory_space=pl.ANY)
VMEM = pl.BlockSpec(memory_space=pltpu.VMEM)
SMEM = pl.BlockSpec(memory_space=pltpu.SMEM)
HBM = pl.BlockSpec(memory_space=pltpu.HBM)
RING = 4
OWN_SHIFTS = (0, 0)
A_SHIFTS = (2, 2)
W_SHIFTS = (3, 1)
X_SHIFTS = (1, 3)


def shape(*dims):
    return jax.ShapeDtypeStruct(dims, F32)


def cost(flops, bytes_accessed):
    return pl.CostEstimate(flops=flops, bytes_accessed=bytes_accessed, transcendentals=0)


def face(eta_l, eta_r, z_l, z_r, rough, flow_left, flow_mid, flow_right):
    depth = jnp.maximum(eta_l, eta_r) - jnp.maximum(z_l, z_r)
    floored = jnp.maximum(depth, DEPTH_FLOOR)
    blended = CENTRE_WEIGHT * flow_mid + 0.5 * (1.0 - CENTRE_WEIGHT) * (flow_left + flow_right)
    slope = (GRAVITY * TIMESTEP / SPACING) * depth * (eta_r - eta_l)
    friction = 1.0 + (GRAVITY * TIMESTEP) * rough * rough * jnp.abs(flow_mid) * jnp.exp(
        (-7.0 / 3.0) * jnp.log(floored)
    )
    return (blended - slope) / friction


def core():
    return lax.rem(lax.axis_index("tile"), 2)


def params(mib):
    return pltpu.CompilerParams(vmem_limit_bytes=mib << 20)


def tile_offset(dest_ref, tile, slot):
    tiles = lax.axis_size("tile")
    return lax.rem(lax.div(dest_ref[0, tile * BLOCKS + slot], BLOCKS) - tile + tiles, tiles)


def leaving_slot(dest_ref, shift):
    me = lax.axis_index("tile")
    slot = jnp.int32(0)
    for j in range(1, BLOCKS):
        slot = jnp.where(tile_offset(dest_ref, me, j) == shift, j, slot)
    return slot


def landing_slot(dest_ref, shift, back=0):
    tiles = lax.axis_size("tile")
    sender = lax.rem(lax.axis_index("tile") - shift - back + 2 * tiles, tiles)
    slot = jnp.int32(0)
    for j in range(BLOCKS):
        place = lax.rem(dest_ref[0, sender * BLOCKS + j], BLOCKS)
        slot = jnp.where(tile_offset(dest_ref, sender, j) == shift, place, slot)
    return slot


def lanes(rows, columns):
    return lax.broadcasted_iota(jnp.int32, (rows, columns), 1)


def in_hbm(x):
    return pltpu.with_memory_space_constraint(x, pltpu.HBM)


def pick_kernel(dest, state, block_a, block_w, sems):
    slots = [leaving_slot(dest, k) for k in range(1, BLOCKS)]
    slot_w = jnp.where(core() == 0, slots[0], slots[2])
    loads = [
        pltpu.make_async_copy(state.at[0, slot], ref, sems.at[i])
        for i, (slot, ref) in enumerate(((slots[1], block_a), (slot_w, block_w)))
    ]
    for load in loads:
        load.start()
    for load in loads:
        load.wait()


def pick_early(dest, state):
    return pl.pallas_call(
        pick_kernel,
        out_shape=[shape(3, SIDE, SIDE)] * 2,
        in_specs=[SMEM, HBM],
        out_specs=[VMEM] * 2,
        scratch_shapes=[pltpu.SemaphoreType.DMA((2,))],
        compiler_params=params(4),
        cost_estimate=cost(0, 0),
    )(dest, state)


def prepare_kernel(
    dest, entries, state, block_a, block_w, ground_in, cells, rates,
    own, block_x, low, high, pack0, pack1, pack2, pack3, pack4, pack_back, terrain, sems,
):
    slots = [leaving_slot(dest, k) for k in range(BLOCKS)]
    first_core = core() == 0
    slot_x = jnp.where(first_core, slots[3], slots[1])
    held = (block_x, own)
    loads = [pltpu.make_async_copy(ground_in, terrain, sems.at[3])]
    for i, (slot, ref) in enumerate(zip((slot_x, slots[0]), held)):
        loads.append(pltpu.make_async_copy(state.at[0, slot], ref, sems.at[i]))
    for load in loads:
        load.start()
    lane = lanes(SIDE, HALF)

    def strips(ref, write):
        west = [ref[f, :, :HALF] for f in range(3)]
        east = [ref[f, :, HALF:] for f in range(3)]
        packed = jnp.where(lane < 3, west[0], pltpu.roll(west[1], 3, 1))
        packed = jnp.where(lane < 6, packed, pltpu.roll(west[2], 6, 1))
        packed = jnp.where(lane < 8, packed, pltpu.roll(east[0], 10, 1))
        packed = jnp.where(lane < 10, packed, pltpu.roll(east[1], 13, 1))
        packed = jnp.where(lane < 13, packed, pltpu.roll(east[2], 14, 1))
        turned = packed.T
        south = jnp.concatenate([ref[0, 0:3], ref[2, 0:3], ref[1, 0:2]])
        north = jnp.concatenate(
            [ref[0, SIDE - 2 : SIDE], ref[2, SIDE - 3 : SIDE], ref[1, SIDE - 1 : SIDE], jnp.zeros((2, SIDE), F32)]
        )
        write(turned[0:8], south, turned[8:16], north)

    strip_out = (pack0, pack1, pack2, pack3)
    west_out = (pack_back.at[0], pack0.at[4], pack1.at[5], pack2.at[5])
    east_out = (pack1.at[4], pack2.at[4], pack3.at[4], pack4.at[0])

    def write(k, west, south, east, north):
        for i, value in enumerate((west, south, east, north)):
            strip_out[k][i] = value
        east_out[k][...] = east
        west_out[k][...] = west

    def write_by_core(first, second):
        def both(*values):
            pl.when(first_core)(lambda: write(first, *values))
            pl.when(jnp.logical_not(first_core))(lambda: write(second, *values))

        return both

    strips(block_a, functools.partial(write, 2))
    strips(block_w, write_by_core(1, 3))
    along = lanes(BLOCKS, SIDE)
    spills = [jnp.zeros((BLOCKS, SIDE), F32) for _ in range(2)]
    for p in range(RIVERS):
        cell = cells[0, :, p : p + 1] - along * SIDE
        rate = GAIN * rates[0, :, p : p + 1]
        for i, place in enumerate((0, SIDE - 1)):
            spills[i] = spills[i] + jnp.where(cell == place, rate, 0.0)
    loads[0].wait()
    for b in range(BLOCKS):
        west = [terrain[0, b, f, :, :HALF] for f in range(2)]
        east = [terrain[0, b, f, :, HALF:] for f in range(2)]
        packed = jnp.where(lane < 3, west[0], pltpu.roll(west[1], 3, 1))
        packed = jnp.where(lane < 5, packed, pltpu.roll(east[0], 7, 1))
        packed = jnp.where(lane < 7, packed, pltpu.roll(east[1], 9, 1))
        turned = packed.T
        for q in range(5):
            low[q, b : b + 1] = turned[q : q + 1]
        for q in range(4):
            high[q, b : b + 1] = turned[5 + q : 6 + q]
        for q in range(3):
            low[q, 4 + b : 5 + b] = terrain[0, b, 0, q : q + 1]
        for q in range(2):
            low[3 + q, 4 + b : 5 + b] = terrain[0, b, 1, q : q + 1]
            high[q, 4 + b : 5 + b] = terrain[0, b, 0, SIDE - 2 + q : SIDE - 1 + q]
            high[2 + q, 4 + b : 5 + b] = terrain[0, b, 1, SIDE - 2 + q : SIDE - 1 + q]
    for b in range(BLOCKS):
        line = slice(b, b + 1)
        links = [jnp.full((1, SIDE), entries[0, b, side].astype(F32), F32) for side in (2, 3)]
        blank = [jnp.zeros((1, SIDE), F32)]
        pack1[6 + b] = jnp.concatenate([high[q, line] for q in range(4)] + [spills[1][line]] + links + blank)
        pack_back[1 + b] = jnp.concatenate(
            [low[0, line], low[1, line], low[3, line], spills[0][line]] + links + blank * 2
        )
    writers = (write_by_core(3, 1), functools.partial(write, 0))
    for load, ref, write_out in zip(loads[1:], held, writers):
        load.wait()
        strips(ref, write_out)


def prepare(dest, entries, state, block_a, block_w, terrain, cells, rates):
    packs = [shape(count, 8, SIDE) for count in (5, 10, 6, 5, 1, 5)]
    return pl.pallas_call(
        prepare_kernel,
        out_shape=[shape(3, SIDE, SIDE)] * 2 + [shape(5, 8, SIDE), shape(4, 8, SIDE)] + packs,
        in_specs=[SMEM, SMEM, HBM, VMEM, VMEM, HBM, VMEM, VMEM],
        out_specs=[VMEM] * 10,
        scratch_shapes=[
            pltpu.VMEM((1, BLOCKS, 2, SIDE, SIDE), F32),
            pltpu.SemaphoreType.DMA((BLOCKS,)),
        ],
        compiler_params=params(12),
        cost_estimate=cost(0, 0),
    )(dest, entries, state, block_a, block_w, terrain, cells, rates)


def gate_kernel(count, *refs):
    del count, refs


def gate(values, keys):
    count = len(values)
    return pl.pallas_call(
        functools.partial(gate_kernel, count),
        out_shape=[jax.ShapeDtypeStruct(v.shape, v.dtype) for v in values],
        in_specs=[ANY] * (count + len(keys)),
        out_specs=[ANY] * count,
        input_output_aliases={i: i for i in range(count)},
        compiler_params=params(1),
        cost_estimate=cost(0, 0),
    )(*values, *keys)


def sides_swapped(x):
    return pltpu.roll(x, 4, 0)


def column(x, at):
    return x[:, at : at + 1]


def put_rim(entry, sub, near_state, near_fixed, far_state, far_fixed, wide, has):
    near = jnp.clip(entry, 0, BLOCKS - 1)
    far = jnp.clip(entry - BLOCKS, 0, BLOCKS - 1)
    alive = entry >= 0
    for i, (close, distant) in enumerate(((near_state, far_state), (near_fixed, far_fixed))):
        rows = jnp.where(entry >= BLOCKS, distant(far), close(near))
        rows = jnp.where(alive, rows, 0.0)
        for q in range(8):
            wide[8 * i + q, sub : sub + 1] = rows[q : q + 1]
    has[sub : sub + 1] = jnp.full((1, SIDE), jnp.where(alive, 1.0, 0.0), F32)


def faces_low(low, ground_low, wide):
    h0, h1, h2, q0, q1, q2 = (low[q] for q in range(6))
    z0, z1, z2, n0, n1 = (ground_low[q] for q in range(5))
    hm, qmm, qm, zm, nm = (wide[q] for q in (1, 3, 4, 9, 11))
    return (
        face(hm + zm, h0 + z0, zm, z0, nm, qmm, qm, q0),
        face(h0 + z0, h1 + z1, z0, z1, n0, qm, q0, q1),
        face(h1 + z1, h2 + z2, z1, z2, n1, q0, q1, q2),
    )


def faces_high(high, ground_high, wide):
    hy, hz, qx, qy, qz = (high[q] for q in range(5))
    zy, zz, ny, nz = (ground_high[q] for q in range(4))
    hp, qp, zp = (wide[q] for q in (0, 3, 8))
    return (
        face(hy + zy, hz + zz, zy, zz, ny, qx, qy, qz),
        face(hz + zz, hp + zp, zz, zp, nz, qy, qz, qp),
    )


def arrange_kernel(
    dest, entries, pack0, pack1, pack2, pack3, pack4, pack_back, ground_low, ground_high, edge_spill,
    low, high, wide_low, wide_high, has_low, has_high, far_east, far_west, to_south, to_north,
    west, east,
):
    for out in (low, high, wide_low, wide_high, has_low, has_high):
        out[...] = jnp.zeros_like(out)
    strips = (pack0, pack1, pack2, pack3)
    west_in = (pack_back.at[0], pack0.at[4], pack1.at[5], pack2.at[5])
    east_in = (pack1.at[4], pack2.at[4], pack3.at[4], pack4.at[0])
    for k in range(BLOCKS):
        strip = strips[k]
        slot = landing_slot(dest, k)
        for side in range(2):
            row = pl.ds(side * 4 + slot, 1)
            for q in range(8):
                low[q, row] = strip[side, q : q + 1]
            for q in range(6):
                high[q, row] = strip[2 + side, q : q + 1]
        for i, out in enumerate((west, to_south, east, to_north)):
            out[slot] = strip[i]
        slot = landing_slot(dest, k, 1)
        far_east[slot] = east_in[k][...]
        slot = landing_slot(dest, k, -1)
        far_west[slot] = west_in[k][...]

    def fixed_low(slot):
        row = pl.ds(slot, 1)
        rows = [ground_low[0, row], ground_low[1, row], ground_low[3, row]]
        return jnp.concatenate(rows + [jnp.zeros((5, SIDE), F32)])

    def fixed_high(slot):
        row = pl.ds(slot, 1)
        return jnp.concatenate([ground_high[q, row] for q in range(4)] + [jnp.zeros((4, SIDE), F32)])

    for b in range(BLOCKS):
        put_rim(
            entries[0, b, 0], b, lambda s: east[s], fixed_high,
            lambda s: far_east[s], lambda s: pack1[6 + s], wide_low, has_low,
        )
        put_rim(
            entries[0, b, 1], b, lambda s: west[s], fixed_low,
            lambda s: far_west[s], lambda s: pack_back[1 + s], wide_high, has_high,
        )
    face_m, face_0, _ = faces_low(low, ground_low, wide_low)
    _, face_z = faces_high(high, ground_high, wide_high)
    face_m = face_m * has_low[...]
    face_z = face_z * has_high[...]
    for b in range(BLOCKS):
        sub = slice(4 + b, 5 + b)
        beside = [f[b : b + 1] for f in (face_m, face_0, face_z)]
        blank = [jnp.zeros((1, SIDE), F32)]
        to_north[4 + b] = jnp.concatenate([ground_high[q, sub] for q in range(4)] + [edge_spill[2, sub]] + beside)
        to_south[4 + b] = jnp.concatenate(
            [ground_low[0, sub], ground_low[1, sub], ground_low[3, sub], edge_spill[0, sub]] + beside + blank
        )
        passed = jnp.concatenate(
            [
                far_east[b, 1:2], far_east[b, 5:6], pack1[6 + b, 1:2], pack1[6 + b, 3:4],
                far_west[b, 0:1], far_west[b, 6:7], pack_back[1 + b, 0:1], pack_back[1 + b, 2:3],
            ]
        )
        to_north[8 + b] = passed
        to_south[8 + b] = passed


def arrange(dest, entries, packs, ground, edge_spill):
    outs = [(8, 8), (6, 8), (16, 8), (16, 8), (8,), (8,), (BLOCKS, 8), (BLOCKS, 8), (3 * BLOCKS, 8), (3 * BLOCKS, 8)]
    return pl.pallas_call(
        arrange_kernel,
        out_shape=[shape(*dims, SIDE) for dims in outs],
        in_specs=[SMEM] * 2 + [VMEM] * 9,
        out_specs=[VMEM] * len(outs),
        scratch_shapes=[pltpu.VMEM((BLOCKS, 8, SIDE), F32)] * 2,
        compiler_params=params(4),
        cost_estimate=cost(0, 0),
    )(dest, entries, *packs, *ground, edge_spill)


def along_edge(h, z, rough, flow, face_before, face_first, face_last):
    lane = lanes(8, SIDE)
    eta = h + z
    flux = face(
        eta, pltpu.roll(eta, SIDE - 1, 1), z, pltpu.roll(z, SIDE - 1, 1), rough,
        pltpu.roll(flow, 1, 1), flow, pltpu.roll(flow, SIDE - 1, 1),
    )
    flux = jnp.where(lane == 0, face_first, flux)
    flux = jnp.where(lane == SIDE - 1, face_last, flux)
    lower = jnp.where(lane == 0, face_before, pltpu.roll(flux, 1, 1))
    return lower - flux


def corner_faces(h, z, rough, flow, entry_s, entry_n, corners_s, corners_n):
    def chosen(entry, corners, q):
        value = jnp.zeros((8, SIDE), F32)
        for j in range(2 * BLOCKS):
            value = jnp.where(entry == j, corners[q][j : j + 1], value)
        return value

    h_s, t_s, z_s, n_s = (chosen(entry_s, corners_s, q) for q in range(4))
    h_n, t_n, z_n = (chosen(entry_n, corners_n, q) for q in range(3))
    last = SIDE - 1
    has_s = jnp.where(column(entry_s, 0) >= 0.0, 1.0, 0.0)
    has_n = jnp.where(column(entry_n, 0) >= 0.0, 1.0, 0.0)
    eta, eta_s, eta_n = h + z, h_s + z_s, h_n + z_n
    before = face(
        column(eta_s, last), column(eta, 0), column(z_s, last), column(z, 0), column(n_s, last),
        column(t_s, last - 1), column(t_s, last), column(flow, 0),
    ) * has_s
    first = face(
        column(eta, 0), column(eta, 1), column(z, 0), column(z, 1), column(rough, 0),
        column(t_s, last), column(flow, 0), column(flow, 1),
    )
    final = face(
        column(eta, last), column(eta_n, 0), column(z, last), column(z_n, 0), column(rough, last),
        column(flow, last - 1), column(flow, last), column(t_n, 0),
    ) * has_n
    return before, first, final


def edges_kernel(
    entries, wet, edge_spill, low, high, ground_low, ground_high, wide_low_in, wide_high_in, has_low_in, has_high_in,
    far_east, far_west, pack1, pack_back, to_south, to_north, from_north, from_south,
    columns, rows,
    wide_low, wide_high, has_low, has_high, wetness, edge, rim_low, rim_high, corners, stack,
):
    wide_low[...] = wide_low_in[...]
    wide_high[...] = wide_high_in[...]
    has_low[...] = has_low_in[...]
    has_high[...] = has_high_in[...]
    for b in range(BLOCKS):
        value = jnp.full((1, SIDE), wet[0, b].astype(F32), F32)
        wetness[b : b + 1] = value
        wetness[4 + b : 5 + b] = value
        for entry, near, far, wide, has in (
            (entries[0, b, 2], to_north, from_south, wide_low, has_low),
            (entries[0, b, 3], to_south, from_north, wide_high, has_high),
        ):
            put_rim(
                entry, 4 + b, lambda s, r=near: r[s], lambda s, r=near: r[BLOCKS + s],
                lambda s, r=far: r[s], lambda s, r=far: r[BLOCKS + s], wide, has,
            )
    for j in range(BLOCKS):
        near = slice(j, j + 1)
        far = slice(BLOCKS + j, BLOCKS + j + 1)
        for q, row in enumerate(
            (
                far_east[j, 1:2], far_east[j, 5:6], pack1[6 + j, 1:2], pack1[6 + j, 3:4],
                far_west[j, 0:1], far_west[j, 6:7], pack_back[1 + j, 0:1], pack_back[1 + j, 2:3],
            )
        ):
            for i, passed in enumerate((from_south, from_north)):
                corners[i, q, near] = row
                corners[i, q, far] = passed[2 * BLOCKS + j, q : q + 1]

    def seen(i, first):
        return [corners[i, first + q] for q in range(4)]

    h0, h1, h2, q0, q1, q2, t0, t1 = (low[q] for q in range(8))
    z0, z1, z2, n0, n1 = (ground_low[q] for q in range(5))
    hy, hz, qx, qy, qz, tz = (high[q] for q in range(6))
    zy, zz, ny, nz = (ground_high[q] for q in range(4))
    face_m, face_0, face_1 = faces_low(low, ground_low, wide_low)
    face_y, face_z = faces_high(high, ground_high, wide_high)
    face_m = face_m * has_low[...]
    face_z = face_z * has_high[...]
    swapped = [sides_swapped(f) for f in (face_m, face_0, face_z)]

    def beside(spot):
        return [column(f, spot) for f in swapped]

    wets = wetness[...]
    last = SIDE - 1
    new_0 = (h0 + RATIO * (face_m - face_0 + along_edge(h0, z0, n0, t0, *beside(0))) + edge_spill[0]) * wets
    new_1 = (h1 + RATIO * (face_0 - face_1 + along_edge(h1, z1, n1, t1, *beside(1))) + edge_spill[1]) * wets
    new_z = (hz + RATIO * (face_y - face_z + along_edge(hz, zz, nz, tz, *beside(last))) + edge_spill[2]) * wets
    flow_0, flow_1, flow_y, flow_z = (f * wets for f in (face_0, face_1, face_y, face_z))
    for i, value in enumerate((new_z, flow_y, flow_z, new_0, flow_0)):
        edge[i] = value

    sides = lax.broadcasted_iota(jnp.int32, (8, 1), 0) < 4
    ghy, ghz, gqx, gqy, gqz, gtz = (wide_low[q] for q in range(6))
    gzy, gzz, gny, gnz, gspill = (wide_low[8 + q] for q in range(5))
    across = corner_faces(ghz, gzz, gnz, gtz, wide_low[13], wide_low[14], seen(0, 0), seen(1, 0))
    given = [column(wide_low[13 + q], last) for q in range(3)]
    ends = [jnp.where(sides, a, g) for a, g in zip(across, given)]
    far_face = face(ghy + gzy, ghz + gzz, gzy, gzz, gny, gqx, gqy, gqz)
    far_low = (
        ghz + RATIO * (far_face - face_m + along_edge(ghz, gzz, gnz, gtz, *ends)) + gspill,
        far_face,
        face_m,
    )
    gh0, gh1, gq0, gq1, gt0 = (wide_high[q] for q in (0, 1, 3, 4, 6))
    gz0, gz1, gn0, gspill = (wide_high[8 + q] for q in range(4))
    across = corner_faces(gh0, gz0, gn0, gt0, wide_high[12], wide_high[13], seen(0, 4), seen(1, 4))
    given = [column(wide_high[12 + q], 0) for q in range(3)]
    ends = [jnp.where(sides, a, g) for a, g in zip(across, given)]
    far_face = face(gh0 + gz0, gh1 + gz1, gz0, gz1, gn0, qz, gq0, gq1)
    far_high = (
        gh0 + RATIO * (face_z - far_face + along_edge(gh0, gz0, gn0, gt0, *ends)) + gspill,
        far_face,
    )
    for rim, far_rows, first, group in ((rim_low, far_low, 0, 0), (rim_high, far_high, 3, 1)):
        for q, far_row in enumerate(far_rows):
            rim[q] = far_row
        for b in range(BLOCKS):
            for side in range(2):
                entry = entries[0, b, 2 * side + group]
                sub = slice(side * 4 + b, side * 4 + b + 1)
                near = pl.ds(side * 4 + jnp.clip(entry, 0, BLOCKS - 1), 1)
                for q in range(len(far_rows)):
                    row = jnp.where(entry >= BLOCKS, rim[q, sub], edge[first + q, near])
                    rim[q, sub] = jnp.where(entry >= 0, row, 0.0)

    hm, qmm, qm = (rim_low[q] for q in range(3))
    hp, qp = (rim_high[q] for q in range(2))
    zm, nm, zp = wide_low[9], wide_low[11], wide_high[8]
    next_m = face(hm + zm, new_0 + z0, zm, z0, nm, qmm, qm, flow_0) * has_low[...]
    next_0 = face(new_0 + z0, new_1 + z1, z0, z1, n0, qm, flow_0, flow_1)
    next_z = face(new_z + zz, hp + zp, zz, zp, nz, flow_y, flow_z, qp) * has_high[...]
    stack[...] = jnp.zeros_like(stack)
    rows[...] = jnp.zeros_like(rows)
    for b in range(BLOCKS):
        for i, value in enumerate((face_m, face_0, face_z, next_m, next_0, next_z)):
            stack[b * 8 + i : b * 8 + i + 1] = value[b : b + 1]
            rows[b, i : i + 1] = value[4 + b : 5 + b]
    turned = stack[...].T
    columns[0] = turned
    for b in range(1, BLOCKS):
        columns[b] = pltpu.roll(turned, HALF - 8 * b, 1)


def inflow_kernel(cells, rates, spill, edge_spill):
    spill[...] = jnp.zeros_like(spill)
    edge_spill[...] = jnp.zeros_like(edge_spill)
    lane = lanes(1, SIDE)
    for b in range(BLOCKS):

        def point(p, carry, b=b):
            cell = cells[0, b, p]
            row = lax.div(cell, SIDE)
            column = lax.rem(cell, SIDE)
            rate = GAIN * rates[0, b, p]
            at_column = jnp.where(lane == column, rate, 0.0)
            at_row = jnp.where(lane == row, rate, 0.0)
            line = pl.ds(row, 1)
            spill[b, line] = spill[b, line] + at_column
            for i, place in enumerate((0, 1, SIDE - 1)):
                edge_spill[i, b : b + 1] += jnp.where(column == place, at_row, 0.0)
                edge_spill[i, 4 + b : 5 + b] += jnp.where(row == place, at_column, 0.0)
            return carry

        lax.fori_loop(0, RIVERS, point, 0)


def lay_inflow(cells, rates):
    return pl.pallas_call(
        inflow_kernel,
        out_shape=[shape(BLOCKS, SIDE, SIDE), shape(3, 8, SIDE)],
        in_specs=[SMEM, SMEM],
        out_specs=[VMEM] * 2,
        compiler_params=params(4),
        cost_estimate=cost(0, 0),
    )(cells, rates)


def block_step(now, ground, spill, columns, rows, base, wetness, write):
    lane = lanes(ROWS, SIDE)
    sub = lax.broadcasted_iota(jnp.int32, (ROWS, SIDE), 0)

    def at(load, field, first, shift):
        if 0 <= first + shift <= SIDE - ROWS:
            return load(field, first + shift)
        return pltpu.roll(load(field, first), -shift % ROWS, 0)

    below = rows(base)
    for first in range(0, SIDE, ROWS):
        h, qx, qy = (at(now, f, first, 0) for f in range(3))
        z, rough = (at(ground, f, first, 0) for f in range(2))
        eta = h + z
        flux_x = face(
            eta, pltpu.roll(eta, SIDE - 1, 1), z, pltpu.roll(z, SIDE - 1, 1), rough,
            pltpu.roll(qx, 1, 1), qx, pltpu.roll(qx, SIDE - 1, 1),
        )
        edge = columns(pl.ds(first, ROWS))
        flux_x = jnp.where(lane == 0, edge[:, base + 1 : base + 2], flux_x)
        flux_x = jnp.where(lane == SIDE - 1, edge[:, base + 2 : base + 3], flux_x)
        flux_w = jnp.where(lane == 0, edge[:, base : base + 1], pltpu.roll(flux_x, 1, 1))
        z_up = at(ground, 0, first, 1)
        flux_y = face(
            eta, at(now, 0, first, 1) + z_up, z, z_up, rough, at(now, 2, first, -1), qy, at(now, 2, first, 1)
        )
        if first == 0:
            flux_y = jnp.where(sub == 0, rows(base + 1), flux_y)
        if first == SIDE - ROWS:
            flux_y = jnp.where(sub == ROWS - 1, rows(base + 2), flux_y)
        flux_s = jnp.where(sub == 0, below, pltpu.roll(flux_y, 1, 0))
        below = flux_y[ROWS - 1 : ROWS]
        depth = h + RATIO * (flux_w - flux_x + flux_s - flux_y) + spill(pl.ds(first, ROWS))
        write(first, depth * wetness, flux_x * wetness, flux_y * wetness)


def block(shifts, dest, wet, terrain, columns, rows, spill, states, out, then, done, sems):
    slot = landing_slot(dest, jnp.where(core() == 0, *shifts))
    wetness = wet[0, slot].astype(F32)
    state = states[0]
    if shifts == W_SHIFTS:
        for here, ref in enumerate(states):

            @pl.when(core() == 1 - here)
            def _(ref=ref):
                copy = pltpu.make_async_copy(ref, done, sems.at[0])
                copy.start()
                copy.wait()

        state = done
    copies = []

    def now(field, first):
        return state[field, first : first + ROWS]

    def ground(field, first):
        return terrain[0, slot, field, first : first + ROWS]

    def keep(first, *fields):
        for f, value in enumerate(fields):
            then[f, first : first + ROWS] = value

    def finish(first, *fields):
        for f, value in enumerate(fields):
            done[f, first : first + ROWS] = value
        lines = pl.ds(first, ROWS)
        copies.append(pltpu.make_async_copy(done.at[:, lines], out.at[0, slot, :, lines], sems.at[len(copies)]))
        copies[-1].start()

    shared = (
        lambda at: spill[slot, at],
        lambda at: columns[slot, at],
        lambda q: rows[slot, q : q + 1],
    )
    block_step(now, ground, *shared, 0, wetness, keep)
    block_step(lambda f, first: then[f, first : first + ROWS], ground, *shared, 3, wetness, finish)
    return copies


EDGE_INPUTS = 19
EDGE_SCRATCH = 10


def block_scratch():
    return [pltpu.VMEM((3, SIDE, SIDE), F32)] * 3 + [pltpu.SemaphoreType.DMA((SIDE // ROWS,))] * 2


def early_kernel(dest, *refs):
    ins, refs = refs[:EDGE_INPUTS], refs[EDGE_INPUTS:]
    terrain, spill, own, arrived_a, out, columns, rows = refs[:7]
    edge_scratch, (then, done1, done2, sems1, sems2) = refs[7 : 7 + EDGE_SCRATCH], refs[7 + EDGE_SCRATCH :]
    edges_kernel(*ins, columns, rows, *edge_scratch)
    shared = (dest, ins[1], terrain, columns, rows, spill)
    copies = block(OWN_SHIFTS, *shared, (own,), out, then, done1, sems1)
    later = block(A_SHIFTS, *shared, (arrived_a,), out, then, done2, sems2)
    for copy in copies + later:
        copy.wait()


def early_blocks(dest, edge_inputs, terrain, spill, own, arrived_a):
    return pl.pallas_call(
        early_kernel,
        out_shape=[shape(1, BLOCKS, 3, SIDE, SIDE), shape(BLOCKS, SIDE, HALF), shape(BLOCKS, 8, SIDE)],
        in_specs=[SMEM] * 3 + [VMEM] * (EDGE_INPUTS - 2 + 4),
        out_specs=[HBM, VMEM, VMEM],
        scratch_shapes=[
            pltpu.VMEM((16, 8, SIDE), F32),
            pltpu.VMEM((16, 8, SIDE), F32),
            pltpu.VMEM((8, SIDE), F32),
            pltpu.VMEM((8, SIDE), F32),
            pltpu.VMEM((8, SIDE), F32),
            pltpu.VMEM((5, 8, SIDE), F32),
            pltpu.VMEM((3, 8, SIDE), F32),
            pltpu.VMEM((2, 8, SIDE), F32),
            pltpu.VMEM((2, 8, 8, SIDE), F32),
            pltpu.VMEM((HALF, SIDE), F32),
        ]
        + block_scratch(),
        compiler_params=params(16),
        cost_estimate=cost(0, 0),
    )(dest, *edge_inputs, terrain, spill, own, arrived_a)


def late_kernel(shifts, dest, wet, terrain, columns, rows, spill, *refs):
    out, then, done, sems = refs[-4:]
    shared = (dest, wet, terrain, columns, rows, spill)
    for copy in block(shifts, *shared, refs[:-5], out, then, done, sems):
        copy.wait()


def late_block(shifts, dest, wet, terrain, columns, rows, spill, states, out):
    return pl.pallas_call(
        functools.partial(late_kernel, shifts),
        out_shape=shape(1, BLOCKS, 3, SIDE, SIDE),
        in_specs=[SMEM] * 2 + [VMEM] * 4 + [ANY if shifts == W_SHIFTS else VMEM] * len(states) + [HBM],
        out_specs=HBM,
        input_output_aliases={6 + len(states): 0},
        scratch_shapes=[pltpu.VMEM((3, SIDE, SIDE), F32)] * 2 + [pltpu.SemaphoreType.DMA((SIDE // ROWS,))],
        compiler_params=params(16),
        cost_estimate=cost(0, 0),
    )(dest, wet, terrain, columns, rows, spill, *states, out)


def passed_along(x, axis, by, wrap=True):
    devices = lax.axis_size(axis)
    return lax.ppermute(x, axis, [(i, (i + by) % devices) for i in range(devices)])


def passed_to(x, target):
    devices = lax.axis_size("tile")
    pairs = [(i, target(i // 2, i % 2)) for i in range(devices)]
    return lax.ppermute(x, "tile", [(i, t % devices) for i, t in pairs if t is not None])


def back_one(chip):
    return chip // RING * RING + (chip - 1) % RING


def first_leg(chip, at):
    return 2 * chip + 1 if at == 0 else 2 * back_one(chip)


def second_leg(chip, at):
    sender = chip // RING * RING + (chip + 1) % RING
    return 2 * (sender + 2) if at == 0 else None


def next_chip_swapped(chip, at):
    return 2 * (chip + 1) + 1 - at


def body(flood_state, terrain, destination, wet_mask, neighbours, inflow_cells, inflow_rates):
    dest, state = in_hbm(destination), in_hbm(flood_state)
    block_a, block_w = pick_early(dest, state)
    arrived_a = passed_along(block_a, "tile", 2)
    arrived_w = passed_to(block_w, first_leg)
    own, block_x, ground_low, ground_high, *packs = prepare(
        dest, in_hbm(neighbours), state, block_a, block_w,
        in_hbm(terrain), in_hbm(inflow_cells), in_hbm(inflow_rates),
    )
    ground = (ground_low, ground_high)
    spill, edge_spill = lay_inflow(inflow_cells, inflow_rates)
    packs[5] = passed_along(packs[5], "tile", -1)
    packs[1:3] = [passed_along(packs[d], "tile", d) for d in (1, 2)]
    packs[3], packs[4], arrived_w = gate((packs[3], packs[4], arrived_w), (packs[5], edge_spill))
    packs[3:5] = [passed_along(packs[d], "tile", d) for d in (3, 4)]
    block_x, arrived_w = gate((block_x, arrived_w), (*packs[1:5], arrived_a))
    arrived_x = passed_to(block_x, next_chip_swapped)
    relayed = passed_to(arrived_w, second_leg)
    low, high, wide_low, wide_high, has_low, has_high, far_east, far_west, to_south, to_north = arrange(
        destination, neighbours, packs, ground, edge_spill
    )
    from_north = passed_along(to_south, "grp", -1)
    from_south = passed_along(to_north, "grp", 1)
    edge_inputs = (
        neighbours, wet_mask, edge_spill, low, high, *ground, wide_low, wide_high, has_low, has_high,
        far_east, far_west, packs[1], packs[5], to_south, to_north, from_north, from_south,
    )
    out, columns, rows = early_blocks(destination, edge_inputs, terrain, spill, own, arrived_a)
    shared = (destination, wet_mask, terrain, columns, rows, spill)
    out = late_block(W_SHIFTS, *shared, (arrived_w, relayed), out)
    return late_block(X_SHIFTS, *shared, (arrived_x,), out)


def solution(mesh):
    in_specs = (
        P("grp", "tile", None, None, None),
        P("grp", "tile", None, None, None),
        P("grp", None),
        P("grp", "tile"),
        P("grp", "tile", None),
        P("grp", "tile", None),
        P("grp", "tile", None),
    )
    out_specs = P("grp", "tile", None, None, None)
    return jax.shard_map(body, mesh=mesh, in_specs=in_specs, out_specs=out_specs, check_vma=False)
```

```python
import functools

import jax
import jax.numpy as jnp
from jax import lax
from jax.experimental import pallas as pl
from jax.experimental.pallas import tpu as pltpu
from jax.sharding import PartitionSpec as P

F32 = jnp.float32
GRAVITY = 9.81
SPACING = 10.0
TIMESTEP = 0.2
CENTRE_WEIGHT = 0.7
DEPTH_FLOOR = 0.1
SIDE = 256
HALF = 128
BLOCKS = 4
RIVERS = 16
ROWS = 64
GAIN = TIMESTEP / (SPACING * SPACING)
RATIO = TIMESTEP / SPACING

ANY = pl.BlockSpec(memory_space=pl.ANY)
VMEM = pl.BlockSpec(memory_space=pltpu.VMEM)
SMEM = pl.BlockSpec(memory_space=pltpu.SMEM)
HBM = pl.BlockSpec(memory_space=pltpu.HBM)
RING = 4
OWN_SHIFTS = (0, 0)
A_SHIFTS = (2, 2)
W_SHIFTS = (3, 1)
X_SHIFTS = (1, 3)


def shape(*dims):
    return jax.ShapeDtypeStruct(dims, F32)


def cost(flops, bytes_accessed):
    return pl.CostEstimate(flops=flops, bytes_accessed=bytes_accessed, transcendentals=0)


def face(eta_l, eta_r, z_l, z_r, rough, flow_left, flow_mid, flow_right):
    depth = jnp.maximum(eta_l, eta_r) - jnp.maximum(z_l, z_r)
    floored = jnp.maximum(depth, DEPTH_FLOOR)
    blended = CENTRE_WEIGHT * flow_mid + 0.5 * (1.0 - CENTRE_WEIGHT) * (flow_left + flow_right)
    slope = (GRAVITY * TIMESTEP / SPACING) * depth * (eta_r - eta_l)
    friction = 1.0 + (GRAVITY * TIMESTEP) * rough * rough * jnp.abs(flow_mid) * jnp.exp(
        (-7.0 / 3.0) * jnp.log(floored)
    )
    return (blended - slope) / friction


def core():
    return lax.rem(lax.axis_index("tile"), 2)


def params(mib):
    return pltpu.CompilerParams(vmem_limit_bytes=mib << 20)


def tile_offset(dest_ref, tile, slot):
    tiles = lax.axis_size("tile")
    return lax.rem(lax.div(dest_ref[0, tile * BLOCKS + slot], BLOCKS) - tile + tiles, tiles)


def leaving_slot(dest_ref, shift):
    me = lax.axis_index("tile")
    slot = jnp.int32(0)
    for j in range(1, BLOCKS):
        slot = jnp.where(tile_offset(dest_ref, me, j) == shift, j, slot)
    return slot


def landing_slot(dest_ref, shift, back=0):
    tiles = lax.axis_size("tile")
    sender = lax.rem(lax.axis_index("tile") - shift - back + 2 * tiles, tiles)
    slot = jnp.int32(0)
    for j in range(BLOCKS):
        place = lax.rem(dest_ref[0, sender * BLOCKS + j], BLOCKS)
        slot = jnp.where(tile_offset(dest_ref, sender, j) == shift, place, slot)
    return slot


def lanes(rows, columns):
    return lax.broadcasted_iota(jnp.int32, (rows, columns), 1)


def in_hbm(x):
    return pltpu.with_memory_space_constraint(x, pltpu.HBM)


def pick_kernel(dest, state, block_a, block_w, sems):
    slots = [leaving_slot(dest, k) for k in range(1, BLOCKS)]
    slot_w = jnp.where(core() == 0, slots[0], slots[2])
    loads = [
        pltpu.make_async_copy(state.at[0, slot], ref, sems.at[i])
        for i, (slot, ref) in enumerate(((slots[1], block_a), (slot_w, block_w)))
    ]
    for load in loads:
        load.start()
    for load in loads:
        load.wait()


def pick_early(dest, state):
    return pl.pallas_call(
        pick_kernel,
        out_shape=[shape(3, SIDE, SIDE)] * 2,
        in_specs=[SMEM, HBM],
        out_specs=[VMEM] * 2,
        scratch_shapes=[pltpu.SemaphoreType.DMA((2,))],
        compiler_params=params(4),
        cost_estimate=cost(0, 0),
    )(dest, state)


def prepare_kernel(
    dest, entries, state, block_a, block_w, ground_in, cells, rates,
    own, block_x, low, high, pack0, pack1, pack2, pack3, pack4, pack_back, terrain, sems,
):
    slots = [leaving_slot(dest, k) for k in range(BLOCKS)]
    first_core = core() == 0
    slot_x = jnp.where(first_core, slots[3], slots[1])
    held = (block_x, own)
    loads = [pltpu.make_async_copy(ground_in, terrain, sems.at[3])]
    for i, (slot, ref) in enumerate(zip((slot_x, slots[0]), held)):
        loads.append(pltpu.make_async_copy(state.at[0, slot], ref, sems.at[i]))
    for load in loads:
        load.start()
    lane = lanes(SIDE, HALF)

    def strips(ref, write):
        west = [ref[f, :, :HALF] for f in range(3)]
        east = [ref[f, :, HALF:] for f in range(3)]
        packed = jnp.where(lane < 3, west[0], pltpu.roll(west[1], 3, 1))
        packed = jnp.where(lane < 6, packed, pltpu.roll(west[2], 6, 1))
        packed = jnp.where(lane < 8, packed, pltpu.roll(east[0], 10, 1))
        packed = jnp.where(lane < 10, packed, pltpu.roll(east[1], 13, 1))
        packed = jnp.where(lane < 13, packed, pltpu.roll(east[2], 14, 1))
        turned = packed.T
        south = jnp.concatenate([ref[0, 0:3], ref[2, 0:3], ref[1, 0:2]])
        north = jnp.concatenate(
            [ref[0, SIDE - 2 : SIDE], ref[2, SIDE - 3 : SIDE], ref[1, SIDE - 1 : SIDE], jnp.zeros((2, SIDE), F32)]
        )
        write(turned[0:8], south, turned[8:16], north)

    strip_out = (pack0, pack1, pack2, pack3)
    west_out = (pack_back.at[0], pack0.at[4], pack1.at[5], pack2.at[5])
    east_out = (pack1.at[4], pack2.at[4], pack3.at[4], pack4.at[0])

    def write(k, west, south, east, north):
        for i, value in enumerate((west, south, east, north)):
            strip_out[k][i] = value
        east_out[k][...] = east
        west_out[k][...] = west

    def write_by_core(first, second):
        def both(*values):
            pl.when(first_core)(lambda: write(first, *values))
            pl.when(jnp.logical_not(first_core))(lambda: write(second, *values))

        return both

    strips(block_a, functools.partial(write, 2))
    strips(block_w, write_by_core(1, 3))
    along = lanes(BLOCKS, SIDE)
    spills = [jnp.zeros((BLOCKS, SIDE), F32) for _ in range(2)]
    for p in range(RIVERS):
        cell = cells[0, :, p : p + 1] - along * SIDE
        rate = GAIN * rates[0, :, p : p + 1]
        for i, place in enumerate((0, SIDE - 1)):
            spills[i] = spills[i] + jnp.where(cell == place, rate, 0.0)
    loads[0].wait()
    for b in range(BLOCKS):
        west = [terrain[0, b, f, :, :HALF] for f in range(2)]
        east = [terrain[0, b, f, :, HALF:] for f in range(2)]
        packed = jnp.where(lane < 3, west[0], pltpu.roll(west[1], 3, 1))
        packed = jnp.where(lane < 5, packed, pltpu.roll(east[0], 7, 1))
        packed = jnp.where(lane < 7, packed, pltpu.roll(east[1], 9, 1))
        turned = packed.T
        for q in range(5):
            low[q, b : b + 1] = turned[q : q + 1]
        for q in range(4):
            high[q, b : b + 1] = turned[5 + q : 6 + q]
        for q in range(3):
            low[q, 4 + b : 5 + b] = terrain[0, b, 0, q : q + 1]
        for q in range(2):
            low[3 + q, 4 + b : 5 + b] = terrain[0, b, 1, q : q + 1]
            high[q, 4 + b : 5 + b] = terrain[0, b, 0, SIDE - 2 + q : SIDE - 1 + q]
            high[2 + q, 4 + b : 5 + b] = terrain[0, b, 1, SIDE - 2 + q : SIDE - 1 + q]
    for b in range(BLOCKS):
        line = slice(b, b + 1)
        links = [jnp.full((1, SIDE), entries[0, b, side].astype(F32), F32) for side in (2, 3)]
        blank = [jnp.zeros((1, SIDE), F32)]
        pack1[6 + b] = jnp.concatenate([high[q, line] for q in range(4)] + [spills[1][line]] + links + blank)
        pack_back[1 + b] = jnp.concatenate(
            [low[0, line], low[1, line], low[3, line], spills[0][line]] + links + blank * 2
        )
    writers = (write_by_core(3, 1), functools.partial(write, 0))
    for load, ref, write_out in zip(loads[1:], held, writers):
        load.wait()
        strips(ref, write_out)


def prepare(dest, entries, state, block_a, block_w, terrain, cells, rates):
    packs = [shape(count, 8, SIDE) for count in (5, 10, 6, 5, 1, 5)]
    return pl.pallas_call(
        prepare_kernel,
        out_shape=[shape(3, SIDE, SIDE)] * 2 + [shape(5, 8, SIDE), shape(4, 8, SIDE)] + packs,
        in_specs=[SMEM, SMEM, HBM, VMEM, VMEM, HBM, VMEM, VMEM],
        out_specs=[VMEM] * 10,
        scratch_shapes=[
            pltpu.VMEM((1, BLOCKS, 2, SIDE, SIDE), F32),
            pltpu.SemaphoreType.DMA((BLOCKS,)),
        ],
        compiler_params=params(12),
        cost_estimate=cost(0, 0),
    )(dest, entries, state, block_a, block_w, terrain, cells, rates)


def gate_kernel(count, *refs):
    del count, refs


def gate(values, keys):
    count = len(values)
    return pl.pallas_call(
        functools.partial(gate_kernel, count),
        out_shape=[jax.ShapeDtypeStruct(v.shape, v.dtype) for v in values],
        in_specs=[ANY] * (count + len(keys)),
        out_specs=[ANY] * count,
        input_output_aliases={i: i for i in range(count)},
        compiler_params=params(1),
        cost_estimate=cost(0, 0),
    )(*values, *keys)


def sides_swapped(x):
    return pltpu.roll(x, 4, 0)


def column(x, at):
    return x[:, at : at + 1]


def put_rim(entry, sub, near_state, near_fixed, far_state, far_fixed, wide, has):
    near = jnp.clip(entry, 0, BLOCKS - 1)
    far = jnp.clip(entry - BLOCKS, 0, BLOCKS - 1)
    alive = entry >= 0
    for i, (close, distant) in enumerate(((near_state, far_state), (near_fixed, far_fixed))):
        rows = jnp.where(entry >= BLOCKS, distant(far), close(near))
        rows = jnp.where(alive, rows, 0.0)
        for q in range(8):
            wide[8 * i + q, sub : sub + 1] = rows[q : q + 1]
    has[sub : sub + 1] = jnp.full((1, SIDE), jnp.where(alive, 1.0, 0.0), F32)


def faces_low(low, ground_low, wide):
    h0, h1, h2, q0, q1, q2 = (low[q] for q in range(6))
    z0, z1, z2, n0, n1 = (ground_low[q] for q in range(5))
    hm, qmm, qm, zm, nm = (wide[q] for q in (1, 3, 4, 9, 11))
    return (
        face(hm + zm, h0 + z0, zm, z0, nm, qmm, qm, q0),
        face(h0 + z0, h1 + z1, z0, z1, n0, qm, q0, q1),
        face(h1 + z1, h2 + z2, z1, z2, n1, q0, q1, q2),
    )


def faces_high(high, ground_high, wide):
    hy, hz, qx, qy, qz = (high[q] for q in range(5))
    zy, zz, ny, nz = (ground_high[q] for q in range(4))
    hp, qp, zp = (wide[q] for q in (0, 3, 8))
    return (
        face(hy + zy, hz + zz, zy, zz, ny, qx, qy, qz),
        face(hz + zz, hp + zp, zz, zp, nz, qy, qz, qp),
    )


def arrange_kernel(
    dest, entries, pack0, pack1, pack2, pack3, pack4, pack_back, ground_low, ground_high, edge_spill,
    low, high, wide_low, wide_high, has_low, has_high, far_east, far_west, to_south, to_north,
    west, east,
):
    for out in (low, high, wide_low, wide_high, has_low, has_high):
        out[...] = jnp.zeros_like(out)
    strips = (pack0, pack1, pack2, pack3)
    west_in = (pack_back.at[0], pack0.at[4], pack1.at[5], pack2.at[5])
    east_in = (pack1.at[4], pack2.at[4], pack3.at[4], pack4.at[0])
    for k in range(BLOCKS):
        strip = strips[k]
        slot = landing_slot(dest, k)
        for side in range(2):
            row = pl.ds(side * 4 + slot, 1)
            for q in range(8):
                low[q, row] = strip[side, q : q + 1]
            for q in range(6):
                high[q, row] = strip[2 + side, q : q + 1]
        for i, out in enumerate((west, to_south, east, to_north)):
            out[slot] = strip[i]
        slot = landing_slot(dest, k, 1)
        far_east[slot] = east_in[k][...]
        slot = landing_slot(dest, k, -1)
        far_west[slot] = west_in[k][...]

    def fixed_low(slot):
        row = pl.ds(slot, 1)
        rows = [ground_low[0, row], ground_low[1, row], ground_low[3, row]]
        return jnp.concatenate(rows + [jnp.zeros((5, SIDE), F32)])

    def fixed_high(slot):
        row = pl.ds(slot, 1)
        return jnp.concatenate([ground_high[q, row] for q in range(4)] + [jnp.zeros((4, SIDE), F32)])

    for b in range(BLOCKS):
        put_rim(
            entries[0, b, 0], b, lambda s: east[s], fixed_high,
            lambda s: far_east[s], lambda s: pack1[6 + s], wide_low, has_low,
        )
        put_rim(
            entries[0, b, 1], b, lambda s: west[s], fixed_low,
            lambda s: far_west[s], lambda s: pack_back[1 + s], wide_high, has_high,
        )
    face_m, face_0, _ = faces_low(low, ground_low, wide_low)
    _, face_z = faces_high(high, ground_high, wide_high)
    face_m = face_m * has_low[...]
    face_z = face_z * has_high[...]
    for b in range(BLOCKS):
        sub = slice(4 + b, 5 + b)
        beside = [f[b : b + 1] for f in (face_m, face_0, face_z)]
        blank = [jnp.zeros((1, SIDE), F32)]
        to_north[4 + b] = jnp.concatenate([ground_high[q, sub] for q in range(4)] + [edge_spill[2, sub]] + beside)
        to_south[4 + b] = jnp.concatenate(
            [ground_low[0, sub], ground_low[1, sub], ground_low[3, sub], edge_spill[0, sub]] + beside + blank
        )
        passed = jnp.concatenate(
            [
                far_east[b, 1:2], far_east[b, 5:6], pack1[6 + b, 1:2], pack1[6 + b, 3:4],
                far_west[b, 0:1], far_west[b, 6:7], pack_back[1 + b, 0:1], pack_back[1 + b, 2:3],
            ]
        )
        to_north[8 + b] = passed
        to_south[8 + b] = passed


def arrange(dest, entries, packs, ground, edge_spill):
    outs = [(8, 8), (6, 8), (16, 8), (16, 8), (8,), (8,), (BLOCKS, 8), (BLOCKS, 8), (3 * BLOCKS, 8), (3 * BLOCKS, 8)]
    return pl.pallas_call(
        arrange_kernel,
        out_shape=[shape(*dims, SIDE) for dims in outs],
        in_specs=[SMEM] * 2 + [VMEM] * 9,
        out_specs=[VMEM] * len(outs),
        scratch_shapes=[pltpu.VMEM((BLOCKS, 8, SIDE), F32)] * 2,
        compiler_params=params(4),
        cost_estimate=cost(0, 0),
    )(dest, entries, *packs, *ground, edge_spill)


def along_edge(h, z, rough, flow, face_before, face_first, face_last):
    lane = lanes(8, SIDE)
    eta = h + z
    flux = face(
        eta, pltpu.roll(eta, SIDE - 1, 1), z, pltpu.roll(z, SIDE - 1, 1), rough,
        pltpu.roll(flow, 1, 1), flow, pltpu.roll(flow, SIDE - 1, 1),
    )
    flux = jnp.where(lane == 0, face_first, flux)
    flux = jnp.where(lane == SIDE - 1, face_last, flux)
    lower = jnp.where(lane == 0, face_before, pltpu.roll(flux, 1, 1))
    return lower - flux


def corner_faces(h, z, rough, flow, entry_s, entry_n, corners_s, corners_n):
    def chosen(entry, corners, q):
        value = jnp.zeros((8, SIDE), F32)
        for j in range(2 * BLOCKS):
            value = jnp.where(entry == j, corners[q][j : j + 1], value)
        return value

    h_s, t_s, z_s, n_s = (chosen(entry_s, corners_s, q) for q in range(4))
    h_n, t_n, z_n = (chosen(entry_n, corners_n, q) for q in range(3))
    last = SIDE - 1
    has_s = jnp.where(column(entry_s, 0) >= 0.0, 1.0, 0.0)
    has_n = jnp.where(column(entry_n, 0) >= 0.0, 1.0, 0.0)
    eta, eta_s, eta_n = h + z, h_s + z_s, h_n + z_n
    before = face(
        column(eta_s, last), column(eta, 0), column(z_s, last), column(z, 0), column(n_s, last),
        column(t_s, last - 1), column(t_s, last), column(flow, 0),
    ) * has_s
    first = face(
        column(eta, 0), column(eta, 1), column(z, 0), column(z, 1), column(rough, 0),
        column(t_s, last), column(flow, 0), column(flow, 1),
    )
    final = face(
        column(eta, last), column(eta_n, 0), column(z, last), column(z_n, 0), column(rough, last),
        column(flow, last - 1), column(flow, last), column(t_n, 0),
    ) * has_n
    return before, first, final


def edges_kernel(
    entries, wet, edge_spill, low, high, ground_low, ground_high, wide_low_in, wide_high_in, has_low_in, has_high_in,
    far_east, far_west, pack1, pack_back, to_south, to_north, from_north, from_south,
    columns, rows,
    wide_low, wide_high, has_low, has_high, wetness, edge, rim_low, rim_high, corners, stack,
):
    wide_low[...] = wide_low_in[...]
    wide_high[...] = wide_high_in[...]
    has_low[...] = has_low_in[...]
    has_high[...] = has_high_in[...]
    for b in range(BLOCKS):
        value = jnp.full((1, SIDE), wet[0, b].astype(F32), F32)
        wetness[b : b + 1] = value
        wetness[4 + b : 5 + b] = value
        for entry, near, far, wide, has in (
            (entries[0, b, 2], to_north, from_south, wide_low, has_low),
            (entries[0, b, 3], to_south, from_north, wide_high, has_high),
        ):
            put_rim(
                entry, 4 + b, lambda s, r=near: r[s], lambda s, r=near: r[BLOCKS + s],
                lambda s, r=far: r[s], lambda s, r=far: r[BLOCKS + s], wide, has,
            )
    for j in range(BLOCKS):
        near = slice(j, j + 1)
        far = slice(BLOCKS + j, BLOCKS + j + 1)
        for q, row in enumerate(
            (
                far_east[j, 1:2], far_east[j, 5:6], pack1[6 + j, 1:2], pack1[6 + j, 3:4],
                far_west[j, 0:1], far_west[j, 6:7], pack_back[1 + j, 0:1], pack_back[1 + j, 2:3],
            )
        ):
            for i, passed in enumerate((from_south, from_north)):
                corners[i, q, near] = row
                corners[i, q, far] = passed[2 * BLOCKS + j, q : q + 1]

    def seen(i, first):
        return [corners[i, first + q] for q in range(4)]

    h0, h1, h2, q0, q1, q2, t0, t1 = (low[q] for q in range(8))
    z0, z1, z2, n0, n1 = (ground_low[q] for q in range(5))
    hy, hz, qx, qy, qz, tz = (high[q] for q in range(6))
    zy, zz, ny, nz = (ground_high[q] for q in range(4))
    face_m, face_0, face_1 = faces_low(low, ground_low, wide_low)
    face_y, face_z = faces_high(high, ground_high, wide_high)
    face_m = face_m * has_low[...]
    face_z = face_z * has_high[...]
    swapped = [sides_swapped(f) for f in (face_m, face_0, face_z)]

    def beside(spot):
        return [column(f, spot) for f in swapped]

    wets = wetness[...]
    last = SIDE - 1
    new_0 = (h0 + RATIO * (face_m - face_0 + along_edge(h0, z0, n0, t0, *beside(0))) + edge_spill[0]) * wets
    new_1 = (h1 + RATIO * (face_0 - face_1 + along_edge(h1, z1, n1, t1, *beside(1))) + edge_spill[1]) * wets
    new_z = (hz + RATIO * (face_y - face_z + along_edge(hz, zz, nz, tz, *beside(last))) + edge_spill[2]) * wets
    flow_0, flow_1, flow_y, flow_z = (f * wets for f in (face_0, face_1, face_y, face_z))
    for i, value in enumerate((new_z, flow_y, flow_z, new_0, flow_0)):
        edge[i] = value

    sides = lax.broadcasted_iota(jnp.int32, (8, 1), 0) < 4
    ghy, ghz, gqx, gqy, gqz, gtz = (wide_low[q] for q in range(6))
    gzy, gzz, gny, gnz, gspill = (wide_low[8 + q] for q in range(5))
    across = corner_faces(ghz, gzz, gnz, gtz, wide_low[13], wide_low[14], seen(0, 0), seen(1, 0))
    given = [column(wide_low[13 + q], last) for q in range(3)]
    ends = [jnp.where(sides, a, g) for a, g in zip(across, given)]
    far_face = face(ghy + gzy, ghz + gzz, gzy, gzz, gny, gqx, gqy, gqz)
    far_low = (
        ghz + RATIO * (far_face - face_m + along_edge(ghz, gzz, gnz, gtz, *ends)) + gspill,
        far_face,
        face_m,
    )
    gh0, gh1, gq0, gq1, gt0 = (wide_high[q] for q in (0, 1, 3, 4, 6))
    gz0, gz1, gn0, gspill = (wide_high[8 + q] for q in range(4))
    across = corner_faces(gh0, gz0, gn0, gt0, wide_high[12], wide_high[13], seen(0, 4), seen(1, 4))
    given = [column(wide_high[12 + q], 0) for q in range(3)]
    ends = [jnp.where(sides, a, g) for a, g in zip(across, given)]
    far_face = face(gh0 + gz0, gh1 + gz1, gz0, gz1, gn0, qz, gq0, gq1)
    far_high = (
        gh0 + RATIO * (face_z - far_face + along_edge(gh0, gz0, gn0, gt0, *ends)) + gspill,
        far_face,
    )
    for rim, far_rows, first, group in ((rim_low, far_low, 0, 0), (rim_high, far_high, 3, 1)):
        for q, far_row in enumerate(far_rows):
            rim[q] = far_row
        for b in range(BLOCKS):
            for side in range(2):
                entry = entries[0, b, 2 * side + group]
                sub = slice(side * 4 + b, side * 4 + b + 1)
                near = pl.ds(side * 4 + jnp.clip(entry, 0, BLOCKS - 1), 1)
                for q in range(len(far_rows)):
                    row = jnp.where(entry >= BLOCKS, rim[q, sub], edge[first + q, near])
                    rim[q, sub] = jnp.where(entry >= 0, row, 0.0)

    hm, qmm, qm = (rim_low[q] for q in range(3))
    hp, qp = (rim_high[q] for q in range(2))
    zm, nm, zp = wide_low[9], wide_low[11], wide_high[8]
    next_m = face(hm + zm, new_0 + z0, zm, z0, nm, qmm, qm, flow_0) * has_low[...]
    next_0 = face(new_0 + z0, new_1 + z1, z0, z1, n0, qm, flow_0, flow_1)
    next_z = face(new_z + zz, hp + zp, zz, zp, nz, flow_y, flow_z, qp) * has_high[...]
    stack[...] = jnp.zeros_like(stack)
    rows[...] = jnp.zeros_like(rows)
    for b in range(BLOCKS):
        for i, value in enumerate((face_m, face_0, face_z, next_m, next_0, next_z)):
            stack[b * 8 + i : b * 8 + i + 1] = value[b : b + 1]
            rows[b, i : i + 1] = value[4 + b : 5 + b]
    turned = stack[...].T
    columns[0] = turned
    for b in range(1, BLOCKS):
        columns[b] = pltpu.roll(turned, HALF - 8 * b, 1)


def inflow_kernel(cells, rates, spill, edge_spill):
    spill[...] = jnp.zeros_like(spill)
    edge_spill[...] = jnp.zeros_like(edge_spill)
    lane = lanes(1, SIDE)
    for b in range(BLOCKS):

        def point(p, carry, b=b):
            cell = cells[0, b, p]
            row = lax.div(cell, SIDE)
            column = lax.rem(cell, SIDE)
            rate = GAIN * rates[0, b, p]
            at_column = jnp.where(lane == column, rate, 0.0)
            at_row = jnp.where(lane == row, rate, 0.0)
            line = pl.ds(row, 1)
            spill[b, line] = spill[b, line] + at_column
            for i, place in enumerate((0, 1, SIDE - 1)):
                edge_spill[i, b : b + 1] += jnp.where(column == place, at_row, 0.0)
                edge_spill[i, 4 + b : 5 + b] += jnp.where(row == place, at_column, 0.0)
            return carry

        lax.fori_loop(0, RIVERS, point, 0)


def lay_inflow(cells, rates):
    return pl.pallas_call(
        inflow_kernel,
        out_shape=[shape(BLOCKS, SIDE, SIDE), shape(3, 8, SIDE)],
        in_specs=[SMEM, SMEM],
        out_specs=[VMEM] * 2,
        compiler_params=params(4),
        cost_estimate=cost(0, 0),
    )(cells, rates)


def block_step(now, ground, spill, columns, rows, base, wetness, write):
    lane = lanes(ROWS, SIDE)
    sub = lax.broadcasted_iota(jnp.int32, (ROWS, SIDE), 0)

    def at(load, field, first, shift):
        if 0 <= first + shift <= SIDE - ROWS:
            return load(field, first + shift)
        return pltpu.roll(load(field, first), -shift % ROWS, 0)

    below = rows(base)
    for first in range(0, SIDE, ROWS):
        h, qx, qy = (at(now, f, first, 0) for f in range(3))
        z, rough = (at(ground, f, first, 0) for f in range(2))
        eta = h + z
        flux_x = face(
            eta, pltpu.roll(eta, SIDE - 1, 1), z, pltpu.roll(z, SIDE - 1, 1), rough,
            pltpu.roll(qx, 1, 1), qx, pltpu.roll(qx, SIDE - 1, 1),
        )
        edge = columns(pl.ds(first, ROWS))
        flux_x = jnp.where(lane == 0, edge[:, base + 1 : base + 2], flux_x)
        flux_x = jnp.where(lane == SIDE - 1, edge[:, base + 2 : base + 3], flux_x)
        flux_w = jnp.where(lane == 0, edge[:, base : base + 1], pltpu.roll(flux_x, 1, 1))
        z_up = at(ground, 0, first, 1)
        flux_y = face(
            eta, at(now, 0, first, 1) + z_up, z, z_up, rough, at(now, 2, first, -1), qy, at(now, 2, first, 1)
        )
        if first == 0:
            flux_y = jnp.where(sub == 0, rows(base + 1), flux_y)
        if first == SIDE - ROWS:
            flux_y = jnp.where(sub == ROWS - 1, rows(base + 2), flux_y)
        flux_s = jnp.where(sub == 0, below, pltpu.roll(flux_y, 1, 0))
        below = flux_y[ROWS - 1 : ROWS]
        depth = h + RATIO * (flux_w - flux_x + flux_s - flux_y) + spill(pl.ds(first, ROWS))
        write(first, depth * wetness, flux_x * wetness, flux_y * wetness)


def block(shifts, dest, wet, terrain, columns, rows, spill, states, out, then, done, sems):
    slot = landing_slot(dest, jnp.where(core() == 0, *shifts))
    wetness = wet[0, slot].astype(F32)
    state = states[0]
    if shifts == W_SHIFTS:
        for here, ref in enumerate(states):

            @pl.when(core() == 1 - here)
            def _(ref=ref):
                copy = pltpu.make_async_copy(ref, done, sems.at[0])
                copy.start()
                copy.wait()

        state = done
    copies = []

    def now(field, first):
        return state[field, first : first + ROWS]

    def ground(field, first):
        return terrain[0, slot, field, first : first + ROWS]

    def keep(first, *fields):
        for f, value in enumerate(fields):
            then[f, first : first + ROWS] = value

    def finish(first, *fields):
        for f, value in enumerate(fields):
            done[f, first : first + ROWS] = value
        lines = pl.ds(first, ROWS)
        copies.append(pltpu.make_async_copy(done.at[:, lines], out.at[0, slot, :, lines], sems.at[len(copies)]))
        copies[-1].start()

    shared = (
        lambda at: spill[slot, at],
        lambda at: columns[slot, at],
        lambda q: rows[slot, q : q + 1],
    )
    block_step(now, ground, *shared, 0, wetness, keep)
    block_step(lambda f, first: then[f, first : first + ROWS], ground, *shared, 3, wetness, finish)
    return copies


EDGE_INPUTS = 19
EDGE_SCRATCH = 10


def block_scratch():
    return [pltpu.VMEM((3, SIDE, SIDE), F32)] * 3 + [pltpu.SemaphoreType.DMA((SIDE // ROWS,))] * 2


def early_kernel(dest, *refs):
    ins, refs = refs[:EDGE_INPUTS], refs[EDGE_INPUTS:]
    terrain, spill, own, arrived_a, out, columns, rows = refs[:7]
    edge_scratch, (then, done1, done2, sems1, sems2) = refs[7 : 7 + EDGE_SCRATCH], refs[7 + EDGE_SCRATCH :]
    edges_kernel(*ins, columns, rows, *edge_scratch)
    shared = (dest, ins[1], terrain, columns, rows, spill)
    copies = block(OWN_SHIFTS, *shared, (own,), out, then, done1, sems1)
    later = block(A_SHIFTS, *shared, (arrived_a,), out, then, done2, sems2)
    for copy in copies + later:
        copy.wait()


def early_blocks(dest, edge_inputs, terrain, spill, own, arrived_a):
    return pl.pallas_call(
        early_kernel,
        out_shape=[shape(1, BLOCKS, 3, SIDE, SIDE), shape(BLOCKS, SIDE, HALF), shape(BLOCKS, 8, SIDE)],
        in_specs=[SMEM] * 3 + [VMEM] * (EDGE_INPUTS - 2 + 4),
        out_specs=[HBM, VMEM, VMEM],
        scratch_shapes=[
            pltpu.VMEM((16, 8, SIDE), F32),
            pltpu.VMEM((16, 8, SIDE), F32),
            pltpu.VMEM((8, SIDE), F32),
            pltpu.VMEM((8, SIDE), F32),
            pltpu.VMEM((8, SIDE), F32),
            pltpu.VMEM((5, 8, SIDE), F32),
            pltpu.VMEM((3, 8, SIDE), F32),
            pltpu.VMEM((2, 8, SIDE), F32),
            pltpu.VMEM((2, 8, 8, SIDE), F32),
            pltpu.VMEM((HALF, SIDE), F32),
        ]
        + block_scratch(),
        compiler_params=params(16),
        cost_estimate=cost(0, 0),
    )(dest, *edge_inputs, terrain, spill, own, arrived_a)


def late_kernel(shifts, dest, wet, terrain, columns, rows, spill, *refs):
    out, then, done, sems = refs[-4:]
    shared = (dest, wet, terrain, columns, rows, spill)
    for copy in block(shifts, *shared, refs[:-5], out, then, done, sems):
        copy.wait()


def late_block(shifts, dest, wet, terrain, columns, rows, spill, states, out):
    return pl.pallas_call(
        functools.partial(late_kernel, shifts),
        out_shape=shape(1, BLOCKS, 3, SIDE, SIDE),
        in_specs=[SMEM] * 2 + [VMEM] * 4 + [ANY if shifts == W_SHIFTS else VMEM] * len(states) + [HBM],
        out_specs=HBM,
        input_output_aliases={6 + len(states): 0},
        scratch_shapes=[pltpu.VMEM((3, SIDE, SIDE), F32)] * 2 + [pltpu.SemaphoreType.DMA((SIDE // ROWS,))],
        compiler_params=params(16),
        cost_estimate=cost(0, 0),
    )(dest, wet, terrain, columns, rows, spill, *states, out)


def passed_along(x, axis, by, wrap=True):
    devices = lax.axis_size(axis)
    return lax.ppermute(x, axis, [(i, (i + by) % devices) for i in range(devices)])


def passed_to(x, target):
    devices = lax.axis_size("tile")
    pairs = [(i, target(i // 2, i % 2)) for i in range(devices)]
    return lax.ppermute(x, "tile", [(i, t % devices) for i, t in pairs if t is not None])


def back_one(chip):
    return chip // RING * RING + (chip - 1) % RING


def first_leg(chip, at):
    return 2 * chip + 1 if at == 0 else 2 * back_one(chip)


def second_leg(chip, at):
    sender = chip // RING * RING + (chip + 1) % RING
    return 2 * (sender + 2) if at == 0 else None


def next_chip_swapped(chip, at):
    return 2 * (chip + 1) + 1 - at


def body(flood_state, terrain, destination, wet_mask, neighbours, inflow_cells, inflow_rates):
    dest, state = in_hbm(destination), in_hbm(flood_state)
    block_a, block_w = pick_early(dest, state)
    arrived_a = passed_along(block_a, "tile", 2)
    arrived_w = passed_to(block_w, first_leg)
    own, block_x, ground_low, ground_high, *packs = prepare(
        dest, in_hbm(neighbours), state, block_a, block_w,
        in_hbm(terrain), in_hbm(inflow_cells), in_hbm(inflow_rates),
    )
    ground = (ground_low, ground_high)
    spill, edge_spill = lay_inflow(inflow_cells, inflow_rates)
    packs[5] = passed_along(packs[5], "tile", -1)
    packs[1:3] = [passed_along(packs[d], "tile", d) for d in (1, 2)]
    packs[3], packs[4], arrived_w = gate((packs[3], packs[4], arrived_w), (packs[5],))
    packs[3:5] = [passed_along(packs[d], "tile", d) for d in (3, 4)]
    block_x, arrived_w = gate((block_x, arrived_w), (*packs[1:5], arrived_a, edge_spill))
    arrived_x = passed_to(block_x, next_chip_swapped)
    relayed = passed_to(arrived_w, second_leg)
    low, high, wide_low, wide_high, has_low, has_high, far_east, far_west, to_south, to_north = arrange(
        destination, neighbours, packs, ground, edge_spill
    )
    from_north = passed_along(to_south, "grp", -1)
    from_south = passed_along(to_north, "grp", 1)
    edge_inputs = (
        neighbours, wet_mask, edge_spill, low, high, *ground, wide_low, wide_high, has_low, has_high,
        far_east, far_west, packs[1], packs[5], to_south, to_north, from_north, from_south,
    )
    out, columns, rows = early_blocks(destination, edge_inputs, terrain, spill, own, arrived_a)
    shared = (destination, wet_mask, terrain, columns, rows, spill)
    out = late_block(W_SHIFTS, *shared, (arrived_w, relayed), out)
    return late_block(X_SHIFTS, *shared, (arrived_x,), out)


def solution(mesh):
    in_specs = (
        P("grp", "tile", None, None, None),
        P("grp", "tile", None, None, None),
        P("grp", None),
        P("grp", "tile"),
        P("grp", "tile", None),
        P("grp", "tile", None),
        P("grp", "tile", None),
    )
    out_specs = P("grp", "tile", None, None, None)
    return jax.shard_map(body, mesh=mesh, in_specs=in_specs, out_specs=out_specs, check_vma=False)
```
